32 devices in a mesh: section: 2 (over core), seq: 4 (over y, x), fsdp: 4 (over z).
Axes of the slice: x: 2, y: 2, z: 4, core: 2. Of those that a mesh axis runs over, the one named last changes fastest.
Arguments:
- tokens: bfloat16 [2, 4, 256, 1536], P(None, 'fsdp', 'seq'), may hold values from -6 to 6
- cotangent: bfloat16 [2, 4, 256, 1536], P(None, 'fsdp', 'seq'), may hold values from -6 to 6
- norm_gain: float32 [2, 1536], P('section'), may hold values from 0.25 to 1.75
- w_in: bfloat16 [2, 1536, 6448], P('section', 'fsdp'), may hold values from -0.15625 to 0.15625
- conv_weight: float32 [2, 4, 3328], P('section'), may hold values from -3 to 3
- conv_bias: float32 [2, 3328], P('section'), may hold values from -3 to 3
- dt_bias: float32 [2, 48], P('section'), may hold values from -4 to -2
- a_log: float32 [2, 48], P('section'), as said below
- skip_gain: float32 [2, 48], P('section'), may hold values from 0.5 to 1.5
- gate_gain: float32 [2, 3072], P('section'), may hold values from 0.25 to 1.75
- w_out: bfloat16 [2, 3072, 1536], P('section', 'fsdp'), may hold values from -0.109375 to 0.109375
Outputs:
- layer_out: bfloat16 [2, 2, 4, 256, 1536], P('section', None, 'fsdp', 'seq')
- input_grad: bfloat16 [2, 2, 4, 256, 1536], P('section', None, 'fsdp', 'seq')
- grad_norm_gain: float32 [2, 1536], P('section')
- grad_w_in: float32 [2, 1536, 6448], P('section', 'fsdp')
- grad_conv_weight: float32 [2, 4, 3328], P('section')
- grad_conv_bias: float32 [2, 3328], P('section')
- grad_dt_bias: float32 [2, 48], P('section')
- grad_a_log: float32 [2, 48], P('section')
- grad_skip_gain: float32 [2, 48], P('section')
- grad_gate_gain: float32 [2, 3072], P('section')
- grad_w_out: float32 [2, 3072, 1536], P('section', 'fsdp')
The draws below stay inside these ranges and needn't reach their ends.
Inputs may be any that keep to these rules, and one draw needn't show every extreme that they name: exp(a_log) is the decay coefficient of each head.
All inputs are finite; a program needn't handle non-finite values.
Results may differ from the reference program's by a relative error of at most 0.025.
The reference program's roundings to bfloat16 on the way count: a program that leaves them out, or rounds other values in their place, can miss the bound.
Values may be sent and summed in bfloat16 or wider, within the bound.
A program may use at most 256 MiB of HBM per device.

```python
import math
from functools import partial
import jax
import jax.numpy as jnp
from jax import lax

D = 1536
HEADS = 48
HEADDIM = 64
STATE = 128
CONV = 4
SPAN = 256
MICRO = 2
INNER = 3072
XBC = 3328
PROJ = 6448
LEN = 256
SEQS = 4
LAYERS = 2


def draw_a_log(key, part):
    key = jax.random.fold_in(key, 11)
    level_key = jax.random.fold_in(key, 1)
    shape = (LAYERS, HEADS)
    slow_low = math.log(0.2 / LEN)
    level = jax.random.uniform(level_key, shape, jnp.float32)
    log_rate = slow_low + (math.log(1.0 / 30.0) - slow_low) * level
    return log_rate - math.log(0.08)


def level_of(own_key, shape, cuts, least, largest):
    loudness = 1.0
    for position, parts in cuts:
        heights = jax.random.uniform(jax.random.fold_in(jax.random.fold_in(own_key, 6), position), (parts,), jnp.float32, least / len(cuts), largest / len(cuts))
        loudness = loudness * jnp.repeat(jnp.exp(heights), shape[position] // parts).reshape((-1,) + (1,) * (len(shape) - 1 - position))
    return loudness


def centred(rng, shape, spread, bound, cuts=(), kind=jnp.bfloat16):
    result = jax.random.normal(rng, shape, jnp.float32) * spread
    if len(cuts) > 0:
        result = level_of(rng, shape, cuts, -0.22, 0.18) * result
    return jnp.clip(result, min=-bound, max=bound).astype(kind)


def setup_inputs(seed: int = 0) -> dict:
    keys = jax.random.split(jax.random.key(seed), 12)
    return {
        "tokens": centred(keys[0], (MICRO, SEQS, LEN, D), 1.0, 6.0, ((1, 4), (2, 4))),
        "cotangent": centred(keys[1], (MICRO, SEQS, LEN, D), 1.0, 6.0, ((1, 4), (2, 4))),
        "norm_gain": jnp.clip(1.0 + 0.15 * jax.random.normal(keys[2], (LAYERS, D), jnp.float32), 0.25, 1.75),
        "w_in": centred(keys[3], (LAYERS, D, PROJ), D ** -0.5, 0.15625, ((0, 2), (1, 4))),
        "conv_weight": centred(keys[4], (LAYERS, CONV, XBC), CONV ** -0.5, 3.0, ((0, 2),), jnp.float32),
        "conv_bias": centred(keys[5], (LAYERS, XBC), 0.5, 3.0, ((0, 2),), jnp.float32),
        "dt_bias": jnp.clip(-4.0 + 2.0 * jax.random.uniform(keys[6], (LAYERS, HEADS), jnp.float32) ** level_of(keys[6], (LAYERS, HEADS), ((0, 2),), -0.2, 0.2), -4.0, -2.0),
        "a_log": draw_a_log(jax.random.fold_in(keys[11], 71), 0),
        "skip_gain": jnp.clip(0.5 + 1.0 * jax.random.uniform(keys[8], (LAYERS, HEADS), jnp.float32) ** level_of(keys[8], (LAYERS, HEADS), ((0, 2),), -0.2, 0.2), 0.5, 1.5),
        "gate_gain": jnp.clip(1.0 + 0.15 * jax.random.normal(keys[9], (LAYERS, INNER), jnp.float32), 0.25, 1.75),
        "w_out": centred(keys[10], (LAYERS, INNER, D), INNER ** -0.5, 0.109375, ((0, 2), (1, 4))),
    }


HIGHEST_PRECISION = lax.Precision.HIGHEST
NORM_EPS = 1e-05

@jax.custom_vjp
def low(v):
    return lax.optimization_barrier(v.astype(jnp.bfloat16)).astype(jnp.float32)

@jax.custom_vjp
def low_back(v):
    return v

def low_keep(v):
    return (low(v), None)

def low_pass(kept, grad):
    return (grad,)

def back_keep(v):
    return (v, None)

def back_low(kept, grad):
    return (low(grad),)
low.defvjp(low_keep, low_pass)
low_back.defvjp(back_keep, back_low)

def mix_heads(head_inputs, step_size, decay_rates, state_in, state_out, skip_terms):
    length, head_count, head_width = head_inputs.shape
    blocks = length // SPAN
    row_ids = lax.broadcasted_iota(jnp.int32, (SPAN, SPAN), 0)
    col_ids = lax.broadcasted_iota(jnp.int32, (SPAN, SPAN), 1)
    causal = (row_ids >= col_ids)[:, :, None]

    def advance(carry_state, pieces):
        block_x, block_dt, block_b, block_c = pieces
        log_decay = jnp.cumsum(-decay_rates[None, :] * block_dt, axis=0)
        log_gaps = jnp.where(causal, log_decay[:, None, :] - log_decay[None, :, :], 0.0)
        decay_mask = jnp.where(causal, jnp.exp(log_gaps), 0.0)
        scores = jnp.dot(block_c, block_b.T, precision=HIGHEST_PRECISION)
        weights = low(scores[:, :, None] * decay_mask * block_dt[None, :, :])
        within = jnp.einsum('tsh,shp->thp', weights, block_x, precision=HIGHEST_PRECISION)
        carried = jnp.einsum('tn,hnp->thp', block_c, low(carry_state), precision=HIGHEST_PRECISION)
        carried = carried * jnp.exp(log_decay)[:, :, None]
        tail_decay = jnp.exp(log_decay[-1][None, :] - log_decay) * block_dt
        shaped = low(block_b[:, None, :] * tail_decay[:, :, None])
        fresh_state = jnp.einsum('shn,shp->hnp', shaped, block_x, precision=HIGHEST_PRECISION)
        carry_state = jnp.exp(log_decay[-1])[:, None, None] * carry_state + fresh_state
        return (carry_state, within + carried + skip_terms[None, :, None] * block_x)
    pieces = (head_inputs.reshape(blocks, SPAN, head_count, head_width), step_size.reshape(blocks, SPAN, head_count), state_in.reshape(blocks, SPAN, state_in.shape[1]), state_out.reshape(blocks, SPAN, state_out.shape[1]))
    initial = jnp.zeros((head_count, state_in.shape[1], head_width), jnp.float32)
    _, results = lax.scan(jax.checkpoint(advance), initial, pieces)
    return results.reshape(length, head_count, head_width)

def mamba_layer(rows_in, norm_gain, w_in, conv_weight, conv_bias, dt_bias, a_log, skip_gain, gate_gain, w_out):
    length = rows_in.shape[0]
    row_scale = lax.rsqrt(lax.optimization_barrier(jnp.mean(rows_in * rows_in, axis=-1, keepdims=True)) + NORM_EPS)
    normed = low(rows_in * row_scale * norm_gain)
    projected = low_back(jnp.dot(normed, w_in, precision=HIGHEST_PRECISION))
    gate_part = projected[:, :INNER]
    xbc_raw = low(projected[:, INNER:INNER + XBC])
    dt_raw = low(projected[:, INNER + XBC:])
    padded = jnp.pad(xbc_raw, ((CONV - 1, 0), (0, 0)))
    conv_sum = conv_bias[None, :] + conv_weight[0][None, :] * padded[0:length]
    for offset in range(1, CONV):
        conv_sum = conv_sum + conv_weight[offset][None, :] * padded[offset:offset + length]
    activated = low(jax.nn.silu(conv_sum))
    head_inputs = activated[:, :INNER].reshape(length, HEADS, HEADDIM)
    step_size = jax.nn.softplus(dt_raw + dt_bias[None, :])
    mixed = mix_heads(head_inputs, step_size, jnp.exp(a_log), activated[:, INNER:INNER + STATE], activated[:, INNER + STATE:], skip_gain)
    mixed = low_back(low(mixed.reshape(length, INNER)))
    gated = mixed * jax.nn.silu(gate_part)
    gscale = lax.rsqrt(lax.optimization_barrier(jnp.mean(gated * gated, axis=-1, keepdims=True)) + NORM_EPS)
    normed_out = low(gated * gscale * gate_gain)
    return rows_in + jnp.dot(normed_out, w_out, precision=HIGHEST_PRECISION)

def apply_layer(weights, sequence):
    return mamba_layer(sequence, *weights)

def forward(rows, probes, params):
    values = []
    for layer_index in range(LAYERS):
        weights = tuple((param_set[layer_index] for param_set in params))
        if layer_index > 0:
            rows = low_back(low(rows))
        rows = rows + probes[layer_index]
        rows = lax.map(jax.checkpoint(partial(apply_layer, weights)), rows)
        values.append(low(rows))
    return (rows, jnp.stack(values))

def reference(tokens, cotangent, norm_gain, w_in, conv_weight, conv_bias, dt_bias, a_log, skip_gain, gate_gain, w_out):
    params = (norm_gain, w_in.astype(jnp.float32), conv_weight, conv_bias, dt_bias, a_log, skip_gain, gate_gain, w_out.astype(jnp.float32))
    flat = tokens.astype(jnp.float32).reshape(MICRO * SEQS, LEN, D)
    probes = jnp.zeros((LAYERS, MICRO * SEQS, LEN, D), jnp.float32)
    _, pullback, layer_vals = jax.vjp(forward, flat, probes, params, has_aux=True)
    _, probe_grads, grads = pullback(cotangent.astype(jnp.float32).reshape(MICRO * SEQS, LEN, D))
    shape = (LAYERS, MICRO, SEQS, LEN, D)
    return (layer_vals.reshape(shape).astype(jnp.bfloat16), probe_grads.reshape(shape).astype(jnp.bfloat16), grads[0], grads[1], grads[2], grads[3], grads[4], grads[5], grads[6], grads[7], grads[8])
```

```python
from functools import partial

import jax
import jax.numpy as jnp
from jax import lax
from jax.experimental import pallas as pl
from jax.experimental.pallas import tpu as pltpu
from jax.sharding import PartitionSpec as P

HEADS = 48
HEADDIM = 64
STATE = 128
CONV = 4
SPAN = 256
INNER = 3072
XBC = 3328
SHARED = 2 * STATE
LANES = 128
NORM_EPS = 1e-05
HIGHEST = lax.Precision.HIGHEST
BF16 = jnp.bfloat16
F32 = jnp.float32


def dot(left, right, contract=((1,), (0,)), precision=None):
    return lax.dot_general(
        left, right, (contract, ((), ())), preferred_element_type=F32, precision=precision
    )


def dot_nt(left, right):
    return dot(left, right, ((1,), (1,)))


def dot_tn(left, right):
    return dot(left, right, ((0,), (0,)))


def sigmoid(value):
    return 1.0 / (1.0 + jnp.exp(-value))


def shifted(value, distance):
    if distance == 0:
        return value
    length = value.shape[0]
    rows = lax.broadcasted_iota(jnp.int32, value.shape, 0)
    moved = pltpu.roll(value, distance % length, 0)
    if distance > 0:
        return jnp.where(rows >= distance, moved, 0.0)
    return jnp.where(rows < length + distance, moved, 0.0)


def conv_sum(raw, taps):
    total = taps[CONV : CONV + 1]
    for k in range(CONV):
        total = total + taps[k : k + 1] * shifted(raw, CONV - 1 - k)
    return total


def conv_back(grad, raw, taps):
    grad_raw = 0.0
    rows = []
    for k in range(CONV):
        grad_raw = grad_raw + taps[k : k + 1] * shifted(grad, -(CONV - 1 - k))
        rows.append(jnp.sum(grad * shifted(raw, CONV - 1 - k), axis=0, keepdims=True))
    rows.append(jnp.sum(grad, axis=0, keepdims=True))
    return grad_raw, rows


def stacked(rows, count):
    width = rows[0].shape[1]
    short = count - len(rows)
    return jnp.concatenate(rows + [jnp.zeros((short, width), F32)], axis=0)


def triangles():
    row_ids = lax.broadcasted_iota(jnp.int32, (SPAN, SPAN), 0)
    col_ids = lax.broadcasted_iota(jnp.int32, (SPAN, SPAN), 1)
    return row_ids >= col_ids


def step_sizes(dt_raw, dt_row):
    shift = dt_raw + dt_row
    step = jnp.maximum(shift, 0.0) + jnp.log1p(jnp.exp(-jnp.abs(shift)))
    return step, sigmoid(shift)


def low_half():
    return lax.broadcasted_iota(jnp.int32, (SPAN, LANES), 1) < HEADDIM


def head_lanes(h):
    lanes = lax.broadcasted_iota(jnp.int32, (1, LANES), 1)
    return (lanes < HEADDIM) if h % 2 == 0 else (lanes >= HEADDIM)


def forward_kernel(
    heads, u_ref, gain_ref, w_ref, ch_ref, bc_ref, dtp_ref, wo_ref,
    out_ref, ss_ref, normed_ref, gate_ref, xraw_ref, bcraw_ref, dtraw_ref, mixed_ref,
):
    length = u_ref.shape[1]
    wide = ch_ref.shape[1]
    blocks = length // SPAN
    rows = u_ref[0].astype(F32)
    scale = lax.rsqrt(jnp.mean(rows * rows, axis=-1, keepdims=True) + NORM_EPS)
    normed = (rows * scale * gain_ref[...]).astype(BF16)
    normed_ref[0] = normed
    gate = dot(normed, w_ref[:, :wide])
    gate_ref[0] = gate
    x_raw = dot(normed, w_ref[:, wide : 2 * wide]).astype(BF16)
    xraw_ref[0] = x_raw
    rest = dot(normed, w_ref[:, 2 * wide :]).astype(BF16)
    bcraw_ref[0] = rest[:, :SHARED]
    dtraw_ref[0] = rest[:, SHARED:]
    conv_x = conv_sum(x_raw.astype(F32), ch_ref[...])
    act_x = (conv_x * sigmoid(conv_x)).astype(BF16)
    conv_bc = conv_sum(rest[:, :SHARED].astype(F32), bc_ref[...])
    act_bc = (conv_bc * sigmoid(conv_bc)).astype(BF16)
    step, _ = step_sizes(rest[:, SHARED:].astype(F32), dtp_ref[0:1])
    rate = jnp.exp(dtp_ref[1:2])
    causal = triangles()
    ones = causal.astype(F32)
    lower = low_half()
    carries = [None] * heads
    for b in range(blocks):
        span = slice(b * SPAN, (b + 1) * SPAN)
        step_b = step[span]
        decay = -dot(ones, rate * step_b, precision=HIGHEST)
        decay_t, step_t = decay.T, step_b.T
        b_in, c_out = act_bc[span, :STATE], act_bc[span, STATE:]
        scores = dot_nt(c_out, b_in)
        for first in range(0, heads, 2):
            lanes = slice(first * HEADDIM, first * HEADDIM + LANES)
            x_pair = act_x[span, lanes]
            parts = []
            for h in range(first, min(first + 2, heads)):
                gap = decay[:, h : h + 1] - decay_t[h : h + 1]
                mask = jnp.exp(jnp.where(causal, gap, -1e30))
                weights = (scores * mask * step_t[h : h + 1]).astype(BF16)
                part = dot(weights, x_pair)
                if carries[h] is not None:
                    part += jnp.exp(decay[:, h : h + 1]) * dot(c_out, carries[h].astype(BF16))
                if b + 1 < blocks:
                    last = decay[SPAN - 1 :, h : h + 1]
                    tail = jnp.exp(last - decay[:, h : h + 1]) * step_b[:, h : h + 1]
                    shaped = (b_in.astype(F32) * tail).astype(BF16)
                    fresh = dot_tn(shaped, x_pair)
                    if carries[h] is not None:
                        fresh += jnp.exp(last) * carries[h]
                    carries[h] = fresh
                parts.append(part)
            if len(parts) == 1:
                parts.append(jnp.zeros_like(parts[0]))
            within = jnp.where(lower, parts[0], parts[1])
            mixed = within + ch_ref[5:6, lanes] * x_pair.astype(F32)
            mixed_ref[0, span, lanes] = mixed.astype(BF16)
    gated = mixed_ref[0].astype(F32) * (gate * sigmoid(gate))
    ss_ref[0] = jnp.broadcast_to(jnp.sum(gated * gated, axis=-1, keepdims=True), ss_ref.shape[1:])
    out_ref[0] = dot((gated * ch_ref[6:7]).astype(BF16), wo_ref[...]).astype(BF16)


def backward_kernel(
    heads, h_ref, aux_ref, gate_ref, xraw_ref, bcraw_ref, dtraw_ref, mixed_ref,
    w_ref, ch_ref, bc_ref, dtp_ref, wo_ref,
    dn_ref, pg_ref, no_ref, gch_ref, gbc_ref, gdt_ref,
    dmix_s, dx_s, dbc_s, ddt_s,
):
    length = h_ref.shape[1]
    wide = ch_ref.shape[1]
    blocks = length // SPAN
    scale, rdot = aux_ref[0, :, 0:1], aux_ref[0, :, 1:2]
    gate = gate_ref[0]
    mixed = mixed_ref[0].astype(F32)
    sig = sigmoid(gate)
    silu = gate * sig
    gated = mixed * silu
    gain = ch_ref[6:7]
    grad_no = dot_nt(h_ref[0], wo_ref[...])
    grad_g = scale * (gain * grad_no) - gated * (scale * scale * (1.0 / INNER) * rdot)
    scaled = gated * scale
    no_ref[0] = (scaled * gain).astype(BF16)
    gain_row = jnp.sum(grad_no * scaled, axis=0, keepdims=True)
    dmix_s[...] = (grad_g * silu).astype(BF16)
    pg_ref[0, :, :wide] = (grad_g * mixed * (sig * (1.0 + gate * (1.0 - sig)))).astype(BF16)

    x_raw = xraw_ref[0].astype(F32)
    bc_raw = bcraw_ref[0].astype(F32)
    conv_x = conv_sum(x_raw, ch_ref[...])
    sig_x = sigmoid(conv_x)
    act_x = (conv_x * sig_x).astype(BF16)
    conv_bc = conv_sum(bc_raw, bc_ref[...])
    sig_bc = sigmoid(conv_bc)
    act_bc = (conv_bc * sig_bc).astype(BF16)
    step, slope = step_sizes(dtraw_ref[0].astype(F32), dtp_ref[0:1])
    rate = jnp.exp(dtp_ref[1:2])
    causal = triangles()
    ones = causal.astype(F32)
    lower = low_half()
    lane_ids = lax.broadcasted_iota(jnp.int32, (SPAN, LANES), 1)
    last_row = lax.broadcasted_iota(jnp.int32, (SPAN, 1), 0) == SPAN - 1
    decays = []
    for b in range(blocks):
        decays.append(-dot(ones, rate * step[b * SPAN : (b + 1) * SPAN], precision=HIGHEST))
    entering = [[None] * heads for _ in range(blocks)]
    for b in range(blocks - 1):
        span = slice(b * SPAN, (b + 1) * SPAN)
        b_in = act_bc[span, :STATE].astype(F32)
        for h in range(heads):
            lanes = slice(h // 2 * LANES, h // 2 * LANES + LANES)
            column = decays[b][:, h : h + 1]
            last = column[SPAN - 1 :]
            tail = jnp.exp(last - column) * step[span, h : h + 1]
            fresh = dot_tn((b_in * tail).astype(BF16), act_x[span, lanes])
            if entering[b][h] is not None:
                fresh += jnp.exp(last) * entering[b][h]
            entering[b + 1][h] = fresh
    leaving = [None] * heads
    rate_row = jnp.zeros((1, LANES), F32)
    for b in reversed(range(blocks)):
        span = slice(b * SPAN, (b + 1) * SPAN)
        step_b, decay = step[span], decays[b]
        decay_t, step_t = decay.T, step_b.T
        b_in, c_out = act_bc[span, :STATE], act_bc[span, STATE:]
        scores = dot_nt(c_out, b_in)
        grad_scores = jnp.zeros((SPAN, SPAN), F32)
        grad_b = jnp.zeros((SPAN, STATE), F32)
        grad_c = jnp.zeros((SPAN, STATE), F32)
        row_sums = jnp.zeros((SPAN, LANES), F32)
        grad_step = jnp.zeros((SPAN, LANES), F32)
        col_rows = []
        for first in range(0, heads, 2):
            lanes = slice(first * HEADDIM, first * HEADDIM + LANES)
            x_pair = act_x[span, lanes]
            grad_pair = dmix_s[span, lanes]
            parts = []
            for h in range(first, min(first + 2, heads)):
                own = head_lanes(h)
                grad_own = jnp.where(own, grad_pair, jnp.zeros((), BF16))
                column = decay[:, h : h + 1]
                mask = jnp.exp(jnp.where(causal, column - decay_t[h : h + 1], -1e30))
                spread = mask * step_t[h : h + 1]
                weights = (scores * spread).astype(BF16)
                part = dot_tn(weights, grad_pair)
                grad_w = dot_nt(grad_own, x_pair)
                grad_scores += grad_w * spread
                pulled = grad_w * (scores * mask)
                col_rows.append(jnp.sum(pulled, axis=0, keepdims=True))
                row_sum = jnp.sum(pulled * step_t[h : h + 1], axis=1, keepdims=True)
                if entering[b][h] is not None:
                    carry = entering[b][h].astype(BF16)
                    grown = jnp.exp(column)
                    grad_grown = grad_own.astype(F32) * grown
                    grad_c += dot_nt(grad_grown.astype(BF16), carry)
                    grad_carry = dot_tn(c_out, grad_grown.astype(BF16))
                    row_sum += jnp.sum(grad_grown * dot(c_out, carry), axis=1, keepdims=True)
                else:
                    grad_carry = None
                if leaving[h] is not None:
                    last = column[SPAN - 1 :]
                    fade = jnp.exp(last - column)
                    tail = fade * step_b[:, h : h + 1]
                    b_wide = b_in.astype(F32)
                    grad_state = leaving[h].astype(BF16)
                    grad_shaped = dot_nt(x_pair, grad_state)
                    part += dot((b_wide * tail).astype(BF16), grad_state)
                    grad_b += grad_shaped * tail
                    grad_tail = jnp.sum(grad_shaped * b_wide, axis=1, keepdims=True)
                    grad_step += jnp.where(lane_ids == h, grad_tail * fade, 0.0)
                    moved = grad_tail * tail
                    total = jnp.sum(moved, axis=0, keepdims=True)
                    if entering[b][h] is not None:
                        faded = jnp.exp(last) * leaving[h]
                        kept = jnp.sum(faded * entering[b][h], axis=1, keepdims=True)
                        total += jnp.sum(kept, axis=0, keepdims=True)
                        grad_carry += faded
                    row_sum += jnp.where(last_row, total, 0.0) - moved
                leaving[h] = grad_carry
                row_sums += jnp.where(lane_ids == h, row_sum, 0.0)
                parts.append(part)
            if len(parts) == 1:
                parts.append(jnp.zeros_like(parts[0]))
            grad_x = jnp.where(lower, parts[0], parts[1])
            dx_s[span, lanes] = grad_x + ch_ref[5:6, lanes] * grad_pair.astype(F32)
        col_sums = stacked(col_rows, LANES).T
        low_scores = grad_scores.astype(BF16)
        dbc_s[span, :STATE] = grad_b + dot_tn(low_scores, c_out)
        dbc_s[span, STATE:] = grad_c + dot(low_scores, b_in)
        grad_decay = dot(
            ones, row_sums - step_b * col_sums, ((0,), (0,)), precision=HIGHEST
        )
        ddt_s[span] = col_sums + grad_step - rate * grad_decay
        rate_row -= jnp.sum(grad_decay * step_b, axis=0, keepdims=True)

    skip_row = jnp.sum(dmix_s[...].astype(F32) * act_x.astype(F32), axis=0, keepdims=True)
    grad_conv = dx_s[...] * (sig_x * (1.0 + conv_x * (1.0 - sig_x)))
    grad_raw, ch_rows = conv_back(grad_conv, x_raw, ch_ref[...])
    pg_ref[0, :, wide : 2 * wide] = grad_raw.astype(BF16)
    grad_conv = dbc_s[...] * (sig_bc * (1.0 + conv_bc * (1.0 - sig_bc)))
    grad_raw, bc_rows = conv_back(grad_conv, bc_raw, bc_ref[...])
    pg_ref[0, :, 2 * wide : 2 * wide + SHARED] = grad_raw.astype(BF16)
    grad_dt = ddt_s[...] * slope
    pg_ref[0, :, 2 * wide + SHARED :] = grad_dt.astype(BF16)
    dn_ref[0] = dot_nt(pg_ref[0], w_ref[...]).astype(BF16)
    grads = (
        (gch_ref, ch_rows + [skip_row, gain_row]),
        (gbc_ref, bc_rows),
        (gdt_ref, [jnp.sum(grad_dt, axis=0, keepdims=True), rate_row * rate]),
    )
    for ref, rows in grads:
        value = stacked(rows, 8)

        @pl.when(pl.program_id(0) == 0)
        def _(ref=ref, value=value):
            ref[...] = value

        @pl.when(pl.program_id(0) > 0)
        def _(ref=ref, value=value):
            ref[...] += value


def whole_spec(array):
    return pl.BlockSpec(array.shape, lambda i: (0,) * array.ndim)


def row_spec(length, width):
    return pl.BlockSpec((1, length, width), lambda i: (i, 0, 0))


PARAMS = dict(vmem_limit_bytes=60 * 1024 * 1024)


def run_forward(heads, rows, layer):
    count, length, width = rows.shape
    wide = layer["ch"].shape[1]
    constants = [layer[k] for k in ("gain", "w", "ch", "bc", "dtp", "wo")]
    outs = [
        (width, BF16), (LANES, F32), (width, BF16), (wide, F32),
        (wide, BF16), (SHARED, BF16), (LANES, BF16), (wide, BF16),
    ]
    return pl.pallas_call(
        partial(forward_kernel, heads),
        grid=(count,),
        out_shape=[jax.ShapeDtypeStruct((count, length, n), t) for n, t in outs],
        in_specs=[row_spec(length, width)] + [whole_spec(c) for c in constants],
        out_specs=[row_spec(length, n) for n, _ in outs],
        compiler_params=pltpu.CompilerParams(**PARAMS),
        name="forward",
    )(rows, *constants)


def run_backward(heads, grad_rows, aux, saved, layer):
    count, length, width = grad_rows.shape
    wide = layer["ch"].shape[1]
    columns = layer["w"].shape[1]
    given = [grad_rows, aux, *saved]
    constants = [layer[k] for k in ("w", "ch", "bc", "dtp", "wo")]
    outs = [(width, BF16), (columns, BF16), (wide, BF16)]
    sums = [(8, wide), (8, SHARED), (8, LANES)]
    return pl.pallas_call(
        partial(backward_kernel, heads),
        grid=(count,),
        out_shape=[jax.ShapeDtypeStruct((count, length, n), t) for n, t in outs]
        + [jax.ShapeDtypeStruct(s, F32) for s in sums],
        in_specs=[row_spec(length, g.shape[2]) for g in given] + [whole_spec(c) for c in constants],
        out_specs=[row_spec(length, n) for n, _ in outs]
        + [pl.BlockSpec(s, lambda i: (0, 0)) for s in sums],
        scratch_shapes=[
            pltpu.VMEM((length, wide), BF16),
            pltpu.VMEM((length, wide), F32),
            pltpu.VMEM((length, SHARED), F32),
            pltpu.VMEM((length, LANES), F32),
        ],
        compiler_params=pltpu.CompilerParams(**PARAMS),
        name="backward",
    )(*given, *constants)


class Plan:
    def __init__(self, seq, fsdp):
        self.seq, self.fsdp = seq, fsdp
        halves = 2
        if fsdp % 2 or HEADS % (seq * 2) or (HEADS // fsdp) % seq:
            halves = 1
        self.halves, self.mates = halves, fsdp // halves
        self.heads = HEADS // (seq * halves)
        self.pieces = self.mates if (HEADS // fsdp) % seq == 0 else 1
        channels = self.heads * HEADDIM
        self.channels = channels
        self.wide = -(-channels // LANES) * LANES
        self.peer_groups = [[lo + self.mates * h for h in range(halves)] for lo in range(self.mates)]
        self.mate_groups = [[h * self.mates + j for j in range(self.mates)] for h in range(halves)]

    def split(self, array, axis):
        size = array.shape[axis] // (self.halves * self.pieces * self.seq)
        shape = array.shape[:axis] + (self.halves, self.pieces, self.seq, size) + array.shape[axis + 1 :]
        return array.reshape(shape)

    def take(self, array, axis, place):
        array = lax.dynamic_index_in_dim(self.split(array, axis), place, axis + 2, False)
        shape = array.shape[: axis + 1] + (-1,) + array.shape[axis + 3 :]
        return jnp.moveaxis(array.reshape(shape), axis, 0)

    def put(self, parts, axis):
        size = parts.shape[axis + 2] // self.pieces
        shape = parts.shape[: axis + 2] + (self.pieces, size) + parts.shape[axis + 3 :]
        parts = jnp.moveaxis(parts.reshape(shape), (1, axis + 2, 0), (axis, axis + 1, axis + 2))
        shape = parts.shape[:axis] + (-1,) + parts.shape[axis + 4 :]
        return parts.reshape(shape)


def widened(array, axis, size):
    pads = [(0, 0)] * array.ndim
    pads[axis] = (0, size - array.shape[axis])
    return jnp.pad(array, pads)


def shards(
    tokens, cotangent, norm_gain, w_in, conv_weight, conv_bias, dt_bias, a_log, skip_gain, gate_gain, w_out
):
    section = lax.axis_index("section")
    place = lax.axis_index("seq")
    depth = lax.axis_index("fsdp")
    plan = Plan(lax.axis_size("seq"), lax.axis_size("fsdp"))
    half = depth // plan.mates
    micro, _, span, width = tokens.shape
    layers = lax.axis_size("section")
    wide, channels, heads = plan.wide, plan.channels, plan.heads

    shard = w_in[0]
    gate_part = widened(plan.take(shard[:, :INNER], 1, place), 2, wide)
    x_part = widened(plan.take(shard[:, INNER : 2 * INNER], 1, place), 2, wide)
    shared_part = jnp.broadcast_to(
        shard[:, 2 * INNER : INNER + XBC], (plan.halves, shard.shape[0], SHARED)
    )
    dt_part = widened(plan.take(shard[:, INNER + XBC :], 1, place), 2, LANES)
    tile = jnp.concatenate([gate_part, x_part, shared_part, dt_part], axis=2)
    tile = jnp.repeat(tile, plan.mates, axis=0)
    tile = lax.all_to_all(tile, "fsdp", 0, 0, tiled=True).reshape(width, -1)
    w_tiles = lax.all_gather(tile, "section", axis=0)
    if plan.pieces == plan.mates:
        piece = w_out[0].reshape(plan.seq, -1, width)
        piece = lax.dynamic_index_in_dim(piece, place, 0, False)
        rows_out = lax.all_gather(
            piece, "fsdp", axis=0, tiled=True, axis_index_groups=plan.mate_groups
        )
    else:
        rows_out = lax.all_gather(w_out[0], "fsdp", axis=0, tiled=True)
        rows_out = lax.dynamic_index_in_dim(plan.take(rows_out, 0, place), half, 0, False)
    wo_tiles = lax.all_gather(widened(rows_out, 0, wide), "section", axis=0)

    def own(array, axis, size):
        part = lax.dynamic_index_in_dim(plan.take(array, axis, place), half, 0, False)
        return widened(part, axis, size)

    skip_wide = jnp.repeat(skip_gain[0], HEADDIM)[None]
    by_channel = jnp.concatenate(
        [conv_weight[0, :, :INNER], conv_bias[:, :INNER], skip_wide, gate_gain, jnp.zeros((1, INNER))], 0
    )
    by_channel = own(by_channel, 1, wide)
    by_shared = jnp.concatenate(
        [conv_weight[0, :, INNER:], conv_bias[:, INNER:], jnp.zeros((3, SHARED))], 0
    )
    by_head = jnp.concatenate([dt_bias, a_log, jnp.zeros((6, HEADS))], 0)
    by_head = own(by_head, 1, LANES)
    smalls = jnp.concatenate(
        [by_channel.ravel(), by_shared.ravel(), by_head.ravel(), norm_gain[0]]
    )
    smalls = lax.all_gather(smalls, "section", axis=0)
    cuts = [8 * wide, 8 * (wide + SHARED), 8 * (wide + SHARED + LANES)]
    params = []
    for l in range(layers):
        ch, bc, dtp, gain = jnp.split(smalls[l], cuts)
        params.append(
            dict(
                gain=gain[None], w=w_tiles[l], wo=wo_tiles[l],
                ch=ch.reshape(8, -1), bc=bc.reshape(8, -1), dtp=dtp.reshape(8, -1),
            )
        )

    def gather_rows(own_rows):
        rows = lax.all_gather(own_rows, "seq", axis=0, tiled=True)
        if plan.halves == 1:
            return rows[None]
        return lax.all_gather(rows, "fsdp", axis=0, axis_index_groups=plan.peer_groups)

    def sum_rows(parts):
        if plan.halves == 1:
            rows = parts[0]
        else:
            rows = lax.psum_scatter(
                parts, "fsdp", scatter_dimension=0, axis_index_groups=plan.peer_groups
            )
        return lax.psum_scatter(rows, "seq", scatter_dimension=0, tiled=True)

    own_tokens = lax.dynamic_index_in_dim(tokens, section, 0, False)[0]
    own_cot = lax.dynamic_index_in_dim(cotangent, section, 0, False)[0]
    inputs, outputs, branch, saved, scales = [own_tokens], [], [], [], []
    for l in range(layers):
        rows = gather_rows(inputs[l])
        parts, square, normed, *kept = run_forward(heads, rows, params[l])
        saved.append((normed, kept))
        total = sum_rows(parts).astype(F32)
        square = sum_rows(square)[:, :1]
        scale = lax.rsqrt(square / INNER + NORM_EPS)
        branch.append(total * scale)
        scales.append(scale)
        outputs.append((inputs[l].astype(F32) + branch[l]).astype(BF16))
        inputs.append(outputs[l])
    grads_in, small_grads = [None] * layers, [None] * layers
    w_grads, wo_grads = [None] * layers, [None] * layers
    grad_rows = own_cot
    for l in reversed(range(layers)):
        rdot = jnp.sum(grad_rows.astype(F32) * branch[l], axis=-1, keepdims=True)
        aux = widened(jnp.concatenate([scales[l], rdot], axis=1), 1, LANES)
        all_grads = gather_rows(grad_rows)
        aux = gather_rows(aux)
        normed, kept = saved[l]
        parts, proj_grad, normed_out, g_ch, g_bc, g_dt = run_backward(
            heads, all_grads, aux, kept, params[l]
        )
        w_grads[l] = dot_tn(normed.reshape(-1, width), proj_grad.reshape(-1, proj_grad.shape[-1])).astype(BF16)
        wo_grads[l] = dot_tn(normed_out.reshape(-1, wide), all_grads.reshape(-1, width)).astype(BF16)
        grad_normed = sum_rows(parts).astype(F32)
        rows = inputs[l].astype(F32)
        scale = lax.rsqrt(jnp.mean(rows * rows, axis=-1, keepdims=True) + NORM_EPS)
        scaled = rows * scale
        g_gain = jnp.sum(grad_normed * scaled, axis=0)
        pulled = grad_normed * params[l]["gain"]
        inner = jnp.mean(pulled * scaled, axis=-1, keepdims=True)
        grad = scale * (pulled - scaled * inner) + grad_rows.astype(F32)
        grad_rows = grad.astype(BF16)
        grads_in[l] = grad_rows

        def placed(value, size):
            value = value[..., :size]
            full = jnp.zeros((plan.seq, plan.halves) + value.shape, F32)
            full = lax.dynamic_update_slice(full, value[None, None], (place, half, 0, 0))
            return plan.put(full, 1)

        by_channel = placed(g_ch, channels)
        by_head = placed(g_dt, heads)
        skip = by_channel[5].reshape(HEADS, HEADDIM).sum(-1)
        small_grads[l] = jnp.concatenate(
            [
                g_gain, by_channel[:5].ravel(), g_bc[:5].ravel(), by_head[0], by_head[1], skip, by_channel[6]
            ]
        )

    smalls = lax.psum(jnp.stack(small_grads), ("section", "seq", "fsdp"))
    smalls = lax.dynamic_index_in_dim(smalls, section, 0, False)
    cuts, at = [], 0
    for size in (width, (CONV + 1) * INNER, (CONV + 1) * SHARED, HEADS, HEADS, HEADS):
        at += size
        cuts.append(at)
    g_gain, g_x, g_bc, g_shift, g_rate, g_skip, g_gate = jnp.split(smalls, cuts)
    conv_rows = jnp.concatenate([g_x.reshape(CONV + 1, -1), g_bc.reshape(CONV + 1, -1)], axis=1)

    w_grad = lax.psum_scatter(jnp.stack(w_grads), "section", scatter_dimension=0)
    w_grad = lax.all_to_all(w_grad, "fsdp", 0, 0, tiled=True)
    w_grad = w_grad.reshape(plan.halves, plan.mates, -1, w_grad.shape[-1]).astype(F32).sum(1)
    shared_grad = lax.psum(w_grad[..., 2 * wide : 2 * wide + SHARED].sum(0), "seq")
    head_grads = jnp.concatenate(
        [
            w_grad[..., :channels],
            w_grad[..., wide : wide + channels],
            w_grad[..., 2 * wide + SHARED : 2 * wide + SHARED + heads],
        ],
        axis=-1,
    ).astype(BF16)
    head_grads = lax.all_gather(head_grads, "seq", axis=0)
    grad_w_in = jnp.concatenate(
        [
            plan.put(head_grads[..., :channels], 1),
            plan.put(head_grads[..., channels : 2 * channels], 1),
            shared_grad.astype(BF16),
            plan.put(head_grads[..., 2 * channels :], 1),
        ],
        axis=-1,
    ).astype(F32)
    wo_grad = lax.psum_scatter(jnp.stack(wo_grads)[:, :channels], "section", scatter_dimension=0)
    if plan.pieces == plan.mates:
        wo_grad = lax.psum_scatter(
            wo_grad, "fsdp", scatter_dimension=0, tiled=True, axis_index_groups=plan.mate_groups
        )
        wo_grad = lax.all_gather(wo_grad, "seq", axis=0, tiled=True)
    else:
        full = jnp.zeros((plan.seq, plan.halves) + wo_grad.shape, BF16)
        full = lax.dynamic_update_slice(full, wo_grad[None, None], (place, half, 0, 0))
        full = plan.put(full, 0)
        wo_grad = lax.psum_scatter(full, "fsdp", scatter_dimension=0, tiled=True)
        wo_grad = lax.psum(wo_grad, "seq")

    def home(per_layer):
        return lax.all_to_all(jnp.stack(per_layer), "section", 0, 0, tiled=True)[None, :, None]

    return (
        home(outputs),
        home(grads_in),
        g_gain[None],
        grad_w_in[None],
        conv_rows[None, :CONV],
        conv_rows[CONV:],
        g_shift[None],
        g_rate[None],
        g_skip[None],
        g_gate[None],
        wo_grad.astype(F32)[None],
    )


def solution(mesh):
    return jax.shard_map(
        shards,
        mesh=mesh,
        in_specs=(
            P(None, "fsdp", "seq", None),
            P(None, "fsdp", "seq", None),
            P("section", None),
            P("section", "fsdp", None),
            P("section", None, None),
            P("section", None),
            P("section", None),
            P("section", None),
            P("section", None),
            P("section", None),
            P("section", "fsdp", None),
        ),
        out_specs=(
            P("section", None, "fsdp", "seq", None),
            P("section", None, "fsdp", "seq", None),
            P("section", None),
            P("section", "fsdp", None),
            P("section", None, None),
            P("section", None),
            P("section", None),
            P("section", None),
            P("section", None),
            P("section", None),
            P("section", "fsdp", None),
        ),
        check_vma=False,
    )
```

```python
from functools import partial

import jax
import jax.numpy as jnp
from jax import lax
from jax.experimental import pallas as pl
from jax.experimental.pallas import tpu as pltpu
from jax.sharding import PartitionSpec as P

HEADS = 48
HEADDIM = 64
STATE = 128
CONV = 4
SPAN = 256
INNER = 3072
XBC = 3328
SHARED = 2 * STATE
LANES = 128
GAIN_END = 1536
DT_AT = 1536
RATE_AT = DT_AT + LANES
NORM_EPS = 1e-05
HIGHEST = lax.Precision.HIGHEST
BF16 = jnp.bfloat16
F32 = jnp.float32


def dot(left, right, contract=((1,), (0,)), precision=None):
    return lax.dot_general(
        left, right, (contract, ((), ())), preferred_element_type=F32, precision=precision
    )


def dot_nt(left, right):
    return dot(left, right, ((1,), (1,)))


def dot_tn(left, right):
    return dot(left, right, ((0,), (0,)))


def sigmoid(value):
    return 1.0 / (1.0 + jnp.exp(-value))


def shifted(value, distance):
    if distance == 0:
        return value
    length = value.shape[0]
    rows = lax.broadcasted_iota(jnp.int32, value.shape, 0)
    moved = pltpu.roll(value, distance % length, 0)
    if distance > 0:
        return jnp.where(rows >= distance, moved, 0.0)
    return jnp.where(rows < length + distance, moved, 0.0)


def conv_sum(raw, taps):
    total = taps[CONV : CONV + 1]
    for k in range(CONV):
        total = total + taps[k : k + 1] * shifted(raw, CONV - 1 - k)
    return total


def conv_back(grad, raw, taps):
    grad_raw = 0.0
    rows = []
    for k in range(CONV):
        grad_raw = grad_raw + taps[k : k + 1] * shifted(grad, -(CONV - 1 - k))
        rows.append(jnp.sum(grad * shifted(raw, CONV - 1 - k), axis=0, keepdims=True))
    rows.append(jnp.sum(grad, axis=0, keepdims=True))
    return grad_raw, rows


def stacked(rows, count):
    width = rows[0].shape[1]
    short = count - len(rows)
    return jnp.concatenate(rows + [jnp.zeros((short, width), F32)], axis=0)


def triangles():
    row_ids = lax.broadcasted_iota(jnp.int32, (SPAN, SPAN), 0)
    col_ids = lax.broadcasted_iota(jnp.int32, (SPAN, SPAN), 1)
    return row_ids >= col_ids


def step_sizes(dt_raw, dt_row):
    shift = dt_raw + dt_row
    step = jnp.maximum(shift, 0.0) + jnp.log1p(jnp.exp(-jnp.abs(shift)))
    return step, sigmoid(shift)


def low_half():
    return lax.broadcasted_iota(jnp.int32, (SPAN, LANES), 1) < HEADDIM


def head_lanes(h):
    lanes = lax.broadcasted_iota(jnp.int32, (1, LANES), 1)
    return (lanes < HEADDIM) if h % 2 == 0 else (lanes >= HEADDIM)


def split_three(value):
    lanes = lax.broadcasted_iota(jnp.int32, (value.shape[0], LANES), 1)
    result = jnp.zeros((value.shape[0], LANES), F32)
    for k in range(3):
        part = value.astype(BF16).astype(F32)
        result = jnp.where(lanes == k, part, result)
        value = value - part
    return result.astype(BF16)


def selection(ids_ref):
    rows = lax.broadcasted_iota(jnp.int32, (LANES, LANES), 0)
    columns = lax.broadcasted_iota(jnp.int32, (LANES, LANES), 1)
    target = jnp.full((LANES, LANES), -1, jnp.int32)
    for i in range(3):
        here = (columns >= 2 * i) & (columns < 2 * i + 2)
        target = jnp.where(here, columns + 2 * (ids_ref[i] - i), target)
    return (rows == target).astype(F32)


def pair_lanes(ids_ref, i):
    return pl.ds(pl.multiple_of(ids_ref[i] * LANES, LANES), LANES)


def load_params(refs):
    if len(refs) == 2:
        ids_ref, pack_ref = refs
        sel = selection(ids_ref)
        ch = jnp.concatenate([pack_ref[:, pair_lanes(ids_ref, i)] for i in range(3)], axis=1)
        rows = [pack_ref[7:8, at : at + LANES] for at in (DT_AT, RATE_AT)]
        dtp = dot(stacked(rows, 8), sel, precision=HIGHEST)
        return pack_ref[7:8, :GAIN_END], ch, pack_ref[:, INNER:XBC], dtp, sel.astype(BF16)
    gain_ref, ch_ref, bc_ref, dtp_ref = refs
    return gain_ref[...], ch_ref[...], bc_ref[...], dtp_ref[...], None


def forward_kernel(heads, n_params, with_grad, *refs):
    u_ref, w_ref, wo_ref, *refs = refs
    gain, ch, bc, dtp, sel = load_params(refs[:n_params])
    refs = refs[n_params:]
    if with_grad:
        h_ref, *refs = refs
    out_ref, sums_ref, normed_ref, gate_ref, xraw_ref, bcraw_ref, dtraw_ref, mixed_ref = refs
    length, width = u_ref.shape[1:]
    wide = ch.shape[1]
    blocks = length // SPAN
    rows = u_ref[0].astype(F32)
    scale = lax.rsqrt(jnp.mean(rows * rows, axis=-1, keepdims=True) + NORM_EPS)
    normed = (rows * scale * gain).astype(BF16)
    normed_ref[0] = normed
    gate = dot(normed, w_ref[:, :wide])
    gate_ref[0] = gate
    x_raw = dot(normed, w_ref[:, wide : 2 * wide]).astype(BF16)
    xraw_ref[0] = x_raw
    rest = dot(normed, w_ref[:, 2 * wide :]).astype(BF16)
    bcraw_ref[0] = rest[:, :SHARED]
    dt_raw = rest[:, SHARED:]
    if sel is not None:
        dt_raw = dot(dt_raw, sel).astype(BF16)
    dtraw_ref[0] = dt_raw
    conv_x = conv_sum(x_raw.astype(F32), ch)
    act_x = (conv_x * sigmoid(conv_x)).astype(BF16)
    conv_bc = conv_sum(rest[:, :SHARED].astype(F32), bc)
    act_bc = (conv_bc * sigmoid(conv_bc)).astype(BF16)
    step, _ = step_sizes(dt_raw.astype(F32), dtp[0:1])
    rate = jnp.exp(dtp[1:2])
    causal = triangles()
    ones = causal.astype(F32)
    lower = low_half()
    carries = [None] * heads
    for b in range(blocks):
        span = slice(b * SPAN, (b + 1) * SPAN)
        step_b = step[span]
        decay = -dot(ones, rate * step_b, precision=HIGHEST)
        decay_t, step_t = decay.T, step_b.T
        b_in, c_out = act_bc[span, :STATE], act_bc[span, STATE:]
        scores = dot_nt(c_out, b_in)
        for first in range(0, heads, 2):
            lanes = slice(first * HEADDIM, first * HEADDIM + LANES)
            x_pair = act_x[span, lanes]
            parts = []
            for h in range(first, min(first + 2, heads)):
                gap = decay[:, h : h + 1] - decay_t[h : h + 1]
                mask = jnp.exp(jnp.where(causal, gap, -1e30))
                weights = (scores * mask * step_t[h : h + 1]).astype(BF16)
                part = dot(weights, x_pair)
                if carries[h] is not None:
                    part += jnp.exp(decay[:, h : h + 1]) * dot(c_out, carries[h].astype(BF16))
                if b + 1 < blocks:
                    last = decay[SPAN - 1 :, h : h + 1]
                    tail = jnp.exp(last - decay[:, h : h + 1]) * step_b[:, h : h + 1]
                    shaped = (b_in.astype(F32) * tail).astype(BF16)
                    fresh = dot_tn(shaped, x_pair)
                    if carries[h] is not None:
                        fresh += jnp.exp(last) * carries[h]
                    carries[h] = fresh
                parts.append(part)
            if len(parts) == 1:
                parts.append(jnp.zeros_like(parts[0]))
            within = jnp.where(lower, parts[0], parts[1])
            mixed = within + ch[5:6, lanes] * x_pair.astype(F32)
            mixed_ref[0, span, lanes] = mixed.astype(BF16)
    gated = mixed_ref[0].astype(F32) * (gate * sigmoid(gate))
    square = jnp.sum(gated * gated, axis=-1, keepdims=True)
    scaled = gated * ch[6:7]
    out_ref[0, :, :width] = dot(scaled.astype(BF16), wo_ref[...]).astype(BF16)
    if sel is None:
        sums_ref[0] = jnp.broadcast_to(square, sums_ref.shape[1:])
        return
    out_ref[0, :, width:] = split_three(square)
    if with_grad:
        grad_no = dot_nt(h_ref[0], wo_ref[...])
        cross = jnp.sum(grad_no * scaled, axis=-1, keepdims=True)
        lane_ids = lax.broadcasted_iota(jnp.int32, (length, LANES), 1)
        both = jnp.where(lane_ids == 0, square, jnp.where(lane_ids == 1, cross, 0.0))
        sums_ref[0] = both.T[:8]
    else:
        sums_ref[0] = jnp.zeros(sums_ref.shape[1:], F32)


def backward_kernel(heads, n_params, aux_kind, *refs):
    h_ref, *refs = refs
    if aux_kind != "columns":
        aux_ref, *refs = refs
    gate_ref, xraw_ref, bcraw_ref, dtraw_ref, mixed_ref, w_ref, wo_ref, *refs = refs
    _, ch, bc, dtp, sel = load_params(refs[:n_params])
    param_refs, refs = refs[:n_params], refs[n_params:]
    dn_ref, pg_ref, no_ref, *sum_refs = refs[:-4]
    dmix_s, dx_s, dbc_s, ddt_s = refs[-4:]
    length, width = dn_ref.shape[1:]
    wide = ch.shape[1]
    blocks = length // SPAN
    h_rows = h_ref[0, :, :width]
    if aux_kind == "columns":
        aux = h_ref[0, :, width:].astype(F32)
        scale = aux[:, 0:1] + aux[:, 1:2] + aux[:, 2:3]
        rdot = aux[:, 3:4] + aux[:, 4:5] + aux[:, 5:6]
    elif aux_kind == "rows":
        sums = aux_ref[0]
        aux = jnp.concatenate([sums, jnp.zeros((LANES - 8, length), F32)], axis=0).T
        scale = lax.rsqrt(aux[:, 0:1] * (1.0 / INNER) + NORM_EPS)
        rdot = aux[:, 1:2] * scale
    else:
        scale, rdot = aux_ref[0, :, 0:1], aux_ref[0, :, 1:2]
    gate = gate_ref[0]
    mixed = mixed_ref[0].astype(F32)
    sig = sigmoid(gate)
    silu = gate * sig
    gated = mixed * silu
    gain = ch[6:7]
    grad_no = dot_nt(h_rows, wo_ref[...])
    grad_g = scale * (gain * grad_no) - gated * (scale * scale * (1.0 / INNER) * rdot)
    scaled = gated * scale
    no_ref[0] = (scaled * gain).astype(BF16)
    gain_row = jnp.sum(grad_no * scaled, axis=0, keepdims=True)
    dmix_s[...] = (grad_g * silu).astype(BF16)
    pg_ref[0, :, :wide] = (grad_g * mixed * (sig * (1.0 + gate * (1.0 - sig)))).astype(BF16)

    x_raw = xraw_ref[0].astype(F32)
    bc_raw = bcraw_ref[0].astype(F32)
    conv_x = conv_sum(x_raw, ch)
    sig_x = sigmoid(conv_x)
    act_x = (conv_x * sig_x).astype(BF16)
    conv_bc = conv_sum(bc_raw, bc)
    sig_bc = sigmoid(conv_bc)
    act_bc = (conv_bc * sig_bc).astype(BF16)
    step, slope = step_sizes(dtraw_ref[0].astype(F32), dtp[0:1])
    rate = jnp.exp(dtp[1:2])
    causal = triangles()
    ones = causal.astype(F32)
    lower = low_half()
    lane_ids = lax.broadcasted_iota(jnp.int32, (SPAN, LANES), 1)
    last_row = lax.broadcasted_iota(jnp.int32, (SPAN, 1), 0) == SPAN - 1
    decays = []
    for b in range(blocks):
        decays.append(-dot(ones, rate * step[b * SPAN : (b + 1) * SPAN], precision=HIGHEST))
    entering = [[None] * heads for _ in range(blocks)]
    for b in range(blocks - 1):
        span = slice(b * SPAN, (b + 1) * SPAN)
        b_in = act_bc[span, :STATE].astype(F32)
        for h in range(heads):
            lanes = slice(h // 2 * LANES, h // 2 * LANES + LANES)
            column = decays[b][:, h : h + 1]
            last = column[SPAN - 1 :]
            tail = jnp.exp(last - column) * step[span, h : h + 1]
            fresh = dot_tn((b_in * tail).astype(BF16), act_x[span, lanes])
            if entering[b][h] is not None:
                fresh += jnp.exp(last) * entering[b][h]
            entering[b + 1][h] = fresh
    leaving = [None] * heads
    rate_row = jnp.zeros((1, LANES), F32)
    for b in reversed(range(blocks)):
        span = slice(b * SPAN, (b + 1) * SPAN)
        step_b, decay = step[span], decays[b]
        decay_t, step_t = decay.T, step_b.T
        b_in, c_out = act_bc[span, :STATE], act_bc[span, STATE:]
        scores = dot_nt(c_out, b_in)
        grad_scores = jnp.zeros((SPAN, SPAN), F32)
        grad_b = jnp.zeros((SPAN, STATE), F32)
        grad_c = jnp.zeros((SPAN, STATE), F32)
        row_sums = jnp.zeros((SPAN, LANES), F32)
        grad_step = jnp.zeros((SPAN, LANES), F32)
        col_rows = []
        for first in range(0, heads, 2):
            lanes = slice(first * HEADDIM, first * HEADDIM + LANES)
            x_pair = act_x[span, lanes]
            grad_pair = dmix_s[span, lanes]
            parts = []
            for h in range(first, min(first + 2, heads)):
                own = head_lanes(h)
                grad_own = jnp.where(own, grad_pair, jnp.zeros((), BF16))
                column = decay[:, h : h + 1]
                mask = jnp.exp(jnp.where(causal, column - decay_t[h : h + 1], -1e30))
                spread = mask * step_t[h : h + 1]
                weights = (scores * spread).astype(BF16)
                part = dot_tn(weights, grad_pair)
                grad_w = dot_nt(grad_own, x_pair)
                grad_scores += grad_w * spread
                pulled = grad_w * (scores * mask)
                col_rows.append(jnp.sum(pulled, axis=0, keepdims=True))
                row_sum = jnp.sum(pulled * step_t[h : h + 1], axis=1, keepdims=True)
                if entering[b][h] is not None:
                    carry = entering[b][h].astype(BF16)
                    grown = jnp.exp(column)
                    grad_grown = grad_own.astype(F32) * grown
                    grad_c += dot_nt(grad_grown.astype(BF16), carry)
                    grad_carry = dot_tn(c_out, grad_grown.astype(BF16))
                    row_sum += jnp.sum(grad_grown * dot(c_out, carry), axis=1, keepdims=True)
                else:
                    grad_carry = None
                if leaving[h] is not None:
                    last = column[SPAN - 1 :]
                    fade = jnp.exp(last - column)
                    tail = fade * step_b[:, h : h + 1]
                    b_wide = b_in.astype(F32)
                    grad_state = leaving[h].astype(BF16)
                    grad_shaped = dot_nt(x_pair, grad_state)
                    part += dot((b_wide * tail).astype(BF16), grad_state)
                    grad_b += grad_shaped * tail
                    grad_tail = jnp.sum(grad_shaped * b_wide, axis=1, keepdims=True)
                    grad_step += jnp.where(lane_ids == h, grad_tail * fade, 0.0)
                    moved = grad_tail * tail
                    total = jnp.sum(moved, axis=0, keepdims=True)
                    if entering[b][h] is not None:
                        faded = jnp.exp(last) * leaving[h]
                        kept = jnp.sum(faded * entering[b][h], axis=1, keepdims=True)
                        total += jnp.sum(kept, axis=0, keepdims=True)
                        grad_carry += faded
                    row_sum += jnp.where(last_row, total, 0.0) - moved
                leaving[h] = grad_carry
                row_sums += jnp.where(lane_ids == h, row_sum, 0.0)
                parts.append(part)
            if len(parts) == 1:
                parts.append(jnp.zeros_like(parts[0]))
            grad_x = jnp.where(lower, parts[0], parts[1])
            dx_s[span, lanes] = grad_x + ch[5:6, lanes] * grad_pair.astype(F32)
        col_sums = stacked(col_rows, LANES).T
        low_scores = grad_scores.astype(BF16)
        dbc_s[span, :STATE] = grad_b + dot_tn(low_scores, c_out)
        dbc_s[span, STATE:] = grad_c + dot(low_scores, b_in)
        grad_decay = dot(
            ones, row_sums - step_b * col_sums, ((0,), (0,)), precision=HIGHEST
        )
        ddt_s[span] = col_sums + grad_step - rate * grad_decay
        rate_row -= jnp.sum(grad_decay * step_b, axis=0, keepdims=True)

    skip_row = jnp.sum(dmix_s[...].astype(F32) * act_x.astype(F32), axis=0, keepdims=True)
    grad_conv = dx_s[...] * (sig_x * (1.0 + conv_x * (1.0 - sig_x)))
    grad_raw, ch_rows = conv_back(grad_conv, x_raw, ch)
    pg_ref[0, :, wide : 2 * wide] = grad_raw.astype(BF16)
    grad_conv = dbc_s[...] * (sig_bc * (1.0 + conv_bc * (1.0 - sig_bc)))
    grad_raw, bc_rows = conv_back(grad_conv, bc_raw, bc)
    pg_ref[0, :, 2 * wide : 2 * wide + SHARED] = grad_raw.astype(BF16)
    grad_dt = ddt_s[...] * slope
    low_dt = grad_dt.astype(BF16)
    if sel is not None:
        low_dt = dot_nt(low_dt, sel).astype(BF16)
    pg_ref[0, :, 2 * wide + SHARED :] = low_dt
    dn_ref[0] = dot_nt(pg_ref[0], w_ref[...]).astype(BF16)
    by_channel = stacked(ch_rows + [skip_row, gain_row], 8)
    by_shared = stacked(bc_rows, 8)
    by_head = stacked([jnp.sum(grad_dt, axis=0, keepdims=True), rate_row * rate], 8)
    first = pl.program_id(0) == 0
    if sel is not None:
        by_head = lax.dot_general(
            by_head, sel.astype(F32), (((1,), (1,)), ((), ())),
            preferred_element_type=F32, precision=HIGHEST,
        )
        ids_ref, (sum_ref,) = param_refs[0], sum_refs

        @pl.when(first)
        def _():
            sum_ref[...] = jnp.zeros_like(sum_ref)

        for i in range(3):
            sum_ref[:, pair_lanes(ids_ref, i)] += by_channel[:, i * LANES : (i + 1) * LANES]
        sum_ref[:, INNER:XBC] += by_shared
        sum_ref[7:8, DT_AT : DT_AT + LANES] += by_head[0:1]
        sum_ref[7:8, RATE_AT : RATE_AT + LANES] += by_head[1:2]
        return
    for ref, value in zip(sum_refs, (by_channel, by_shared, by_head)):

        @pl.when(first)
        def _(ref=ref, value=value):
            ref[...] = value

        @pl.when(jnp.logical_not(first))
        def _(ref=ref, value=value):
            ref[...] += value


def whole_spec(array):
    if array.dtype == jnp.int32:
        return pl.BlockSpec(memory_space=pltpu.SMEM)
    return pl.BlockSpec(array.shape, lambda i: (0,) * array.ndim)


def row_spec(length, width):
    return pl.BlockSpec((1, length, width), lambda i: (i, 0, 0))


def block_spec(array):
    return pl.BlockSpec((1,) + array.shape[1:], lambda i: (i, 0, 0))


PARAMS = dict(vmem_limit_bytes=60 * 1024 * 1024)


def run_forward(heads, wide, rows, w, wo, params, grad_rows=None):
    count, length, width = rows.shape
    compact = len(params) == 2
    constants = [w, wo, *params]
    given = [] if grad_rows is None else [grad_rows]
    outs = [
        (length, width + LANES if compact else width, BF16),
        (8, length, F32) if compact else (length, LANES, F32),
        (length, width, BF16), (length, wide, F32),
        (length, wide, BF16), (length, SHARED, BF16), (length, LANES, BF16), (length, wide, BF16),
    ]
    return pl.pallas_call(
        partial(forward_kernel, heads, len(params), grad_rows is not None),
        grid=(count,),
        out_shape=[jax.ShapeDtypeStruct((count, r, n), t) for r, n, t in outs],
        in_specs=[block_spec(rows)]
        + [whole_spec(c) for c in constants]
        + [block_spec(g) for g in given],
        out_specs=[row_spec(r, n) for r, n, _ in outs],
        compiler_params=pltpu.CompilerParams(**PARAMS),
        name="forward",
    )(rows, *constants, *given)


def run_backward(heads, wide, grad_rows, aux, aux_kind, saved, w, wo, params):
    count, length, _ = grad_rows.shape
    width, columns = w.shape
    given = [grad_rows] + ([] if aux is None else [aux]) + list(saved)
    constants = [w, wo, *params]
    outs = [(width, BF16), (columns, BF16), (wide, BF16)]
    sums = [(8, wide), (8, SHARED), (8, LANES)]
    if len(params) == 2:
        sums = [params[1].shape]
    return pl.pallas_call(
        partial(backward_kernel, heads, len(params), aux_kind),
        grid=(count,),
        out_shape=[jax.ShapeDtypeStruct((count, length, n), t) for n, t in outs]
        + [jax.ShapeDtypeStruct(s, F32) for s in sums],
        in_specs=[block_spec(g) for g in given] + [whole_spec(c) for c in constants],
        out_specs=[row_spec(length, n) for n, _ in outs]
        + [pl.BlockSpec(s, lambda i: (0, 0)) for s in sums],
        scratch_shapes=[
            pltpu.VMEM((length, wide), BF16),
            pltpu.VMEM((length, wide), F32),
            pltpu.VMEM((length, SHARED), F32),
            pltpu.VMEM((length, LANES), F32),
        ],
        compiler_params=pltpu.CompilerParams(**PARAMS),
        name="backward",
    )(*given, *constants)


class Plan:
    def __init__(self, seq, fsdp):
        self.seq, self.fsdp = seq, fsdp
        halves = 2
        if fsdp % 2 or HEADS % (seq * 2) or (HEADS // fsdp) % seq:
            halves = 1
        self.halves, self.mates = halves, fsdp // halves
        self.heads = HEADS // (seq * halves)
        self.pieces = self.mates if (HEADS // fsdp) % seq == 0 else 1
        channels = self.heads * HEADDIM
        self.channels = channels
        self.wide = -(-channels // LANES) * LANES
        self.peer_groups = [[lo + self.mates * h for h in range(halves)] for lo in range(self.mates)]
        self.mate_groups = [[h * self.mates + j for j in range(self.mates)] for h in range(halves)]

    def split(self, array, axis):
        size = array.shape[axis] // (self.halves * self.pieces * self.seq)
        shape = array.shape[:axis] + (self.halves, self.pieces, self.seq, size) + array.shape[axis + 1 :]
        return array.reshape(shape)

    def take(self, array, axis, place):
        array = lax.dynamic_index_in_dim(self.split(array, axis), place, axis + 2, False)
        shape = array.shape[: axis + 1] + (-1,) + array.shape[axis + 3 :]
        return jnp.moveaxis(array.reshape(shape), axis, 0)

    def put(self, parts, axis):
        size = parts.shape[axis + 2] // self.pieces
        shape = parts.shape[: axis + 2] + (self.pieces, size) + parts.shape[axis + 3 :]
        parts = jnp.moveaxis(parts.reshape(shape), (1, axis + 2, 0), (axis, axis + 1, axis + 2))
        shape = parts.shape[:axis] + (-1,) + parts.shape[axis + 4 :]
        return parts.reshape(shape)


def widened(array, axis, size):
    pads = [(0, 0)] * array.ndim
    pads[axis] = (0, size - array.shape[axis])
    return jnp.pad(array, pads)


MESH = pl.DeviceIdType.MESH
ANY = pl.BlockSpec(memory_space=pl.ANY)
VMEM = pl.BlockSpec(memory_space=pltpu.VMEM)
DMA = pltpu.SemaphoreType.DMA


class Spot:
    def __init__(self):
        self.s, self.q, self.z = (lax.axis_index(a) for a in ("section", "seq", "fsdp"))
        self.half, self.lo = self.z // 2, self.z % 2
        self.mate, self.twin = self.z + 1 - 2 * self.lo, (self.z + 2) % 4
        self.around = [None, self.q + 1 - 2 * (self.q % 2), (self.q + 2) % 4, 3 - self.q]
        self.sibling = (1 - self.s, self.q, self.z)
        self.at_mate, self.at_twin = (self.s, self.q, self.mate), (self.s, self.q, self.twin)

    def plane(self, k):
        return (self.s, self.around[k], self.z)

    def column(self, z):
        return (self.s, self.q, z)

    def pair(self, half, i):
        odd, third = self.q % 2, self.q // 2 * 3
        return 12 * half + third + [2 * odd, 1 + 6 * odd, 6 + 2 * odd][i]


def greet(places):
    barrier = pltpu.get_barrier_semaphore()
    for place in places:
        pl.semaphore_signal(barrier, inc=1, device_id=place, device_id_type=MESH)
    pl.semaphore_wait(barrier, len(places))


def remote(src, dst, send_sem, recv_sem, place):
    return pltpu.make_async_remote_copy(
        src_ref=src, dst_ref=dst, send_sem=send_sem, recv_sem=recv_sem, device_id=place, device_id_type=MESH
    )


class Spread:
    SEMS = [DMA((7,)), DMA((7,)), DMA]

    def __init__(self, spot, own, all_rows, sems):
        self.spot, self.own, self.all = spot, own, all_rows
        self.send, self.recv, self.local = sems

    def copy(self, j):
        spot = self.spot
        slot = self.all.at[spot.half, spot.q]
        if j == 3:
            return remote(self.own, slot, self.send.at[3], self.recv.at[3], spot.at_twin)
        if j < 3:
            return remote(self.own, slot, self.send.at[j], self.recv.at[j], spot.plane(j + 1))
        slot = self.all.at[1 - spot.half, spot.q]
        return remote(slot, slot, self.send.at[j], self.recv.at[j], spot.plane(j - 3))

    def here(self):
        return pltpu.make_async_copy(self.own, self.all.at[self.spot.half, self.spot.q], self.local)

    def start(self):
        for j in (3, 0, 1, 2):
            self.copy(j).start()
        self.here().start()

    def forward(self):
        self.copy(3).wait_recv()
        for j in (4, 5, 6):
            self.copy(j).start()

    def finish(self):
        for j in (0, 1, 2, 4, 5, 6):
            self.copy(j).wait_recv()
        for j in range(7):
            self.copy(j).wait_send()
        self.here().wait()


class Sum:
    @staticmethod
    def scratch(rows, columns):
        return [
            pltpu.VMEM((3, 2, rows, columns), BF16),
            pltpu.VMEM((2, rows, columns), BF16),
            pltpu.VMEM((2, rows, columns), BF16),
            DMA((7,)),
            DMA((7,)),
            DMA((2,)),
        ]

    def __init__(self, spot, parts, width, scratch):
        self.spot, self.parts, self.width = spot, parts, width
        self.recv_rows, self.own, self.twin_rows, self.send, self.recv, self.local = scratch

    def copy(self, k, i):
        spot = self.spot
        half = (1 - spot.half) if i == 0 else spot.half
        j = 3 * i + k - 1
        return remote(
            self.parts.at[half, spot.around[k]], self.recv_rows.at[k - 1, i],
            self.send.at[j], self.recv.at[j], spot.plane(k),
        )

    def here(self, i):
        half = (1 - self.spot.half) if i == 0 else self.spot.half
        return pltpu.make_async_copy(
            self.parts.at[half, self.spot.q], self.own.at[i], self.local.at[i]
        )

    def across(self):
        return remote(
            self.twin_rows.at[0], self.twin_rows.at[1], self.send.at[6], self.recv.at[6], self.spot.at_twin
        )

    def start(self):
        for i in range(2):
            for k in (1, 2, 3):
                self.copy(k, i).start()
            self.here(i).start()

    def plane_total(self, i):
        self.here(i).wait()
        total = self.own[i].astype(F32)
        for k in (1, 2, 3):
            self.copy(k, i).wait_recv()
            total += self.recv_rows[k - 1, i].astype(F32)
        return total

    def forward(self):
        total = self.plane_total(0)
        width = self.width
        self.twin_rows[0, :, :width] = total[:, :width].astype(BF16)
        if total.shape[1] > width:
            column = jnp.sum(total[:, width:], axis=1, keepdims=True)
            self.twin_rows[0, :, width:] = split_three(column)
        self.across().start()

    def finish(self):
        total = self.plane_total(1)
        self.across().wait_recv()
        total += self.twin_rows[1].astype(F32)
        return total

    def close(self):
        for i in range(2):
            for k in (1, 2, 3):
                self.copy(k, i).wait_send()
        self.across().wait_send()


class Weights:
    LOCAL = 20

    @staticmethod
    def scratch(rows, columns):
        return [pltpu.VMEM((rows, columns), BF16), DMA((Weights.LOCAL,)), DMA((24,)), DMA((24,))]

    def __init__(self, spot, layer, w_in, dt_in, w_out, tile, tile_out, scratch):
        self.spot, self.layer = spot, layer
        self.w_in, self.dt_in, self.w_out, self.tile, self.tile_out = w_in, dt_in, w_out, tile, tile_out
        self.stage, self.local, self.send, self.recv = scratch
        self.rows = w_in.shape[0]
        self.others = 2 * (1 - spot.half)
        self.gateway = 2 - spot.half
        self.is_gateway = (spot.z == 1) | (spot.z == 2)

    def at_source(self, step):
        pl.when(self.spot.s == self.layer)(step)

    def block(self, z):
        return self.tile.at[pl.ds(z * self.rows, self.rows)]

    def staged(self, own):
        spot = self.spot
        half = spot.half if own else 1 - spot.half
        target = self.block(spot.z) if own else self.stage
        jobs = []
        for i in range(3):
            for part in range(2):
                at = part * INNER + LANES * spot.pair(half, i)
                source = self.w_in.at[:, pl.ds(pl.multiple_of(at, LANES), LANES)]
                jobs.append((source, target.at[:, pl.ds((3 * part + i) * LANES, LANES)]))
        jobs.append((self.w_in.at[:, pl.ds(2 * INNER, SHARED)], target.at[:, pl.ds(6 * LANES, SHARED)]))
        jobs.append((self.dt_in, target.at[:, pl.ds(6 * LANES + SHARED, LANES)]))
        first = 0 if own else len(jobs)
        return [
            pltpu.make_async_copy(a, b, self.local.at[first + n]) for n, (a, b) in enumerate(jobs)
        ]

    def out_rows(self, i):
        at = (self.spot.pair(self.spot.half, i) % 6) * LANES
        source = self.w_out.at[pl.ds(pl.multiple_of(at, LANES), LANES)]
        return source, self.tile_out.at[pl.ds(i * LANES, LANES)]

    def owns(self, i):
        return self.spot.lo == [0, self.spot.q % 2, 1][i]

    def out_local(self, i):
        return pltpu.make_async_copy(*self.out_rows(i), self.local.at[16 + i])

    def out_to(self, i, sibling, from_tile=False):
        source, target = self.out_rows(i)
        j = 8 + 3 * sibling + i
        place = self.spot.sibling if sibling else self.spot.at_mate
        return remote(target if from_tile else source, target, self.send.at[j], self.recv.at[j], place)

    def own_to_mate(self):
        block = self.block(self.spot.z)
        return remote(block, block, self.send.at[0], self.recv.at[0], self.spot.at_mate)

    def stage_to_gateway(self):
        j = 1 + self.spot.lo
        place = self.spot.column(self.gateway)
        return remote(self.stage, self.block(self.spot.z), self.send.at[1], self.recv.at[j], place)

    def passed(self, n):
        block = self.block(self.others + n)
        return remote(block, block, self.send.at[2 + n], self.recv.at[1 + n], self.spot.at_mate)

    def to_sibling(self, n):
        z = [self.spot.z, self.spot.mate, self.others, self.others + 1][n]
        block = self.block(z)
        return remote(block, block, self.send.at[4 + n], self.recv.at[4 + n], self.spot.sibling)

    def begin(self):
        @self.at_source
        def _():
            for copy in self.staged(True) + self.staged(False):
                copy.start()
            for i in range(3):
                pl.when(self.owns(i))(lambda i=i: self.out_local(i).start())

    def start(self):
        @self.at_source
        def _():
            for copy in self.staged(True):
                copy.wait()
            self.own_to_mate().start()
            self.to_sibling(0).start()
            for copy in self.staged(False):
                copy.wait()
            self.stage_to_gateway().start()
            for i in range(3):

                @pl.when(self.owns(i))
                def _(i=i):
                    self.out_to(i, 0).start()
                    self.out_to(i, 1).start()

    def relay_mate(self):
        @self.at_source
        def _():
            self.own_to_mate().wait_recv()
            self.to_sibling(1).start()

    def relay_others(self):
        @self.at_source
        def _():
            for n in range(2):
                self.passed(n).wait_recv()
                pl.when(self.is_gateway)(lambda n=n: self.passed(n).start())
                self.to_sibling(2 + n).start()
            for i in range(3):

                @pl.when(jnp.logical_not(self.owns(i)))
                def _(i=i):
                    self.out_to(i, 0).wait_recv()
                    self.out_to(i, 1, True).start()

    def finish(self):
        @self.at_source
        def _():
            self.own_to_mate().wait_send()
            self.stage_to_gateway().wait_send()
            for n in range(2):
                pl.when(self.is_gateway)(lambda n=n: self.passed(n).wait_send())
            for n in range(4):
                self.to_sibling(n).wait_send()
            for i in range(3):
                self.out_to(i, 1).wait_send()

                @pl.when(self.owns(i))
                def _(i=i):
                    self.out_to(i, 0).wait_send()
                    self.out_local(i).wait()

        @pl.when(self.spot.s != self.layer)
        def _():
            for n in range(4):
                self.to_sibling(n).wait_recv()
            for i in range(3):
                self.out_to(i, 1).wait_recv()


def take(refs, counts):
    refs = list(refs)
    return [[refs.pop(0) for _ in range(n)] for n in counts]


def all_places(spot):
    places = [spot.plane(k) for k in (1, 2, 3)]
    places += [spot.column((spot.z + k) % 4) for k in (1, 2, 3)]
    return places + [spot.sibling]


def open_kernel(*refs):
    ins, outs, weight_s, spread_a, spread_b, (pack_send, pack_recv, pack_local) = take(
        refs, (6, 5, 4, 3, 3, 3)
    )
    w_in, dt_in, w_out, pack, tokens, cotangent = ins
    tile, tile_out, packs, all_tokens, all_cot = outs
    spot = Spot()
    weights = Weights(spot, 0, w_in, dt_in, w_out, tile, tile_out, weight_s)
    rows = Spread(spot, tokens.at[spot.s], all_tokens, spread_a)
    grads = Spread(spot, cotangent.at[spot.s], all_cot, spread_b)
    pack_here = pltpu.make_async_copy(pack, packs.at[spot.s], pack_local)
    pack_there = remote(pack, packs.at[spot.s], pack_send, pack_recv, spot.sibling)
    weights.begin()
    greet(all_places(spot))
    rows.start()
    pack_here.start()
    pack_there.start()
    weights.start()
    rows.forward()
    weights.relay_mate()
    grads.start()
    weights.relay_others()
    grads.forward()
    rows.finish()
    grads.finish()
    weights.finish()
    pack_here.wait()
    pack_there.wait()


def middle_kernel(*refs):
    ins, outs, weight_s, sum_s, spread_s = take(refs, (5, 6, 4, 6, 3))
    w_in, dt_in, w_out, parts, rows_in = ins
    tile, tile_out, all_rows, branch, scales, rows_out = outs
    spot = Spot()
    weights = Weights(spot, 1, w_in, dt_in, w_out, tile, tile_out, weight_s)
    total = Sum(spot, parts, rows_in.shape[1], sum_s)
    spread = Spread(spot, rows_out, all_rows, spread_s)
    weights.begin()
    greet(all_places(spot))
    total.start()
    weights.start()
    total.forward()
    layer_rows(total.finish(), rows_in, branch, scales, rows_out)
    spread.start()
    weights.relay_mate()
    spread.forward()
    weights.relay_others()
    spread.finish()
    total.close()
    weights.finish()


def layer_rows(total, rows_in, branch, scales, rows_out):
    width = rows_in.shape[1]
    square = jnp.sum(total[:, width:], axis=1, keepdims=True)
    scale = lax.rsqrt(square * (1.0 / INNER) + NORM_EPS)
    part = total[:, :width] * scale
    rows_out[...] = (rows_in[...].astype(F32) + part).astype(BF16)
    if branch is not None:
        branch[...] = part
        scales[...] = jnp.broadcast_to(scale, scales.shape)


def sums_kernel(mine_ref, total_ref, others, send, recv):
    spot = Spot()
    places = [spot.plane(k) for k in (1, 2, 3)]
    places += [(spot.s, spot.around[k], spot.twin) for k in (1, 2, 3)] + [spot.at_twin]
    greet(places)
    copies = [
        remote(mine_ref, others.at[j], send.at[j], recv.at[j], place) for j, place in enumerate(places)
    ]
    for copy in copies:
        copy.start()
    total = mine_ref[...]
    for j, copy in enumerate(copies):
        copy.wait_recv()
        total += others[j]
    total_ref[...] = total
    for copy in copies:
        copy.wait_send()


def norm_back(total, rows_in, gain, grad_out):
    rows = rows_in[...].astype(F32)
    scale = lax.rsqrt(jnp.mean(rows * rows, axis=-1, keepdims=True) + NORM_EPS)
    scaled = rows * scale
    pulled = total * gain
    inner = jnp.mean(pulled * scaled, axis=-1, keepdims=True)
    grad = scale * (pulled - scaled * inner) + grad_out[...].astype(F32)
    return grad, jnp.sum(total * scaled, axis=0, keepdims=True)


def turn_kernel(*refs):
    ins, outs, sum_s, last_s, spread_s, (payload,) = take(refs, (8, 4, 6, 6, 3, 1))
    parts, last_parts, rows_in, grad_out, packs, branch, scales, last_in = ins
    all_rows, grad_rows, grad_gain, last_rows = outs
    spot = Spot()
    width = rows_in.shape[1]
    total = Sum(spot, parts, width, sum_s)
    last = Sum(spot, last_parts, width, last_s)
    spread = Spread(spot, payload, all_rows, spread_s)
    greet([spot.plane(k) for k in (1, 2, 3)] + [spot.at_twin])
    total.start()
    total.forward()
    grad, gain_row = norm_back(total.finish(), rows_in, packs[1, 7:8, :width], grad_out)
    low = grad.astype(BF16)
    grad_rows[...] = low
    grad_gain[...] = stacked([gain_row], 8)
    cross = jnp.sum(low.astype(F32) * branch[...], axis=1, keepdims=True)
    payload[:, :width] = low
    lanes = lax.broadcasted_iota(jnp.int32, (rows_in.shape[0], LANES), 1)
    first = split_three(scales[:, 0:1]).astype(F32)
    second = pltpu.roll(split_three(cross).astype(F32), 3, 1)
    payload[:, width:] = jnp.where(lanes < 3, first, second).astype(BF16)
    spread.start()
    last.start()
    spread.forward()
    last.forward()
    spread.finish()
    layer_rows(last.finish(), last_in, None, None, last_rows)
    total.close()
    last.close()


def add_rows(target, sources, chunk=64):
    @pl.loop(0, target.shape[0] // chunk)
    def _(n):
        rows = pl.ds(pl.multiple_of(n * chunk, chunk), chunk)
        total = sources[0][rows, :].astype(F32)
        for source in sources[1:]:
            total += source[rows, :].astype(F32)
        target[rows, :] = total.astype(target.dtype)


class Grads:
    @staticmethod
    def scratch(shard, columns, wide, width):
        half = columns - SHARED - LANES
        return [
            pltpu.VMEM((2, 4 * shard, columns), BF16),
            pltpu.VMEM((2, wide, width), BF16),
            pltpu.VMEM((3, shard, columns), BF16),
            pltpu.VMEM((wide, width), BF16),
            pltpu.VMEM((2, shard, half), BF16),
            pltpu.VMEM((4, shard, columns - half), BF16),
            pltpu.VMEM((shard, columns - half), BF16),
            pltpu.VMEM((6, 8, XBC), F32),
            DMA((4,)),
            DMA((68,)),
            DMA((68,)),
        ]

    def __init__(self, spot, w_grads, wo_grads, final, final_out, scratch):
        self.spot, self.w_grads, self.wo_grads = spot, w_grads, wo_grads
        self.final, self.final_out = final, final_out
        (
            self.cores, self.cores_out, self.planes, self.mate_out, self.reduced, self.shared,
            self.shared_sum, self.small, self.local, self.send, self.recv,
        ) = scratch
        self.rows = self.planes.shape[1]
        self.others = 2 * (1 - spot.half)

    def block(self, z):
        return pl.ds(pl.multiple_of(z * self.rows, self.rows), self.rows)

    def core_copy(self, layer, n):
        if n == 4:
            source, target = self.wo_grads[layer], self.cores_out.at[1]
        else:
            z = [self.others, self.others + 1, self.spot.mate, self.spot.z][n]
            source = self.w_grads[layer].at[self.block(z)]
            target = self.cores.at[1, self.block(z)]
        return remote(source, target, self.send.at[n], self.recv.at[n], self.spot.sibling)

    def own_copy(self, layer, n):
        pair = [(self.w_grads[layer], self.cores.at[0]), (self.wo_grads[layer], self.cores_out.at[0])][n]
        return pltpu.make_async_copy(*pair, self.local.at[n])

    def begin(self):
        for s in range(2):

            @pl.when(self.spot.s == s)
            def _(s=s):
                for n in range(5):
                    self.core_copy(1 - s, n).start()
                for n in range(2):
                    self.own_copy(s, n).start()

    def plane_copy(self, n):
        spot = self.spot
        if n == 2:
            slot, place, j = self.planes.at[2], spot.at_mate, 7
            source = self.cores.at[0, self.block(spot.mate)]
        else:
            slot, place, j = self.planes.at[spot.lo], spot.column(self.others + n), 5 + spot.lo
            source = self.cores.at[0, self.block(self.others + n)]
        return remote(source, slot, self.send.at[5 + n], self.recv.at[j], place)

    def came(self, n):
        slot = self.planes.at[n]
        return remote(slot, slot, self.send.at[5 + n], self.recv.at[5 + n], self.spot.at_mate)

    def owns(self, i, k=0):
        odd = self.spot.q % 2
        if k % 2:
            odd = 1 - odd
        return self.spot.lo == [0, odd, 1][i]

    def out_rows(self, i):
        return pl.ds(i * LANES, LANES)

    def mate_copy(self, i):
        rows = self.out_rows(i)
        return remote(
            self.cores_out.at[0, rows], self.mate_out.at[rows],
            self.send.at[8 + i], self.recv.at[8 + i], self.spot.at_mate,
        )

    def to_planes(self):
        for n in range(2):
            self.own_copy(0, n).wait()
        for n, z in enumerate((self.others, self.others + 1, self.spot.mate, self.spot.z)):
            self.core_copy(0, n).wait_recv()
            rows = self.block(z)
            own, sibling = self.cores.at[0, rows], self.cores.at[1, rows]
            add_rows(own, [own, sibling])
            if n < 3:
                self.plane_copy(n).start()
        self.core_copy(0, 4).wait_recv()
        add_rows(self.cores_out.at[0], [self.cores_out.at[0], self.cores_out.at[1]])
        for i in range(3):
            pl.when(jnp.logical_not(self.owns(i)))(lambda i=i: self.mate_copy(i).start())

    def around_copy(self, k, n):
        i, part, pair = n // 6, n // 3 % 2, n % 3
        half = self.spot.half if i == 0 else 1 - self.spot.half
        at = part * INNER + LANES * self.spot.pair(half, pair)
        source = self.reduced.at[i, :, pl.ds((3 * part + pair) * LANES, LANES)]
        target = self.final.at[:, pl.ds(pl.multiple_of(at, LANES), LANES)]
        if k == 0:
            return pltpu.make_async_copy(source, target, self.send.at[11 + n])
        j = 11 + 12 * k + n
        return remote(source, target, self.send.at[j], self.recv.at[j], self.spot.plane(k))

    def shared_copy(self, k):
        return remote(
            self.shared.at[0], self.shared.at[k], self.send.at[58 + k], self.recv.at[58 + k], self.spot.plane(k)
        )

    def out_target(self, i):
        at = (self.spot.pair(self.spot.half, i) % 6) * LANES
        return self.final_out.at[pl.ds(pl.multiple_of(at, LANES), LANES)]

    def out_copy(self, k, i, sems):
        source = self.cores_out.at[0, self.out_rows(i)]
        if k == 0:
            return pltpu.make_async_copy(source, self.out_target(i), sems[0].at[i])
        j = 3 * k + i
        return remote(source, self.out_target(i), sems[0].at[j], sems[1].at[j], self.spot.plane(k))

    def around(self, out_sems):
        half = self.reduced.shape[2]
        self.came(2).wait_recv()
        own = self.cores.at[0, self.block(self.spot.z)]
        add_rows(own, [own, self.planes.at[2]])
        for n in range(2):
            self.came(n).wait_recv()

        @pl.loop(0, self.rows // 64)
        def _(n):
            rows = pl.ds(pl.multiple_of(n * 64, 64), 64)
            own = self.cores[0, pl.ds(pl.multiple_of(self.spot.z * self.rows + n * 64, 64), 64), :].astype(F32)
            other = self.planes[0, rows, :].astype(F32) + self.planes[1, rows, :].astype(F32)
            self.reduced[0, rows, :] = own[:, :half].astype(BF16)
            self.reduced[1, rows, :] = other[:, :half].astype(BF16)
            self.shared[0, rows, :] = (own[:, half:] + other[:, half:]).astype(BF16)

        for k in (1, 2, 3):
            self.shared_copy(k).start()
        for n in range(12):
            for k in (1, 2, 3, 0):
                self.around_copy(k, n).start()
        for i in range(3):

            @pl.when(self.owns(i))
            def _(i=i):
                rows = self.out_rows(i)
                self.mate_copy(i).wait_recv()
                total = self.cores_out[0, rows, :].astype(F32) + self.mate_out[rows, :].astype(F32)
                self.cores_out[0, rows, :] = total.astype(BF16)
                for k in (1, 2, 3, 0):
                    self.out_copy(k, i, out_sems).start()

    def small_copy(self, n):
        spot = self.spot
        place = [spot.sibling, spot.at_mate, spot.at_twin, spot.plane(1), spot.plane(2)][n]
        return remote(
            self.small.at[0], self.small.at[1 + n], self.send.at[62 + n], self.recv.at[62 + n], place
        )

    def finish(self, out_sems):
        for k in (1, 2, 3):
            self.shared_copy(k).wait_recv()

        @pl.loop(0, self.rows // 64)
        def _(n):
            rows = pl.ds(pl.multiple_of(n * 64, 64), 64)
            a, b, c, d = (self.shared[k, rows, :].astype(F32) for k in range(4))
            self.shared_sum[rows, :] = ((a + b) + (c + d)).astype(BF16)

        tail = self.final.at[:, pl.ds(2 * INNER, self.shared_sum.shape[1])]
        copy = pltpu.make_async_copy(self.shared_sum, tail, self.local.at[2])
        copy.start()
        for n in range(12):
            for k in (1, 2, 3):
                self.around_copy(k, n).wait_recv()
            self.around_copy(0, n).wait()
        for k in (1, 2, 3):
            for i in range(3):
                pl.when(self.owns(i, k))(lambda k=k, i=i: self.out_copy(k, i, out_sems).wait_recv())
        copy.wait()
        for n in range(5):
            self.core_copy(0, n).wait_send()
        for n in range(3):
            self.plane_copy(n).wait_send()
        for k in (1, 2, 3):
            self.shared_copy(k).wait_send()
            for n in range(12):
                self.around_copy(k, n).wait_send()
        for i in range(3):

            @pl.when(self.owns(i))
            def _(i=i):
                for k in (1, 2, 3):
                    self.out_copy(k, i, out_sems).wait_send()
                self.out_copy(0, i, out_sems).wait()

            pl.when(jnp.logical_not(self.owns(i)))(lambda i=i: self.mate_copy(i).wait_send())


def close_kernel(*refs):
    ins, outs, sum_s, grads_s, (grad_rows, small_in, send, recv, local, out_send, out_recv) = take(
        refs, (14, 5, 6, 11, 7)
    )
    parts, rows_in, grad_out, packs, first_rows, last_rows, last_grad, *rest = ins
    w_grads, wo_grads, (small_0, small_1, gain_1) = rest[:2], rest[2:4], rest[4:]
    home_rows, home_grads, final, final_out, small_out = outs
    spot = Spot()
    width = rows_in.shape[1]
    total = Sum(spot, parts, width, sum_s)
    grads = Grads(spot, w_grads, wo_grads, final, final_out, grads_s)
    out_sems = (out_send, out_recv)
    greet(all_places(spot))
    grads.begin()
    total.start()
    grads.to_planes()
    total.forward()
    grad, gain_row = norm_back(total.finish(), rows_in, packs[0, 7:8, :width], grad_out)
    grad_rows[...] = grad.astype(BF16)
    layers = ((first_rows, grad_rows), (last_rows, last_grad))

    def home_copies(s):
        copies = []
        for n, target in enumerate((home_rows, home_grads)):
            copies.append(remote(layers[1 - s][n], target.at[s], send.at[n], recv.at[n], spot.sibling))
            copies.append(pltpu.make_async_copy(layers[s][n], target.at[s], local.at[n]))
        return copies

    small_in[0] = small_0[...]
    small_in[1] = small_1[...]
    small_in[0, 7:8, :width] = gain_row
    small_in[1, 7:8, :width] = gain_1[0:1]
    grads.small[0] = small_in[1 - spot.s]
    grads.small_copy(0).start()
    for s in range(2):

        @pl.when(spot.s == s)
        def _(s=s):
            for copy in home_copies(s):
                copy.start()

    grads.around(out_sems)
    grads.small_copy(0).wait()
    running = small_in[spot.s] + grads.small[1]
    for n in range(1, 5):
        grads.small[0] = running
        grads.small_copy(n).start()
        grads.small_copy(n).wait()
        running = running + grads.small[1 + n]
    small_out[...] = running
    grads.finish(out_sems)
    for s in range(2):

        @pl.when(spot.s == s)
        def _(s=s):
            for copy in home_copies(s):
                copy.wait()

    total.close()


def comm_call(kernel, collective, ins, in_specs, outs, out_specs, scratch, name):
    return pl.pallas_call(
        kernel,
        out_shape=[jax.ShapeDtypeStruct(s, t) for s, t in outs],
        in_specs=in_specs,
        out_specs=out_specs,
        scratch_shapes=scratch,
        compiler_params=pltpu.CompilerParams(
            collective_id=collective, has_side_effects=True, vmem_limit_bytes=60 * 1024 * 1024
        ),
        name=name,
    )(*ins)


def fast_shards(
    tokens, cotangent, norm_gain, w_in, conv_weight, conv_bias, dt_bias, a_log, skip_gain, gate_gain, w_out
):
    section, place, half = lax.axis_index("section"), lax.axis_index("seq"), lax.axis_index("fsdp") // 2
    span, width = tokens.shape[2:]
    heads = HEADS // 8
    wide = heads * HEADDIM
    columns = 2 * wide + SHARED + LANES
    shard = w_in.shape[1]
    odd, third = place % 2, place // 2 * 3
    ids = 12 * half + third + jnp.stack([2 * odd, 1 + 6 * odd, 6 + 2 * odd]).astype(jnp.int32)
    dt_in = widened(w_in[0, :, INNER + XBC :], 1, LANES)
    last_row = jnp.concatenate(
        [norm_gain, widened(dt_bias, 1, LANES), widened(a_log, 1, LANES)], axis=1
    )
    pack = jnp.concatenate(
        [
            conv_weight[0],
            conv_bias,
            widened(jnp.repeat(skip_gain[0], HEADDIM)[None], 1, XBC),
            widened(gate_gain, 1, XBC),
            widened(last_row, 1, XBC),
        ]
    )
    group = (2, 4, span, width)
    weight_outs = [((width, columns), BF16), ((wide, width), BF16)]
    weight_s = Weights.scratch(shard, columns)
    payload = width + LANES
    tile, tile_out, packs, all_rows, all_cot = comm_call(
        open_kernel, 1,
        [w_in[0], dt_in, w_out[0], pack, tokens[:, 0], cotangent[:, 0]], [ANY] * 6,
        weight_outs + [((2, 8, XBC), F32), (group, BF16), (group, BF16)], [ANY] * 5,
        weight_s + Spread.SEMS + Spread.SEMS + [DMA, DMA, DMA], "open",
    )
    own_rows = [lax.dynamic_index_in_dim(tokens[:, 0], section, 0, False)]
    own_cot = lax.dynamic_index_in_dim(cotangent[:, 0], section, 0, False)

    def joined(rows):
        return rows.reshape(2, 4 * span, rows.shape[-1])

    def cut(rows):
        return rows.reshape(2, 4, span, rows.shape[-1])

    tiles = [(tile, tile_out)]
    parts, _, normed, *kept = run_forward(
        heads, wide, joined(all_rows), tile, tile_out, (ids, packs[0])
    )
    saved = [(normed, kept)]
    tile, tile_out, all_rows, branch, scales, rows = comm_call(
        middle_kernel, 2,
        [w_in[0], dt_in, w_out[0], cut(parts), own_rows[0]], [ANY] * 4 + [VMEM],
        weight_outs
        + [(group, BF16), ((span, width), F32), ((span, LANES), F32), ((span, width), BF16)],
        [ANY] * 3 + [VMEM] * 3,
        weight_s + Sum.scratch(span, payload) + Spread.SEMS, "middle",
    )
    own_rows.append(rows)
    tiles.append((tile, tile_out))
    last_parts, sums, normed, *kept = run_forward(
        heads, wide, joined(all_rows), tile, tile_out, (ids, packs[1]), joined(all_cot)
    )
    saved.append((normed, kept))
    sums = comm_call(
        sums_kernel, 3, [sums], [VMEM], [(sums.shape, F32)], [VMEM],
        [pltpu.VMEM((7,) + sums.shape, F32), DMA((7,)), DMA((7,))], "sums",
    )[0]
    w_grads, wo_grads, small = [None, None], [None, None], [None, None]

    def products(l, proj_grad, normed_out, grads):
        w_grads[l] = dot_tn(saved[l][0].reshape(-1, width), proj_grad.reshape(-1, columns)).astype(BF16)
        wo_grads[l] = dot_tn(normed_out.reshape(-1, wide), grads.reshape(-1, width)).astype(BF16)

    parts, proj_grad, normed_out, small[1] = run_backward(
        heads, wide, joined(all_cot), sums, "rows", saved[1][1], *tiles[1], (ids, packs[1])
    )
    products(1, proj_grad, normed_out, joined(all_cot))
    rows_spec = ((span, width), BF16)
    all_grads, last_grad, gain_1, last_rows = comm_call(
        turn_kernel, 4,
        [cut(parts), cut(last_parts), own_rows[1], own_cot, packs, branch, scales, own_rows[1]],
        [ANY, ANY] + [VMEM] * 6,
        [((2, 4, span, payload), BF16), rows_spec, ((8, width), F32), rows_spec], [ANY] + [VMEM] * 3,
        Sum.scratch(span, width) + Sum.scratch(span, payload) + Spread.SEMS
        + [pltpu.VMEM((span, payload), BF16)], "turn",
    )
    all_grads = joined(all_grads)
    parts, proj_grad, normed_out, small[0] = run_backward(
        heads, wide, all_grads, None, "columns", saved[0][1], *tiles[0], (ids, packs[0])
    )
    products(0, proj_grad, normed_out, all_grads[..., :width])
    final_columns = 2 * INNER + SHARED + LANES
    home_rows, home_grads, final, final_out, small = comm_call(
        close_kernel, 5,
        [
            cut(parts), own_rows[0], last_grad, packs, own_rows[1], last_rows, last_grad,
            *w_grads, *wo_grads, *small, gain_1,
        ],
        [ANY] + [VMEM] * 6 + [ANY] * 4 + [VMEM] * 3,
        [
            ((2, span, width), BF16), ((2, span, width), BF16),
            ((shard, final_columns), BF16), (w_out.shape[1:], BF16), ((8, XBC), F32),
        ],
        [ANY] * 4 + [VMEM],
        Sum.scratch(span, width) + Grads.scratch(shard, columns, wide, width)
        + [
            pltpu.VMEM((span, width), BF16), pltpu.VMEM((2, 8, XBC), F32),
            DMA((2,)), DMA((2,)), DMA((2,)), DMA((12,)), DMA((12,)),
        ],
        "close",
    )
    return (
        home_rows[None, :, None],
        home_grads[None, :, None],
        small[7:8, :width],
        final[None, :, : INNER + XBC + HEADS].astype(F32),
        small[None, :CONV],
        small[CONV : CONV + 1],
        small[7:8, DT_AT : DT_AT + HEADS],
        small[7:8, RATE_AT : RATE_AT + HEADS],
        small[5:6, :INNER].reshape(1, HEADS, HEADDIM).sum(-1),
        small[6:7, :INNER],
        final_out[None].astype(F32),
    )


def shards(
    tokens, cotangent, norm_gain, w_in, conv_weight, conv_bias, dt_bias, a_log, skip_gain, gate_gain, w_out
):
    section = lax.axis_index("section")
    place = lax.axis_index("seq")
    depth = lax.axis_index("fsdp")
    plan = Plan(lax.axis_size("seq"), lax.axis_size("fsdp"))
    half = depth // plan.mates
    micro, _, span, width = tokens.shape
    layers = lax.axis_size("section")
    wide, channels, heads = plan.wide, plan.channels, plan.heads

    shard = w_in[0]
    gate_part = widened(plan.take(shard[:, :INNER], 1, place), 2, wide)
    x_part = widened(plan.take(shard[:, INNER : 2 * INNER], 1, place), 2, wide)
    shared_part = jnp.broadcast_to(
        shard[:, 2 * INNER : INNER + XBC], (plan.halves, shard.shape[0], SHARED)
    )
    dt_part = widened(plan.take(shard[:, INNER + XBC :], 1, place), 2, LANES)
    tile = jnp.concatenate([gate_part, x_part, shared_part, dt_part], axis=2)
    tile = jnp.repeat(tile, plan.mates, axis=0)
    tile = lax.all_to_all(tile, "fsdp", 0, 0, tiled=True).reshape(width, -1)
    w_tiles = lax.all_gather(tile, "section", axis=0)
    if plan.pieces == plan.mates:
        piece = w_out[0].reshape(plan.seq, -1, width)
        piece = lax.dynamic_index_in_dim(piece, place, 0, False)
        rows_out = lax.all_gather(
            piece, "fsdp", axis=0, tiled=True, axis_index_groups=plan.mate_groups
        )
    else:
        rows_out = lax.all_gather(w_out[0], "fsdp", axis=0, tiled=True)
        rows_out = lax.dynamic_index_in_dim(plan.take(rows_out, 0, place), half, 0, False)
    wo_tiles = lax.all_gather(widened(rows_out, 0, wide), "section", axis=0)

    def own(array, axis, size):
        part = lax.dynamic_index_in_dim(plan.take(array, axis, place), half, 0, False)
        return widened(part, axis, size)

    skip_wide = jnp.repeat(skip_gain[0], HEADDIM)[None]
    by_channel = jnp.concatenate(
        [conv_weight[0, :, :INNER], conv_bias[:, :INNER], skip_wide, gate_gain, jnp.zeros((1, INNER))], 0
    )
    by_channel = own(by_channel, 1, wide)
    by_shared = jnp.concatenate(
        [conv_weight[0, :, INNER:], conv_bias[:, INNER:], jnp.zeros((3, SHARED))], 0
    )
    by_head = jnp.concatenate([dt_bias, a_log, jnp.zeros((6, HEADS))], 0)
    by_head = own(by_head, 1, LANES)
    smalls = jnp.concatenate(
        [by_channel.ravel(), by_shared.ravel(), by_head.ravel(), norm_gain[0]]
    )
    smalls = lax.all_gather(smalls, "section", axis=0)
    cuts = [8 * wide, 8 * (wide + SHARED), 8 * (wide + SHARED + LANES)]
    params = []
    for l in range(layers):
        ch, bc, dtp, gain = jnp.split(smalls[l], cuts)
        params.append((gain[None], ch.reshape(8, -1), bc.reshape(8, -1), dtp.reshape(8, -1)))

    def gather_rows(own_rows):
        rows = lax.all_gather(own_rows, "seq", axis=0, tiled=True)
        if plan.halves == 1:
            return rows[None]
        return lax.all_gather(rows, "fsdp", axis=0, axis_index_groups=plan.peer_groups)

    def sum_rows(parts):
        if plan.halves == 1:
            rows = parts[0]
        else:
            rows = lax.psum_scatter(
                parts, "fsdp", scatter_dimension=0, axis_index_groups=plan.peer_groups
            )
        return lax.psum_scatter(rows, "seq", scatter_dimension=0, tiled=True)

    own_tokens = lax.dynamic_index_in_dim(tokens, section, 0, False)[0]
    own_cot = lax.dynamic_index_in_dim(cotangent, section, 0, False)[0]
    inputs, outputs, branch, saved, scales = [own_tokens], [], [], [], []
    for l in range(layers):
        rows = gather_rows(inputs[l])
        parts, square, normed, *kept = run_forward(
            heads, wide, rows, w_tiles[l], wo_tiles[l], params[l]
        )
        saved.append((normed, kept))
        total = sum_rows(parts).astype(F32)
        square = sum_rows(square)[:, :1]
        scale = lax.rsqrt(square / INNER + NORM_EPS)
        branch.append(total * scale)
        scales.append(scale)
        outputs.append((inputs[l].astype(F32) + branch[l]).astype(BF16))
        inputs.append(outputs[l])
    grads_in, small_grads = [None] * layers, [None] * layers
    w_grads, wo_grads = [None] * layers, [None] * layers
    grad_rows = own_cot
    for l in reversed(range(layers)):
        rdot = jnp.sum(grad_rows.astype(F32) * branch[l], axis=-1, keepdims=True)
        aux = widened(jnp.concatenate([scales[l], rdot], axis=1), 1, LANES)
        all_grads = gather_rows(grad_rows)
        aux = gather_rows(aux)
        normed, kept = saved[l]
        parts, proj_grad, normed_out, g_ch, g_bc, g_dt = run_backward(
            heads, wide, all_grads, aux, "lanes", kept, w_tiles[l], wo_tiles[l], params[l]
        )
        w_grads[l] = dot_tn(normed.reshape(-1, width), proj_grad.reshape(-1, proj_grad.shape[-1])).astype(BF16)
        wo_grads[l] = dot_tn(normed_out.reshape(-1, wide), all_grads.reshape(-1, width)).astype(BF16)
        grad_normed = sum_rows(parts).astype(F32)
        rows = inputs[l].astype(F32)
        scale = lax.rsqrt(jnp.mean(rows * rows, axis=-1, keepdims=True) + NORM_EPS)
        scaled = rows * scale
        g_gain = jnp.sum(grad_normed * scaled, axis=0)
        pulled = grad_normed * params[l][0]
        inner = jnp.mean(pulled * scaled, axis=-1, keepdims=True)
        grad = scale * (pulled - scaled * inner) + grad_rows.astype(F32)
        grad_rows = grad.astype(BF16)
        grads_in[l] = grad_rows

        def placed(value, size):
            value = value[..., :size]
            full = jnp.zeros((plan.seq, plan.halves) + value.shape, F32)
            full = lax.dynamic_update_slice(full, value[None, None], (place, half, 0, 0))
            return plan.put(full, 1)

        by_channel = placed(g_ch, channels)
        by_head = placed(g_dt, heads)
        skip = by_channel[5].reshape(HEADS, HEADDIM).sum(-1)
        small_grads[l] = jnp.concatenate(
            [
                g_gain, by_channel[:5].ravel(), g_bc[:5].ravel(), by_head[0], by_head[1], skip, by_channel[6]
            ]
        )

    smalls = lax.psum(jnp.stack(small_grads), ("section", "seq", "fsdp"))
    smalls = lax.dynamic_index_in_dim(smalls, section, 0, False)
    cuts, at = [], 0
    for size in (width, (CONV + 1) * INNER, (CONV + 1) * SHARED, HEADS, HEADS, HEADS):
        at += size
        cuts.append(at)
    g_gain, g_x, g_bc, g_shift, g_rate, g_skip, g_gate = jnp.split(smalls, cuts)
    conv_rows = jnp.concatenate([g_x.reshape(CONV + 1, -1), g_bc.reshape(CONV + 1, -1)], axis=1)

    w_grad = lax.psum_scatter(jnp.stack(w_grads), "section", scatter_dimension=0)
    w_grad = lax.all_to_all(w_grad, "fsdp", 0, 0, tiled=True)
    w_grad = w_grad.reshape(plan.halves, plan.mates, -1, w_grad.shape[-1]).astype(F32).sum(1)
    shared_grad = lax.psum(w_grad[..., 2 * wide : 2 * wide + SHARED].sum(0), "seq")
    head_grads = jnp.concatenate(
        [
            w_grad[..., :channels],
            w_grad[..., wide : wide + channels],
            w_grad[..., 2 * wide + SHARED : 2 * wide + SHARED + heads],
        ],
        axis=-1,
    ).astype(BF16)
    head_grads = lax.all_gather(head_grads, "seq", axis=0)
    grad_w_in = jnp.concatenate(
        [
            plan.put(head_grads[..., :channels], 1),
            plan.put(head_grads[..., channels : 2 * channels], 1),
            shared_grad.astype(BF16),
            plan.put(head_grads[..., 2 * channels :], 1),
        ],
        axis=-1,
    ).astype(F32)
    wo_grad = lax.psum_scatter(jnp.stack(wo_grads)[:, :channels], "section", scatter_dimension=0)
    if plan.pieces == plan.mates:
        wo_grad = lax.psum_scatter(
            wo_grad, "fsdp", scatter_dimension=0, tiled=True, axis_index_groups=plan.mate_groups
        )
        wo_grad = lax.all_gather(wo_grad, "seq", axis=0, tiled=True)
    else:
        full = jnp.zeros((plan.seq, plan.halves) + wo_grad.shape, BF16)
        full = lax.dynamic_update_slice(full, wo_grad[None, None], (place, half, 0, 0))
        full = plan.put(full, 0)
        wo_grad = lax.psum_scatter(full, "fsdp", scatter_dimension=0, tiled=True)
        wo_grad = lax.psum(wo_grad, "seq")

    def home(per_layer):
        return lax.all_to_all(jnp.stack(per_layer), "section", 0, 0, tiled=True)[None, :, None]

    return (
        home(outputs),
        home(grads_in),
        g_gain[None],
        grad_w_in[None],
        conv_rows[None, :CONV],
        conv_rows[CONV:],
        g_shift[None],
        g_rate[None],
        g_skip[None],
        g_gate[None],
        wo_grad.astype(F32)[None],
    )


def solution(mesh):
    shape = tuple(mesh.shape[a] for a in ("section", "seq", "fsdp"))
    return jax.shard_map(
        fast_shards if shape == (2, 4, 4) else shards,
        mesh=mesh,
        in_specs=(
            P(None, "fsdp", "seq", None),
            P(None, "fsdp", "seq", None),
            P("section", None),
            P("section", "fsdp", None),
            P("section", None, None),
            P("section", None),
            P("section", None),
            P("section", None),
            P("section", None),
            P("section", None),
            P("section", "fsdp", None),
        ),
        out_specs=(
            P("section", None, "fsdp", "seq", None),
            P("section", None, "fsdp", "seq", None),
            P("section", None),
            P("section", "fsdp", None),
            P("section", None, None),
            P("section", None),
            P("section", None),
            P("section", None),
            P("section", None),
            P("section", None),
            P("section", "fsdp", None),
        ),
        check_vma=False,
    )
```

```python
from functools import partial

import jax
import jax.numpy as jnp
from jax import lax
from jax.experimental import pallas as pl
from jax.experimental.pallas import tpu as pltpu
from jax.sharding import PartitionSpec as P

HEADS = 48
HEADDIM = 64
STATE = 128
CONV = 4
SPAN = 256
INNER = 3072
XBC = 3328
SHARED = 2 * STATE
LANES = 128
THIRD = 192
PIECE = 256
GAIN_END = 1536
DT_AT = 1536
RATE_AT = DT_AT + LANES
NORM_EPS = 1e-05
HIGHEST = lax.Precision.HIGHEST
BF16 = jnp.bfloat16
F32 = jnp.float32


def dot(left, right, contract=((1,), (0,)), precision=None):
    return lax.dot_general(
        left, right, (contract, ((), ())), preferred_element_type=F32, precision=precision
    )


def dot_nt(left, right):
    return dot(left, right, ((1,), (1,)))


def dot_tn(left, right):
    return dot(left, right, ((0,), (0,)))


def sigmoid(value):
    return 1.0 / (1.0 + jnp.exp(-value))


def shifted(value, distance):
    if distance == 0:
        return value
    length = value.shape[0]
    rows = lax.broadcasted_iota(jnp.int32, value.shape, 0)
    moved = pltpu.roll(value, distance % length, 0)
    if distance > 0:
        return jnp.where(rows >= distance, moved, 0.0)
    return jnp.where(rows < length + distance, moved, 0.0)


def conv_sum(raw, taps):
    total = taps[CONV : CONV + 1]
    for k in range(CONV):
        total = total + taps[k : k + 1] * shifted(raw, CONV - 1 - k)
    return total


def conv_back(grad, raw, taps):
    grad_raw = 0.0
    rows = []
    for k in range(CONV):
        grad_raw = grad_raw + taps[k : k + 1] * shifted(grad, -(CONV - 1 - k))
        rows.append(jnp.sum(grad * shifted(raw, CONV - 1 - k), axis=0, keepdims=True))
    rows.append(jnp.sum(grad, axis=0, keepdims=True))
    return grad_raw, rows


def stacked(rows, count):
    width = rows[0].shape[1]
    short = count - len(rows)
    return jnp.concatenate(rows + [jnp.zeros((short, width), F32)], axis=0)


def triangles():
    row_ids = lax.broadcasted_iota(jnp.int32, (SPAN, SPAN), 0)
    col_ids = lax.broadcasted_iota(jnp.int32, (SPAN, SPAN), 1)
    return row_ids >= col_ids


def step_sizes(dt_raw, dt_row):
    shift = dt_raw + dt_row
    step = jnp.maximum(shift, 0.0) + jnp.log1p(jnp.exp(-jnp.abs(shift)))
    return step, sigmoid(shift)


def low_half():
    return lax.broadcasted_iota(jnp.int32, (SPAN, LANES), 1) < HEADDIM


def head_lanes(h):
    lanes = lax.broadcasted_iota(jnp.int32, (1, LANES), 1)
    return (lanes < HEADDIM) if h % 2 == 0 else (lanes >= HEADDIM)


def split_three(value):
    lanes = lax.broadcasted_iota(jnp.int32, (value.shape[0], LANES), 1)
    result = jnp.zeros((value.shape[0], LANES), F32)
    for k in range(3):
        part = value.astype(BF16).astype(F32)
        result = jnp.where(lanes == k, part, result)
        value = value - part
    return result.astype(BF16)


def selection(ids_ref):
    rows = lax.broadcasted_iota(jnp.int32, (HEADS, LANES), 0)
    columns = lax.broadcasted_iota(jnp.int32, (HEADS, LANES), 1)
    target = jnp.full((HEADS, LANES), -1, jnp.int32)
    for j in range(2):
        here = (columns >= 3 * j) & (columns < 3 * j + 3)
        target = jnp.where(here, columns + 3 * (ids_ref[j] - j), target)
    return (rows == target).astype(F32)


def piece_lanes(ids_ref, j):
    return pl.ds(pl.multiple_of(ids_ref[j] * PIECE, PIECE), PIECE)


def load_params(refs):
    if len(refs) == 2:
        ids_ref, pack_ref = refs
        sel = selection(ids_ref)
        ch = jnp.concatenate([pack_ref[:, piece_lanes(ids_ref, j)][:, :THIRD] for j in range(2)], axis=1)
        rows = [pack_ref[7:8, at : at + HEADS] for at in (DT_AT, RATE_AT)]
        dtp = dot(stacked(rows, 8), sel, precision=HIGHEST)
        return pack_ref[7:8, :GAIN_END], ch, pack_ref[:, -SHARED:], dtp, sel.astype(BF16)
    gain_ref, ch_ref, bc_ref, dtp_ref = refs
    return gain_ref[...], ch_ref[...], bc_ref[...], dtp_ref[...], None


def forward_kernel(heads, n_params, with_grad, *refs):
    u_ref, w_ref, wo_ref, *refs = refs
    gain, ch, bc, dtp, sel = load_params(refs[:n_params])
    refs = refs[n_params:]
    if with_grad:
        h_ref, *refs = refs
    out_ref, sums_ref, normed_ref, gate_ref, xraw_ref, bcraw_ref, dtraw_ref, mixed_ref = refs
    length, width = u_ref.shape[1:]
    wide = ch.shape[1]
    blocks = length // SPAN
    rows = u_ref[0].astype(F32)
    scale = lax.rsqrt(jnp.mean(rows * rows, axis=-1, keepdims=True) + NORM_EPS)
    normed = (rows * scale * gain).astype(BF16)
    normed_ref[0] = normed
    gate = dot_nt(normed, w_ref[:wide])
    gate_ref[0] = gate
    x_raw = dot_nt(normed, w_ref[wide : 2 * wide]).astype(BF16)
    xraw_ref[0] = x_raw
    rest = dot_nt(normed, w_ref[2 * wide :]).astype(BF16)
    bcraw_ref[0] = rest[:, :SHARED]
    dt_raw = rest[:, SHARED:]
    if sel is not None:
        dt_raw = dot(dt_raw, sel).astype(BF16)
    dtraw_ref[0] = dt_raw
    conv_x = conv_sum(x_raw.astype(F32), ch)
    act_x = (conv_x * sigmoid(conv_x)).astype(BF16)
    conv_bc = conv_sum(rest[:, :SHARED].astype(F32), bc)
    act_bc = (conv_bc * sigmoid(conv_bc)).astype(BF16)
    step, _ = step_sizes(dt_raw.astype(F32), dtp[0:1])
    rate = jnp.exp(dtp[1:2])
    causal = triangles()
    ones = causal.astype(F32)
    lower = low_half()
    carries = [None] * heads
    for b in range(blocks):
        span = slice(b * SPAN, (b + 1) * SPAN)
        step_b = step[span]
        decay = -dot(ones, rate * step_b, precision=HIGHEST)
        decay_t, step_t = decay.T, step_b.T
        b_in, c_out = act_bc[span, :STATE], act_bc[span, STATE:]
        scores = dot_nt(c_out, b_in)
        for first in range(0, heads, 2):
            lanes = slice(first * HEADDIM, first * HEADDIM + LANES)
            x_pair = act_x[span, lanes]
            parts = []
            for h in range(first, min(first + 2, heads)):
                gap = decay[:, h : h + 1] - decay_t[h : h + 1]
                mask = jnp.exp(jnp.where(causal, gap, -1e30))
                weights = (scores * mask * step_t[h : h + 1]).astype(BF16)
                part = dot(weights, x_pair)
                if carries[h] is not None:
                    part += jnp.exp(decay[:, h : h + 1]) * dot(c_out, carries[h].astype(BF16))
                if b + 1 < blocks:
                    last = decay[SPAN - 1 :, h : h + 1]
                    tail = jnp.exp(last - decay[:, h : h + 1]) * step_b[:, h : h + 1]
                    shaped = (b_in.astype(F32) * tail).astype(BF16)
                    fresh = dot_tn(shaped, x_pair)
                    if carries[h] is not None:
                        fresh += jnp.exp(last) * carries[h]
                    carries[h] = fresh
                parts.append(part)
            if len(parts) == 1:
                parts.append(jnp.zeros_like(parts[0]))
            within = jnp.where(lower, parts[0], parts[1])
            mixed = within + ch[5:6, lanes] * x_pair.astype(F32)
            mixed_ref[0, span, lanes] = mixed.astype(BF16)
    gated = mixed_ref[0].astype(F32) * (gate * sigmoid(gate))
    square = jnp.sum(gated * gated, axis=-1, keepdims=True)
    scaled = gated * ch[6:7]
    out_ref[0, :, :width] = dot(scaled.astype(BF16), wo_ref[...]).astype(BF16)
    if sel is None:
        sums_ref[0] = jnp.broadcast_to(square, sums_ref.shape[1:])
        return
    out_ref[0, :, width:] = split_three(square)
    if with_grad:
        grad_no = dot_nt(h_ref[0], wo_ref[...])
        cross = jnp.sum(grad_no * scaled, axis=-1, keepdims=True)
        lane_ids = lax.broadcasted_iota(jnp.int32, (length, LANES), 1)
        both = jnp.where(lane_ids == 0, square, jnp.where(lane_ids == 1, cross, 0.0))
        sums_ref[0] = both.T[:8]
    else:
        sums_ref[0] = jnp.zeros(sums_ref.shape[1:], F32)


def backward_kernel(heads, n_params, aux_kind, *refs):
    h_ref, *refs = refs
    if aux_kind != "columns":
        aux_ref, *refs = refs
    gate_ref, xraw_ref, bcraw_ref, dtraw_ref, mixed_ref, w_ref, wo_ref, *refs = refs
    _, ch, bc, dtp, sel = load_params(refs[:n_params])
    param_refs, refs = refs[:n_params], refs[n_params:]
    dn_ref, pg_ref, no_ref, *sum_refs = refs[:-4]
    dmix_s, dx_s, dbc_s, ddt_s = refs[-4:]
    length, width = dn_ref.shape[1:]
    wide = ch.shape[1]
    blocks = length // SPAN
    h_rows = h_ref[0, :, :width]
    if aux_kind == "columns":
        aux = h_ref[0, :, width:].astype(F32)
        scale = aux[:, 0:1] + aux[:, 1:2] + aux[:, 2:3]
        rdot = aux[:, 3:4] + aux[:, 4:5] + aux[:, 5:6]
    elif aux_kind == "rows":
        sums = aux_ref[0]
        aux = jnp.concatenate([sums, jnp.zeros((LANES - 8, length), F32)], axis=0).T
        scale = lax.rsqrt(aux[:, 0:1] * (1.0 / INNER) + NORM_EPS)
        rdot = aux[:, 1:2] * scale
    else:
        scale, rdot = aux_ref[0, :, 0:1], aux_ref[0, :, 1:2]
    gate = gate_ref[0]
    mixed = mixed_ref[0].astype(F32)
    sig = sigmoid(gate)
    silu = gate * sig
    gated = mixed * silu
    gain = ch[6:7]
    grad_no = dot_nt(h_rows, wo_ref[...])
    grad_g = scale * (gain * grad_no) - gated * (scale * scale * (1.0 / INNER) * rdot)
    scaled = gated * scale
    no_ref[0] = (scaled * gain).astype(BF16)
    gain_row = jnp.sum(grad_no * scaled, axis=0, keepdims=True)
    dmix_s[...] = (grad_g * silu).astype(BF16)
    pg_ref[0, :, :wide] = (grad_g * mixed * (sig * (1.0 + gate * (1.0 - sig)))).astype(BF16)

    x_raw = xraw_ref[0].astype(F32)
    bc_raw = bcraw_ref[0].astype(F32)
    conv_x = conv_sum(x_raw, ch)
    sig_x = sigmoid(conv_x)
    act_x = (conv_x * sig_x).astype(BF16)
    conv_bc = conv_sum(bc_raw, bc)
    sig_bc = sigmoid(conv_bc)
    act_bc = (conv_bc * sig_bc).astype(BF16)
    step, slope = step_sizes(dtraw_ref[0].astype(F32), dtp[0:1])
    rate = jnp.exp(dtp[1:2])
    causal = triangles()
    ones = causal.astype(F32)
    lower = low_half()
    lane_ids = lax.broadcasted_iota(jnp.int32, (SPAN, LANES), 1)
    last_row = lax.broadcasted_iota(jnp.int32, (SPAN, 1), 0) == SPAN - 1
    decays = []
    for b in range(blocks):
        decays.append(-dot(ones, rate * step[b * SPAN : (b + 1) * SPAN], precision=HIGHEST))
    entering = [[None] * heads for _ in range(blocks)]
    for b in range(blocks - 1):
        span = slice(b * SPAN, (b + 1) * SPAN)
        b_in = act_bc[span, :STATE].astype(F32)
        for h in range(heads):
            lanes = slice(h // 2 * LANES, h // 2 * LANES + LANES)
            column = decays[b][:, h : h + 1]
            last = column[SPAN - 1 :]
            tail = jnp.exp(last - column) * step[span, h : h + 1]
            fresh = dot_tn((b_in * tail).astype(BF16), act_x[span, lanes])
            if entering[b][h] is not None:
                fresh += jnp.exp(last) * entering[b][h]
            entering[b + 1][h] = fresh
    leaving = [None] * heads
    rate_row = jnp.zeros((1, LANES), F32)
    for b in reversed(range(blocks)):
        span = slice(b * SPAN, (b + 1) * SPAN)
        step_b, decay = step[span], decays[b]
        decay_t, step_t = decay.T, step_b.T
        b_in, c_out = act_bc[span, :STATE], act_bc[span, STATE:]
        scores = dot_nt(c_out, b_in)
        grad_scores = jnp.zeros((SPAN, SPAN), F32)
        grad_b = jnp.zeros((SPAN, STATE), F32)
        grad_c = jnp.zeros((SPAN, STATE), F32)
        row_sums = jnp.zeros((SPAN, LANES), F32)
        grad_step = jnp.zeros((SPAN, LANES), F32)
        col_rows = []
        for first in range(0, heads, 2):
            lanes = slice(first * HEADDIM, first * HEADDIM + LANES)
            x_pair = act_x[span, lanes]
            grad_pair = dmix_s[span, lanes]
            parts = []
            for h in range(first, min(first + 2, heads)):
                own = head_lanes(h)
                grad_own = jnp.where(own, grad_pair, jnp.zeros((), BF16))
                column = decay[:, h : h + 1]
                mask = jnp.exp(jnp.where(causal, column - decay_t[h : h + 1], -1e30))
                spread = mask * step_t[h : h + 1]
                weights = (scores * spread).astype(BF16)
                part = dot_tn(weights, grad_pair)
                grad_w = dot_nt(grad_own, x_pair)
                grad_scores += grad_w * spread
                pulled = grad_w * (scores * mask)
                col_rows.append(jnp.sum(pulled, axis=0, keepdims=True))
                row_sum = jnp.sum(pulled * step_t[h : h + 1], axis=1, keepdims=True)
                if entering[b][h] is not None:
                    carry = entering[b][h].astype(BF16)
                    grown = jnp.exp(column)
                    grad_grown = grad_own.astype(F32) * grown
                    grad_c += dot_nt(grad_grown.astype(BF16), carry)
                    grad_carry = dot_tn(c_out, grad_grown.astype(BF16))
                    row_sum += jnp.sum(grad_grown * dot(c_out, carry), axis=1, keepdims=True)
                else:
                    grad_carry = None
                if leaving[h] is not None:
                    last = column[SPAN - 1 :]
                    fade = jnp.exp(last - column)
                    tail = fade * step_b[:, h : h + 1]
                    b_wide = b_in.astype(F32)
                    grad_state = leaving[h].astype(BF16)
                    grad_shaped = dot_nt(x_pair, grad_state)
                    part += dot((b_wide * tail).astype(BF16), grad_state)
                    grad_b += grad_shaped * tail
                    grad_tail = jnp.sum(grad_shaped * b_wide, axis=1, keepdims=True)
                    grad_step += jnp.where(lane_ids == h, grad_tail * fade, 0.0)
                    moved = grad_tail * tail
                    total = jnp.sum(moved, axis=0, keepdims=True)
                    if entering[b][h] is not None:
                        faded = jnp.exp(last) * leaving[h]
                        kept = jnp.sum(faded * entering[b][h], axis=1, keepdims=True)
                        total += jnp.sum(kept, axis=0, keepdims=True)
                        grad_carry += faded
                    row_sum += jnp.where(last_row, total, 0.0) - moved
                leaving[h] = grad_carry
                row_sums += jnp.where(lane_ids == h, row_sum, 0.0)
                parts.append(part)
            if len(parts) == 1:
                parts.append(jnp.zeros_like(parts[0]))
            grad_x = jnp.where(lower, parts[0], parts[1])
            dx_s[span, lanes] = grad_x + ch[5:6, lanes] * grad_pair.astype(F32)
        col_sums = stacked(col_rows, LANES).T
        low_scores = grad_scores.astype(BF16)
        dbc_s[span, :STATE] = grad_b + dot_tn(low_scores, c_out)
        dbc_s[span, STATE:] = grad_c + dot(low_scores, b_in)
        grad_decay = dot(
            ones, row_sums - step_b * col_sums, ((0,), (0,)), precision=HIGHEST
        )
        ddt_s[span] = col_sums + grad_step - rate * grad_decay
        rate_row -= jnp.sum(grad_decay * step_b, axis=0, keepdims=True)

    skip_row = jnp.sum(dmix_s[...].astype(F32) * act_x.astype(F32), axis=0, keepdims=True)
    grad_conv = dx_s[...] * (sig_x * (1.0 + conv_x * (1.0 - sig_x)))
    grad_raw, ch_rows = conv_back(grad_conv, x_raw, ch)
    pg_ref[0, :, wide : 2 * wide] = grad_raw.astype(BF16)
    grad_conv = dbc_s[...] * (sig_bc * (1.0 + conv_bc * (1.0 - sig_bc)))
    grad_raw, bc_rows = conv_back(grad_conv, bc_raw, bc)
    pg_ref[0, :, 2 * wide : 2 * wide + SHARED] = grad_raw.astype(BF16)
    grad_dt = ddt_s[...] * slope
    low_dt = grad_dt.astype(BF16)
    if sel is not None:
        low_dt = dot_nt(low_dt, sel).astype(BF16)
    pg_ref[0, :, 2 * wide + SHARED :] = low_dt
    dn_ref[0] = dot(pg_ref[0], w_ref[...]).astype(BF16)
    by_channel = stacked(ch_rows + [skip_row, gain_row], 8)
    by_shared = stacked(bc_rows, 8)
    by_head = stacked([jnp.sum(grad_dt, axis=0, keepdims=True), rate_row * rate], 8)
    first = pl.program_id(0) == 0
    if sel is not None:
        by_head = lax.dot_general(
            by_head, sel.astype(F32), (((1,), (1,)), ((), ())),
            preferred_element_type=F32, precision=HIGHEST,
        )
        ids_ref, (sum_ref,) = param_refs[0], sum_refs

        @pl.when(first)
        def _():
            sum_ref[...] = jnp.zeros_like(sum_ref)

        for j in range(2):
            part = by_channel[:, j * THIRD : (j + 1) * THIRD]
            part = jnp.concatenate([part, jnp.zeros((8, PIECE - THIRD), F32)], axis=1)
            sum_ref[:, piece_lanes(ids_ref, j)] += part
        sum_ref[:, -SHARED:] += by_shared
        sum_ref[7:8, DT_AT : DT_AT + HEADS] += by_head[0:1]
        sum_ref[7:8, RATE_AT : RATE_AT + HEADS] += by_head[1:2]
        return
    for ref, value in zip(sum_refs, (by_channel, by_shared, by_head)):

        @pl.when(first)
        def _(ref=ref, value=value):
            ref[...] = value

        @pl.when(jnp.logical_not(first))
        def _(ref=ref, value=value):
            ref[...] += value


def whole_spec(array):
    if array.dtype == jnp.int32:
        return pl.BlockSpec(memory_space=pltpu.SMEM)
    return pl.BlockSpec(array.shape, lambda i: (0,) * array.ndim)


def row_spec(length, width):
    return pl.BlockSpec((1, length, width), lambda i: (i, 0, 0))


def block_spec(array):
    return pl.BlockSpec((1,) + array.shape[1:], lambda i: (i, 0, 0))


PARAMS = dict(vmem_limit_bytes=60 * 1024 * 1024)


def run_forward(heads, wide, rows, w, wo, params, grad_rows=None):
    count, length, width = rows.shape
    compact = len(params) == 2
    constants = [w, wo, *params]
    given = [] if grad_rows is None else [grad_rows]
    outs = [
        (length, width + LANES if compact else width, BF16),
        (8, length, F32) if compact else (length, LANES, F32),
        (length, width, BF16), (length, wide, F32),
        (length, wide, BF16), (length, SHARED, BF16), (length, LANES, BF16), (length, wide, BF16),
    ]
    return pl.pallas_call(
        partial(forward_kernel, heads, len(params), grad_rows is not None),
        grid=(count,),
        out_shape=[jax.ShapeDtypeStruct((count, r, n), t) for r, n, t in outs],
        in_specs=[block_spec(rows)]
        + [whole_spec(c) for c in constants]
        + [block_spec(g) for g in given],
        out_specs=[row_spec(r, n) for r, n, _ in outs],
        compiler_params=pltpu.CompilerParams(**PARAMS),
        name="forward",
    )(rows, *constants, *given)


def run_backward(heads, wide, grad_rows, aux, aux_kind, saved, w, wo, params):
    count, length, _ = grad_rows.shape
    columns, width = w.shape
    given = [grad_rows] + ([] if aux is None else [aux]) + list(saved)
    constants = [w, wo, *params]
    outs = [(width, BF16), (columns, BF16), (wide, BF16)]
    sums = [(8, wide), (8, SHARED), (8, LANES)]
    if len(params) == 2:
        sums = [params[1].shape]
    return pl.pallas_call(
        partial(backward_kernel, heads, len(params), aux_kind),
        grid=(count,),
        out_shape=[jax.ShapeDtypeStruct((count, length, n), t) for n, t in outs]
        + [jax.ShapeDtypeStruct(s, F32) for s in sums],
        in_specs=[block_spec(g) for g in given] + [whole_spec(c) for c in constants],
        out_specs=[row_spec(length, n) for n, _ in outs]
        + [pl.BlockSpec(s, lambda i: (0, 0)) for s in sums],
        scratch_shapes=[
            pltpu.VMEM((length, wide), BF16),
            pltpu.VMEM((length, wide), F32),
            pltpu.VMEM((length, SHARED), F32),
            pltpu.VMEM((length, LANES), F32),
        ],
        compiler_params=pltpu.CompilerParams(**PARAMS),
        name="backward",
    )(*given, *constants)


class Plan:
    def __init__(self, seq, fsdp):
        self.seq, self.fsdp = seq, fsdp
        halves = 2
        if fsdp % 2 or HEADS % (seq * 2) or (HEADS // fsdp) % seq:
            halves = 1
        self.halves, self.mates = halves, fsdp // halves
        self.heads = HEADS // (seq * halves)
        self.pieces = self.mates if (HEADS // fsdp) % seq == 0 else 1
        channels = self.heads * HEADDIM
        self.channels = channels
        self.wide = -(-channels // LANES) * LANES
        self.peer_groups = [[lo + self.mates * h for h in range(halves)] for lo in range(self.mates)]
        self.mate_groups = [[h * self.mates + j for j in range(self.mates)] for h in range(halves)]

    def split(self, array, axis):
        size = array.shape[axis] // (self.halves * self.pieces * self.seq)
        shape = array.shape[:axis] + (self.halves, self.pieces, self.seq, size) + array.shape[axis + 1 :]
        return array.reshape(shape)

    def take(self, array, axis, place):
        array = lax.dynamic_index_in_dim(self.split(array, axis), place, axis + 2, False)
        shape = array.shape[: axis + 1] + (-1,) + array.shape[axis + 3 :]
        return jnp.moveaxis(array.reshape(shape), axis, 0)

    def put(self, parts, axis):
        size = parts.shape[axis + 2] // self.pieces
        shape = parts.shape[: axis + 2] + (self.pieces, size) + parts.shape[axis + 3 :]
        parts = jnp.moveaxis(parts.reshape(shape), (1, axis + 2, 0), (axis, axis + 1, axis + 2))
        shape = parts.shape[:axis] + (-1,) + parts.shape[axis + 4 :]
        return parts.reshape(shape)


def widened(array, axis, size):
    pads = [(0, 0)] * array.ndim
    pads[axis] = (0, size - array.shape[axis])
    return jnp.pad(array, pads)


MESH = pl.DeviceIdType.MESH
ANY = pl.BlockSpec(memory_space=pl.ANY)
VMEM = pl.BlockSpec(memory_space=pltpu.VMEM)
DMA = pltpu.SemaphoreType.DMA


class Spot:
    def __init__(self):
        self.s, self.q, self.z = (lax.axis_index(a) for a in ("section", "seq", "fsdp"))
        self.half, self.lo = self.z // 2, self.z % 2
        self.mate, self.twin = self.z + 1 - 2 * self.lo, (self.z + 2) % 4
        self.around = [None, self.q + 1 - 2 * (self.q % 2), (self.q + 2) % 4, 3 - self.q]
        self.sibling = (1 - self.s, self.q, self.z)
        self.at_mate, self.at_twin = (self.s, self.q, self.mate), (self.s, self.q, self.twin)

    def plane(self, k):
        return (self.s, self.around[k], self.z)

    def column(self, z):
        return (self.s, self.q, z)

    def piece(self, half, j):
        return 8 * half + 4 * j + self.q


def greet(places):
    barrier = pltpu.get_barrier_semaphore()
    for place in places:
        pl.semaphore_signal(barrier, inc=1, device_id=place, device_id_type=MESH)
    pl.semaphore_wait(barrier, len(places))


def remote(src, dst, send_sem, recv_sem, place):
    return pltpu.make_async_remote_copy(
        src_ref=src, dst_ref=dst, send_sem=send_sem, recv_sem=recv_sem, device_id=place, device_id_type=MESH
    )


class Home:
    def __init__(self, src, buffer, dst, sems):
        self.load = pltpu.make_async_copy(src, buffer, sems[0])
        self.store = pltpu.make_async_copy(buffer, dst, sems[1])

    def begin(self):
        self.load.start()

    def go_on(self):
        self.load.wait()
        self.store.start()

    def end(self):
        self.store.wait()


class Spread:
    SEMS = [DMA((7,)), DMA((7,)), DMA]

    def __init__(self, spot, own, all_rows, sems):
        self.spot, self.own, self.all = spot, own, all_rows
        self.send, self.recv, self.local = sems

    def copy(self, j):
        spot = self.spot
        slot = self.all.at[spot.half, spot.q]
        if j == 3:
            return remote(self.own, slot, self.send.at[3], self.recv.at[3], spot.at_twin)
        if j < 3:
            return remote(self.own, slot, self.send.at[j], self.recv.at[j], spot.plane(j + 1))
        slot = self.all.at[1 - spot.half, spot.q]
        return remote(slot, slot, self.send.at[j], self.recv.at[j], spot.plane(j - 3))

    def here(self):
        return pltpu.make_async_copy(self.own, self.all.at[self.spot.half, self.spot.q], self.local)

    def start(self):
        for j in (3, 0, 1, 2):
            self.copy(j).start()
        self.here().start()

    def forward(self):
        self.copy(3).wait_recv()
        for j in (4, 5, 6):
            self.copy(j).start()

    def finish(self):
        for j in (0, 1, 2, 4, 5, 6):
            self.copy(j).wait_recv()
        for j in range(7):
            self.copy(j).wait_send()
        self.here().wait()


class Sum:
    @staticmethod
    def scratch(rows, columns):
        return [
            pltpu.VMEM((3, 2, rows, columns), BF16),
            pltpu.VMEM((2, rows, columns), BF16),
            pltpu.VMEM((2, rows, columns), BF16),
            DMA((7,)),
            DMA((7,)),
            DMA((2,)),
        ]

    def __init__(self, spot, parts, width, scratch):
        self.spot, self.parts, self.width = spot, parts, width
        self.recv_rows, self.own, self.twin_rows, self.send, self.recv, self.local = scratch

    def copy(self, k, i):
        spot = self.spot
        half = (1 - spot.half) if i == 0 else spot.half
        j = 3 * i + k - 1
        return remote(
            self.parts.at[half, spot.around[k]], self.recv_rows.at[k - 1, i],
            self.send.at[j], self.recv.at[j], spot.plane(k),
        )

    def here(self, i):
        half = (1 - self.spot.half) if i == 0 else self.spot.half
        return pltpu.make_async_copy(
            self.parts.at[half, self.spot.q], self.own.at[i], self.local.at[i]
        )

    def across(self):
        return remote(
            self.twin_rows.at[0], self.twin_rows.at[1], self.send.at[6], self.recv.at[6], self.spot.at_twin
        )

    def start(self):
        for i in range(2):
            self.here(i).start()
        for k in (1, 2, 3):
            self.copy(k, 0).start()

    def plane_total(self, i):
        self.here(i).wait()
        total = self.own[i].astype(F32)
        for k in (1, 2, 3):
            self.copy(k, i).wait_recv()
            total += self.recv_rows[k - 1, i].astype(F32)
        return total

    def forward(self):
        for k in (1, 2, 3):
            self.copy(k, 0).wait_send()
            self.copy(k, 1).start()
        total = self.plane_total(0)
        width = self.width
        self.twin_rows[0, :, :width] = total[:, :width].astype(BF16)
        if total.shape[1] > width:
            column = jnp.sum(total[:, width:], axis=1, keepdims=True)
            self.twin_rows[0, :, width:] = split_three(column)
        self.across().start()

    def finish(self):
        total = self.plane_total(1)
        self.across().wait_recv()
        total += self.twin_rows[1].astype(F32)
        return total

    def close(self):
        for k in (1, 2, 3):
            self.copy(k, 1).wait_send()
        self.across().wait_send()


def tile_parts(spot, half):
    parts = []
    for part in range(2):
        for j in range(2):
            at = part * INNER + THIRD * spot.piece(half, j)
            parts.append((pl.multiple_of(at, 64), (2 * part + j) * THIRD, THIRD))
    return parts + [(2 * INNER, 4 * THIRD, SHARED + HEADS)]


class Weights:
    PARTS = 5

    @staticmethod
    def scratch(columns, shard, width):
        buffers = [pltpu.VMEM((columns, shard), BF16), pltpu.VMEM((THIRD, width), BF16)]
        return buffers + [DMA((4,)), DMA((43,)), DMA((43,))]

    def __init__(self, spot, layer, w_in, w_out, tile, tile_out, scratch):
        self.spot, self.layer = spot, layer
        self.w_in, self.w_out, self.tile, self.tile_out = w_in, w_out, tile, tile_out
        self.buffer, self.out_buffer, self.local, self.send, self.recv = scratch
        self.shard = w_in.shape[1]
        self.others = 2 * (1 - spot.half)
        self.gateway = 2 - spot.half
        self.is_gateway = (spot.z == 1) | (spot.z == 2)

    def at_source(self, step):
        pl.when(self.spot.s == self.layer)(step)

    def source(self, half, n):
        first, _, size = tile_parts(self.spot, half)[n]
        return self.w_in.at[pl.ds(first, size)]

    def target(self, z, n):
        _, first, size = tile_parts(self.spot, 0)[n]
        columns = pl.ds(pl.multiple_of(z * self.shard, LANES), self.shard)
        return self.tile.at[pl.ds(first, size), columns]

    def load(self, n):
        part = self.buffer.at[pl.ds(*tile_parts(self.spot, 0)[n][1:])]
        return pltpu.make_async_copy(self.source(self.spot.half, n), part, self.send.at[n])

    def store(self):
        columns = pl.ds(pl.multiple_of(self.spot.z * self.shard, LANES), self.shard)
        return pltpu.make_async_copy(self.buffer, self.tile.at[:, columns], self.local.at[0])

    def out_home(self):
        return Home(
            self.out_source(), self.out_buffer, self.out_part(self.spot.lo),
            (self.local.at[1], self.local.at[2]),
        )

    def to_mate(self, n):
        source, target = self.source(self.spot.half, n), self.target(self.spot.z, n)
        return remote(source, target, self.send.at[n], self.recv.at[n], self.spot.at_mate)

    def to_gateway(self, n):
        source, target = self.source(1 - self.spot.half, n), self.target(self.spot.z, n)
        j = 5 + 5 * self.spot.lo + n
        return remote(source, target, self.send.at[5 + n], self.recv.at[j], self.spot.column(self.gateway))

    def passed(self, c, n):
        part = self.target(self.others + c, n)
        j = 5 * c + n
        return remote(part, part, self.send.at[10 + j], self.recv.at[5 + j], self.spot.at_mate)

    def to_sibling(self, b, n):
        j = 20 + 5 * b + n
        part = self.target([self.spot.z, self.spot.mate, self.others, self.others + 1][b], n)
        source = self.source(self.spot.half, n) if b == 0 else part
        return remote(source, part, self.send.at[j], self.recv.at[j], self.spot.sibling)

    def out_part(self, lo):
        return self.tile_out.at[pl.ds(pl.multiple_of(lo * THIRD, 64), THIRD)]

    def out_source(self):
        return self.w_out.at[pl.ds(pl.multiple_of(self.spot.q * THIRD, 64), THIRD)]

    def out_to(self, n):
        part = self.out_part(self.spot.lo if n < 2 else 1 - self.spot.lo)
        place = self.spot.sibling if n else self.spot.at_mate
        source = self.out_source() if n < 2 else part
        return remote(source, part, self.send.at[40 + n], self.recv.at[40 + n], place)

    def send_part(self, n):
        if n < self.PARTS:
            self.to_gateway(n).start()
            self.to_mate(n).start()
        elif n == self.PARTS:
            self.out_to(0).start()

    def begin(self):
        @self.at_source
        def _():
            for n in range(self.PARTS):
                self.load(n).start()
            self.out_home().begin()

    def start(self):
        @self.at_source
        def _():
            for n in range(self.PARTS):
                self.load(n).wait()
            for n in range(self.PARTS):
                self.to_gateway(n).start()
                self.to_mate(n).start()
            self.out_to(0).start()
            for n in range(self.PARTS):
                self.to_sibling(0, n).start()
            self.out_to(1).start()
            self.store().start()
            self.out_home().go_on()

    def step(self, n):
        @self.at_source
        def _():
            for b in range(2):
                self.passed(b, n).wait_recv()
                pl.when(self.is_gateway)(lambda b=b: self.passed(b, n).start())
                self.to_sibling(2 + b, n).start()
            self.to_mate(n).wait_recv()
            self.to_sibling(1, n).start()

    def finish(self):
        @self.at_source
        def _():
            self.out_to(0).wait_recv()
            self.out_to(2).start()
            for n in range(self.PARTS):
                self.to_gateway(n).wait_send()
                self.to_mate(n).wait_send()
                for c in range(2):
                    pl.when(self.is_gateway)(lambda c=c, n=n: self.passed(c, n).wait_send())
                for b in range(4):
                    self.to_sibling(b, n).wait_send()
            self.store().wait()
            self.out_home().end()
            for n in range(3):
                self.out_to(n).wait_send()

        @pl.when(self.spot.s != self.layer)
        def _():
            for b in range(4):
                for n in range(self.PARTS):
                    self.to_sibling(b, n).wait_recv()
            for n in (1, 2):
                self.out_to(n).wait_recv()


def take(refs, counts):
    refs = list(refs)
    return [[refs.pop(0) for _ in range(n)] for n in counts]


def all_places(spot):
    places = [spot.plane(k) for k in (1, 2, 3)]
    places += [spot.column((spot.z + k) % 4) for k in (1, 2, 3)]
    return places + [spot.sibling]


def open_kernel(*refs):
    ins, outs, weight_s, spread_a, spread_b, (own_tokens, own_cot, own_pack, load, *pack_sems) = take(
        refs, (5, 5, 5, 3, 3, 7)
    )
    w_in, w_out, pack, tokens, cotangent = ins
    tile, tile_out, packs, all_tokens, all_cot = outs
    spot = Spot()
    weights = Weights(spot, 0, w_in, w_out, tile, tile_out, weight_s)
    rows = Spread(spot, own_tokens, all_tokens, spread_a)
    grads = Spread(spot, own_cot, all_cot, spread_b)
    loads = [
        pltpu.make_async_copy(src, dst, load.at[n])
        for n, (src, dst) in enumerate(
            ((tokens.at[spot.s], own_tokens), (cotangent.at[spot.s], own_cot), (pack, own_pack))
        )
    ]
    pack_here = pltpu.make_async_copy(own_pack, packs.at[spot.s], pack_sems[0])
    pack_there = remote(own_pack, packs.at[spot.s], pack_sems[1], pack_sems[2], spot.sibling)
    for copy in loads:
        copy.start()
    weights.begin()
    greet(all_places(spot))
    for copy in loads:
        copy.wait()
    rows.start()
    weights.start()
    pack_here.start()
    pack_there.start()
    rows.forward()
    grads.start()
    weights.step(0)
    weights.step(1)
    weights.step(2)
    grads.forward()
    weights.step(3)
    weights.step(4)
    rows.finish()
    grads.finish()
    weights.finish()
    pack_here.wait()
    pack_there.wait()


def middle_kernel(*refs):
    ins, outs, weight_s, sum_s, spread_s = take(refs, (4, 6, 5, 6, 3))
    w_in, w_out, parts, rows_in = ins
    tile, tile_out, all_rows, branch, scales, rows_out = outs
    spot = Spot()
    weights = Weights(spot, 1, w_in, w_out, tile, tile_out, weight_s)
    total = Sum(spot, parts, rows_in.shape[1], sum_s)
    spread = Spread(spot, rows_out, all_rows, spread_s)
    weights.begin()
    greet(all_places(spot))
    total.start()
    weights.start()
    total.forward()
    weights.step(0)
    layer_rows(total.finish(), rows_in, branch, scales, rows_out)
    spread.start()
    weights.step(1)
    weights.step(2)
    spread.forward()
    weights.step(3)
    weights.step(4)
    spread.finish()
    total.close()
    weights.finish()


def layer_rows(total, rows_in, branch, scales, rows_out):
    width = rows_in.shape[1]
    square = jnp.sum(total[:, width:], axis=1, keepdims=True)
    scale = lax.rsqrt(square * (1.0 / INNER) + NORM_EPS)
    part = total[:, :width] * scale
    rows_out[...] = (rows_in[...].astype(F32) + part).astype(BF16)
    if branch is not None:
        branch[...] = part
        scales[...] = jnp.broadcast_to(scale, scales.shape)


def sums_kernel(mine_ref, total_ref, others, send, recv):
    spot = Spot()
    places = [spot.plane(k) for k in (1, 2, 3)]
    places += [(spot.s, spot.around[k], spot.twin) for k in (1, 2, 3)] + [spot.at_twin]
    greet(places)
    copies = [
        remote(mine_ref, others.at[j], send.at[j], recv.at[j], place) for j, place in enumerate(places)
    ]
    for copy in copies:
        copy.start()
    total = mine_ref[...]
    for j, copy in enumerate(copies):
        copy.wait_recv()
        total += others[j]
    total_ref[...] = total
    for copy in copies:
        copy.wait_send()


def norm_back(total, rows_in, gain, grad_out):
    rows = rows_in[...].astype(F32)
    scale = lax.rsqrt(jnp.mean(rows * rows, axis=-1, keepdims=True) + NORM_EPS)
    scaled = rows * scale
    pulled = total * gain
    inner = jnp.mean(pulled * scaled, axis=-1, keepdims=True)
    grad = scale * (pulled - scaled * inner) + grad_out[...].astype(F32)
    return grad, jnp.sum(total * scaled, axis=0, keepdims=True)


def add_rows(target, sources, chunk=64):
    @pl.loop(0, target.shape[0] // chunk)
    def _(n):
        rows = pl.ds(pl.multiple_of(n * chunk, chunk), chunk)
        total = sources[0][rows, :].astype(F32)
        for source in sources[1:]:
            total += source[rows, :].astype(F32)
        target[rows, :] = total.astype(target.dtype)


class GradsAcross:
    ORDER = (4, 0, 1, 2, 3, 5)

    @staticmethod
    def scratch(shard, columns, wide, width):
        return [
            pltpu.VMEM((2, columns, width), BF16),
            pltpu.VMEM((2, wide, width), BF16),
            pltpu.VMEM((3, columns, shard), BF16),
            pltpu.VMEM((THIRD, width), BF16),
            DMA((6,)),
            DMA((22,)),
            DMA((22,)),
        ]

    @staticmethod
    def results(shard, width):
        return [((2, 4 * THIRD, shard), BF16), ((SHARED + HEADS, shard), BF16), ((THIRD, width), BF16)]

    def __init__(self, spot, layer, w_grad, wo_grad, results, scratch):
        self.spot, self.layer, self.w_grad, self.wo_grad = spot, layer, w_grad, wo_grad
        self.reduced, self.shared, self.out = results
        self.cores, self.cores_out, self.planes, self.mate_out, self.local, self.send, self.recv = scratch
        self.shard = self.planes.shape[2]
        self.others = 2 * (1 - spot.half)

    def here(self, step):
        pl.when(self.spot.s == self.layer)(step)

    def rows(self, n):
        _, first, size = tile_parts(self.spot, 0)[n]
        return pl.ds(first, size)

    def columns(self, z):
        return pl.ds(pl.multiple_of(z * self.shard, LANES), self.shard)

    def pair(self, n, slot):
        if n == 5:
            return self.wo_grad, self.cores_out.at[slot]
        return self.w_grad.at[self.rows(n)], self.cores.at[slot, self.rows(n)]

    def core_copy(self, n):
        source, target = self.pair(n, 1)
        return remote(source, target, self.send.at[n], self.recv.at[n], self.spot.sibling)

    def own_copy(self, n):
        return pltpu.make_async_copy(*self.pair(n, 0), self.local.at[n])

    def begin(self):
        @self.here
        def _():
            for n in self.ORDER:
                self.own_copy(n).start()

        @pl.when(self.spot.s != self.layer)
        def _():
            for at, n in enumerate(self.ORDER):
                if at >= 2:
                    self.core_copy(self.ORDER[at - 2]).wait_send()
                self.core_copy(n).start()
            for n in self.ORDER[-2:]:
                self.core_copy(n).wait_send()

    def plane_copy(self, c, n):
        spot, rows = self.spot, self.rows(n)
        z = spot.mate if c == 2 else self.others + c
        slot = 2 if c == 2 else spot.lo
        place = spot.at_mate if c == 2 else spot.column(z)
        return remote(
            self.cores.at[0, rows, self.columns(z)], self.planes.at[slot, rows],
            self.send.at[6 + 3 * n + c], self.recv.at[6 + 3 * n + slot], place,
        )

    def came(self, c, n):
        part = self.planes.at[c, self.rows(n)]
        j = 6 + 3 * n + c
        return remote(part, part, self.send.at[j], self.recv.at[j], self.spot.at_mate)

    def out_rows(self, lo):
        return pl.ds(pl.multiple_of(lo * THIRD, 64), THIRD)

    def mate_copy(self):
        source = self.cores_out.at[0, self.out_rows(1 - self.spot.lo)]
        return remote(source, self.mate_out, self.send.at[21], self.recv.at[21], self.spot.at_mate)

    def sent(self, n):
        @self.here
        def _():
            for c in range(3):
                self.plane_copy(c, n).wait_send()

    def to_planes(self, n):
        @self.here
        def _():
            self.own_copy(n).wait()
            self.core_copy(n).wait_recv()
            if n == 5:
                add_rows(self.cores_out.at[0], [self.cores_out.at[0], self.cores_out.at[1]])
                self.mate_copy().start()
                return
            own, sibling = self.cores.at[0, self.rows(n)], self.cores.at[1, self.rows(n)]
            add_rows(own, [own, sibling], 48 if n < 4 else 16)
            for c in range(3):
                self.plane_copy(c, n).start()

    def gather(self, n):
        @self.here
        def _():
            if n == 5:
                self.mate_copy().wait_recv()
                add_rows(self.out, [self.cores_out.at[0, self.out_rows(self.spot.lo)], self.mate_out], 48)
                return
            for c in range(3):
                self.came(c, n).wait_recv()
            _, first, size = tile_parts(self.spot, 0)[n]
            mine = self.columns(self.spot.z)
            chunk = 48 if n < 4 else 16

            @pl.loop(0, size // chunk)
            def _(r):
                rows = pl.ds(pl.multiple_of(first + r * chunk, 16), chunk)
                own = self.cores[0, rows, mine].astype(F32) + self.planes[2, rows, :].astype(F32)
                other = self.planes[0, rows, :].astype(F32) + self.planes[1, rows, :].astype(F32)
                if n < 4:
                    self.reduced[0, rows, :] = own.astype(BF16)
                    self.reduced[1, rows, :] = other.astype(BF16)
                else:
                    rows = pl.ds(pl.multiple_of(r * chunk, 16), chunk)
                    self.shared[rows, :] = (own + other).astype(BF16)

    def finish(self):
        @self.here
        def _():
            self.mate_copy().wait_send()


class GradsAround:
    @staticmethod
    def scratch(shard):
        return [
            pltpu.VMEM((4, SHARED + HEADS, shard), BF16),
            DMA((11,)),
            DMA((34,)),
            DMA((34,)),
        ]

    def __init__(self, spot, results, final, final_out, scratch):
        self.spot, self.final, self.final_out = spot, final, final_out
        self.reduced, self.shared, self.out = results
        self.sums, self.local, self.send, self.recv = scratch

    def region(self, k, i, n):
        q = self.spot.q if k == 0 else self.spot.around[k]
        half = self.spot.half if i == 0 else 1 - self.spot.half
        at = n // 2 * INNER + THIRD * (8 * half + 4 * (n % 2) + q)
        return self.final.at[pl.ds(pl.multiple_of(at, 64), THIRD)]

    def copy(self, k, i, n):
        source = self.reduced.at[i, pl.ds(n * THIRD, THIRD)]
        target = self.region(0, i, n)
        j = 4 * i + n
        if k == 0:
            return pltpu.make_async_copy(source, target, self.local.at[j])
        if k < 3:
            j += 8 * (k - 1)
            return remote(source, target, self.send.at[j], self.recv.at[j], self.spot.plane(k))
        source = target = self.region(1 if i == 0 else 2, i, n)
        place = self.spot.plane(2 if i == 0 else 1)
        return remote(source, target, self.send.at[16 + j], self.recv.at[16 + j], place)

    def send_part(self, n):
        for i in range(2):
            for k in (1, 2, 0):
                self.copy(k, i, n).start()

    def pass_part(self, n):
        for i in range(2):
            self.copy(1 + i, i, n).wait_recv()
            self.copy(3, i, n).start()

    def out_region(self, k, i):
        q = self.spot.q if k == 0 else self.spot.around[k]
        size = THIRD if i is None else THIRD // 2
        at = q * THIRD + (0 if i is None else i * size)
        return self.final_out.at[pl.ds(pl.multiple_of(at, 32), size)]

    def out_copy(self, k, i=None):
        target = self.out_region(0, None)
        if k == 0:
            return pltpu.make_async_copy(self.out, target, self.local.at[8])
        if k < 3:
            return remote(self.out, target, self.send.at[23 + k], self.recv.at[23 + k], self.spot.plane(k))
        part = self.out_region(1 + i, i)
        return remote(part, part, self.send.at[26 + i], self.recv.at[26 + i], self.spot.plane(2 - i))

    def send_out(self):
        for k in (1, 2, 0):
            self.out_copy(k).start()

    def pass_out(self):
        for i in range(2):
            self.out_copy(1 + i).wait_recv()
            self.out_copy(3, i).start()

    def shared_copy(self, k):
        source = self.shared if k == 1 else self.sums.at[1]
        target = self.sums.at[0 if k == 1 else 2]
        return remote(source, target, self.send.at[27 + k], self.recv.at[27 + k], self.spot.plane(k))

    def shared_home(self):
        tail = self.final.at[pl.ds(2 * INNER, SHARED + HEADS)]
        return pltpu.make_async_copy(self.sums.at[3], tail, self.local.at[9])

    def shared_step(self, n):
        if n > 0:
            self.shared_copy(n).wait_recv()
            sources = [self.shared, self.sums.at[0]] if n == 1 else [self.sums.at[1], self.sums.at[2]]
            add_rows(self.sums.at[1 if n == 1 else 3], sources, 16)
        if n < 2:
            self.shared_copy(n + 1).start()
        else:
            self.shared_home().start()

    def finish(self):
        for i in range(2):
            for n in range(4):
                self.copy(2 - i, i, n).wait_recv()
                self.copy(3, i, n).wait_recv()
                for k in (1, 2, 3):
                    self.copy(k, i, n).wait_send()
                self.copy(0, i, n).wait()
            self.out_copy(3, i).wait_recv()
            self.out_copy(3, i).wait_send()
        for k in (1, 2):
            self.out_copy(k).wait_send()
            self.shared_copy(k).wait_send()
        self.out_copy(0).wait()
        self.shared_home().wait()


class SmallSum:
    @staticmethod
    def scratch(pack):
        return [pltpu.VMEM((6, 8, pack), F32), DMA((5,)), DMA((5,))]

    def __init__(self, spot, scratch):
        self.spot = spot
        self.small, self.send, self.recv = scratch

    def copy(self, n):
        spot = self.spot
        place = [spot.sibling, spot.at_mate, spot.at_twin, spot.plane(1), spot.plane(2)][n]
        return remote(self.small.at[0], self.small.at[1 + n], self.send.at[n], self.recv.at[n], place)

    def start(self, n, value):
        self.small[0] = value
        self.copy(n).start()

    def end(self, n):
        self.copy(n).wait()
        return self.small[1 + n]


def turn_kernel(*refs):
    ins, outs, sum_s, last_s, spread_s, across_s, (payload,) = take(refs, (10, 7, 6, 6, 3, 7, 1))
    parts, last_parts, rows_in, grad_out, packs, branch, scales, last_in, w_grad, wo_grad = ins
    all_rows, grad_rows, grad_gain, last_rows, *results = outs
    spot = Spot()
    width = rows_in.shape[1]
    total = Sum(spot, parts, width, sum_s)
    last = Sum(spot, last_parts, width, last_s)
    spread = Spread(spot, payload, all_rows, spread_s)
    across = GradsAcross(spot, 1, w_grad, wo_grad, results, across_s)
    greet(all_places(spot))
    total.start()
    across.begin()
    across.to_planes(4)
    across.to_planes(0)
    total.forward()
    grad, gain_row = norm_back(total.finish(), rows_in, packs[1, 7:8, :width], grad_out)
    low = grad.astype(BF16)
    grad_rows[...] = low
    grad_gain[...] = stacked([gain_row], 8)
    cross = jnp.sum(low.astype(F32) * branch[...], axis=1, keepdims=True)
    payload[:, :width] = low
    lanes = lax.broadcasted_iota(jnp.int32, (rows_in.shape[0], LANES), 1)
    first = split_three(scales[:, 0:1]).astype(F32)
    second = pltpu.roll(split_three(cross).astype(F32), 3, 1)
    payload[:, width:] = jnp.where(lanes < 3, first, second).astype(BF16)
    spread.start()
    last.start()
    spread.forward()
    for n in (1, 2, 3, 5):
        across.to_planes(n)
    last.forward()
    spread.finish()
    for n in GradsAcross.ORDER:
        across.gather(n)
    layer_rows(last.finish(), last_in, None, None, last_rows)
    for n in range(5):
        across.sent(n)
    across.finish()
    total.close()
    last.close()


def close_kernel(*refs):
    ins, outs, sum_s, across_s, results, around_s, small_s, rest = take(refs, (15, 5, 6, 7, 3, 4, 3, 6))
    parts, rows_in, grad_out, packs, first_rows, last_rows, last_grad, *ins = ins
    w_grad, wo_grad, small_0, small_1, gain_1, *last_results = ins
    home_rows, home_grads, final, final_out, small_out = outs
    grad_rows, small_in, send, recv, local, load = rest
    spot = Spot()
    width = rows_in.shape[1]
    total = Sum(spot, parts, width, sum_s)
    across = GradsAcross(spot, 0, w_grad, wo_grad, results, across_s)
    around = GradsAround(spot, results, final, final_out, around_s)
    small = SmallSum(spot, small_s)
    first_core, last_core = pl.when(spot.s == 0), pl.when(spot.s == 1)
    loads = [
        pltpu.make_async_copy(src, dst, load.at[n]) for n, (src, dst) in enumerate(zip(last_results, results))
    ]

    @last_core
    def _():
        for copy in loads:
            copy.start()

    greet(all_places(spot))
    total.start()
    across.begin()

    @last_core
    def _():
        for copy in loads:
            copy.wait()
        around.shared_step(0)
        for n in range(4):
            around.send_part(n)
        around.send_out()

    order = GradsAcross.ORDER
    for n in order[:3]:
        across.to_planes(n)
    total.forward()
    for at in range(3, 6):
        across.sent(order[at - 3])
        across.to_planes(order[at])
    across.gather(4)
    first_core(lambda: around.shared_step(0))
    across.gather(0)
    first_core(lambda: around.send_part(0))
    grad, gain_row = norm_back(total.finish(), rows_in, packs[0, 7:8, :width], grad_out)
    grad_rows[...] = grad.astype(BF16)
    layers = ((first_rows, grad_rows), (last_rows, last_grad))

    def home_copies(s):
        copies = []
        for n, target in enumerate((home_rows, home_grads)):
            copies.append(remote(layers[1 - s][n], target.at[s], send.at[n], recv.at[n], spot.sibling))
            copies.append(pltpu.make_async_copy(layers[s][n], target.at[s], local.at[n]))
        return copies

    small_in[0] = small_0[...]
    small_in[1] = small_1[...]
    small_in[0, 7:8, :width] = gain_row
    small_in[1, 7:8, :width] = gain_1[0:1]
    small.start(0, small_in[1 - spot.s])
    for s in range(2):

        @pl.when(spot.s == s)
        def _(s=s):
            for copy in home_copies(s):
                copy.start()

    across.gather(1)
    first_core(lambda: around.send_part(1))
    running = small_in[spot.s] + small.end(0)
    small.start(1, running)
    around.shared_step(1)
    around.pass_part(0)
    across.gather(2)
    first_core(lambda: around.send_part(2))
    running = running + small.end(1)
    small.start(2, running)
    around.pass_part(1)
    across.gather(3)
    first_core(lambda: around.send_part(3))
    running = running + small.end(2)
    small.start(3, running)
    around.shared_step(2)
    across.gather(5)
    first_core(around.send_out)
    around.pass_part(2)
    running = running + small.end(3)
    small.start(4, running)
    around.pass_part(3)
    around.pass_out()
    small_out[...] = running + small.end(4)
    around.finish()
    for n in order[3:5]:
        across.sent(n)
    across.finish()
    for s in range(2):

        @pl.when(spot.s == s)
        def _(s=s):
            for copy in home_copies(s):
                copy.wait()

    total.close()


def comm_call(kernel, collective, ins, in_specs, outs, out_specs, scratch, name):
    return pl.pallas_call(
        kernel,
        out_shape=[jax.ShapeDtypeStruct(s, t) for s, t in outs],
        in_specs=in_specs,
        out_specs=out_specs,
        scratch_shapes=scratch,
        compiler_params=pltpu.CompilerParams(
            collective_id=collective, has_side_effects=True, vmem_limit_bytes=60 * 1024 * 1024
        ),
        name=name,
    )(*ins)


def fast_shards(
    tokens, cotangent, norm_gain, w_in, conv_weight, conv_bias, dt_bias, a_log, skip_gain, gate_gain, w_out
):
    section, place, half = lax.axis_index("section"), lax.axis_index("seq"), lax.axis_index("fsdp") // 2
    span, width = tokens.shape[2:]
    heads = HEADS // 8
    wide = heads * HEADDIM
    columns = 2 * wide + SHARED + HEADS
    shard = w_in.shape[1]
    ids = 8 * half + place + jnp.array([0, 4], jnp.int32)
    rows_in = w_in[0].T
    channels = jnp.concatenate(
        [
            conv_weight[0, :, :INNER], conv_bias[:, :INNER],
            jnp.repeat(skip_gain[0], HEADDIM)[None], gate_gain,
        ]
    )
    channels = widened(channels.reshape(7, -1, THIRD), 2, PIECE).reshape(7, -1)
    shared = jnp.concatenate([conv_weight[0, :, INNER:], conv_bias[:, INNER:], jnp.zeros((2, SHARED))])
    last_row = jnp.concatenate(
        [norm_gain, widened(dt_bias, 1, LANES), widened(a_log, 1, LANES)], axis=1
    )
    pack = jnp.concatenate([channels, shared], axis=1)
    pack = jnp.concatenate([pack, widened(last_row, 1, pack.shape[1])])
    group = (2, 4, span, width)
    weight_outs = [((columns, width), BF16), ((wide, width), BF16)]
    weight_s = Weights.scratch(columns, shard, width)
    payload = width + LANES
    tile, tile_out, packs, all_rows, all_cot = comm_call(
        open_kernel, 1,
        [rows_in, w_out[0], pack, tokens[:, 0], cotangent[:, 0]], [ANY] * 5,
        weight_outs + [((2,) + pack.shape, F32), (group, BF16), (group, BF16)], [ANY] * 5,
        weight_s + Spread.SEMS + Spread.SEMS
        + [pltpu.VMEM((span, width), BF16)] * 2 + [pltpu.VMEM(pack.shape, F32), DMA((3,)), DMA, DMA, DMA],
        "open",
    )
    own_rows = [lax.dynamic_index_in_dim(tokens[:, 0], section, 0, False)]
    own_cot = lax.dynamic_index_in_dim(cotangent[:, 0], section, 0, False)

    def joined(rows):
        return rows.reshape(2, 4 * span, rows.shape[-1])

    def cut(rows):
        return rows.reshape(2, 4, span, rows.shape[-1])

    tiles = [(tile, tile_out)]
    parts, _, normed, *kept = run_forward(
        heads, wide, joined(all_rows), tile, tile_out, (ids, packs[0])
    )
    saved = [(normed, kept)]
    tile, tile_out, all_rows, branch, scales, rows = comm_call(
        middle_kernel, 2,
        [rows_in, w_out[0], cut(parts), own_rows[0]], [ANY] * 3 + [VMEM],
        weight_outs
        + [(group, BF16), ((span, width), F32), ((span, LANES), F32), ((span, width), BF16)],
        [ANY] * 3 + [VMEM] * 3,
        weight_s + Sum.scratch(span, payload) + Spread.SEMS, "middle",
    )
    own_rows.append(rows)
    tiles.append((tile, tile_out))
    last_parts, sums, normed, *kept = run_forward(
        heads, wide, joined(all_rows), tile, tile_out, (ids, packs[1]), joined(all_cot)
    )
    saved.append((normed, kept))
    sums = comm_call(
        sums_kernel, 3, [sums], [VMEM], [(sums.shape, F32)], [VMEM],
        [pltpu.VMEM((7,) + sums.shape, F32), DMA((7,)), DMA((7,))], "sums",
    )[0]
    w_grads, wo_grads, small = [None, None], [None, None], [None, None]

    def products(l, proj_grad, normed_out, grads):
        w_grads[l] = dot_tn(proj_grad.reshape(-1, columns), saved[l][0].reshape(-1, width)).astype(BF16)
        wo_grads[l] = dot_tn(normed_out.reshape(-1, wide), grads.reshape(-1, width)).astype(BF16)

    parts, proj_grad, normed_out, small[1] = run_backward(
        heads, wide, joined(all_cot), sums, "rows", saved[1][1], *tiles[1], (ids, packs[1])
    )
    products(1, proj_grad, normed_out, joined(all_cot))
    rows_spec = ((span, width), BF16)
    results = GradsAcross.results(shard, width)
    across_s = GradsAcross.scratch(shard, columns, wide, width)
    all_grads, last_grad, gain_1, last_rows, *last_results = comm_call(
        turn_kernel, 4,
        [
            cut(parts), cut(last_parts), own_rows[1], own_cot, packs, branch, scales, own_rows[1],
            w_grads[1], wo_grads[1],
        ],
        [ANY, ANY] + [VMEM] * 6 + [ANY] * 2,
        [((2, 4, span, payload), BF16), rows_spec, ((8, width), F32), rows_spec] + results,
        [ANY] + [VMEM] * 6,
        Sum.scratch(span, width) + Sum.scratch(span, payload) + Spread.SEMS + across_s
        + [pltpu.VMEM((span, payload), BF16)], "turn",
    )
    all_grads = joined(all_grads)
    parts, proj_grad, normed_out, small[0] = run_backward(
        heads, wide, all_grads, None, "columns", saved[0][1], *tiles[0], (ids, packs[0])
    )
    products(0, proj_grad, normed_out, all_grads[..., :width])
    home_rows, home_grads, final, final_out, small = comm_call(
        close_kernel, 5,
        [
            cut(parts), own_rows[0], last_grad, packs, own_rows[1], last_rows, last_grad,
            w_grads[0], wo_grads[0], *small, gain_1, *last_results,
        ],
        [ANY] + [VMEM] * 6 + [ANY] * 2 + [VMEM] * 3 + [ANY] * 3,
        [
            ((2, span, width), BF16), ((2, span, width), BF16),
            ((2 * INNER + SHARED + HEADS, shard), BF16), (w_out.shape[1:], BF16), (pack.shape, F32),
        ],
        [ANY] * 4 + [VMEM],
        Sum.scratch(span, width) + across_s + [pltpu.VMEM(*r) for r in results]
        + GradsAround.scratch(shard) + SmallSum.scratch(pack.shape[1])
        + [
            pltpu.VMEM((span, width), BF16), pltpu.VMEM((2,) + pack.shape, F32),
            DMA((2,)), DMA((2,)), DMA((2,)), DMA((3,)),
        ],
        "close",
    )
    by_channel = small[:7, :-SHARED].reshape(7, -1, PIECE)[:, :, :THIRD].reshape(7, INNER)
    conv_rows = jnp.concatenate([by_channel[: CONV + 1], small[: CONV + 1, -SHARED:]], axis=1)
    return (
        home_rows[None, :, None],
        home_grads[None, :, None],
        small[7:8, :width],
        final.astype(F32).T[None],
        conv_rows[None, :CONV],
        conv_rows[CONV:],
        small[7:8, DT_AT : DT_AT + HEADS],
        small[7:8, RATE_AT : RATE_AT + HEADS],
        by_channel[5].reshape(HEADS, HEADDIM).sum(-1)[None],
        by_channel[6:7],
        final_out[None].astype(F32),
    )


def shards(
    tokens, cotangent, norm_gain, w_in, conv_weight, conv_bias, dt_bias, a_log, skip_gain, gate_gain, w_out
):
    section = lax.axis_index("section")
    place = lax.axis_index("seq")
    depth = lax.axis_index("fsdp")
    plan = Plan(lax.axis_size("seq"), lax.axis_size("fsdp"))
    half = depth // plan.mates
    micro, _, span, width = tokens.shape
    layers = lax.axis_size("section")
    wide, channels, heads = plan.wide, plan.channels, plan.heads

    shard = w_in[0]
    gate_part = widened(plan.take(shard[:, :INNER], 1, place), 2, wide)
    x_part = widened(plan.take(shard[:, INNER : 2 * INNER], 1, place), 2, wide)
    shared_part = jnp.broadcast_to(
        shard[:, 2 * INNER : INNER + XBC], (plan.halves, shard.shape[0], SHARED)
    )
    dt_part = widened(plan.take(shard[:, INNER + XBC :], 1, place), 2, LANES)
    tile = jnp.concatenate([gate_part, x_part, shared_part, dt_part], axis=2)
    tile = jnp.repeat(tile, plan.mates, axis=0)
    tile = lax.all_to_all(tile, "fsdp", 0, 0, tiled=True).reshape(width, -1).T
    w_tiles = lax.all_gather(tile, "section", axis=0)
    if plan.pieces == plan.mates:
        piece = w_out[0].reshape(plan.seq, -1, width)
        piece = lax.dynamic_index_in_dim(piece, place, 0, False)
        rows_out = lax.all_gather(
            piece, "fsdp", axis=0, tiled=True, axis_index_groups=plan.mate_groups
        )
    else:
        rows_out = lax.all_gather(w_out[0], "fsdp", axis=0, tiled=True)
        rows_out = lax.dynamic_index_in_dim(plan.take(rows_out, 0, place), half, 0, False)
    wo_tiles = lax.all_gather(widened(rows_out, 0, wide), "section", axis=0)

    def own(array, axis, size):
        part = lax.dynamic_index_in_dim(plan.take(array, axis, place), half, 0, False)
        return widened(part, axis, size)

    skip_wide = jnp.repeat(skip_gain[0], HEADDIM)[None]
    by_channel = jnp.concatenate(
        [conv_weight[0, :, :INNER], conv_bias[:, :INNER], skip_wide, gate_gain, jnp.zeros((1, INNER))], 0
    )
    by_channel = own(by_channel, 1, wide)
    by_shared = jnp.concatenate(
        [conv_weight[0, :, INNER:], conv_bias[:, INNER:], jnp.zeros((3, SHARED))], 0
    )
    by_head = jnp.concatenate([dt_bias, a_log, jnp.zeros((6, HEADS))], 0)
    by_head = own(by_head, 1, LANES)
    smalls = jnp.concatenate(
        [by_channel.ravel(), by_shared.ravel(), by_head.ravel(), norm_gain[0]]
    )
    smalls = lax.all_gather(smalls, "section", axis=0)
    cuts = [8 * wide, 8 * (wide + SHARED), 8 * (wide + SHARED + LANES)]
    params = []
    for l in range(layers):
        ch, bc, dtp, gain = jnp.split(smalls[l], cuts)
        params.append((gain[None], ch.reshape(8, -1), bc.reshape(8, -1), dtp.reshape(8, -1)))

    def gather_rows(own_rows):
        rows = lax.all_gather(own_rows, "seq", axis=0, tiled=True)
        if plan.halves == 1:
            return rows[None]
        return lax.all_gather(rows, "fsdp", axis=0, axis_index_groups=plan.peer_groups)

    def sum_rows(parts):
        if plan.halves == 1:
            rows = parts[0]
        else:
            rows = lax.psum_scatter(
                parts, "fsdp", scatter_dimension=0, axis_index_groups=plan.peer_groups
            )
        return lax.psum_scatter(rows, "seq", scatter_dimension=0, tiled=True)

    own_tokens = lax.dynamic_index_in_dim(tokens, section, 0, False)[0]
    own_cot = lax.dynamic_index_in_dim(cotangent, section, 0, False)[0]
    inputs, outputs, branch, saved, scales = [own_tokens], [], [], [], []
    for l in range(layers):
        rows = gather_rows(inputs[l])
        parts, square, normed, *kept = run_forward(
            heads, wide, rows, w_tiles[l], wo_tiles[l], params[l]
        )
        saved.append((normed, kept))
        total = sum_rows(parts).astype(F32)
        square = sum_rows(square)[:, :1]
        scale = lax.rsqrt(square / INNER + NORM_EPS)
        branch.append(total * scale)
        scales.append(scale)
        outputs.append((inputs[l].astype(F32) + branch[l]).astype(BF16))
        inputs.append(outputs[l])
    grads_in, small_grads = [None] * layers, [None] * layers
    w_grads, wo_grads = [None] * layers, [None] * layers
    grad_rows = own_cot
    for l in reversed(range(layers)):
        rdot = jnp.sum(grad_rows.astype(F32) * branch[l], axis=-1, keepdims=True)
        aux = widened(jnp.concatenate([scales[l], rdot], axis=1), 1, LANES)
        all_grads = gather_rows(grad_rows)
        aux = gather_rows(aux)
        normed, kept = saved[l]
        parts, proj_grad, normed_out, g_ch, g_bc, g_dt = run_backward(
            heads, wide, all_grads, aux, "lanes", kept, w_tiles[l], wo_tiles[l], params[l]
        )
        w_grads[l] = dot_tn(normed.reshape(-1, width), proj_grad.reshape(-1, proj_grad.shape[-1])).astype(BF16)
        wo_grads[l] = dot_tn(normed_out.reshape(-1, wide), all_grads.reshape(-1, width)).astype(BF16)
        grad_normed = sum_rows(parts).astype(F32)
        rows = inputs[l].astype(F32)
        scale = lax.rsqrt(jnp.mean(rows * rows, axis=-1, keepdims=True) + NORM_EPS)
        scaled = rows * scale
        g_gain = jnp.sum(grad_normed * scaled, axis=0)
        pulled = grad_normed * params[l][0]
        inner = jnp.mean(pulled * scaled, axis=-1, keepdims=True)
        grad = scale * (pulled - scaled * inner) + grad_rows.astype(F32)
        grad_rows = grad.astype(BF16)
        grads_in[l] = grad_rows

        def placed(value, size):
            value = value[..., :size]
            full = jnp.zeros((plan.seq, plan.halves) + value.shape, F32)
            full = lax.dynamic_update_slice(full, value[None, None], (place, half, 0, 0))
            return plan.put(full, 1)

        by_channel = placed(g_ch, channels)
        by_head = placed(g_dt, heads)
        skip = by_channel[5].reshape(HEADS, HEADDIM).sum(-1)
        small_grads[l] = jnp.concatenate(
            [
                g_gain, by_channel[:5].ravel(), g_bc[:5].ravel(), by_head[0], by_head[1], skip, by_channel[6]
            ]
        )

    smalls = lax.psum(jnp.stack(small_grads), ("section", "seq", "fsdp"))
    smalls = lax.dynamic_index_in_dim(smalls, section, 0, False)
    cuts, at = [], 0
    for size in (width, (CONV + 1) * INNER, (CONV + 1) * SHARED, HEADS, HEADS, HEADS):
        at += size
        cuts.append(at)
    g_gain, g_x, g_bc, g_shift, g_rate, g_skip, g_gate = jnp.split(smalls, cuts)
    conv_rows = jnp.concatenate([g_x.reshape(CONV + 1, -1), g_bc.reshape(CONV + 1, -1)], axis=1)

    w_grad = lax.psum_scatter(jnp.stack(w_grads), "section", scatter_dimension=0)
    w_grad = lax.all_to_all(w_grad, "fsdp", 0, 0, tiled=True)
    w_grad = w_grad.reshape(plan.halves, plan.mates, -1, w_grad.shape[-1]).astype(F32).sum(1)
    shared_grad = lax.psum(w_grad[..., 2 * wide : 2 * wide + SHARED].sum(0), "seq")
    head_grads = jnp.concatenate(
        [
            w_grad[..., :channels],
            w_grad[..., wide : wide + channels],
            w_grad[..., 2 * wide + SHARED : 2 * wide + SHARED + heads],
        ],
        axis=-1,
    ).astype(BF16)
    head_grads = lax.all_gather(head_grads, "seq", axis=0)
    grad_w_in = jnp.concatenate(
        [
            plan.put(head_grads[..., :channels], 1),
            plan.put(head_grads[..., channels : 2 * channels], 1),
            shared_grad.astype(BF16),
            plan.put(head_grads[..., 2 * channels :], 1),
        ],
        axis=-1,
    ).astype(F32)
    wo_grad = lax.psum_scatter(jnp.stack(wo_grads)[:, :channels], "section", scatter_dimension=0)
    if plan.pieces == plan.mates:
        wo_grad = lax.psum_scatter(
            wo_grad, "fsdp", scatter_dimension=0, tiled=True, axis_index_groups=plan.mate_groups
        )
        wo_grad = lax.all_gather(wo_grad, "seq", axis=0, tiled=True)
    else:
        full = jnp.zeros((plan.seq, plan.halves) + wo_grad.shape, BF16)
        full = lax.dynamic_update_slice(full, wo_grad[None, None], (place, half, 0, 0))
        full = plan.put(full, 0)
        wo_grad = lax.psum_scatter(full, "fsdp", scatter_dimension=0, tiled=True)
        wo_grad = lax.psum(wo_grad, "seq")

    def home(per_layer):
        return lax.all_to_all(jnp.stack(per_layer), "section", 0, 0, tiled=True)[None, :, None]

    return (
        home(outputs),
        home(grads_in),
        g_gain[None],
        grad_w_in[None],
        conv_rows[None, :CONV],
        conv_rows[CONV:],
        g_shift[None],
        g_rate[None],
        g_skip[None],
        g_gate[None],
        wo_grad.astype(F32)[None],
    )


def solution(mesh):
    shape = tuple(mesh.shape[a] for a in ("section", "seq", "fsdp"))
    return jax.shard_map(
        fast_shards if shape == (2, 4, 4) else shards,
        mesh=mesh,
        in_specs=(
            P(None, "fsdp", "seq", None),
            P(None, "fsdp", "seq", None),
            P("section", None),
            P("section", "fsdp", None),
            P("section", None, None),
            P("section", None),
            P("section", None),
            P("section", None),
            P("section", None),
            P("section", None),
            P("section", "fsdp", None),
        ),
        out_specs=(
            P("section", None, "fsdp", "seq", None),
            P("section", None, "fsdp", "seq", None),
            P("section", None),
            P("section", "fsdp", None),
            P("section", None, None),
            P("section", None),
            P("section", None),
            P("section", None),
            P("section", None),
            P("section", None),
            P("section", "fsdp", None),
        ),
        check_vma=False,
    )
```

```python
from functools import partial

import jax
import jax.numpy as jnp
from jax import lax
from jax.experimental import pallas as pl
from jax.experimental.pallas import tpu as pltpu
from jax.sharding import PartitionSpec as P

HEADS = 48
HEADDIM = 64
STATE = 128
CONV = 4
SPAN = 256
INNER = 3072
XBC = 3328
SHARED = 2 * STATE
LANES = 128
THIRD = 192
PIECE = 256
GAIN_END = 1536
DT_AT = 1536
RATE_AT = DT_AT + LANES
NORM_EPS = 1e-05
HIGHEST = lax.Precision.HIGHEST
BF16 = jnp.bfloat16
F32 = jnp.float32


def take(refs, counts):
    refs = list(refs)
    return [[refs.pop(0) for _ in range(n)] for n in counts]


def dot(left, right, contract=((1,), (0,)), precision=None):
    return lax.dot_general(
        left, right, (contract, ((), ())), preferred_element_type=F32, precision=precision
    )


def dot_nt(left, right):
    return dot(left, right, ((1,), (1,)))


def dot_tn(left, right):
    return dot(left, right, ((0,), (0,)))


def sigmoid(value):
    return 1.0 / (1.0 + jnp.exp(-value))


def shifted(value, distance):
    if distance == 0:
        return value
    length = value.shape[0]
    rows = lax.broadcasted_iota(jnp.int32, value.shape, 0)
    moved = pltpu.roll(value, distance % length, 0)
    if distance > 0:
        return jnp.where(rows >= distance, moved, 0.0)
    return jnp.where(rows < length + distance, moved, 0.0)


def conv_sum(raw, taps):
    total = taps[CONV : CONV + 1]
    for k in range(CONV):
        total = total + taps[k : k + 1] * shifted(raw, CONV - 1 - k)
    return total


def conv_back(grad, raw, taps):
    grad_raw = 0.0
    rows = []
    for k in range(CONV):
        grad_raw = grad_raw + taps[k : k + 1] * shifted(grad, -(CONV - 1 - k))
        rows.append(jnp.sum(grad * shifted(raw, CONV - 1 - k), axis=0, keepdims=True))
    rows.append(jnp.sum(grad, axis=0, keepdims=True))
    return grad_raw, rows


def stacked(rows, count):
    width = rows[0].shape[1]
    short = count - len(rows)
    return jnp.concatenate(rows + [jnp.zeros((short, width), F32)], axis=0)


def triangles():
    row_ids = lax.broadcasted_iota(jnp.int32, (SPAN, SPAN), 0)
    col_ids = lax.broadcasted_iota(jnp.int32, (SPAN, SPAN), 1)
    return row_ids >= col_ids


def step_sizes(dt_raw, dt_row):
    shift = dt_raw + dt_row
    step = jnp.maximum(shift, 0.0) + jnp.log1p(jnp.exp(-jnp.abs(shift)))
    return step, sigmoid(shift)


def low_half():
    return lax.broadcasted_iota(jnp.int32, (SPAN, LANES), 1) < HEADDIM


def head_lanes(h):
    lanes = lax.broadcasted_iota(jnp.int32, (1, LANES), 1)
    return (lanes < HEADDIM) if h % 2 == 0 else (lanes >= HEADDIM)


def split_three(value):
    lanes = lax.broadcasted_iota(jnp.int32, (value.shape[0], LANES), 1)
    result = jnp.zeros((value.shape[0], LANES), F32)
    for k in range(3):
        part = value.astype(BF16).astype(F32)
        result = jnp.where(lanes == k, part, result)
        value = value - part
    return result.astype(BF16)


def selection(ids):
    rows = lax.broadcasted_iota(jnp.int32, (HEADS, LANES), 0)
    columns = lax.broadcasted_iota(jnp.int32, (HEADS, LANES), 1)
    target = jnp.full((HEADS, LANES), -1, jnp.int32)
    for j in range(2):
        here = (columns >= 3 * j) & (columns < 3 * j + 3)
        target = jnp.where(here, columns + 3 * (ids[j] - j), target)
    return (rows == target).astype(F32)


def piece_lanes(ids, j):
    return pl.ds(pl.multiple_of(ids[j] * PIECE, PIECE), PIECE)


def load_params(refs):
    if len(refs) == 2:
        ids, pack_ref = refs
        sel = selection(ids)
        ch = jnp.concatenate([pack_ref[:, piece_lanes(ids, j)][:, :THIRD] for j in range(2)], axis=1)
        rows = [pack_ref[7:8, at : at + HEADS] for at in (DT_AT, RATE_AT)]
        dtp = dot(stacked(rows, 8), sel, precision=HIGHEST)
        return pack_ref[7:8, :GAIN_END], ch, pack_ref[:, -SHARED:], dtp, sel.astype(BF16)
    gain_ref, ch_ref, bc_ref, dtp_ref = refs
    return gain_ref[...], ch_ref[...], bc_ref[...], dtp_ref[...], None


def forward_kernel(heads, *refs):
    u_ref, w_ref, wo_ref, *refs = refs
    forward_rows(heads, load_params(refs[:4]), 0, u_ref, w_ref, wo_ref, None, refs[4:])


def forward_rows(heads, params, i, u_ref, w_ref, wo_ref, h_ref, outs):
    gain, ch, bc, dtp, sel = params
    out_ref, sums_ref, normed_ref, gate_ref, xraw_ref, bcraw_ref, dtraw_ref, mixed_ref = outs
    length, width = u_ref.shape[1:]
    wide = ch.shape[1]
    blocks = length // SPAN
    rows = u_ref[i].astype(F32)
    scale = lax.rsqrt(jnp.mean(rows * rows, axis=-1, keepdims=True) + NORM_EPS)
    normed = (rows * scale * gain).astype(BF16)
    normed_ref[i] = normed
    gate = dot_nt(normed, w_ref[:wide])
    gate_ref[i] = gate
    x_raw = dot_nt(normed, w_ref[wide : 2 * wide]).astype(BF16)
    xraw_ref[i] = x_raw
    rest = dot_nt(normed, w_ref[2 * wide :]).astype(BF16)
    bcraw_ref[i] = rest[:, :SHARED]
    dt_raw = rest[:, SHARED:]
    if sel is not None:
        dt_raw = dot(dt_raw, sel).astype(BF16)
    dtraw_ref[i] = dt_raw
    conv_x = conv_sum(x_raw.astype(F32), ch)
    act_x = (conv_x * sigmoid(conv_x)).astype(BF16)
    conv_bc = conv_sum(rest[:, :SHARED].astype(F32), bc)
    act_bc = (conv_bc * sigmoid(conv_bc)).astype(BF16)
    step, _ = step_sizes(dt_raw.astype(F32), dtp[0:1])
    rate = jnp.exp(dtp[1:2])
    causal = triangles()
    ones = causal.astype(F32)
    lower = low_half()
    carries = [None] * heads
    for b in range(blocks):
        span = slice(b * SPAN, (b + 1) * SPAN)
        step_b = step[span]
        decay = -dot(ones, rate * step_b, precision=HIGHEST)
        decay_t, step_t = decay.T, step_b.T
        b_in, c_out = act_bc[span, :STATE], act_bc[span, STATE:]
        scores = dot_nt(c_out, b_in)
        for first in range(0, heads, 2):
            lanes = slice(first * HEADDIM, first * HEADDIM + LANES)
            x_pair = act_x[span, lanes]
            parts = []
            for h in range(first, min(first + 2, heads)):
                gap = decay[:, h : h + 1] - decay_t[h : h + 1]
                mask = jnp.exp(jnp.where(causal, gap, -1e30))
                weights = (scores * mask * step_t[h : h + 1]).astype(BF16)
                part = dot(weights, x_pair)
                if carries[h] is not None:
                    part += jnp.exp(decay[:, h : h + 1]) * dot(c_out, carries[h].astype(BF16))
                if b + 1 < blocks:
                    last = decay[SPAN - 1 :, h : h + 1]
                    tail = jnp.exp(last - decay[:, h : h + 1]) * step_b[:, h : h + 1]
                    shaped = (b_in.astype(F32) * tail).astype(BF16)
                    fresh = dot_tn(shaped, x_pair)
                    if carries[h] is not None:
                        fresh += jnp.exp(last) * carries[h]
                    carries[h] = fresh
                parts.append(part)
            if len(parts) == 1:
                parts.append(jnp.zeros_like(parts[0]))
            within = jnp.where(lower, parts[0], parts[1])
            mixed = within + ch[5:6, lanes] * x_pair.astype(F32)
            mixed_ref[i, span, lanes] = mixed.astype(BF16)
    gated = mixed_ref[i].astype(F32) * (gate * sigmoid(gate))
    square = jnp.sum(gated * gated, axis=-1, keepdims=True)
    scaled = gated * ch[6:7]
    out_ref[i, :, :width] = dot(scaled.astype(BF16), wo_ref[...]).astype(BF16)
    if sel is None:
        sums_ref[i] = jnp.broadcast_to(square, sums_ref.shape[1:])
        return
    out_ref[i, :, width:] = split_three(square)
    if h_ref is not None:
        grad_no = dot_nt(h_ref[i], wo_ref[...])
        cross = jnp.sum(grad_no * scaled, axis=-1, keepdims=True)
        lane_ids = lax.broadcasted_iota(jnp.int32, (length, LANES), 1)
        both = jnp.where(lane_ids == 0, square, jnp.where(lane_ids == 1, cross, 0.0))
        sums_ref[i] = both.T[:8]


def backward_kernel(heads, *refs):
    h_ref, aux_ref, *refs = refs
    saved, (w_ref, wo_ref), params, outs, sum_refs, scratch = take(refs, (5, 2, 4, 3, 3, 4))
    params = load_params(params)
    aux = aux_ref[0, :, 0:1], aux_ref[0, :, 1:2]
    sums = backward_rows(heads, params, 0, h_ref, aux, saved, w_ref, wo_ref, outs, scratch)
    for ref, value in zip(sum_refs, sums):

        @pl.when(pl.program_id(0) == 0)
        def _(ref=ref, value=value):
            ref[...] = value

        @pl.when(pl.program_id(0) > 0)
        def _(ref=ref, value=value):
            ref[...] += value


def aux_of_columns(h_ref, i, width):
    aux = h_ref[i, :, width:].astype(F32)
    return aux[:, 0:1] + aux[:, 1:2] + aux[:, 2:3], aux[:, 3:4] + aux[:, 4:5] + aux[:, 5:6]


def aux_of_rows(sums):
    aux = jnp.concatenate([sums, jnp.zeros((LANES - 8, sums.shape[1]), F32)], axis=0).T
    scale = lax.rsqrt(aux[:, 0:1] * (1.0 / INNER) + NORM_EPS)
    return scale, aux[:, 1:2] * scale


def backward_rows(heads, params, i, h_ref, aux, saved, w_ref, wo_ref, outs, scratch):
    _, ch, bc, dtp, sel = params
    gate_ref, xraw_ref, bcraw_ref, dtraw_ref, mixed_ref = saved
    dn_ref, pg_ref, no_ref = outs
    dmix_s, dx_s, dbc_s, ddt_s = scratch
    length, width = dn_ref.shape[1:]
    wide = ch.shape[1]
    blocks = length // SPAN
    h_rows = h_ref[i, :, :width]
    scale, rdot = aux
    gate = gate_ref[i]
    mixed = mixed_ref[i].astype(F32)
    sig = sigmoid(gate)
    silu = gate * sig
    gated = mixed * silu
    gain = ch[6:7]
    grad_no = dot_nt(h_rows, wo_ref[...])
    grad_g = scale * (gain * grad_no) - gated * (scale * scale * (1.0 / INNER) * rdot)
    scaled = gated * scale
    no_ref[i] = (scaled * gain).astype(BF16)
    gain_row = jnp.sum(grad_no * scaled, axis=0, keepdims=True)
    dmix_s[...] = (grad_g * silu).astype(BF16)
    pg_ref[i, :, :wide] = (grad_g * mixed * (sig * (1.0 + gate * (1.0 - sig)))).astype(BF16)

    x_raw = xraw_ref[i].astype(F32)
    bc_raw = bcraw_ref[i].astype(F32)
    conv_x = conv_sum(x_raw, ch)
    sig_x = sigmoid(conv_x)
    act_x = (conv_x * sig_x).astype(BF16)
    conv_bc = conv_sum(bc_raw, bc)
    sig_bc = sigmoid(conv_bc)
    act_bc = (conv_bc * sig_bc).astype(BF16)
    step, slope = step_sizes(dtraw_ref[i].astype(F32), dtp[0:1])
    rate = jnp.exp(dtp[1:2])
    causal = triangles()
    ones = causal.astype(F32)
    lower = low_half()
    lane_ids = lax.broadcasted_iota(jnp.int32, (SPAN, LANES), 1)
    last_row = lax.broadcasted_iota(jnp.int32, (SPAN, 1), 0) == SPAN - 1
    decays = []
    for b in range(blocks):
        decays.append(-dot(ones, rate * step[b * SPAN : (b + 1) * SPAN], precision=HIGHEST))
    entering = [[None] * heads for _ in range(blocks)]
    for b in range(blocks - 1):
        span = slice(b * SPAN, (b + 1) * SPAN)
        b_in = act_bc[span, :STATE].astype(F32)
        for h in range(heads):
            lanes = slice(h // 2 * LANES, h // 2 * LANES + LANES)
            column = decays[b][:, h : h + 1]
            last = column[SPAN - 1 :]
            tail = jnp.exp(last - column) * step[span, h : h + 1]
            fresh = dot_tn((b_in * tail).astype(BF16), act_x[span, lanes])
            if entering[b][h] is not None:
                fresh += jnp.exp(last) * entering[b][h]
            entering[b + 1][h] = fresh
    leaving = [None] * heads
    rate_row = jnp.zeros((1, LANES), F32)
    for b in reversed(range(blocks)):
        span = slice(b * SPAN, (b + 1) * SPAN)
        step_b, decay = step[span], decays[b]
        decay_t, step_t = decay.T, step_b.T
        b_in, c_out = act_bc[span, :STATE], act_bc[span, STATE:]
        scores = dot_nt(c_out, b_in)
        grad_scores = jnp.zeros((SPAN, SPAN), F32)
        grad_b = jnp.zeros((SPAN, STATE), F32)
        grad_c = jnp.zeros((SPAN, STATE), F32)
        row_sums = jnp.zeros((SPAN, LANES), F32)
        grad_step = jnp.zeros((SPAN, LANES), F32)
        col_rows = []
        for first in range(0, heads, 2):
            lanes = slice(first * HEADDIM, first * HEADDIM + LANES)
            x_pair = act_x[span, lanes]
            grad_pair = dmix_s[span, lanes]
            parts = []
            for h in range(first, min(first + 2, heads)):
                own = head_lanes(h)
                grad_own = jnp.where(own, grad_pair, jnp.zeros((), BF16))
                column = decay[:, h : h + 1]
                mask = jnp.exp(jnp.where(causal, column - decay_t[h : h + 1], -1e30))
                spread = mask * step_t[h : h + 1]
                weights = (scores * spread).astype(BF16)
                part = dot_tn(weights, grad_pair)
                grad_w = dot_nt(grad_own, x_pair)
                grad_scores += grad_w * spread
                pulled = grad_w * (scores * mask)
                col_rows.append(jnp.sum(pulled, axis=0, keepdims=True))
                row_sum = jnp.sum(pulled * step_t[h : h + 1], axis=1, keepdims=True)
                if entering[b][h] is not None:
                    carry = entering[b][h].astype(BF16)
                    grown = jnp.exp(column)
                    grad_grown = grad_own.astype(F32) * grown
                    grad_c += dot_nt(grad_grown.astype(BF16), carry)
                    grad_carry = dot_tn(c_out, grad_grown.astype(BF16))
                    row_sum += jnp.sum(grad_grown * dot(c_out, carry), axis=1, keepdims=True)
                else:
                    grad_carry = None
                if leaving[h] is not None:
                    last = column[SPAN - 1 :]
                    fade = jnp.exp(last - column)
                    tail = fade * step_b[:, h : h + 1]
                    b_wide = b_in.astype(F32)
                    grad_state = leaving[h].astype(BF16)
                    grad_shaped = dot_nt(x_pair, grad_state)
                    part += dot((b_wide * tail).astype(BF16), grad_state)
                    grad_b += grad_shaped * tail
                    grad_tail = jnp.sum(grad_shaped * b_wide, axis=1, keepdims=True)
                    grad_step += jnp.where(lane_ids == h, grad_tail * fade, 0.0)
                    moved = grad_tail * tail
                    total = jnp.sum(moved, axis=0, keepdims=True)
                    if entering[b][h] is not None:
                        faded = jnp.exp(last) * leaving[h]
                        kept = jnp.sum(faded * entering[b][h], axis=1, keepdims=True)
                        total += jnp.sum(kept, axis=0, keepdims=True)
                        grad_carry += faded
                    row_sum += jnp.where(last_row, total, 0.0) - moved
                leaving[h] = grad_carry
                row_sums += jnp.where(lane_ids == h, row_sum, 0.0)
                parts.append(part)
            if len(parts) == 1:
                parts.append(jnp.zeros_like(parts[0]))
            grad_x = jnp.where(lower, parts[0], parts[1])
            dx_s[span, lanes] = grad_x + ch[5:6, lanes] * grad_pair.astype(F32)
        col_sums = stacked(col_rows, LANES).T
        low_scores = grad_scores.astype(BF16)
        dbc_s[span, :STATE] = grad_b + dot_tn(low_scores, c_out)
        dbc_s[span, STATE:] = grad_c + dot(low_scores, b_in)
        grad_decay = dot(
            ones, row_sums - step_b * col_sums, ((0,), (0,)), precision=HIGHEST
        )
        ddt_s[span] = col_sums + grad_step - rate * grad_decay
        rate_row -= jnp.sum(grad_decay * step_b, axis=0, keepdims=True)

    skip_row = jnp.sum(dmix_s[...].astype(F32) * act_x.astype(F32), axis=0, keepdims=True)
    grad_conv = dx_s[...] * (sig_x * (1.0 + conv_x * (1.0 - sig_x)))
    grad_raw, ch_rows = conv_back(grad_conv, x_raw, ch)
    pg_ref[i, :, wide : 2 * wide] = grad_raw.astype(BF16)
    grad_conv = dbc_s[...] * (sig_bc * (1.0 + conv_bc * (1.0 - sig_bc)))
    grad_raw, bc_rows = conv_back(grad_conv, bc_raw, bc)
    pg_ref[i, :, 2 * wide : 2 * wide + SHARED] = grad_raw.astype(BF16)
    grad_dt = ddt_s[...] * slope
    low_dt = grad_dt.astype(BF16)
    if sel is not None:
        low_dt = dot_nt(low_dt, sel).astype(BF16)
    pg_ref[i, :, 2 * wide + SHARED :] = low_dt
    dn_ref[i] = dot(pg_ref[i], w_ref[...]).astype(BF16)
    by_channel = stacked(ch_rows + [skip_row, gain_row], 8)
    by_shared = stacked(bc_rows, 8)
    by_head = stacked([jnp.sum(grad_dt, axis=0, keepdims=True), rate_row * rate], 8)
    if sel is not None:
        by_head = lax.dot_general(
            by_head, sel.astype(F32), (((1,), (1,)), ((), ())),
            preferred_element_type=F32, precision=HIGHEST,
        )
    return by_channel, by_shared, by_head


def add_small(sum_ref, ids, by_channel, by_shared, by_head):
    for j in range(2):
        part = by_channel[:, j * THIRD : (j + 1) * THIRD]
        part = jnp.concatenate([part, jnp.zeros((8, PIECE - THIRD), F32)], axis=1)
        sum_ref[:, piece_lanes(ids, j)] += part
    sum_ref[:, -SHARED:] += by_shared
    sum_ref[7:8, DT_AT : DT_AT + HEADS] += by_head[0:1]
    sum_ref[7:8, RATE_AT : RATE_AT + HEADS] += by_head[1:2]


def whole_spec(array):
    return pl.BlockSpec(array.shape, lambda i: (0,) * array.ndim)


def row_spec(length, width):
    return pl.BlockSpec((1, length, width), lambda i: (i, 0, 0))


def block_spec(array):
    return pl.BlockSpec((1,) + array.shape[1:], lambda i: (i, 0, 0))


PARAMS = dict(vmem_limit_bytes=60 * 1024 * 1024)


def run_forward(heads, wide, rows, w, wo, params):
    count, length, width = rows.shape
    constants = [w, wo, *params]
    outs = [
        (width, BF16), (LANES, F32), (width, BF16), (wide, F32),
        (wide, BF16), (SHARED, BF16), (LANES, BF16), (wide, BF16),
    ]
    return pl.pallas_call(
        partial(forward_kernel, heads),
        grid=(count,),
        out_shape=[jax.ShapeDtypeStruct((count, length, n), t) for n, t in outs],
        in_specs=[block_spec(rows)] + [whole_spec(c) for c in constants],
        out_specs=[row_spec(length, n) for n, _ in outs],
        compiler_params=pltpu.CompilerParams(**PARAMS),
        name="forward",
    )(rows, *constants)


def run_backward(heads, wide, grad_rows, aux, saved, w, wo, params):
    count, length, _ = grad_rows.shape
    columns, width = w.shape
    given = [grad_rows, aux, *saved]
    constants = [w, wo, *params]
    outs = [(width, BF16), (columns, BF16), (wide, BF16)]
    sums = [(8, wide), (8, SHARED), (8, LANES)]
    return pl.pallas_call(
        partial(backward_kernel, heads),
        grid=(count,),
        out_shape=[jax.ShapeDtypeStruct((count, length, n), t) for n, t in outs]
        + [jax.ShapeDtypeStruct(s, F32) for s in sums],
        in_specs=[block_spec(g) for g in given] + [whole_spec(c) for c in constants],
        out_specs=[row_spec(length, n) for n, _ in outs]
        + [pl.BlockSpec(s, lambda i: (0, 0)) for s in sums],
        scratch_shapes=backward_scratch(length, wide),
        compiler_params=pltpu.CompilerParams(**PARAMS),
        name="backward",
    )(*given, *constants)


def backward_scratch(length, wide):
    return [
        pltpu.VMEM((length, wide), BF16),
        pltpu.VMEM((length, wide), F32),
        pltpu.VMEM((length, SHARED), F32),
        pltpu.VMEM((length, LANES), F32),
    ]


class Plan:
    def __init__(self, seq, fsdp):
        self.seq, self.fsdp = seq, fsdp
        halves = 2
        if fsdp % 2 or HEADS % (seq * 2) or (HEADS // fsdp) % seq:
            halves = 1
        self.halves, self.mates = halves, fsdp // halves
        self.heads = HEADS // (seq * halves)
        self.pieces = self.mates if (HEADS // fsdp) % seq == 0 else 1
        channels = self.heads * HEADDIM
        self.channels = channels
        self.wide = -(-channels // LANES) * LANES
        self.peer_groups = [[lo + self.mates * h for h in range(halves)] for lo in range(self.mates)]
        self.mate_groups = [[h * self.mates + j for j in range(self.mates)] for h in range(halves)]

    def split(self, array, axis):
        size = array.shape[axis] // (self.halves * self.pieces * self.seq)
        shape = array.shape[:axis] + (self.halves, self.pieces, self.seq, size) + array.shape[axis + 1 :]
        return array.reshape(shape)

    def take(self, array, axis, place):
        array = lax.dynamic_index_in_dim(self.split(array, axis), place, axis + 2, False)
        shape = array.shape[: axis + 1] + (-1,) + array.shape[axis + 3 :]
        return jnp.moveaxis(array.reshape(shape), axis, 0)

    def put(self, parts, axis):
        size = parts.shape[axis + 2] // self.pieces
        shape = parts.shape[: axis + 2] + (self.pieces, size) + parts.shape[axis + 3 :]
        parts = jnp.moveaxis(parts.reshape(shape), (1, axis + 2, 0), (axis, axis + 1, axis + 2))
        shape = parts.shape[:axis] + (-1,) + parts.shape[axis + 4 :]
        return parts.reshape(shape)


def widened(array, axis, size):
    pads = [(0, 0)] * array.ndim
    pads[axis] = (0, size - array.shape[axis])
    return jnp.pad(array, pads)


MESH = pl.DeviceIdType.MESH
ANY = pl.BlockSpec(memory_space=pl.ANY)
VMEM = pl.BlockSpec(memory_space=pltpu.VMEM)
DMA = pltpu.SemaphoreType.DMA


class Spot:
    def __init__(self):
        self.s, self.q, self.z = (lax.axis_index(a) for a in ("section", "seq", "fsdp"))
        self.half, self.lo = self.z // 2, self.z % 2
        self.mate, self.twin = self.z + 1 - 2 * self.lo, (self.z + 2) % 4
        self.around = [None, self.q + 1 - 2 * (self.q % 2), (self.q + 2) % 4, 3 - self.q]
        self.sibling = (1 - self.s, self.q, self.z)
        self.at_mate, self.at_twin = (self.s, self.q, self.mate), (self.s, self.q, self.twin)

    def plane(self, k):
        return (self.s, self.around[k], self.z)

    def column(self, z):
        return (self.s, self.q, z)

    def piece(self, half, j):
        return 8 * half + 4 * j + self.q


def greet(places):
    barrier = pltpu.get_barrier_semaphore()
    for place in places:
        pl.semaphore_signal(barrier, inc=1, device_id=place, device_id_type=MESH)
    pl.semaphore_wait(barrier, len(places))


def remote(src, dst, send_sem, recv_sem, place):
    return pltpu.make_async_remote_copy(
        src_ref=src, dst_ref=dst, send_sem=send_sem, recv_sem=recv_sem, device_id=place, device_id_type=MESH
    )


class Home:
    def __init__(self, src, buffer, dst, sems):
        self.load = pltpu.make_async_copy(src, buffer, sems[0])
        self.store = pltpu.make_async_copy(buffer, dst, sems[1])

    def begin(self):
        self.load.start()

    def go_on(self):
        self.load.wait()
        self.store.start()

    def end(self):
        self.store.wait()


class Spread:
    SEMS = [DMA((7,)), DMA((7,)), DMA]

    def __init__(self, spot, own, all_rows, sems):
        self.spot, self.own, self.all = spot, own, all_rows
        self.send, self.recv, self.local = sems

    def slot(self, half):
        rows = self.own.shape[0]
        return self.all.at[half, pl.ds(pl.multiple_of(self.spot.q * rows, rows), rows)]

    def copy(self, j):
        spot = self.spot
        slot = self.slot(spot.half)
        if j == 3:
            return remote(self.own, slot, self.send.at[3], self.recv.at[3], spot.at_twin)
        if j < 3:
            return remote(self.own, slot, self.send.at[j], self.recv.at[j], spot.plane(j + 1))
        slot = self.slot(1 - spot.half)
        return remote(slot, slot, self.send.at[j], self.recv.at[j], spot.plane(j - 3))

    def here(self):
        return pltpu.make_async_copy(self.own, self.slot(self.spot.half), self.local)

    def start(self):
        for j in (3, 0, 1, 2):
            self.copy(j).start()
        self.here().start()

    def forward(self):
        self.copy(3).wait_recv()
        for j in (4, 5, 6):
            self.copy(j).start()

    def finish(self):
        for j in (0, 1, 2, 4, 5, 6):
            self.copy(j).wait_recv()
        for j in range(7):
            self.copy(j).wait_send()
        self.here().wait()


class Sum:
    @staticmethod
    def scratch(rows, columns):
        return [
            pltpu.VMEM((2, 4 * rows, columns), BF16),
            pltpu.VMEM((3, 2, rows, columns), BF16),
            pltpu.VMEM((2, rows, columns), BF16),
            DMA((7,)),
            DMA((7,)),
        ]

    def __init__(self, spot, width, scratch):
        self.spot, self.width = spot, width
        self.parts, self.recv_rows, self.twin_rows, self.send, self.recv = scratch
        self.rows = self.twin_rows.shape[1]

    def half(self, i):
        return 1 - self.spot.half + i * (2 * self.spot.half - 1)

    def block(self, q):
        return pl.ds(pl.multiple_of(q * self.rows, self.rows), self.rows)

    def copy(self, k, i):
        spot = self.spot
        j = 3 * i + k - 1
        return remote(
            self.parts.at[self.half(i), self.block(spot.around[k])], self.recv_rows.at[k - 1, i],
            self.send.at[j], self.recv.at[j], spot.plane(k),
        )

    def across(self):
        return remote(
            self.twin_rows.at[0], self.twin_rows.at[1], self.send.at[6], self.recv.at[6], self.spot.at_twin
        )

    def start(self, i):
        for k in (1, 2, 3):
            self.copy(k, i).start()

    def plane_total(self, i):
        total = self.parts[self.half(i), self.block(self.spot.q), :].astype(F32)
        for k in (1, 2, 3):
            self.copy(k, i).wait_recv()
            total += self.recv_rows[k - 1, i].astype(F32)
        return total

    def forward(self):
        total = self.plane_total(0)
        width = self.width
        self.twin_rows[0, :, :width] = total[:, :width].astype(BF16)
        if total.shape[1] > width:
            column = jnp.sum(total[:, width:], axis=1, keepdims=True)
            self.twin_rows[0, :, width:] = split_three(column)
        self.across().start()

    def finish(self):
        total = self.plane_total(1)
        self.across().wait_recv()
        total += self.twin_rows[1].astype(F32)
        return total

    def close(self):
        for i in range(2):
            for k in (1, 2, 3):
                self.copy(k, i).wait_send()
        self.across().wait_send()


def tile_parts(spot, half):
    parts = []
    for part in range(2):
        for j in range(2):
            at = part * INNER + THIRD * spot.piece(half, j)
            parts.append((pl.multiple_of(at, 64), (2 * part + j) * THIRD, THIRD))
    return parts + [(2 * INNER, 4 * THIRD, SHARED + HEADS)]


class Weights:
    PARTS = 5

    @staticmethod
    def scratch(columns, shard, width):
        buffers = [pltpu.VMEM((columns, shard), BF16), pltpu.VMEM((THIRD, width), BF16)]
        return buffers + [DMA((4,)), DMA((43,)), DMA((43,))]

    def __init__(self, spot, layer, w_in, w_out, tile, tile_out, scratch):
        self.spot, self.layer = spot, layer
        self.w_in, self.w_out, self.tile, self.tile_out = w_in, w_out, tile, tile_out
        self.buffer, self.out_buffer, self.local, self.send, self.recv = scratch
        self.shard = w_in.shape[1]
        self.others = 2 * (1 - spot.half)
        self.gateway = 2 - spot.half
        self.is_gateway = (spot.z == 1) | (spot.z == 2)

    def at_source(self, step):
        pl.when(self.spot.s == self.layer)(step)

    def source(self, half, n):
        first, _, size = tile_parts(self.spot, half)[n]
        return self.w_in.at[pl.ds(first, size)]

    def target(self, z, n):
        _, first, size = tile_parts(self.spot, 0)[n]
        columns = pl.ds(pl.multiple_of(z * self.shard, LANES), self.shard)
        return self.tile.at[pl.ds(first, size), columns]

    def load(self, n):
        part = self.buffer.at[pl.ds(*tile_parts(self.spot, 0)[n][1:])]
        return pltpu.make_async_copy(self.source(self.spot.half, n), part, self.send.at[n])

    def store(self):
        columns = pl.ds(pl.multiple_of(self.spot.z * self.shard, LANES), self.shard)
        return pltpu.make_async_copy(self.buffer, self.tile.at[:, columns], self.local.at[0])

    def out_home(self):
        return Home(
            self.out_source(), self.out_buffer, self.out_part(self.spot.lo),
            (self.local.at[1], self.local.at[2]),
        )

    def to_mate(self, n):
        source, target = self.source(self.spot.half, n), self.target(self.spot.z, n)
        return remote(source, target, self.send.at[n], self.recv.at[n], self.spot.at_mate)

    def to_gateway(self, n):
        source, target = self.source(1 - self.spot.half, n), self.target(self.spot.z, n)
        j = 5 + 5 * self.spot.lo + n
        return remote(source, target, self.send.at[5 + n], self.recv.at[j], self.spot.column(self.gateway))

    def passed(self, c, n):
        part = self.target(self.others + c, n)
        j = 5 * c + n
        return remote(part, part, self.send.at[10 + j], self.recv.at[5 + j], self.spot.at_mate)

    def to_sibling(self, b, n):
        j = 20 + 5 * b + n
        part = self.target([self.spot.z, self.spot.mate, self.others, self.others + 1][b], n)
        source = self.source(self.spot.half, n) if b == 0 else part
        return remote(source, part, self.send.at[j], self.recv.at[j], self.spot.sibling)

    def out_part(self, lo):
        return self.tile_out.at[pl.ds(pl.multiple_of(lo * THIRD, 64), THIRD)]

    def out_source(self):
        return self.w_out.at[pl.ds(pl.multiple_of(self.spot.q * THIRD, 64), THIRD)]

    def out_to(self, n):
        part = self.out_part(self.spot.lo if n < 2 else 1 - self.spot.lo)
        place = self.spot.sibling if n else self.spot.at_mate
        source = self.out_source() if n < 2 else part
        return remote(source, part, self.send.at[40 + n], self.recv.at[40 + n], place)

    def send_part(self, n):
        if n < self.PARTS:
            self.to_gateway(n).start()
            self.to_mate(n).start()
        elif n == self.PARTS:
            self.out_to(0).start()

    def begin(self):
        @self.at_source
        def _():
            for n in range(self.PARTS):
                self.load(n).start()
            self.out_home().begin()

    def start(self):
        @self.at_source
        def _():
            for n in range(self.PARTS):
                self.load(n).wait()
            for n in range(self.PARTS):
                self.to_gateway(n).start()
                self.to_mate(n).start()
            self.out_to(0).start()
            for n in range(self.PARTS):
                self.to_sibling(0, n).start()
            self.out_to(1).start()
            self.store().start()
            self.out_home().go_on()

    def step(self, n):
        @self.at_source
        def _():
            for b in range(2):
                self.passed(b, n).wait_recv()
                pl.when(self.is_gateway)(lambda b=b: self.passed(b, n).start())
                self.to_sibling(2 + b, n).start()
            self.to_mate(n).wait_recv()
            self.to_sibling(1, n).start()

    def finish(self):
        @self.at_source
        def _():
            self.out_to(0).wait_recv()
            self.out_to(2).start()
            for n in range(self.PARTS):
                self.to_gateway(n).wait_send()
                self.to_mate(n).wait_send()
                for c in range(2):
                    pl.when(self.is_gateway)(lambda c=c, n=n: self.passed(c, n).wait_send())
                for b in range(4):
                    self.to_sibling(b, n).wait_send()
            self.store().wait()
            self.out_home().end()
            for n in range(3):
                self.out_to(n).wait_send()

        @pl.when(self.spot.s != self.layer)
        def _():
            for b in range(4):
                for n in range(self.PARTS):
                    self.to_sibling(b, n).wait_recv()
            for n in (1, 2):
                self.out_to(n).wait_recv()


def all_places(spot):
    places = [spot.plane(k) for k in (1, 2, 3)]
    places += [spot.column((spot.z + k) % 4) for k in (1, 2, 3)]
    return places + [spot.sibling]


def open_kernel(*refs):
    ins, outs, weight_s, spread_a, spread_b, (own_tokens, own_cot, own_pack, load, *pack_sems) = take(
        refs, (5, 5, 5, 3, 3, 7)
    )
    w_in, w_out, pack, tokens, cotangent = ins
    tile, tile_out, packs, all_tokens, all_cot = outs
    spot = Spot()
    weights = Weights(spot, 0, w_in, w_out, tile, tile_out, weight_s)
    rows = Spread(spot, own_tokens, all_tokens, spread_a)
    grads = Spread(spot, own_cot, all_cot, spread_b)
    loads = [
        pltpu.make_async_copy(src, dst, load.at[n])
        for n, (src, dst) in enumerate(
            ((tokens.at[spot.s], own_tokens), (cotangent.at[spot.s], own_cot), (pack, own_pack))
        )
    ]
    pack_here = pltpu.make_async_copy(own_pack, packs.at[spot.s], pack_sems[0])
    pack_there = remote(own_pack, packs.at[spot.s], pack_sems[1], pack_sems[2], spot.sibling)
    for copy in loads:
        copy.start()
    weights.begin()
    greet(all_places(spot))
    for copy in loads:
        copy.wait()
    rows.start()
    weights.start()
    pack_here.start()
    pack_there.start()
    rows.forward()
    grads.start()
    weights.step(0)
    weights.step(1)
    weights.step(2)
    grads.forward()
    weights.step(3)
    weights.step(4)
    rows.finish()
    grads.finish()
    weights.finish()
    pack_here.wait()
    pack_there.wait()


def layer_rows(total, rows_in, branch, scales, rows_out):
    width = rows_in.shape[1]
    square = jnp.sum(total[:, width:], axis=1, keepdims=True)
    scale = lax.rsqrt(square * (1.0 / INNER) + NORM_EPS)
    part = total[:, :width] * scale
    rows_out[...] = (rows_in[...].astype(F32) + part).astype(BF16)
    if branch is not None:
        branch[...] = part
        scales[...] = jnp.broadcast_to(scale, scales.shape)


def norm_back(total, rows_in, gain, grad_out):
    rows = rows_in[...].astype(F32)
    scale = lax.rsqrt(jnp.mean(rows * rows, axis=-1, keepdims=True) + NORM_EPS)
    scaled = rows * scale
    pulled = total * gain
    inner = jnp.mean(pulled * scaled, axis=-1, keepdims=True)
    grad = scale * (pulled - scaled * inner) + grad_out[...].astype(F32)
    return grad, jnp.sum(total * scaled, axis=0, keepdims=True)


def add_rows(target, sources, chunk=64):
    @pl.loop(0, target.shape[0] // chunk)
    def _(n):
        rows = pl.ds(pl.multiple_of(n * chunk, chunk), chunk)
        total = sources[0][rows, :].astype(F32)
        for source in sources[1:]:
            total += source[rows, :].astype(F32)
        target[rows, :] = total.astype(target.dtype)


class GradsAcross:
    ORDER = (4, 0, 1, 2, 3, 5)

    @staticmethod
    def scratch(shard, columns, wide, width):
        return [
            pltpu.VMEM((2, columns, width), BF16),
            pltpu.VMEM((2, wide, width), BF16),
            pltpu.VMEM((3, columns, shard), BF16),
            pltpu.VMEM((THIRD, width), BF16),
            DMA((22,)),
            DMA((22,)),
        ]

    @staticmethod
    def results(shard, width):
        return [((2, 4 * THIRD, shard), BF16), ((SHARED + HEADS, shard), BF16), ((THIRD, width), BF16)]

    def __init__(self, spot, layer, results, scratch):
        self.spot, self.layer = spot, layer
        self.reduced, self.shared, self.out = results
        self.cores, self.cores_out, self.planes, self.mate_out, self.send, self.recv = scratch
        self.shard = self.planes.shape[2]
        self.others = 2 * (1 - spot.half)

    def here(self, step):
        pl.when(self.spot.s == self.layer)(step)

    def rows(self, n):
        _, first, size = tile_parts(self.spot, 0)[n]
        return pl.ds(first, size)

    def columns(self, z):
        return pl.ds(pl.multiple_of(z * self.shard, LANES), self.shard)

    def core_copy(self, n):
        buffer, rows = (self.cores_out, pl.ds(0, self.cores_out.shape[1])) if n == 5 else (self.cores, self.rows(n))
        return remote(
            buffer.at[0, rows], buffer.at[1, rows], self.send.at[n], self.recv.at[n], self.spot.sibling
        )

    def product(self, n, proj_grad, normed, normed_out, h_rows):
        def flat(value):
            return value.reshape(-1, value.shape[-1])

        width = self.cores.shape[2]
        if n == 5:
            total = dot_tn(flat(normed_out[...]), flat(h_rows[:, :, :width]))
            self.cores_out[0] = total.astype(BF16)
        else:
            _, first, size = tile_parts(self.spot, 0)[n]
            total = dot_tn(flat(proj_grad[:, :, first : first + size]), flat(normed[...]))
            self.cores[0, first : first + size, :] = total.astype(BF16)
        pl.when(self.spot.s != self.layer)(lambda: self.core_copy(n).start())

    def plane_copy(self, c, n):
        spot, rows = self.spot, self.rows(n)
        z = spot.mate if c == 2 else self.others + c
        slot = 2 if c == 2 else spot.lo
        place = spot.at_mate if c == 2 else spot.column(z)
        return remote(
            self.cores.at[0, rows, self.columns(z)], self.planes.at[slot, rows],
            self.send.at[6 + 3 * n + c], self.recv.at[6 + 3 * n + slot], place,
        )

    def came(self, c, n):
        part = self.planes.at[c, self.rows(n)]
        j = 6 + 3 * n + c
        return remote(part, part, self.send.at[j], self.recv.at[j], self.spot.at_mate)

    def out_rows(self, lo):
        return pl.ds(pl.multiple_of(lo * THIRD, 64), THIRD)

    def mate_copy(self):
        source = self.cores_out.at[0, self.out_rows(1 - self.spot.lo)]
        return remote(source, self.mate_out, self.send.at[21], self.recv.at[21], self.spot.at_mate)

    def sent(self, n):
        @self.here
        def _():
            for c in range(3):
                self.plane_copy(c, n).wait_send()

    def to_planes(self, n):
        @self.here
        def _():
            self.core_copy(n).wait_recv()
            if n == 5:
                add_rows(self.cores_out.at[0], [self.cores_out.at[0], self.cores_out.at[1]])
                self.mate_copy().start()
                return
            own, sibling = self.cores.at[0, self.rows(n)], self.cores.at[1, self.rows(n)]
            add_rows(own, [own, sibling], 48 if n < 4 else 16)
            for c in range(3):
                self.plane_copy(c, n).start()

    def gather(self, n):
        @self.here
        def _():
            if n == 5:
                self.mate_copy().wait_recv()
                add_rows(self.out, [self.cores_out.at[0, self.out_rows(self.spot.lo)], self.mate_out], 48)
                return
            for c in range(3):
                self.came(c, n).wait_recv()
            _, first, size = tile_parts(self.spot, 0)[n]
            mine = self.columns(self.spot.z)
            chunk = 48 if n < 4 else 16

            @pl.loop(0, size // chunk)
            def _(r):
                rows = pl.ds(pl.multiple_of(first + r * chunk, 16), chunk)
                own = self.cores[0, rows, mine].astype(F32) + self.planes[2, rows, :].astype(F32)
                other = self.planes[0, rows, :].astype(F32) + self.planes[1, rows, :].astype(F32)
                if n < 4:
                    self.reduced[0, rows, :] = own.astype(BF16)
                    self.reduced[1, rows, :] = other.astype(BF16)
                else:
                    rows = pl.ds(pl.multiple_of(r * chunk, 16), chunk)
                    self.shared[rows, :] = (own + other).astype(BF16)

    def finish(self):
        @self.here
        def _():
            self.mate_copy().wait_send()

        @pl.when(self.spot.s != self.layer)
        def _():
            for n in self.ORDER:
                self.core_copy(n).wait_send()


class GradsAround:
    @staticmethod
    def scratch(shard):
        return [
            pltpu.VMEM((4, SHARED + HEADS, shard), BF16),
            DMA((11,)),
            DMA((34,)),
            DMA((34,)),
        ]

    def __init__(self, spot, results, final, final_out, scratch):
        self.spot, self.final, self.final_out = spot, final, final_out
        self.reduced, self.shared, self.out = results
        self.sums, self.local, self.send, self.recv = scratch

    def region(self, k, i, n):
        q = self.spot.q if k == 0 else self.spot.around[k]
        half = self.spot.half if i == 0 else 1 - self.spot.half
        at = n // 2 * INNER + THIRD * (8 * half + 4 * (n % 2) + q)
        return self.final.at[pl.ds(pl.multiple_of(at, 64), THIRD)]

    def copy(self, k, i, n):
        source = self.reduced.at[i, pl.ds(n * THIRD, THIRD)]
        target = self.region(0, i, n)
        j = 4 * i + n
        if k == 0:
            return pltpu.make_async_copy(source, target, self.local.at[j])
        if k < 3:
            j += 8 * (k - 1)
            return remote(source, target, self.send.at[j], self.recv.at[j], self.spot.plane(k))
        source = target = self.region(1 if i == 0 else 2, i, n)
        place = self.spot.plane(2 if i == 0 else 1)
        return remote(source, target, self.send.at[16 + j], self.recv.at[16 + j], place)

    def send_part(self, n):
        for i in range(2):
            for k in (1, 2, 0):
                self.copy(k, i, n).start()

    def pass_part(self, n):
        for i in range(2):
            self.copy(1 + i, i, n).wait_recv()
            self.copy(3, i, n).start()

    def out_region(self, k, i):
        q = self.spot.q if k == 0 else self.spot.around[k]
        size = THIRD if i is None else THIRD // 2
        at = q * THIRD + (0 if i is None else i * size)
        return self.final_out.at[pl.ds(pl.multiple_of(at, 32), size)]

    def out_copy(self, k, i=None):
        target = self.out_region(0, None)
        if k == 0:
            return pltpu.make_async_copy(self.out, target, self.local.at[8])
        if k < 3:
            return remote(self.out, target, self.send.at[23 + k], self.recv.at[23 + k], self.spot.plane(k))
        part = self.out_region(1 + i, i)
        return remote(part, part, self.send.at[26 + i], self.recv.at[26 + i], self.spot.plane(2 - i))

    def send_out(self):
        for k in (1, 2, 0):
            self.out_copy(k).start()

    def pass_out(self):
        for i in range(2):
            self.out_copy(1 + i).wait_recv()
            self.out_copy(3, i).start()

    def shared_copy(self, k):
        source = self.shared if k == 1 else self.sums.at[1]
        target = self.sums.at[0 if k == 1 else 2]
        return remote(source, target, self.send.at[27 + k], self.recv.at[27 + k], self.spot.plane(k))

    def shared_home(self):
        tail = self.final.at[pl.ds(2 * INNER, SHARED + HEADS)]
        return pltpu.make_async_copy(self.sums.at[3], tail, self.local.at[9])

    def shared_step(self, n):
        if n > 0:
            self.shared_copy(n).wait_recv()
            sources = [self.shared, self.sums.at[0]] if n == 1 else [self.sums.at[1], self.sums.at[2]]
            add_rows(self.sums.at[1 if n == 1 else 3], sources, 16)
        if n < 2:
            self.shared_copy(n + 1).start()
        else:
            self.shared_home().start()

    def finish(self):
        for i in range(2):
            for n in range(4):
                self.copy(2 - i, i, n).wait_recv()
                self.copy(3, i, n).wait_recv()
                for k in (1, 2, 3):
                    self.copy(k, i, n).wait_send()
                self.copy(0, i, n).wait()
            self.out_copy(3, i).wait_recv()
            self.out_copy(3, i).wait_send()
        for k in (1, 2):
            self.out_copy(k).wait_send()
            self.shared_copy(k).wait_send()
        self.out_copy(0).wait()
        self.shared_home().wait()


class SmallSum:
    @staticmethod
    def scratch(pack):
        return [pltpu.VMEM((6, 8, pack), F32), DMA((5,)), DMA((5,))]

    def __init__(self, spot, scratch):
        self.spot = spot
        self.small, self.send, self.recv = scratch

    def copy(self, n):
        spot = self.spot
        place = [spot.sibling, spot.at_mate, spot.at_twin, spot.plane(1), spot.plane(2)][n]
        return remote(self.small.at[0], self.small.at[1 + n], self.send.at[n], self.recv.at[n], place)

    def start(self, n, value):
        self.small[0] = value
        self.copy(n).start()

    def end(self, n):
        self.copy(n).wait()
        return self.small[1 + n]


def loading(sources, targets, sems):
    return [pltpu.make_async_copy(a, b, sems.at[n]) for n, (a, b) in enumerate(zip(sources, targets))]


def saved_shapes(length, width, wide):
    columns = ((width, BF16), (wide, F32), (wide, BF16), (SHARED, BF16), (LANES, BF16), (wide, BF16))
    return [((2, length, n), t) for n, t in columns]


def middle_kernel(heads, *refs):
    ins, outs, kept, weight_s, sum_s, spread_s, layer_s, (store,) = take(refs, (7, 6, 6, 5, 5, 3, 11, 1))
    w_in, w_out, *layer_ins, rows_in = ins
    tile, tile_out, all_rows, branch, scales, rows_out = outs
    u, w, wo, pack, *saved, load = layer_s
    spot = Spot()
    weights = Weights(spot, 1, w_in, w_out, tile, tile_out, weight_s)
    total = Sum(spot, rows_in.shape[1], sum_s)
    spread = Spread(spot, rows_out, all_rows, spread_s)
    loads = loading(layer_ins[:3] + [layer_ins[3].at[0]], layer_s[:4], load)
    for copy in loads:
        copy.start()
    weights.begin()
    greet(all_places(spot))
    weights.start()
    for copy in loads:
        copy.wait()
    params = load_params(([spot.piece(spot.half, j) for j in range(2)], pack))

    @pl.loop(0, 2)
    def _(i):
        forward_rows(heads, params, total.half(i), u, w, wo, None, [total.parts, None, *saved])
        total.start(i)

    stores = loading(saved, kept, store)
    for copy in stores:
        copy.start()
    weights.step(0)
    total.forward()
    weights.step(1)
    layer_rows(total.finish(), rows_in, branch, scales, rows_out)
    spread.start()
    weights.step(2)
    spread.forward()
    weights.step(3)
    weights.step(4)
    spread.finish()
    total.close()
    weights.finish()
    for copy in stores:
        copy.wait()


class RowSums:
    @staticmethod
    def scratch(length):
        shape = (2, 8, length)
        return [pltpu.VMEM(shape, F32), pltpu.VMEM((7,) + shape, F32), DMA((14,)), DMA((14,))]

    def __init__(self, spot, scratch):
        self.mine, self.others, self.send, self.recv = scratch
        self.places = [spot.plane(k) for k in (1, 2, 3)] + [spot.at_twin]
        self.places += [(spot.s, spot.around[k], spot.twin) for k in (1, 2, 3)]

    def copies(self, seq):
        return [
            remote(
                self.mine.at[seq], self.others.at[j, seq],
                self.send.at[2 * j + seq], self.recv.at[2 * j + seq], place,
            )
            for j, place in enumerate(self.places)
        ]

    def start(self, seq):
        for copy in self.copies(seq):
            copy.start()

    def finish(self, seq):
        total = self.mine[seq]
        for j, copy in enumerate(self.copies(seq)):
            copy.wait_recv()
            total += self.others[j, seq]
        for copy in self.copies(seq):
            copy.wait_send()
        self.mine[seq] = total


def turn_kernel(heads, *refs):
    ins, outs, sum_s, last_s, spread_s, across_s, row_s, back_s, layer_s, (h_rows, payload, *saved) = take(
        refs, (9, 8, 5, 5, 3, 6, 4, 6, 5, 8)
    )
    layer_ins, (rows_in, grad_out, branch, scales) = take(ins, (5, 4))
    all_rows, grad_rows, grad_gain, last_rows, *results, small = outs
    u, w, wo, pack, load = layer_s
    spot = Spot()
    width = rows_in.shape[1]
    total = Sum(spot, width, sum_s)
    last = Sum(spot, width, last_s)
    spread = Spread(spot, payload, all_rows, spread_s)
    across = GradsAcross(spot, 1, results, across_s)
    sums = RowSums(spot, row_s)
    loads = loading(
        layer_ins[:3] + [layer_ins[3].at[1], layer_ins[4]], [u, w, wo, pack, h_rows], load
    )
    for copy in loads:
        copy.start()
    places = [spot.plane(k) for k in (1, 2, 3)] + [spot.column((spot.z + k) % 4) for k in (1, 2, 3)]
    places += [(spot.s, spot.around[k], spot.twin) for k in (1, 2, 3)] + [spot.sibling]
    greet(places)
    for copy in loads:
        copy.wait()
    ids = [spot.piece(spot.half, j) for j in range(2)]
    params = load_params((ids, pack))
    small[...] = jnp.zeros_like(small)

    @pl.loop(0, 2)
    def _(i):
        seq = last.half(i)
        forward_rows(heads, params, seq, u, w, wo, h_rows, [last.parts, sums.mine, *saved])
        sums.start(seq)
        last.start(i)

    proj_grad, normed_out, *scratch = back_s

    @pl.loop(0, 2)
    def _(i):
        seq = total.half(i)
        sums.finish(seq)
        aux = aux_of_rows(sums.mine[seq])
        outs = (total.parts, proj_grad, normed_out)
        parts = backward_rows(heads, params, seq, h_rows, aux, saved[1:], w, wo, outs, scratch)
        add_small(small, ids, *parts)
        total.start(i)

    def product(n):
        across.product(n, proj_grad, saved[0], normed_out, h_rows)

    last.forward()
    product(4)
    product(0)
    total.forward()
    across.to_planes(4)
    across.to_planes(0)
    grad, gain_row = norm_back(total.finish(), rows_in, pack[7:8, :width], grad_out)
    low = grad.astype(BF16)
    grad_rows[...] = low
    grad_gain[...] = stacked([gain_row], 8)
    cross = jnp.sum(low.astype(F32) * branch[...], axis=1, keepdims=True)
    payload[:, :width] = low
    lanes = lax.broadcasted_iota(jnp.int32, (rows_in.shape[0], LANES), 1)
    first = split_three(scales[:, 0:1]).astype(F32)
    second = pltpu.roll(split_three(cross).astype(F32), 3, 1)
    payload[:, width:] = jnp.where(lanes < 3, first, second).astype(BF16)
    spread.start()
    for n in (1, 2, 3, 5):
        product(n)
    spread.forward()
    for n in (1, 2, 3, 5):
        across.to_planes(n)
    layer_rows(last.finish(), rows_in, None, None, last_rows)
    spread.finish()
    for n in GradsAcross.ORDER:
        across.gather(n)
    for n in range(5):
        across.sent(n)
    across.finish()
    total.close()
    last.close()


def close_kernel(heads, *refs):
    ins, outs, sum_s, across_s, results, around_s, small_s, back_s, layer_s, rest = take(
        refs, (19, 5, 5, 6, 3, 4, 3, 6, 11, 6)
    )
    layer_ins, (rows_in, last_rows, last_grad, small_1, gain_1), last_results = take(ins, (11, 5, 3))
    home_rows, home_grads, final, final_out, small_out = outs
    grad_rows, small_in, send, recv, local, load = rest
    first_rows, *layer_ins = layer_ins
    h_rows, w, wo, pack, normed, *saved, layer_load = layer_s
    spot = Spot()
    width = rows_in.shape[1]
    total = Sum(spot, width, sum_s)
    across = GradsAcross(spot, 0, results, across_s)
    layer_loads = loading(
        layer_ins[:3] + [layer_ins[3].at[0]] + layer_ins[4:], layer_s[:-1], layer_load
    )
    around = GradsAround(spot, results, final, final_out, around_s)
    small = SmallSum(spot, small_s)
    first_core, last_core = pl.when(spot.s == 0), pl.when(spot.s == 1)
    loads = [
        pltpu.make_async_copy(src, dst, load.at[n]) for n, (src, dst) in enumerate(zip(last_results, results))
    ]

    @last_core
    def _():
        for copy in loads:
            copy.start()

    for copy in layer_loads:
        copy.start()
    greet(all_places(spot))

    @last_core
    def _():
        for copy in loads:
            copy.wait()
        around.shared_step(0)
        for n in range(4):
            around.send_part(n)
        around.send_out()

    for copy in layer_loads:
        copy.wait()
    proj_grad, normed_out, *scratch = back_s
    ids = [spot.piece(spot.half, j) for j in range(2)]
    params = load_params((ids, pack))
    small_in[...] = jnp.zeros_like(small_in)

    @pl.loop(0, 2)
    def _(i):
        seq = total.half(i)
        aux = aux_of_columns(h_rows, seq, width)
        outs = (total.parts, proj_grad, normed_out)
        sums = backward_rows(heads, params, seq, h_rows, aux, saved, w, wo, outs, scratch)
        add_small(small_in.at[0], ids, *sums)
        total.start(i)

    order = GradsAcross.ORDER

    def product(n):
        across.product(n, proj_grad, normed, normed_out, h_rows)

    for n in order[:3]:
        product(n)
    for n in order[:3]:
        across.to_planes(n)
    total.forward()
    for n in order[3:]:
        product(n)
    for at in range(3, 6):
        across.sent(order[at - 3])
        across.to_planes(order[at])
    across.gather(4)
    first_core(lambda: around.shared_step(0))
    across.gather(0)
    first_core(lambda: around.send_part(0))
    grad, gain_row = norm_back(total.finish(), rows_in, pack[7:8, :width], last_grad)
    grad_rows[...] = grad.astype(BF16)
    layers = ((first_rows, grad_rows), (last_rows, last_grad))

    def home_copies(s):
        copies = []
        for n, target in enumerate((home_rows, home_grads)):
            copies.append(remote(layers[1 - s][n], target.at[s], send.at[n], recv.at[n], spot.sibling))
            copies.append(pltpu.make_async_copy(layers[s][n], target.at[s], local.at[n]))
        return copies

    small_in[1] = small_1[...]
    small_in[0, 7:8, :width] = gain_row
    small_in[1, 7:8, :width] = gain_1[0:1]
    small.start(0, small_in[1 - spot.s])
    for s in range(2):

        @pl.when(spot.s == s)
        def _(s=s):
            for copy in home_copies(s):
                copy.start()

    across.gather(1)
    first_core(lambda: around.send_part(1))
    running = small_in[spot.s] + small.end(0)
    small.start(1, running)
    around.shared_step(1)
    around.pass_part(0)
    across.gather(2)
    first_core(lambda: around.send_part(2))
    running = running + small.end(1)
    small.start(2, running)
    around.pass_part(1)
    across.gather(3)
    first_core(lambda: around.send_part(3))
    running = running + small.end(2)
    small.start(3, running)
    around.shared_step(2)
    across.gather(5)
    first_core(around.send_out)
    around.pass_part(2)
    running = running + small.end(3)
    small.start(4, running)
    around.pass_part(3)
    around.pass_out()
    small_out[...] = running + small.end(4)
    around.finish()
    for n in order[3:5]:
        across.sent(n)
    across.finish()
    for s in range(2):

        @pl.when(spot.s == s)
        def _(s=s):
            for copy in home_copies(s):
                copy.wait()

    total.close()


def comm_call(kernel, collective, ins, in_specs, outs, out_specs, scratch, name):
    return pl.pallas_call(
        kernel,
        out_shape=[jax.ShapeDtypeStruct(s, t) for s, t in outs],
        in_specs=in_specs,
        out_specs=out_specs,
        scratch_shapes=scratch,
        compiler_params=pltpu.CompilerParams(
            collective_id=collective, has_side_effects=True, vmem_limit_bytes=60 * 1024 * 1024
        ),
        name=name,
    )(*ins)


def fast_shards(
    tokens, cotangent, norm_gain, w_in, conv_weight, conv_bias, dt_bias, a_log, skip_gain, gate_gain, w_out
):
    section = lax.axis_index("section")
    span, width = tokens.shape[2:]
    heads = HEADS // 8
    wide = heads * HEADDIM
    columns = 2 * wide + SHARED + HEADS
    shard = w_in.shape[1]
    rows_in = w_in[0].T
    channels = jnp.concatenate(
        [
            conv_weight[0, :, :INNER], conv_bias[:, :INNER],
            jnp.repeat(skip_gain[0], HEADDIM)[None], gate_gain,
        ]
    )
    channels = widened(channels.reshape(7, -1, THIRD), 2, PIECE).reshape(7, -1)
    shared = jnp.concatenate([conv_weight[0, :, INNER:], conv_bias[:, INNER:], jnp.zeros((2, SHARED))])
    last_row = jnp.concatenate(
        [norm_gain, widened(dt_bias, 1, LANES), widened(a_log, 1, LANES)], axis=1
    )
    pack = jnp.concatenate([channels, shared], axis=1)
    pack = jnp.concatenate([pack, widened(last_row, 1, pack.shape[1])])
    group = (2, 4 * span, width)
    weight_outs = [((columns, width), BF16), ((wide, width), BF16)]
    weight_s = Weights.scratch(columns, shard, width)
    payload = width + LANES
    tile, tile_out, packs, all_rows, all_cot = comm_call(
        open_kernel, 1,
        [rows_in, w_out[0], pack, tokens[:, 0], cotangent[:, 0]], [ANY] * 5,
        weight_outs + [((2,) + pack.shape, F32), (group, BF16), (group, BF16)], [ANY] * 5,
        weight_s + Spread.SEMS + Spread.SEMS
        + [pltpu.VMEM((span, width), BF16)] * 2 + [pltpu.VMEM(pack.shape, F32), DMA((3,)), DMA, DMA, DMA],
        "open",
    )
    own_tokens = lax.dynamic_index_in_dim(tokens[:, 0], section, 0, False)
    own_cot = lax.dynamic_index_in_dim(cotangent[:, 0], section, 0, False)
    length = 4 * span
    rows_spec = ((span, width), BF16)
    layer_s = [
        pltpu.VMEM((2, length, width), BF16), pltpu.VMEM((columns, width), BF16),
        pltpu.VMEM((wide, width), BF16), pltpu.VMEM(pack.shape, F32),
    ]
    kept_shapes = saved_shapes(length, width, wide)
    kept_s = [pltpu.VMEM(*k) for k in kept_shapes]
    back_s = [pltpu.VMEM((2, length, columns), BF16), pltpu.VMEM((2, length, wide), BF16)]
    back_s += backward_scratch(length, wide)
    results = GradsAcross.results(shard, width)
    across_s = GradsAcross.scratch(shard, columns, wide, width)
    sum_s = Sum.scratch(span, width)
    first_tiles = [tile, tile_out]
    tile, tile_out, all_rows, branch, scales, rows, *kept = comm_call(
        partial(middle_kernel, heads), 2,
        [rows_in, w_out[0], all_rows, tile, tile_out, packs, own_tokens], [ANY] * 6 + [VMEM],
        weight_outs + [(group, BF16), ((span, width), F32), ((span, LANES), F32), rows_spec] + kept_shapes,
        [ANY] * 3 + [VMEM] * 3 + [ANY] * 6,
        weight_s + Sum.scratch(span, payload) + Spread.SEMS + layer_s + kept_s + [DMA((4,)), DMA((6,))],
        "middle",
    )
    all_grads, last_grad, gain_1, last_rows, *last_results, small_1 = comm_call(
        partial(turn_kernel, heads), 3,
        [all_rows, tile, tile_out, packs, all_cot, rows, own_cot, branch, scales],
        [ANY] * 5 + [VMEM] * 4,
        [((2, length, payload), BF16), rows_spec, ((8, width), F32), rows_spec]
        + results + [(pack.shape, F32)],
        [ANY] + [VMEM] * 7,
        sum_s + Sum.scratch(span, payload) + Spread.SEMS + across_s + RowSums.scratch(length) + back_s
        + layer_s + [DMA((5,)), pltpu.VMEM((2, length, width), BF16), pltpu.VMEM((span, payload), BF16)]
        + kept_s,
        "turn",
    )
    home_rows, home_grads, final, final_out, small = comm_call(
        partial(close_kernel, heads), 4,
        [
            rows, all_grads, *first_tiles, packs, *kept,
            own_tokens, last_rows, last_grad, small_1, gain_1, *last_results,
        ],
        [VMEM] + [ANY] * 10 + [VMEM] * 5 + [ANY] * 3,
        [
            ((2, span, width), BF16), ((2, span, width), BF16),
            ((2 * INNER + SHARED + HEADS, shard), BF16), (w_out.shape[1:], BF16), (pack.shape, F32),
        ],
        [ANY] * 4 + [VMEM],
        sum_s + across_s + [pltpu.VMEM(*r) for r in results]
        + GradsAround.scratch(shard) + SmallSum.scratch(pack.shape[1]) + back_s
        + [pltpu.VMEM((2, length, payload), BF16)] + layer_s[1:] + kept_s + [DMA((10,))]
        + [
            pltpu.VMEM((span, width), BF16), pltpu.VMEM((2,) + pack.shape, F32),
            DMA((2,)), DMA((2,)), DMA((2,)), DMA((3,)),
        ],
        "close",
    )
    by_channel = small[:7, :-SHARED].reshape(7, -1, PIECE)[:, :, :THIRD].reshape(7, INNER)
    conv_rows = jnp.concatenate([by_channel[: CONV + 1], small[: CONV + 1, -SHARED:]], axis=1)
    return (
        home_rows[None, :, None],
        home_grads[None, :, None],
        small[7:8, :width],
        final.astype(F32).T[None],
        conv_rows[None, :CONV],
        conv_rows[CONV:],
        small[7:8, DT_AT : DT_AT + HEADS],
        small[7:8, RATE_AT : RATE_AT + HEADS],
        by_channel[5].reshape(HEADS, HEADDIM).sum(-1)[None],
        by_channel[6:7],
        final_out[None].astype(F32),
    )


def shards(
    tokens, cotangent, norm_gain, w_in, conv_weight, conv_bias, dt_bias, a_log, skip_gain, gate_gain, w_out
):
    section = lax.axis_index("section")
    place = lax.axis_index("seq")
    depth = lax.axis_index("fsdp")
    plan = Plan(lax.axis_size("seq"), lax.axis_size("fsdp"))
    half = depth // plan.mates
    micro, _, span, width = tokens.shape
    layers = lax.axis_size("section")
    wide, channels, heads = plan.wide, plan.channels, plan.heads

    shard = w_in[0]
    gate_part = widened(plan.take(shard[:, :INNER], 1, place), 2, wide)
    x_part = widened(plan.take(shard[:, INNER : 2 * INNER], 1, place), 2, wide)
    shared_part = jnp.broadcast_to(
        shard[:, 2 * INNER : INNER + XBC], (plan.halves, shard.shape[0], SHARED)
    )
    dt_part = widened(plan.take(shard[:, INNER + XBC :], 1, place), 2, LANES)
    tile = jnp.concatenate([gate_part, x_part, shared_part, dt_part], axis=2)
    tile = jnp.repeat(tile, plan.mates, axis=0)
    tile = lax.all_to_all(tile, "fsdp", 0, 0, tiled=True).reshape(width, -1).T
    w_tiles = lax.all_gather(tile, "section", axis=0)
    if plan.pieces == plan.mates:
        piece = w_out[0].reshape(plan.seq, -1, width)
        piece = lax.dynamic_index_in_dim(piece, place, 0, False)
        rows_out = lax.all_gather(
            piece, "fsdp", axis=0, tiled=True, axis_index_groups=plan.mate_groups
        )
    else:
        rows_out = lax.all_gather(w_out[0], "fsdp", axis=0, tiled=True)
        rows_out = lax.dynamic_index_in_dim(plan.take(rows_out, 0, place), half, 0, False)
    wo_tiles = lax.all_gather(widened(rows_out, 0, wide), "section", axis=0)

    def own(array, axis, size):
        part = lax.dynamic_index_in_dim(plan.take(array, axis, place), half, 0, False)
        return widened(part, axis, size)

    skip_wide = jnp.repeat(skip_gain[0], HEADDIM)[None]
    by_channel = jnp.concatenate(
        [conv_weight[0, :, :INNER], conv_bias[:, :INNER], skip_wide, gate_gain, jnp.zeros((1, INNER))], 0
    )
    by_channel = own(by_channel, 1, wide)
    by_shared = jnp.concatenate(
        [conv_weight[0, :, INNER:], conv_bias[:, INNER:], jnp.zeros((3, SHARED))], 0
    )
    by_head = jnp.concatenate([dt_bias, a_log, jnp.zeros((6, HEADS))], 0)
    by_head = own(by_head, 1, LANES)
    smalls = jnp.concatenate(
        [by_channel.ravel(), by_shared.ravel(), by_head.ravel(), norm_gain[0]]
    )
    smalls = lax.all_gather(smalls, "section", axis=0)
    cuts = [8 * wide, 8 * (wide + SHARED), 8 * (wide + SHARED + LANES)]
    params = []
    for l in range(layers):
        ch, bc, dtp, gain = jnp.split(smalls[l], cuts)
        params.append((gain[None], ch.reshape(8, -1), bc.reshape(8, -1), dtp.reshape(8, -1)))

    def gather_rows(own_rows):
        rows = lax.all_gather(own_rows, "seq", axis=0, tiled=True)
        if plan.halves == 1:
            return rows[None]
        return lax.all_gather(rows, "fsdp", axis=0, axis_index_groups=plan.peer_groups)

    def sum_rows(parts):
        if plan.halves == 1:
            rows = parts[0]
        else:
            rows = lax.psum_scatter(
                parts, "fsdp", scatter_dimension=0, axis_index_groups=plan.peer_groups
            )
        return lax.psum_scatter(rows, "seq", scatter_dimension=0, tiled=True)

    own_tokens = lax.dynamic_index_in_dim(tokens, section, 0, False)[0]
    own_cot = lax.dynamic_index_in_dim(cotangent, section, 0, False)[0]
    inputs, outputs, branch, saved, scales = [own_tokens], [], [], [], []
    for l in range(layers):
        rows = gather_rows(inputs[l])
        parts, square, normed, *kept = run_forward(
            heads, wide, rows, w_tiles[l], wo_tiles[l], params[l]
        )
        saved.append((normed, kept))
        total = sum_rows(parts).astype(F32)
        square = sum_rows(square)[:, :1]
        scale = lax.rsqrt(square / INNER + NORM_EPS)
        branch.append(total * scale)
        scales.append(scale)
        outputs.append((inputs[l].astype(F32) + branch[l]).astype(BF16))
        inputs.append(outputs[l])
    grads_in, small_grads = [None] * layers, [None] * layers
    w_grads, wo_grads = [None] * layers, [None] * layers
    grad_rows = own_cot
    for l in reversed(range(layers)):
        rdot = jnp.sum(grad_rows.astype(F32) * branch[l], axis=-1, keepdims=True)
        aux = widened(jnp.concatenate([scales[l], rdot], axis=1), 1, LANES)
        all_grads = gather_rows(grad_rows)
        aux = gather_rows(aux)
        normed, kept = saved[l]
        parts, proj_grad, normed_out, g_ch, g_bc, g_dt = run_backward(
            heads, wide, all_grads, aux, kept, w_tiles[l], wo_tiles[l], params[l]
        )
        w_grads[l] = dot_tn(normed.reshape(-1, width), proj_grad.reshape(-1, proj_grad.shape[-1])).astype(BF16)
        wo_grads[l] = dot_tn(normed_out.reshape(-1, wide), all_grads.reshape(-1, width)).astype(BF16)
        grad_normed = sum_rows(parts).astype(F32)
        rows = inputs[l].astype(F32)
        scale = lax.rsqrt(jnp.mean(rows * rows, axis=-1, keepdims=True) + NORM_EPS)
        scaled = rows * scale
        g_gain = jnp.sum(grad_normed * scaled, axis=0)
        pulled = grad_normed * params[l][0]
        inner = jnp.mean(pulled * scaled, axis=-1, keepdims=True)
        grad = scale * (pulled - scaled * inner) + grad_rows.astype(F32)
        grad_rows = grad.astype(BF16)
        grads_in[l] = grad_rows

        def placed(value, size):
            value = value[..., :size]
            full = jnp.zeros((plan.seq, plan.halves) + value.shape, F32)
            full = lax.dynamic_update_slice(full, value[None, None], (place, half, 0, 0))
            return plan.put(full, 1)

        by_channel = placed(g_ch, channels)
        by_head = placed(g_dt, heads)
        skip = by_channel[5].reshape(HEADS, HEADDIM).sum(-1)
        small_grads[l] = jnp.concatenate(
            [
                g_gain, by_channel[:5].ravel(), g_bc[:5].ravel(), by_head[0], by_head[1], skip, by_channel[6]
            ]
        )

    smalls = lax.psum(jnp.stack(small_grads), ("section", "seq", "fsdp"))
    smalls = lax.dynamic_index_in_dim(smalls, section, 0, False)
    cuts, at = [], 0
    for size in (width, (CONV + 1) * INNER, (CONV + 1) * SHARED, HEADS, HEADS, HEADS):
        at += size
        cuts.append(at)
    g_gain, g_x, g_bc, g_shift, g_rate, g_skip, g_gate = jnp.split(smalls, cuts)
    conv_rows = jnp.concatenate([g_x.reshape(CONV + 1, -1), g_bc.reshape(CONV + 1, -1)], axis=1)

    w_grad = lax.psum_scatter(jnp.stack(w_grads), "section", scatter_dimension=0)
    w_grad = lax.all_to_all(w_grad, "fsdp", 0, 0, tiled=True)
    w_grad = w_grad.reshape(plan.halves, plan.mates, -1, w_grad.shape[-1]).astype(F32).sum(1)
    shared_grad = lax.psum(w_grad[..., 2 * wide : 2 * wide + SHARED].sum(0), "seq")
    head_grads = jnp.concatenate(
        [
            w_grad[..., :channels],
            w_grad[..., wide : wide + channels],
            w_grad[..., 2 * wide + SHARED : 2 * wide + SHARED + heads],
        ],
        axis=-1,
    ).astype(BF16)
    head_grads = lax.all_gather(head_grads, "seq", axis=0)
    grad_w_in = jnp.concatenate(
        [
            plan.put(head_grads[..., :channels], 1),
            plan.put(head_grads[..., channels : 2 * channels], 1),
            shared_grad.astype(BF16),
            plan.put(head_grads[..., 2 * channels :], 1),
        ],
        axis=-1,
    ).astype(F32)
    wo_grad = lax.psum_scatter(jnp.stack(wo_grads)[:, :channels], "section", scatter_dimension=0)
    if plan.pieces == plan.mates:
        wo_grad = lax.psum_scatter(
            wo_grad, "fsdp", scatter_dimension=0, tiled=True, axis_index_groups=plan.mate_groups
        )
        wo_grad = lax.all_gather(wo_grad, "seq", axis=0, tiled=True)
    else:
        full = jnp.zeros((plan.seq, plan.halves) + wo_grad.shape, BF16)
        full = lax.dynamic_update_slice(full, wo_grad[None, None], (place, half, 0, 0))
        full = plan.put(full, 0)
        wo_grad = lax.psum_scatter(full, "fsdp", scatter_dimension=0, tiled=True)
        wo_grad = lax.psum(wo_grad, "seq")

    def home(per_layer):
        return lax.all_to_all(jnp.stack(per_layer), "section", 0, 0, tiled=True)[None, :, None]

    return (
        home(outputs),
        home(grads_in),
        g_gain[None],
        grad_w_in[None],
        conv_rows[None, :CONV],
        conv_rows[CONV:],
        g_shift[None],
        g_rate[None],
        g_skip[None],
        g_gate[None],
        wo_grad.astype(F32)[None],
    )


def solution(mesh):
    shape = tuple(mesh.shape[a] for a in ("section", "seq", "fsdp"))
    return jax.shard_map(
        fast_shards if shape == (2, 4, 4) else shards,
        mesh=mesh,
        in_specs=(
            P(None, "fsdp", "seq", None),
            P(None, "fsdp", "seq", None),
            P("section", None),
            P("section", "fsdp", None),
            P("section", None, None),
            P("section", None),
            P("section", None),
            P("section", None),
            P("section", None),
            P("section", None),
            P("section", "fsdp", None),
        ),
        out_specs=(
            P("section", None, "fsdp", "seq", None),
            P("section", None, "fsdp", "seq", None),
            P("section", None),
            P("section", "fsdp", None),
            P("section", None, None),
            P("section", None),
            P("section", None),
            P("section", None),
            P("section", None),
            P("section", None),
            P("section", "fsdp", None),
        ),
        check_vma=False,
    )
```

```python
from functools import partial

import jax
import jax.numpy as jnp
from jax import lax
from jax.experimental import pallas as pl
from jax.experimental.pallas import tpu as pltpu
from jax.sharding import PartitionSpec as P

HEADS = 48
HEADDIM = 64
STATE = 128
CONV = 4
SPAN = 256
INNER = 3072
XBC = 3328
SHARED = 2 * STATE
LANES = 128
THIRD = 192
PIECE = 256
GAIN_END = 1536
DT_AT = 1536
RATE_AT = DT_AT + LANES
NORM_EPS = 1e-05
HIGHEST = lax.Precision.HIGHEST
BF16 = jnp.bfloat16
F32 = jnp.float32


def take(refs, counts):
    refs = list(refs)
    return [[refs.pop(0) for _ in range(n)] for n in counts]


def dot(left, right, contract=((1,), (0,)), precision=None):
    return lax.dot_general(
        left, right, (contract, ((), ())), preferred_element_type=F32, precision=precision
    )


def dot_nt(left, right):
    return dot(left, right, ((1,), (1,)))


def dot_tn(left, right):
    return dot(left, right, ((0,), (0,)))


def sigmoid(value):
    return 1.0 / (1.0 + jnp.exp(-value))


def shifted(value, distance):
    if distance == 0:
        return value
    length = value.shape[0]
    rows = lax.broadcasted_iota(jnp.int32, value.shape, 0)
    moved = pltpu.roll(value, distance % length, 0)
    if distance > 0:
        return jnp.where(rows >= distance, moved, 0.0)
    return jnp.where(rows < length + distance, moved, 0.0)


def conv_sum(raw, taps):
    total = taps[CONV : CONV + 1]
    for k in range(CONV):
        total = total + taps[k : k + 1] * shifted(raw, CONV - 1 - k)
    return total


def conv_back(grad, raw, taps):
    grad_raw = 0.0
    rows = []
    for k in range(CONV):
        grad_raw = grad_raw + taps[k : k + 1] * shifted(grad, -(CONV - 1 - k))
        rows.append(jnp.sum(grad * shifted(raw, CONV - 1 - k), axis=0, keepdims=True))
    rows.append(jnp.sum(grad, axis=0, keepdims=True))
    return grad_raw, rows


def stacked(rows, count):
    width = rows[0].shape[1]
    short = count - len(rows)
    return jnp.concatenate(rows + [jnp.zeros((short, width), F32)], axis=0)


def triangles():
    row_ids = lax.broadcasted_iota(jnp.int32, (SPAN, SPAN), 0)
    col_ids = lax.broadcasted_iota(jnp.int32, (SPAN, SPAN), 1)
    return row_ids >= col_ids


def step_sizes(dt_raw, dt_row):
    shift = dt_raw + dt_row
    step = jnp.maximum(shift, 0.0) + jnp.log1p(jnp.exp(-jnp.abs(shift)))
    return step, sigmoid(shift)


def low_half():
    return lax.broadcasted_iota(jnp.int32, (SPAN, LANES), 1) < HEADDIM


def head_lanes(h):
    lanes = lax.broadcasted_iota(jnp.int32, (1, LANES), 1)
    return (lanes < HEADDIM) if h % 2 == 0 else (lanes >= HEADDIM)


def split_three(value):
    lanes = lax.broadcasted_iota(jnp.int32, (value.shape[0], LANES), 1)
    result = jnp.zeros((value.shape[0], LANES), F32)
    for k in range(3):
        part = value.astype(BF16).astype(F32)
        result = jnp.where(lanes == k, part, result)
        value = value - part
    return result.astype(BF16)


def selection(ids):
    rows = lax.broadcasted_iota(jnp.int32, (HEADS, LANES), 0)
    columns = lax.broadcasted_iota(jnp.int32, (HEADS, LANES), 1)
    target = jnp.full((HEADS, LANES), -1, jnp.int32)
    for j in range(2):
        here = (columns >= 3 * j) & (columns < 3 * j + 3)
        target = jnp.where(here, columns + 3 * (ids[j] - j), target)
    return (rows == target).astype(F32)


def piece_lanes(ids, j):
    return pl.ds(pl.multiple_of(ids[j] * PIECE, PIECE), PIECE)


def load_params(refs):
    if len(refs) == 2:
        ids, pack_ref = refs
        sel = selection(ids)
        ch = jnp.concatenate([pack_ref[:, piece_lanes(ids, j)][:, :THIRD] for j in range(2)], axis=1)
        rows = [pack_ref[7:8, at : at + HEADS] for at in (DT_AT, RATE_AT)]
        dtp = dot(stacked(rows, 8), sel, precision=HIGHEST)
        return pack_ref[7:8, :GAIN_END], ch, pack_ref[:, -SHARED:], dtp, sel.astype(BF16)
    gain_ref, ch_ref, bc_ref, dtp_ref = refs
    return gain_ref[...], ch_ref[...], bc_ref[...], dtp_ref[...], None


def forward_kernel(heads, *refs):
    u_ref, w_ref, wo_ref, *refs = refs
    forward_rows(heads, load_params(refs[:4]), 0, u_ref, w_ref, wo_ref, None, refs[4:])


def forward_rows(heads, params, i, u_ref, w_ref, wo_ref, h_ref, outs):
    gain, ch, bc, dtp, sel = params
    out_ref, sums_ref, normed_ref, gate_ref, xraw_ref, bcraw_ref, dtraw_ref, mixed_ref = outs
    length, width = u_ref.shape[1:]
    wide = ch.shape[1]
    blocks = length // SPAN
    rows = u_ref[i].astype(F32)
    scale = lax.rsqrt(jnp.mean(rows * rows, axis=-1, keepdims=True) + NORM_EPS)
    normed = (rows * scale * gain).astype(BF16)
    normed_ref[i] = normed
    gate = dot_nt(normed, w_ref[:wide])
    gate_ref[i] = gate
    x_raw = dot_nt(normed, w_ref[wide : 2 * wide]).astype(BF16)
    xraw_ref[i] = x_raw
    rest = dot_nt(normed, w_ref[2 * wide :]).astype(BF16)
    bcraw_ref[i] = rest[:, :SHARED]
    dt_raw = rest[:, SHARED:]
    if sel is not None:
        dt_raw = dot(dt_raw, sel).astype(BF16)
    dtraw_ref[i] = dt_raw
    conv_x = conv_sum(x_raw.astype(F32), ch)
    act_x = (conv_x * sigmoid(conv_x)).astype(BF16)
    conv_bc = conv_sum(rest[:, :SHARED].astype(F32), bc)
    act_bc = (conv_bc * sigmoid(conv_bc)).astype(BF16)
    step, _ = step_sizes(dt_raw.astype(F32), dtp[0:1])
    rate = jnp.exp(dtp[1:2])
    causal = triangles()
    ones = causal.astype(F32)
    lower = low_half()
    carries = [None] * heads
    for b in range(blocks):
        span = slice(b * SPAN, (b + 1) * SPAN)
        step_b = step[span]
        decay = -dot(ones, rate * step_b, precision=HIGHEST)
        decay_t, step_t = decay.T, step_b.T
        b_in, c_out = act_bc[span, :STATE], act_bc[span, STATE:]
        scores = dot_nt(c_out, b_in)
        for first in range(0, heads, 2):
            lanes = slice(first * HEADDIM, first * HEADDIM + LANES)
            x_pair = act_x[span, lanes]
            parts = []
            for h in range(first, min(first + 2, heads)):
                gap = decay[:, h : h + 1] - decay_t[h : h + 1]
                mask = jnp.exp(jnp.where(causal, gap, -1e30))
                weights = (scores * mask * step_t[h : h + 1]).astype(BF16)
                part = dot(weights, x_pair)
                if carries[h] is not None:
                    part += jnp.exp(decay[:, h : h + 1]) * dot(c_out, carries[h].astype(BF16))
                if b + 1 < blocks:
                    last = decay[SPAN - 1 :, h : h + 1]
                    tail = jnp.exp(last - decay[:, h : h + 1]) * step_b[:, h : h + 1]
                    shaped = (b_in.astype(F32) * tail).astype(BF16)
                    fresh = dot_tn(shaped, x_pair)
                    if carries[h] is not None:
                        fresh += jnp.exp(last) * carries[h]
                    carries[h] = fresh
                parts.append(part)
            if len(parts) == 1:
                parts.append(jnp.zeros_like(parts[0]))
            within = jnp.where(lower, parts[0], parts[1])
            mixed = within + ch[5:6, lanes] * x_pair.astype(F32)
            mixed_ref[i, span, lanes] = mixed.astype(BF16)
    gated = mixed_ref[i].astype(F32) * (gate * sigmoid(gate))
    square = jnp.sum(gated * gated, axis=-1, keepdims=True)
    scaled = gated * ch[6:7]
    out_ref[i, :, :width] = dot(scaled.astype(BF16), wo_ref[...]).astype(BF16)
    if sel is None:
        sums_ref[i] = jnp.broadcast_to(square, sums_ref.shape[1:])
        return
    out_ref[i, :, width:] = split_three(square)
    if h_ref is not None:
        grad_no = dot_nt(h_ref[i], wo_ref[...])
        cross = jnp.sum(grad_no * scaled, axis=-1, keepdims=True)
        lane_ids = lax.broadcasted_iota(jnp.int32, (length, LANES), 1)
        both = jnp.where(lane_ids == 0, square, jnp.where(lane_ids == 1, cross, 0.0))
        sums_ref[i] = both.T[:8]


def backward_kernel(heads, *refs):
    h_ref, aux_ref, *refs = refs
    saved, (w_ref, wo_ref), params, outs, sum_refs, scratch = take(refs, (5, 2, 4, 3, 3, 4))
    params = load_params(params)
    aux = aux_ref[0, :, 0:1], aux_ref[0, :, 1:2]
    sums = backward_rows(heads, params, 0, h_ref, aux, saved, w_ref, wo_ref, outs, scratch)
    for ref, value in zip(sum_refs, sums):

        @pl.when(pl.program_id(0) == 0)
        def _(ref=ref, value=value):
            ref[...] = value

        @pl.when(pl.program_id(0) > 0)
        def _(ref=ref, value=value):
            ref[...] += value


def aux_of_columns(h_ref, i, width):
    aux = h_ref[i, :, width:].astype(F32)
    return aux[:, 0:1] + aux[:, 1:2] + aux[:, 2:3], aux[:, 3:4] + aux[:, 4:5] + aux[:, 5:6]


def aux_of_rows(sums):
    aux = jnp.concatenate([sums, jnp.zeros((LANES - 8, sums.shape[1]), F32)], axis=0).T
    scale = lax.rsqrt(aux[:, 0:1] * (1.0 / INNER) + NORM_EPS)
    return scale, aux[:, 1:2] * scale


def backward_rows(heads, params, i, h_ref, aux, saved, w_ref, wo_ref, outs, scratch):
    _, ch, bc, dtp, sel = params
    gate_ref, xraw_ref, bcraw_ref, dtraw_ref, mixed_ref = saved
    dn_ref, pg_ref, no_ref = outs
    dmix_s, dx_s, dbc_s, ddt_s = scratch
    length, width = dn_ref.shape[1:]
    wide = ch.shape[1]
    blocks = length // SPAN
    h_rows = h_ref[i, :, :width]
    scale, rdot = aux
    gate = gate_ref[i]
    mixed = mixed_ref[i].astype(F32)
    sig = sigmoid(gate)
    silu = gate * sig
    gated = mixed * silu
    gain = ch[6:7]
    grad_no = dot_nt(h_rows, wo_ref[...])
    grad_g = scale * (gain * grad_no) - gated * (scale * scale * (1.0 / INNER) * rdot)
    scaled = gated * scale
    no_ref[i] = (scaled * gain).astype(BF16)
    gain_row = jnp.sum(grad_no * scaled, axis=0, keepdims=True)
    dmix_s[...] = (grad_g * silu).astype(BF16)
    pg_ref[i, :, :wide] = (grad_g * mixed * (sig * (1.0 + gate * (1.0 - sig)))).astype(BF16)

    x_raw = xraw_ref[i].astype(F32)
    bc_raw = bcraw_ref[i].astype(F32)
    conv_x = conv_sum(x_raw, ch)
    sig_x = sigmoid(conv_x)
    act_x = (conv_x * sig_x).astype(BF16)
    conv_bc = conv_sum(bc_raw, bc)
    sig_bc = sigmoid(conv_bc)
    act_bc = (conv_bc * sig_bc).astype(BF16)
    step, slope = step_sizes(dtraw_ref[i].astype(F32), dtp[0:1])
    rate = jnp.exp(dtp[1:2])
    causal = triangles()
    ones = causal.astype(F32)
    lower = low_half()
    lane_ids = lax.broadcasted_iota(jnp.int32, (SPAN, LANES), 1)
    last_row = lax.broadcasted_iota(jnp.int32, (SPAN, 1), 0) == SPAN - 1
    decays = []
    for b in range(blocks):
        decays.append(-dot(ones, rate * step[b * SPAN : (b + 1) * SPAN], precision=HIGHEST))
    entering = [[None] * heads for _ in range(blocks)]
    for b in range(blocks - 1):
        span = slice(b * SPAN, (b + 1) * SPAN)
        b_in = act_bc[span, :STATE].astype(F32)
        for h in range(heads):
            lanes = slice(h // 2 * LANES, h // 2 * LANES + LANES)
            column = decays[b][:, h : h + 1]
            last = column[SPAN - 1 :]
            tail = jnp.exp(last - column) * step[span, h : h + 1]
            fresh = dot_tn((b_in * tail).astype(BF16), act_x[span, lanes])
            if entering[b][h] is not None:
                fresh += jnp.exp(last) * entering[b][h]
            entering[b + 1][h] = fresh
    leaving = [None] * heads
    rate_row = jnp.zeros((1, LANES), F32)
    for b in reversed(range(blocks)):
        span = slice(b * SPAN, (b + 1) * SPAN)
        step_b, decay = step[span], decays[b]
        decay_t, step_t = decay.T, step_b.T
        b_in, c_out = act_bc[span, :STATE], act_bc[span, STATE:]
        scores = dot_nt(c_out, b_in)
        grad_scores = jnp.zeros((SPAN, SPAN), F32)
        grad_b = jnp.zeros((SPAN, STATE), F32)
        grad_c = jnp.zeros((SPAN, STATE), F32)
        row_sums = jnp.zeros((SPAN, LANES), F32)
        grad_step = jnp.zeros((SPAN, LANES), F32)
        col_rows = []
        for first in range(0, heads, 2):
            lanes = slice(first * HEADDIM, first * HEADDIM + LANES)
            x_pair = act_x[span, lanes]
            grad_pair = dmix_s[span, lanes]
            parts = []
            for h in range(first, min(first + 2, heads)):
                own = head_lanes(h)
                grad_own = jnp.where(own, grad_pair, jnp.zeros((), BF16))
                column = decay[:, h : h + 1]
                mask = jnp.exp(jnp.where(causal, column - decay_t[h : h + 1], -1e30))
                spread = mask * step_t[h : h + 1]
                weights = (scores * spread).astype(BF16)
                part = dot_tn(weights, grad_pair)
                grad_w = dot_nt(grad_own, x_pair)
                grad_scores += grad_w * spread
                pulled = grad_w * (scores * mask)
                col_rows.append(jnp.sum(pulled, axis=0, keepdims=True))
                row_sum = jnp.sum(pulled * step_t[h : h + 1], axis=1, keepdims=True)
                if entering[b][h] is not None:
                    carry = entering[b][h].astype(BF16)
                    grown = jnp.exp(column)
                    grad_grown = grad_own.astype(F32) * grown
                    grad_c += dot_nt(grad_grown.astype(BF16), carry)
                    grad_carry = dot_tn(c_out, grad_grown.astype(BF16))
                    row_sum += jnp.sum(grad_grown * dot(c_out, carry), axis=1, keepdims=True)
                else:
                    grad_carry = None
                if leaving[h] is not None:
                    last = column[SPAN - 1 :]
                    fade = jnp.exp(last - column)
                    tail = fade * step_b[:, h : h + 1]
                    b_wide = b_in.astype(F32)
                    grad_state = leaving[h].astype(BF16)
                    grad_shaped = dot_nt(x_pair, grad_state)
                    part += dot((b_wide * tail).astype(BF16), grad_state)
                    grad_b += grad_shaped * tail
                    grad_tail = jnp.sum(grad_shaped * b_wide, axis=1, keepdims=True)
                    grad_step += jnp.where(lane_ids == h, grad_tail * fade, 0.0)
                    moved = grad_tail * tail
                    total = jnp.sum(moved, axis=0, keepdims=True)
                    if entering[b][h] is not None:
                        faded = jnp.exp(last) * leaving[h]
                        kept = jnp.sum(faded * entering[b][h], axis=1, keepdims=True)
                        total += jnp.sum(kept, axis=0, keepdims=True)
                        grad_carry += faded
                    row_sum += jnp.where(last_row, total, 0.0) - moved
                leaving[h] = grad_carry
                row_sums += jnp.where(lane_ids == h, row_sum, 0.0)
                parts.append(part)
            if len(parts) == 1:
                parts.append(jnp.zeros_like(parts[0]))
            grad_x = jnp.where(lower, parts[0], parts[1])
            dx_s[span, lanes] = grad_x + ch[5:6, lanes] * grad_pair.astype(F32)
        col_sums = stacked(col_rows, LANES).T
        low_scores = grad_scores.astype(BF16)
        dbc_s[span, :STATE] = grad_b + dot_tn(low_scores, c_out)
        dbc_s[span, STATE:] = grad_c + dot(low_scores, b_in)
        grad_decay = dot(
            ones, row_sums - step_b * col_sums, ((0,), (0,)), precision=HIGHEST
        )
        ddt_s[span] = col_sums + grad_step - rate * grad_decay
        rate_row -= jnp.sum(grad_decay * step_b, axis=0, keepdims=True)

    skip_row = jnp.sum(dmix_s[...].astype(F32) * act_x.astype(F32), axis=0, keepdims=True)
    grad_conv = dx_s[...] * (sig_x * (1.0 + conv_x * (1.0 - sig_x)))
    grad_raw, ch_rows = conv_back(grad_conv, x_raw, ch)
    pg_ref[i, :, wide : 2 * wide] = grad_raw.astype(BF16)
    grad_conv = dbc_s[...] * (sig_bc * (1.0 + conv_bc * (1.0 - sig_bc)))
    grad_raw, bc_rows = conv_back(grad_conv, bc_raw, bc)
    pg_ref[i, :, 2 * wide : 2 * wide + SHARED] = grad_raw.astype(BF16)
    grad_dt = ddt_s[...] * slope
    low_dt = grad_dt.astype(BF16)
    if sel is not None:
        low_dt = dot_nt(low_dt, sel).astype(BF16)
    pg_ref[i, :, 2 * wide + SHARED :] = low_dt
    dn_ref[i] = dot(pg_ref[i], w_ref[...]).astype(BF16)
    by_channel = stacked(ch_rows + [skip_row, gain_row], 8)
    by_shared = stacked(bc_rows, 8)
    by_head = stacked([jnp.sum(grad_dt, axis=0, keepdims=True), rate_row * rate], 8)
    if sel is not None:
        by_head = lax.dot_general(
            by_head, sel.astype(F32), (((1,), (1,)), ((), ())),
            preferred_element_type=F32, precision=HIGHEST,
        )
    return by_channel, by_shared, by_head


def add_small(small, by_channel, by_shared, by_head):
    for j in range(2):
        part = by_channel[:, j * THIRD : (j + 1) * THIRD]
        small[:, j * PIECE : j * PIECE + THIRD] += part
    small[:, 2 * PIECE : 3 * PIECE] += by_shared
    small[7:8, 2 * PIECE : 2 * PIECE + HEADS] += by_head[0:1]
    small[7:8, 2 * PIECE + LANES : 2 * PIECE + LANES + HEADS] += by_head[1:2]


def add_gain(small, row):
    for r in range(8):
        small[r : r + 1, 3 * PIECE : 3 * PIECE + THIRD] = row[:, r * THIRD : (r + 1) * THIRD]


def whole_spec(array):
    return pl.BlockSpec(array.shape, lambda i: (0,) * array.ndim)


def row_spec(length, width):
    return pl.BlockSpec((1, length, width), lambda i: (i, 0, 0))


def block_spec(array):
    return pl.BlockSpec((1,) + array.shape[1:], lambda i: (i, 0, 0))


PARAMS = dict(vmem_limit_bytes=60 * 1024 * 1024)


def run_forward(heads, wide, rows, w, wo, params):
    count, length, width = rows.shape
    constants = [w, wo, *params]
    outs = [
        (width, BF16), (LANES, F32), (width, BF16), (wide, F32),
        (wide, BF16), (SHARED, BF16), (LANES, BF16), (wide, BF16),
    ]
    return pl.pallas_call(
        partial(forward_kernel, heads),
        grid=(count,),
        out_shape=[jax.ShapeDtypeStruct((count, length, n), t) for n, t in outs],
        in_specs=[block_spec(rows)] + [whole_spec(c) for c in constants],
        out_specs=[row_spec(length, n) for n, _ in outs],
        compiler_params=pltpu.CompilerParams(**PARAMS),
        name="forward",
    )(rows, *constants)


def run_backward(heads, wide, grad_rows, aux, saved, w, wo, params):
    count, length, _ = grad_rows.shape
    columns, width = w.shape
    given = [grad_rows, aux, *saved]
    constants = [w, wo, *params]
    outs = [(width, BF16), (columns, BF16), (wide, BF16)]
    sums = [(8, wide), (8, SHARED), (8, LANES)]
    return pl.pallas_call(
        partial(backward_kernel, heads),
        grid=(count,),
        out_shape=[jax.ShapeDtypeStruct((count, length, n), t) for n, t in outs]
        + [jax.ShapeDtypeStruct(s, F32) for s in sums],
        in_specs=[block_spec(g) for g in given] + [whole_spec(c) for c in constants],
        out_specs=[row_spec(length, n) for n, _ in outs]
        + [pl.BlockSpec(s, lambda i: (0, 0)) for s in sums],
        scratch_shapes=backward_scratch(length, wide),
        compiler_params=pltpu.CompilerParams(**PARAMS),
        name="backward",
    )(*given, *constants)


def backward_scratch(length, wide):
    return [
        pltpu.VMEM((length, wide), BF16),
        pltpu.VMEM((length, wide), F32),
        pltpu.VMEM((length, SHARED), F32),
        pltpu.VMEM((length, LANES), F32),
    ]


class Plan:
    def __init__(self, seq, fsdp):
        self.seq, self.fsdp = seq, fsdp
        halves = 2
        if fsdp % 2 or HEADS % (seq * 2) or (HEADS // fsdp) % seq:
            halves = 1
        self.halves, self.mates = halves, fsdp // halves
        self.heads = HEADS // (seq * halves)
        self.pieces = self.mates if (HEADS // fsdp) % seq == 0 else 1
        channels = self.heads * HEADDIM
        self.channels = channels
        self.wide = -(-channels // LANES) * LANES
        self.peer_groups = [[lo + self.mates * h for h in range(halves)] for lo in range(self.mates)]
        self.mate_groups = [[h * self.mates + j for j in range(self.mates)] for h in range(halves)]

    def split(self, array, axis):
        size = array.shape[axis] // (self.halves * self.pieces * self.seq)
        shape = array.shape[:axis] + (self.halves, self.pieces, self.seq, size) + array.shape[axis + 1 :]
        return array.reshape(shape)

    def take(self, array, axis, place):
        array = lax.dynamic_index_in_dim(self.split(array, axis), place, axis + 2, False)
        shape = array.shape[: axis + 1] + (-1,) + array.shape[axis + 3 :]
        return jnp.moveaxis(array.reshape(shape), axis, 0)

    def put(self, parts, axis):
        size = parts.shape[axis + 2] // self.pieces
        shape = parts.shape[: axis + 2] + (self.pieces, size) + parts.shape[axis + 3 :]
        parts = jnp.moveaxis(parts.reshape(shape), (1, axis + 2, 0), (axis, axis + 1, axis + 2))
        shape = parts.shape[:axis] + (-1,) + parts.shape[axis + 4 :]
        return parts.reshape(shape)


def widened(array, axis, size):
    pads = [(0, 0)] * array.ndim
    pads[axis] = (0, size - array.shape[axis])
    return jnp.pad(array, pads)


MESH = pl.DeviceIdType.MESH
ANY = pl.BlockSpec(memory_space=pl.ANY)
VMEM = pl.BlockSpec(memory_space=pltpu.VMEM)
DMA = pltpu.SemaphoreType.DMA


class Spot:
    def __init__(self):
        self.s, self.q, self.z = (lax.axis_index(a) for a in ("section", "seq", "fsdp"))
        self.half, self.lo = self.z // 2, self.z % 2
        self.mate, self.twin = self.z + 1 - 2 * self.lo, (self.z + 2) % 4
        self.around = [None, self.q + 1 - 2 * (self.q % 2), (self.q + 2) % 4, 3 - self.q]
        self.sibling = (1 - self.s, self.q, self.z)
        self.at_mate, self.at_twin = (self.s, self.q, self.mate), (self.s, self.q, self.twin)

    def plane(self, k):
        return (self.s, self.around[k], self.z)

    def column(self, z):
        return (self.s, self.q, z)

    def piece(self, half, j):
        return 8 * half + 4 * j + self.q


def greet(places):
    barrier = pltpu.get_barrier_semaphore()
    for place in places:
        pl.semaphore_signal(barrier, inc=1, device_id=place, device_id_type=MESH)
    pl.semaphore_wait(barrier, len(places))


def remote(src, dst, send_sem, recv_sem, place):
    return pltpu.make_async_remote_copy(
        src_ref=src, dst_ref=dst, send_sem=send_sem, recv_sem=recv_sem, device_id=place, device_id_type=MESH
    )


class Home:
    def __init__(self, src, buffer, dst, sems):
        self.load = pltpu.make_async_copy(src, buffer, sems[0])
        self.store = pltpu.make_async_copy(buffer, dst, sems[1])

    def begin(self):
        self.load.start()

    def go_on(self):
        self.load.wait()
        self.store.start()

    def end(self):
        self.store.wait()


class Spread:
    SEMS = [DMA((7,)), DMA((7,)), DMA]

    def __init__(self, spot, own, all_rows, sems):
        self.spot, self.own, self.all = spot, own, all_rows
        self.send, self.recv, self.local = sems

    def slot(self, half):
        rows = self.own.shape[0]
        return self.all.at[half, pl.ds(pl.multiple_of(self.spot.q * rows, rows), rows)]

    def copy(self, j):
        spot = self.spot
        slot = self.slot(spot.half)
        if j == 3:
            return remote(self.own, slot, self.send.at[3], self.recv.at[3], spot.at_twin)
        if j < 3:
            return remote(self.own, slot, self.send.at[j], self.recv.at[j], spot.plane(j + 1))
        slot = self.slot(1 - spot.half)
        return remote(slot, slot, self.send.at[j], self.recv.at[j], spot.plane(j - 3))

    def here(self):
        return pltpu.make_async_copy(self.own, self.slot(self.spot.half), self.local)

    def start(self):
        for j in (3, 0, 1, 2):
            self.copy(j).start()
        self.here().start()

    def forward(self):
        self.copy(3).wait_recv()
        for j in (4, 5, 6):
            self.copy(j).start()

    def finish(self):
        for j in (0, 1, 2, 4, 5, 6):
            self.copy(j).wait_recv()
        for j in range(7):
            self.copy(j).wait_send()
        self.here().wait()


class Sum:
    @staticmethod
    def scratch(rows, columns):
        return [
            pltpu.VMEM((2, 4 * rows, columns), BF16),
            pltpu.VMEM((3, 2, rows, columns), BF16),
            pltpu.VMEM((2, rows, columns), BF16),
            DMA((7,)),
            DMA((7,)),
        ]

    def __init__(self, spot, width, scratch):
        self.spot, self.width = spot, width
        self.parts, self.recv_rows, self.twin_rows, self.send, self.recv = scratch
        self.rows = self.twin_rows.shape[1]

    def half(self, i):
        return 1 - self.spot.half + i * (2 * self.spot.half - 1)

    def block(self, q):
        return pl.ds(pl.multiple_of(q * self.rows, self.rows), self.rows)

    def copy(self, k, i):
        spot = self.spot
        j = 3 * i + k - 1
        return remote(
            self.parts.at[self.half(i), self.block(spot.around[k])], self.recv_rows.at[k - 1, i],
            self.send.at[j], self.recv.at[j], spot.plane(k),
        )

    def across(self):
        return remote(
            self.twin_rows.at[0], self.twin_rows.at[1], self.send.at[6], self.recv.at[6], self.spot.at_twin
        )

    def start(self, i):
        for k in (1, 2, 3):
            self.copy(k, i).start()

    def plane_total(self, i):
        total = self.parts[self.half(i), self.block(self.spot.q), :].astype(F32)
        for k in (1, 2, 3):
            self.copy(k, i).wait_recv()
            total += self.recv_rows[k - 1, i].astype(F32)
        return total

    def forward(self):
        total = self.plane_total(0)
        width = self.width
        self.twin_rows[0, :, :width] = total[:, :width].astype(BF16)
        if total.shape[1] > width:
            column = jnp.sum(total[:, width:], axis=1, keepdims=True)
            self.twin_rows[0, :, width:] = split_three(column)
        self.across().start()

    def finish(self):
        total = self.plane_total(1)
        self.across().wait_recv()
        total += self.twin_rows[1].astype(F32)
        return total

    def close(self):
        for i in range(2):
            for k in (1, 2, 3):
                self.copy(k, i).wait_send()
        self.across().wait_send()


def tile_parts(spot, half):
    parts = []
    for part in range(2):
        for j in range(2):
            at = part * INNER + THIRD * spot.piece(half, j)
            parts.append((pl.multiple_of(at, 64), (2 * part + j) * THIRD, THIRD))
    return parts + [(2 * INNER, 4 * THIRD, SHARED + HEADS)]


class Weights:
    PARTS = 5

    @staticmethod
    def scratch(columns, shard, width):
        buffers = [pltpu.VMEM((columns, shard), BF16), pltpu.VMEM((THIRD, width), BF16)]
        return buffers + [DMA((4,)), DMA((43,)), DMA((43,))]

    def __init__(self, spot, layer, w_in, w_out, tile, tile_out, scratch):
        self.spot, self.layer = spot, layer
        self.w_in, self.w_out, self.tile, self.tile_out = w_in, w_out, tile, tile_out
        self.buffer, self.out_buffer, self.local, self.send, self.recv = scratch
        self.shard = w_in.shape[1]
        self.others = 2 * (1 - spot.half)
        self.gateway = 2 - spot.half
        self.is_gateway = (spot.z == 1) | (spot.z == 2)

    def at_source(self, step):
        pl.when(self.spot.s == self.layer)(step)

    def source(self, half, n):
        first, _, size = tile_parts(self.spot, half)[n]
        return self.w_in.at[pl.ds(first, size)]

    def target(self, z, n):
        _, first, size = tile_parts(self.spot, 0)[n]
        columns = pl.ds(pl.multiple_of(z * self.shard, LANES), self.shard)
        return self.tile.at[pl.ds(first, size), columns]

    def load(self, n):
        part = self.buffer.at[pl.ds(*tile_parts(self.spot, 0)[n][1:])]
        return pltpu.make_async_copy(self.source(self.spot.half, n), part, self.send.at[n])

    def store(self):
        columns = pl.ds(pl.multiple_of(self.spot.z * self.shard, LANES), self.shard)
        return pltpu.make_async_copy(self.buffer, self.tile.at[:, columns], self.local.at[0])

    def out_home(self):
        return Home(
            self.out_source(), self.out_buffer, self.out_part(self.spot.lo),
            (self.local.at[1], self.local.at[2]),
        )

    def to_mate(self, n):
        source, target = self.source(self.spot.half, n), self.target(self.spot.z, n)
        return remote(source, target, self.send.at[n], self.recv.at[n], self.spot.at_mate)

    def to_gateway(self, n):
        source, target = self.source(1 - self.spot.half, n), self.target(self.spot.z, n)
        j = 5 + 5 * self.spot.lo + n
        return remote(source, target, self.send.at[5 + n], self.recv.at[j], self.spot.column(self.gateway))

    def passed(self, c, n):
        part = self.target(self.others + c, n)
        j = 5 * c + n
        return remote(part, part, self.send.at[10 + j], self.recv.at[5 + j], self.spot.at_mate)

    def to_sibling(self, b, n):
        j = 20 + 5 * b + n
        part = self.target([self.spot.z, self.spot.mate, self.others, self.others + 1][b], n)
        source = self.source(self.spot.half, n) if b == 0 else part
        return remote(source, part, self.send.at[j], self.recv.at[j], self.spot.sibling)

    def out_part(self, lo):
        return self.tile_out.at[pl.ds(pl.multiple_of(lo * THIRD, 64), THIRD)]

    def out_source(self):
        return self.w_out.at[pl.ds(pl.multiple_of(self.spot.q * THIRD, 64), THIRD)]

    def out_to(self, n):
        part = self.out_part(self.spot.lo if n < 2 else 1 - self.spot.lo)
        place = self.spot.sibling if n else self.spot.at_mate
        source = self.out_source() if n < 2 else part
        return remote(source, part, self.send.at[40 + n], self.recv.at[40 + n], place)

    def send_part(self, n):
        if n < self.PARTS:
            self.to_gateway(n).start()
            self.to_mate(n).start()
        elif n == self.PARTS:
            self.out_to(0).start()

    def begin(self):
        @self.at_source
        def _():
            for n in range(self.PARTS):
                self.load(n).start()
            self.out_home().begin()

    def start(self):
        @self.at_source
        def _():
            for n in range(self.PARTS):
                self.load(n).wait()
            for n in range(self.PARTS):
                self.to_gateway(n).start()
                self.to_mate(n).start()
            self.out_to(0).start()
            for n in range(self.PARTS):
                self.to_sibling(0, n).start()
            self.out_to(1).start()
            self.store().start()
            self.out_home().go_on()

    def step(self, n):
        @self.at_source
        def _():
            for b in range(2):
                self.passed(b, n).wait_recv()
                pl.when(self.is_gateway)(lambda b=b: self.passed(b, n).start())
                self.to_sibling(2 + b, n).start()
            self.to_mate(n).wait_recv()
            self.to_sibling(1, n).start()

    def finish(self):
        @self.at_source
        def _():
            self.out_to(0).wait_recv()
            self.out_to(2).start()
            for n in range(self.PARTS):
                self.to_gateway(n).wait_send()
                self.to_mate(n).wait_send()
                for c in range(2):
                    pl.when(self.is_gateway)(lambda c=c, n=n: self.passed(c, n).wait_send())
                for b in range(4):
                    self.to_sibling(b, n).wait_send()
            self.store().wait()
            self.out_home().end()
            for n in range(3):
                self.out_to(n).wait_send()

        @pl.when(self.spot.s != self.layer)
        def _():
            for b in range(4):
                for n in range(self.PARTS):
                    self.to_sibling(b, n).wait_recv()
            for n in (1, 2):
                self.out_to(n).wait_recv()


def all_places(spot):
    places = [spot.plane(k) for k in (1, 2, 3)]
    places += [spot.column((spot.z + k) % 4) for k in (1, 2, 3)]
    return places + [spot.sibling]


def open_kernel(*refs):
    ins, outs, weight_s, spread_a, spread_b, (own_tokens, own_cot, own_pack, load, *pack_sems) = take(
        refs, (11, 5, 5, 3, 3, 7)
    )
    w_in, w_out, tokens, cotangent, *raw = ins
    tile, tile_out, packs, all_tokens, all_cot = outs
    spot = Spot()
    weights = Weights(spot, 0, w_in, w_out, tile, tile_out, weight_s)
    rows = Spread(spot, own_tokens, all_tokens, spread_a)
    grads = Spread(spot, own_cot, all_cot, spread_b)
    loads = [
        pltpu.make_async_copy(src, dst, load.at[n])
        for n, (src, dst) in enumerate(
            ((tokens.at[spot.s], own_tokens), (cotangent.at[spot.s], own_cot))
        )
    ]
    pack_here = pltpu.make_async_copy(own_pack, packs.at[spot.s], pack_sems[0])
    pack_there = remote(own_pack, packs.at[spot.s], pack_sems[1], pack_sems[2], spot.sibling)
    for copy in loads:
        copy.start()
    weights.begin()
    greet(all_places(spot))
    for copy in loads:
        copy.wait()
    rows.start()
    weights.start()
    pack_params(own_pack, *raw)
    pack_here.start()
    pack_there.start()
    rows.forward()
    grads.start()
    weights.step(0)
    weights.step(1)
    weights.step(2)
    grads.forward()
    weights.step(3)
    weights.step(4)
    rows.finish()
    grads.finish()
    weights.finish()
    pack_here.wait()
    pack_there.wait()


def pack_params(pack, conv_weight, conv_bias, gate_gain, skip_gain, norm_gain, dt_bias, a_log):
    pack[...] = jnp.zeros_like(pack)
    for p in range(INNER // THIRD):
        source, target = slice(p * THIRD, (p + 1) * THIRD), slice(p * PIECE, p * PIECE + THIRD)
        pack[0:CONV, target] = conv_weight[:, source]
        pack[CONV : CONV + 1, target] = conv_bias[:, source]
        skips = [jnp.broadcast_to(skip_gain[:, 3 * p + h : 3 * p + h + 1], (1, HEADDIM)) for h in range(3)]
        pack[5:6, target] = jnp.concatenate(skips, axis=1)
        pack[6:7, target] = gate_gain[:, source]
    pack[0:CONV, -SHARED:] = conv_weight[:, INNER:]
    pack[CONV : CONV + 1, -SHARED:] = conv_bias[:, INNER:]
    pack[7:8, :GAIN_END] = norm_gain[...]
    pack[7:8, DT_AT : DT_AT + HEADS] = dt_bias[...]
    pack[7:8, RATE_AT : RATE_AT + HEADS] = a_log[...]


def layer_rows(total, rows_in, branch, scales, rows_out):
    width = rows_in.shape[1]
    square = jnp.sum(total[:, width:], axis=1, keepdims=True)
    scale = lax.rsqrt(square * (1.0 / INNER) + NORM_EPS)
    part = total[:, :width] * scale
    rows_out[...] = (rows_in[...].astype(F32) + part).astype(BF16)
    if branch is not None:
        branch[...] = part
        scales[...] = jnp.broadcast_to(scale, scales.shape)


def norm_back(total, rows_in, gain, grad_out):
    rows = rows_in[...].astype(F32)
    scale = lax.rsqrt(jnp.mean(rows * rows, axis=-1, keepdims=True) + NORM_EPS)
    scaled = rows * scale
    pulled = total * gain
    inner = jnp.mean(pulled * scaled, axis=-1, keepdims=True)
    grad = scale * (pulled - scaled * inner) + grad_out[...].astype(F32)
    return grad, jnp.sum(total * scaled, axis=0, keepdims=True)


def add_rows(target, sources, chunk=64):
    @pl.loop(0, target.shape[0] // chunk)
    def _(n):
        rows = pl.ds(pl.multiple_of(n * chunk, chunk), chunk)
        total = sources[0][rows, :].astype(F32)
        for source in sources[1:]:
            total += source[rows, :].astype(F32)
        target[rows, :] = total.astype(target.dtype)


class Grads:
    ORDER = (4, 0, 1, 2, 3, 5)

    @staticmethod
    def scratch(shard, columns, wide, width):
        return [
            pltpu.VMEM((3, columns, width), BF16),
            pltpu.VMEM((3, wide, width), BF16),
            pltpu.VMEM((2, columns, shard), BF16),
            pltpu.VMEM((2, columns, shard), BF16),
            pltpu.VMEM((THIRD, width), BF16),
            DMA((22,)),
            DMA((27,)),
        ]

    @staticmethod
    def results(shard, width):
        return [((2, 4 * THIRD, shard), BF16), ((SHARED + HEADS, shard), BF16), ((THIRD, width), BF16)]

    def __init__(self, spot, results, scratch):
        self.spot = spot
        self.reduced, self.shared, self.out = results
        self.cores, self.cores_out, self.planes, self.relay, self.mate_out, self.send, self.recv = scratch
        self.shard = self.planes.shape[2]
        self.others = 2 * (1 - spot.half)
        self.is_gateway = (spot.z == 1) | (spot.z == 2)

    def rows(self, n):
        _, first, size = tile_parts(self.spot, 0)[n]
        return pl.ds(first, size)

    def columns(self, z):
        return pl.ds(pl.multiple_of(z * self.shard, LANES), self.shard)

    def core_copy(self, n):
        buffer, rows = (self.cores_out, pl.ds(0, self.cores_out.shape[1])) if n == 5 else (self.cores, self.rows(n))
        return remote(
            buffer.at[2, rows], buffer.at[1, rows], self.send.at[n], self.recv.at[n], self.spot.sibling
        )

    def product(self, layer, n, proj_grad, normed, normed_out, h_rows):
        def flat(value):
            return value.reshape(-1, value.shape[-1])

        width = self.cores.shape[2]
        slot = 2 * (self.spot.s - layer) * (self.spot.s - layer)
        if n == 5:
            total = dot_tn(flat(normed_out[...]), flat(h_rows[:, :, :width]))
            self.cores_out[slot] = total.astype(BF16)
        else:
            _, first, size = tile_parts(self.spot, 0)[n]
            total = dot_tn(flat(proj_grad[:, :, first : first + size]), flat(normed[...]))
            self.cores[slot, first : first + size, :] = total.astype(BF16)
        pl.when(self.spot.s != layer)(lambda: self.core_copy(n).start())

    def far_part(self, c, n):
        return self.cores.at[0, self.rows(n), self.columns(self.others + c)]

    def to_mate(self, n):
        source = self.cores.at[0, self.rows(n), self.columns(self.spot.mate)]
        target = self.planes.at[1, self.rows(n)]
        return remote(source, target, self.send.at[6 + n], self.recv.at[11 + n], self.spot.at_mate)

    def to_relay(self, c, n):
        j = 2 * n + c
        target = self.relay.at[c, self.rows(n)]
        return remote(
            self.far_part(c, n), target, self.send.at[11 + j], self.recv.at[16 + j], self.spot.at_mate
        )

    def to_far(self, c, n):
        target = self.planes.at[0, self.rows(n)]
        place = self.spot.column(self.others + c)
        return remote(
            self.far_part(c, n), target, self.send.at[11 + 2 * n + c], self.recv.at[6 + n], place
        )

    def out_rows(self, lo):
        return pl.ds(pl.multiple_of(lo * THIRD, 64), THIRD)

    def mate_copy(self):
        source = self.cores_out.at[0, self.out_rows(1 - self.spot.lo)]
        return remote(source, self.mate_out, self.send.at[21], self.recv.at[26], self.spot.at_mate)

    def sent(self, n):
        self.to_mate(n).wait_send()
        for c in range(2):
            self.to_relay(c, n).wait_send()

    def to_planes(self, n):
        self.core_copy(n).wait_recv()
        if n == 5:
            add_rows(self.cores_out.at[0], [self.cores_out.at[0], self.cores_out.at[1]])
            self.mate_copy().start()
            return
        own, sibling = self.cores.at[0, self.rows(n)], self.cores.at[1, self.rows(n)]
        add_rows(own, [own, sibling], 48 if n < 4 else 16)

        @pl.when(jnp.logical_not(self.is_gateway))
        def _():
            for c in range(2):
                self.to_relay(c, n).start()

        self.to_mate(n).start()

    def pass_on(self, n):
        @pl.when(self.is_gateway)
        def _():
            for c in range(2):
                self.to_relay(c, n).wait_recv()
                target, relay = self.far_part(c, n), self.relay.at[c, self.rows(n)]
                add_rows(target, [target, relay], 48 if n < 4 else 16)
                self.to_far(c, n).start()

    def gather(self, n):
        if n == 5:
            self.mate_copy().wait_recv()
            add_rows(self.out, [self.cores_out.at[0, self.out_rows(self.spot.lo)], self.mate_out], 48)
            return
        self.to_mate(n).wait_recv()
        self.to_far(0, n).wait_recv()
        _, first, size = tile_parts(self.spot, 0)[n]
        mine = self.columns(self.spot.z)
        chunk = 48 if n < 4 else 16

        @pl.loop(0, size // chunk)
        def _(r):
            rows = pl.ds(pl.multiple_of(first + r * chunk, 16), chunk)
            own = self.cores[0, rows, mine].astype(F32) + self.planes[1, rows, :].astype(F32)
            other = self.planes[0, rows, :]
            if n < 4:
                self.reduced[0, rows, :] = own.astype(BF16)
                self.reduced[1, rows, :] = other
            else:
                rows = pl.ds(pl.multiple_of(r * chunk, 16), chunk)
                self.shared[rows, :] = (own + other.astype(F32)).astype(BF16)

    def finish(self):
        self.mate_copy().wait_send()
        for n in self.ORDER:
            self.core_copy(n).wait_send()


class GradsAround:
    @staticmethod
    def scratch(shard):
        return [
            pltpu.VMEM((4, SHARED + HEADS, shard), BF16),
            DMA((11,)),
            DMA((34,)),
            DMA((34,)),
        ]

    def __init__(self, spot, results, final, final_out, scratch):
        self.spot, self.final, self.final_out = spot, final, final_out
        self.reduced, self.shared, self.out = results
        self.sums, self.local, self.send, self.recv = scratch

    def region(self, k, i, n):
        q = self.spot.q if k == 0 else self.spot.around[k]
        half = self.spot.half if i == 0 else 1 - self.spot.half
        at = n // 2 * INNER + THIRD * (8 * half + 4 * (n % 2) + q)
        return self.final.at[pl.ds(pl.multiple_of(at, 64), THIRD)]

    def copy(self, k, i, n):
        source = self.reduced.at[i, pl.ds(n * THIRD, THIRD)]
        target = self.region(0, i, n)
        j = 4 * i + n
        if k == 0:
            return pltpu.make_async_copy(source, target, self.local.at[j])
        if k < 3:
            j += 8 * (k - 1)
            return remote(source, target, self.send.at[j], self.recv.at[j], self.spot.plane(k))
        source = target = self.region(1 if i == 0 else 2, i, n)
        place = self.spot.plane(2 if i == 0 else 1)
        return remote(source, target, self.send.at[16 + j], self.recv.at[16 + j], place)

    def send_part(self, n):
        for i in range(2):
            for k in (1, 2, 0):
                self.copy(k, i, n).start()

    def pass_part(self, n):
        for i in range(2):
            self.copy(1 + i, i, n).wait_recv()
            self.copy(3, i, n).start()

    def out_region(self, k, i):
        q = self.spot.q if k == 0 else self.spot.around[k]
        size = THIRD if i is None else THIRD // 2
        at = q * THIRD + (0 if i is None else i * size)
        return self.final_out.at[pl.ds(pl.multiple_of(at, 32), size)]

    def out_copy(self, k, i=None):
        target = self.out_region(0, None)
        if k == 0:
            return pltpu.make_async_copy(self.out, target, self.local.at[8])
        if k < 3:
            return remote(self.out, target, self.send.at[23 + k], self.recv.at[23 + k], self.spot.plane(k))
        part = self.out_region(1 + i, i)
        return remote(part, part, self.send.at[26 + i], self.recv.at[26 + i], self.spot.plane(2 - i))

    def send_out(self):
        for k in (1, 2, 0):
            self.out_copy(k).start()

    def pass_out(self):
        for i in range(2):
            self.out_copy(1 + i).wait_recv()
            self.out_copy(3, i).start()

    def shared_copy(self, k):
        source = self.shared if k == 1 else self.sums.at[1]
        target = self.sums.at[0 if k == 1 else 2]
        return remote(source, target, self.send.at[27 + k], self.recv.at[27 + k], self.spot.plane(k))

    def shared_home(self):
        tail = self.final.at[pl.ds(2 * INNER, SHARED + HEADS)]
        return pltpu.make_async_copy(self.sums.at[3], tail, self.local.at[9])

    def shared_step(self, n):
        if n > 0:
            self.shared_copy(n).wait_recv()
            sources = [self.shared, self.sums.at[0]] if n == 1 else [self.sums.at[1], self.sums.at[2]]
            add_rows(self.sums.at[1 if n == 1 else 3], sources, 16)
        if n < 2:
            self.shared_copy(n + 1).start()
        else:
            self.shared_home().start()

    def finish(self):
        for i in range(2):
            for n in range(4):
                self.copy(2 - i, i, n).wait_recv()
                self.copy(3, i, n).wait_recv()
                for k in (1, 2, 3):
                    self.copy(k, i, n).wait_send()
                self.copy(0, i, n).wait()
            self.out_copy(3, i).wait_recv()
            self.out_copy(3, i).wait_send()
        for k in (1, 2):
            self.out_copy(k).wait_send()
            self.shared_copy(k).wait_send()
        self.out_copy(0).wait()
        self.shared_home().wait()


class SmallSum:
    SHAPE = (8, 4 * PIECE)

    @staticmethod
    def scratch():
        return [
            pltpu.VMEM((4,) + SmallSum.SHAPE, F32),
            pltpu.VMEM((8,) + SmallSum.SHAPE, F32),
            DMA((9,)),
            DMA((9,)),
        ]

    def __init__(self, spot, scratch):
        self.spot = spot
        self.small, self.group, self.send, self.recv = scratch

    def to_sibling(self):
        return remote(
            self.small.at[0], self.small.at[1], self.send.at[0], self.recv.at[0], self.spot.sibling
        )

    def to_mate(self):
        return remote(
            self.small.at[2], self.small.at[3], self.send.at[1], self.recv.at[1], self.spot.at_mate
        )

    def to_group(self, j):
        spot = self.spot
        part = self.group.at[4 * spot.half + spot.q]
        places = [spot.plane(k) for k in (1, 2, 3)] + [spot.at_twin]
        places += [(spot.s, spot.around[k], spot.twin) for k in (1, 2, 3)]
        return remote(part, part, self.send.at[2 + j], self.recv.at[2 + j], places[j])

    def begin(self, value):
        self.small[0] = value
        self.to_sibling().start()

    def step(self, n, value=None):
        if n == 0:
            self.to_sibling().wait_recv()
            self.small[2] = value + self.small[1]
            self.to_mate().start()
        else:
            self.to_mate().wait_recv()
            self.group[4 * self.spot.half + self.spot.q] = self.small[2] + self.small[3]
            for j in range(7):
                self.to_group(j).start()

    def finish(self, out):
        for j in range(7):
            self.to_group(j).wait_recv()
        total = self.group[0, :, 2 * PIECE :]
        for n in range(1, 8):
            total += self.group[n, :, 2 * PIECE :]
        for half in range(2):
            for j in range(2):
                for q in range(4):
                    at = (8 * half + 4 * j + q) * PIECE
                    out[:, at : at + PIECE] = self.group[4 * half + q, :, j * PIECE : (j + 1) * PIECE]
        out[:, -SHARED:] = total[:, :SHARED]
        out[7:8, DT_AT : DT_AT + HEADS] = total[7:8, :HEADS]
        out[7:8, RATE_AT : RATE_AT + HEADS] = total[7:8, LANES : LANES + HEADS]
        for r in range(8):
            out[7:8, r * THIRD : (r + 1) * THIRD] = total[r : r + 1, PIECE : PIECE + THIRD]
        self.to_sibling().wait_send()
        self.to_mate().wait_send()
        for j in range(7):
            self.to_group(j).wait_send()


def loading(sources, targets, sems):
    return [pltpu.make_async_copy(a, b, sems.at[n]) for n, (a, b) in enumerate(zip(sources, targets))]


def saved_shapes(length, width, wide):
    columns = ((width, BF16), (wide, F32), (wide, BF16), (SHARED, BF16), (LANES, BF16), (wide, BF16))
    return [((2, length, n), t) for n, t in columns]


def middle_kernel(heads, *refs):
    ins, outs, kept, weight_s, sum_s, spread_s, layer_s, (store,) = take(refs, (7, 6, 6, 5, 5, 3, 11, 1))
    w_in, w_out, *layer_ins, rows_in = ins
    tile, tile_out, all_rows, branch, scales, rows_out = outs
    u, w, wo, pack, *saved, load = layer_s
    spot = Spot()
    rows_in = rows_in.at[spot.s]
    weights = Weights(spot, 1, w_in, w_out, tile, tile_out, weight_s)
    total = Sum(spot, rows_in.shape[1], sum_s)
    spread = Spread(spot, rows_out, all_rows, spread_s)
    loads = loading(layer_ins[:3] + [layer_ins[3].at[0]], layer_s[:4], load)
    for copy in loads:
        copy.start()
    weights.begin()
    greet(all_places(spot))
    weights.start()
    for copy in loads:
        copy.wait()
    params = load_params(([spot.piece(spot.half, j) for j in range(2)], pack))

    @pl.loop(0, 2)
    def _(i):
        forward_rows(heads, params, total.half(i), u, w, wo, None, [total.parts, None, *saved])
        total.start(i)

    stores = loading(saved, kept, store)
    for copy in stores:
        copy.start()
    weights.step(0)
    total.forward()
    weights.step(1)
    layer_rows(total.finish(), rows_in, branch, scales, rows_out)
    spread.start()
    weights.step(2)
    spread.forward()
    weights.step(3)
    weights.step(4)
    spread.finish()
    total.close()
    weights.finish()
    for copy in stores:
        copy.wait()


class RowSums:
    @staticmethod
    def scratch(length):
        shape = (2, 8, length)
        return [pltpu.VMEM(shape, F32), pltpu.VMEM((7,) + shape, F32), DMA((14,)), DMA((14,))]

    def __init__(self, spot, scratch):
        self.mine, self.others, self.send, self.recv = scratch
        self.places = [spot.plane(k) for k in (1, 2, 3)] + [spot.at_twin]
        self.places += [(spot.s, spot.around[k], spot.twin) for k in (1, 2, 3)]

    def copies(self, seq):
        return [
            remote(
                self.mine.at[seq], self.others.at[j, seq],
                self.send.at[2 * j + seq], self.recv.at[2 * j + seq], place,
            )
            for j, place in enumerate(self.places)
        ]

    def start(self, seq):
        for copy in self.copies(seq):
            copy.start()

    def finish(self, seq):
        total = self.mine[seq]
        for j, copy in enumerate(self.copies(seq)):
            copy.wait_recv()
            total += self.others[j, seq]
        for copy in self.copies(seq):
            copy.wait_send()
        self.mine[seq] = total


def back_kernel(heads, *refs):
    ins, outs, first_s, last_s, second_s, spread_s, row_s, back_s, layer_s, grads_s, results, around_s, own_s, rest = take(
        refs, (18, 5, 5, 5, 5, 3, 4, 6, 11, 7, 3, 4, 4, 10)
    )
    (all_rows, all_cot, packs), tiles, kept, own_ins = take(ins, (3, 4, 6, 5))
    first_rows, tokens, grad_out, branch, scales = own_ins
    home_rows, home_grads, final, final_out, small_out = outs
    u, w, wo, pack, *saved, load = layer_s
    h_rows, h_next, payload, last_rows, last_grad, first_grad, small, send, recv, local = rest
    proj_grad, normed_out, *scratch = back_s
    spot = Spot()
    tokens, grad_out = tokens.at[spot.s], grad_out.at[spot.s]
    width = first_rows.shape[1]
    total = Sum(spot, width, first_s)
    last = Sum(spot, width, last_s)
    second = Sum(spot, width, second_s)
    spread = Spread(spot, payload, h_next, spread_s)
    sums = RowSums(spot, row_s)
    grads = Grads(spot, results, grads_s)
    around = GradsAround(spot, results, final, final_out, around_s)
    own = SmallSum(spot, own_s)
    first_core, last_core = pl.when(spot.s == 0), pl.when(spot.s == 1)
    loads = loading([all_rows, *tiles[2:], packs, all_cot], [u, w, wo, pack, h_rows], load)
    reloads = loading([*tiles[:2], *kept], [w, wo, *saved], load)
    for copy in loads:
        copy.start()
    places = [spot.plane(k) for k in (1, 2, 3)] + [spot.column((spot.z + k) % 4) for k in (1, 2, 3)]
    places += [(spot.s, spot.around[k], spot.twin) for k in (1, 2, 3)] + [spot.sibling]
    greet(places)
    for copy in loads:
        copy.wait()
    ids = [spot.piece(spot.half, j) for j in range(2)]
    params = load_params((ids, pack.at[1]))

    @pl.loop(0, 2)
    def _(i):
        seq = last.half(i)
        forward_rows(heads, params, seq, u, w, wo, h_rows, [last.parts, sums.mine, *saved])
        sums.start(seq)
        last.start(i)

    def backward(layer, params, total, h_ref, aux_of):
        small[layer] = jnp.zeros(small.shape[1:], F32)

        @pl.loop(0, 2)
        def _(i):
            seq = total.half(i)
            aux = aux_of(seq)
            outs = (total.parts, proj_grad, normed_out)
            parts = backward_rows(heads, params, seq, h_ref, aux, saved[1:], w, wo, outs, scratch)
            add_small(small.at[layer], *parts)
            total.start(i)

    def row_aux(seq):
        sums.finish(seq)
        return aux_of_rows(sums.mine[seq])

    backward(1, params, total, h_rows, row_aux)

    def product(layer, n):
        grads.product(layer, n, proj_grad, saved[0], normed_out, h_rows if layer else h_next)

    product(1, 4)
    product(1, 0)
    total.forward()
    for n in (1, 2, 3, 5):
        product(1, n)
    for copy in reloads:
        copy.start()
    grad, last_gain = norm_back(total.finish(), first_rows, pack[1, 7:8, :width], grad_out)
    low = grad.astype(BF16)
    last_grad[...] = low
    cross = jnp.sum(low.astype(F32) * branch[...], axis=1, keepdims=True)
    payload[:, :width] = low
    lanes = lax.broadcasted_iota(jnp.int32, (payload.shape[0], LANES), 1)
    scale_part = split_three(scales[:, 0:1]).astype(F32)
    cross_part = pltpu.roll(split_three(cross).astype(F32), 3, 1)
    payload[:, width:] = jnp.where(lanes < 3, scale_part, cross_part).astype(BF16)
    spread.start()
    add_gain(small.at[1], last_gain)
    first_core(lambda: own.begin(small[1]))
    spread.forward()

    @last_core
    def _():
        for n in (4, 0):
            grads.to_planes(n)
        own.step(0, small[1])
        for n in (1, 2):
            grads.to_planes(n)
        grads.pass_on(4)

    spread.finish()

    @last_core
    def _():
        own.step(1)
        for n in (3, 5):
            grads.to_planes(n)
        for n in (0, 1):
            grads.pass_on(n)

    last.forward()
    for copy in reloads:
        copy.wait()
    params = load_params((ids, pack.at[0]))

    backward(0, params, second, h_next, lambda seq: aux_of_columns(h_next, seq, width))
    for n in Grads.ORDER:
        product(0, n)

    @first_core
    def _():
        for n in (4, 0, 1):
            grads.to_planes(n)

    @last_core
    def _():
        for n in (2, 3):
            grads.pass_on(n)
        grads.gather(4)
        around.shared_step(0)
        for n in (0, 1):
            grads.gather(n)
            around.send_part(n)

    second.forward()

    @first_core
    def _():
        grads.pass_on(4)
        grads.to_planes(2)
        grads.pass_on(0)
        grads.to_planes(3)
        grads.gather(4)
        around.shared_step(0)
        grads.pass_on(1)
        grads.gather(0)
        around.send_part(0)
        grads.to_planes(5)
        grads.pass_on(2)

    @last_core
    def _():
        grads.gather(2)
        around.send_part(2)
        around.shared_step(1)
        around.pass_part(0)
        grads.gather(3)
        around.send_part(3)
        grads.gather(5)
        around.send_out()
        around.pass_part(1)

    grad, first_gain = norm_back(second.finish(), tokens, pack[0, 7:8, :width], last_grad)
    first_grad[...] = grad.astype(BF16)
    layers = ((first_rows, first_grad), (last_rows, last_grad))

    def home_copies(s):
        copies = []
        for n, target in enumerate((home_rows, home_grads)):
            copies.append(remote(layers[1 - s][n], target.at[s], send.at[n], recv.at[n], spot.sibling))
            copies.append(pltpu.make_async_copy(layers[s][n], target.at[s], local.at[n]))
        return copies

    add_gain(small.at[0], first_gain)
    last_core(lambda: own.begin(small[0]))
    layer_rows(last.finish(), first_rows, None, None, last_rows)
    for s in range(2):

        @pl.when(spot.s == s)
        def _(s=s):
            for copy in home_copies(s):
                copy.start()

    @first_core
    def _():
        grads.pass_on(3)
        grads.gather(1)
        around.send_part(1)
        around.shared_step(1)
        around.pass_part(0)
        own.step(0, small[0])
        grads.gather(2)
        around.send_part(2)
        around.pass_part(1)
        around.shared_step(2)
        own.step(1)
        grads.gather(3)
        around.send_part(3)
        grads.gather(5)
        around.send_out()
        for n in (2, 3):
            around.pass_part(n)
        around.pass_out()

    @last_core
    def _():
        around.shared_step(2)
        for n in (2, 3):
            around.pass_part(n)
        around.pass_out()

    own.finish(small_out)
    around.finish()
    for n in range(5):
        grads.sent(n)
    grads.finish()
    for s in range(2):

        @pl.when(spot.s == s)
        def _(s=s):
            for copy in home_copies(s):
                copy.wait()

    total.close()
    last.close()
    second.close()


def comm_call(kernel, collective, ins, in_specs, outs, out_specs, scratch, name):
    return pl.pallas_call(
        kernel,
        out_shape=[jax.ShapeDtypeStruct(s, t) for s, t in outs],
        in_specs=in_specs,
        out_specs=out_specs,
        scratch_shapes=scratch,
        compiler_params=pltpu.CompilerParams(
            collective_id=collective, has_side_effects=True, vmem_limit_bytes=60 * 1024 * 1024
        ),
        name=name,
    )(*ins)


def fast_shards(
    tokens, cotangent, norm_gain, w_in, conv_weight, conv_bias, dt_bias, a_log, skip_gain, gate_gain, w_out
):
    span, width = tokens.shape[2:]
    heads = HEADS // 8
    wide = heads * HEADDIM
    columns = 2 * wide + SHARED + HEADS
    shard = w_in.shape[1]
    rows_in = w_in[0].T
    pack_shape = (8, INNER // THIRD * PIECE + SHARED)
    group = (2, 4 * span, width)
    weight_outs = [((columns, width), BF16), ((wide, width), BF16)]
    weight_s = Weights.scratch(columns, shard, width)
    payload = width + LANES
    tile, tile_out, packs, all_rows, all_cot = comm_call(
        open_kernel, 1,
        [
            rows_in, w_out[0], tokens[:, 0], cotangent[:, 0], conv_weight[0], conv_bias, gate_gain, skip_gain,
            norm_gain, dt_bias, a_log,
        ],
        [ANY] * 4 + [VMEM] * 7,
        weight_outs + [((2,) + pack_shape, F32), (group, BF16), (group, BF16)], [ANY] * 5,
        weight_s + Spread.SEMS + Spread.SEMS
        + [pltpu.VMEM((span, width), BF16)] * 2 + [pltpu.VMEM(pack_shape, F32), DMA((2,)), DMA, DMA, DMA],
        "open",
    )
    length = 4 * span
    rows_spec = ((span, width), BF16)
    layer_s = [
        pltpu.VMEM((2, length, width), BF16), pltpu.VMEM((columns, width), BF16),
        pltpu.VMEM((wide, width), BF16), pltpu.VMEM(pack_shape, F32),
    ]
    kept_shapes = saved_shapes(length, width, wide)
    kept_s = [pltpu.VMEM(*k) for k in kept_shapes]
    back_s = [pltpu.VMEM((2, length, columns), BF16), pltpu.VMEM((2, length, wide), BF16)]
    back_s += backward_scratch(length, wide)
    results = Grads.results(shard, width)
    sum_s = Sum.scratch(span, width)
    first_tiles = [tile, tile_out]
    tile, tile_out, all_rows, branch, scales, rows, *kept = comm_call(
        partial(middle_kernel, heads), 2,
        [rows_in, w_out[0], all_rows, tile, tile_out, packs, tokens[:, 0]], [ANY] * 6 + [VMEM],
        weight_outs + [(group, BF16), ((span, width), F32), ((span, LANES), F32), rows_spec] + kept_shapes,
        [ANY] * 3 + [VMEM] * 3 + [ANY] * 6,
        weight_s + Sum.scratch(span, payload) + Spread.SEMS + layer_s + kept_s + [DMA((4,)), DMA((6,))],
        "middle",
    )
    home_rows, home_grads, final, final_out, small = comm_call(
        partial(back_kernel, heads), 3,
        [
            all_rows, all_cot, packs, *first_tiles, tile, tile_out, *kept,
            rows, tokens[:, 0], cotangent[:, 0], branch, scales,
        ],
        [ANY] * 13 + [VMEM] * 5,
        [
            ((2, span, width), BF16), ((2, span, width), BF16),
            ((2 * INNER + SHARED + HEADS, shard), BF16), (w_out.shape[1:], BF16), (pack_shape, F32),
        ],
        [ANY] * 4 + [VMEM],
        sum_s + Sum.scratch(span, payload) + sum_s + Spread.SEMS + RowSums.scratch(length) + back_s
        + layer_s[:3] + [pltpu.VMEM((2,) + pack_shape, F32)] + kept_s + [DMA((8,))]
        + Grads.scratch(shard, columns, wide, width) + [pltpu.VMEM(*r) for r in results]
        + GradsAround.scratch(shard) + SmallSum.scratch()
        + [
            pltpu.VMEM((2, length, width), BF16), pltpu.VMEM((2, length, payload), BF16),
            pltpu.VMEM((span, payload), BF16), *[pltpu.VMEM((span, width), BF16)] * 3,
            pltpu.VMEM((2,) + SmallSum.SHAPE, F32), DMA((2,)), DMA((2,)), DMA((2,)),
        ],
        "back",
    )
    grad_in, grad_out, gain, conv, bias, shift, rate, skip, gate = finish_call(final, final_out, small)
    return (
        home_rows[None, :, None], home_grads[None, :, None], gain, grad_in.T[None], conv[None],
        bias, shift, rate, skip, gate, grad_out[None],
    )


def finish_kernel(final, final_out, small, grad_in, grad_out, gain, conv, bias, shift, rate, skip, gate):
    grad_in[...] = final[...].astype(F32)
    step = pl.program_id(0)
    grad_out[...] = final_out[...].astype(F32)

    @pl.when(step == 0)
    def _():
        gain[...] = small[7:8, :GAIN_END]
        shift[...] = small[7:8, DT_AT : DT_AT + HEADS]
        rate[...] = small[7:8, RATE_AT : RATE_AT + HEADS]
        heads = []
        for p in range(INNER // THIRD):
            source, target = slice(p * PIECE, p * PIECE + THIRD), slice(p * THIRD, (p + 1) * THIRD)
            conv[:, target] = small[0:CONV, source]
            bias[:, target] = small[CONV : CONV + 1, source]
            gate[:, target] = small[6:7, source]
            for h in range(3):
                part = small[5:6, p * PIECE + h * HEADDIM : p * PIECE + (h + 1) * HEADDIM]
                heads.append(jnp.sum(part, axis=1, keepdims=True))
        skip[...] = jnp.concatenate(heads, axis=1)
        conv[:, INNER:] = small[0:CONV, -SHARED:]
        bias[:, INNER:] = small[CONV : CONV + 1, -SHARED:]


def finish_call(final, final_out, small):
    rows, shard = final.shape
    out_rows, width = final_out.shape
    steps = 13
    out_steps = 12
    assert rows % (16 * steps) == 0 and out_rows % (16 * out_steps) == 0
    smalls = [(1, GAIN_END), (CONV, XBC), (1, XBC), (1, HEADS), (1, HEADS), (1, HEADS), (1, INNER)]

    def in_block(i):
        return (i, 0)

    def out_block(i):
        return (jnp.minimum(i, out_steps - 1), 0)

    def same(i):
        return (0, 0)

    return pl.pallas_call(
        finish_kernel,
        grid=(steps,),
        out_shape=[jax.ShapeDtypeStruct(s, F32) for s in [final.shape, final_out.shape] + smalls],
        in_specs=[
            pl.BlockSpec((rows // steps, shard), in_block),
            pl.BlockSpec((out_rows // out_steps, width), out_block),
            pl.BlockSpec(small.shape, same),
        ],
        out_specs=[
            pl.BlockSpec((rows // steps, shard), in_block),
            pl.BlockSpec((out_rows // out_steps, width), out_block),
        ]
        + [pl.BlockSpec(s, same) for s in smalls],
        compiler_params=pltpu.CompilerParams(**PARAMS),
        name="finish",
    )(final, final_out, small)


def shards(
    tokens, cotangent, norm_gain, w_in, conv_weight, conv_bias, dt_bias, a_log, skip_gain, gate_gain, w_out
):
    section = lax.axis_index("section")
    place = lax.axis_index("seq")
    depth = lax.axis_index("fsdp")
    plan = Plan(lax.axis_size("seq"), lax.axis_size("fsdp"))
    half = depth // plan.mates
    micro, _, span, width = tokens.shape
    layers = lax.axis_size("section")
    wide, channels, heads = plan.wide, plan.channels, plan.heads

    shard = w_in[0]
    gate_part = widened(plan.take(shard[:, :INNER], 1, place), 2, wide)
    x_part = widened(plan.take(shard[:, INNER : 2 * INNER], 1, place), 2, wide)
    shared_part = jnp.broadcast_to(
        shard[:, 2 * INNER : INNER + XBC], (plan.halves, shard.shape[0], SHARED)
    )
    dt_part = widened(plan.take(shard[:, INNER + XBC :], 1, place), 2, LANES)
    tile = jnp.concatenate([gate_part, x_part, shared_part, dt_part], axis=2)
    tile = jnp.repeat(tile, plan.mates, axis=0)
    tile = lax.all_to_all(tile, "fsdp", 0, 0, tiled=True).reshape(width, -1).T
    w_tiles = lax.all_gather(tile, "section", axis=0)
    if plan.pieces == plan.mates:
        piece = w_out[0].reshape(plan.seq, -1, width)
        piece = lax.dynamic_index_in_dim(piece, place, 0, False)
        rows_out = lax.all_gather(
            piece, "fsdp", axis=0, tiled=True, axis_index_groups=plan.mate_groups
        )
    else:
        rows_out = lax.all_gather(w_out[0], "fsdp", axis=0, tiled=True)
        rows_out = lax.dynamic_index_in_dim(plan.take(rows_out, 0, place), half, 0, False)
    wo_tiles = lax.all_gather(widened(rows_out, 0, wide), "section", axis=0)

    def own(array, axis, size):
        part = lax.dynamic_index_in_dim(plan.take(array, axis, place), half, 0, False)
        return widened(part, axis, size)

    skip_wide = jnp.repeat(skip_gain[0], HEADDIM)[None]
    by_channel = jnp.concatenate(
        [conv_weight[0, :, :INNER], conv_bias[:, :INNER], skip_wide, gate_gain, jnp.zeros((1, INNER))], 0
    )
    by_channel = own(by_channel, 1, wide)
    by_shared = jnp.concatenate(
        [conv_weight[0, :, INNER:], conv_bias[:, INNER:], jnp.zeros((3, SHARED))], 0
    )
    by_head = jnp.concatenate([dt_bias, a_log, jnp.zeros((6, HEADS))], 0)
    by_head = own(by_head, 1, LANES)
    smalls = jnp.concatenate(
        [by_channel.ravel(), by_shared.ravel(), by_head.ravel(), norm_gain[0]]
    )
    smalls = lax.all_gather(smalls, "section", axis=0)
    cuts = [8 * wide, 8 * (wide + SHARED), 8 * (wide + SHARED + LANES)]
    params = []
    for l in range(layers):
        ch, bc, dtp, gain = jnp.split(smalls[l], cuts)
        params.append((gain[None], ch.reshape(8, -1), bc.reshape(8, -1), dtp.reshape(8, -1)))

    def gather_rows(own_rows):
        rows = lax.all_gather(own_rows, "seq", axis=0, tiled=True)
        if plan.halves == 1:
            return rows[None]
        return lax.all_gather(rows, "fsdp", axis=0, axis_index_groups=plan.peer_groups)

    def sum_rows(parts):
        if plan.halves == 1:
            rows = parts[0]
        else:
            rows = lax.psum_scatter(
                parts, "fsdp", scatter_dimension=0, axis_index_groups=plan.peer_groups
            )
        return lax.psum_scatter(rows, "seq", scatter_dimension=0, tiled=True)

    own_tokens = lax.dynamic_index_in_dim(tokens, section, 0, False)[0]
    own_cot = lax.dynamic_index_in_dim(cotangent, section, 0, False)[0]
    inputs, outputs, branch, saved, scales = [own_tokens], [], [], [], []
    for l in range(layers):
        rows = gather_rows(inputs[l])
        parts, square, normed, *kept = run_forward(
            heads, wide, rows, w_tiles[l], wo_tiles[l], params[l]
        )
        saved.append((normed, kept))
        total = sum_rows(parts).astype(F32)
        square = sum_rows(square)[:, :1]
        scale = lax.rsqrt(square / INNER + NORM_EPS)
        branch.append(total * scale)
        scales.append(scale)
        outputs.append((inputs[l].astype(F32) + branch[l]).astype(BF16))
        inputs.append(outputs[l])
    grads_in, small_grads = [None] * layers, [None] * layers
    w_grads, wo_grads = [None] * layers, [None] * layers
    grad_rows = own_cot
    for l in reversed(range(layers)):
        rdot = jnp.sum(grad_rows.astype(F32) * branch[l], axis=-1, keepdims=True)
        aux = widened(jnp.concatenate([scales[l], rdot], axis=1), 1, LANES)
        all_grads = gather_rows(grad_rows)
        aux = gather_rows(aux)
        normed, kept = saved[l]
        parts, proj_grad, normed_out, g_ch, g_bc, g_dt = run_backward(
            heads, wide, all_grads, aux, kept, w_tiles[l], wo_tiles[l], params[l]
        )
        w_grads[l] = dot_tn(normed.reshape(-1, width), proj_grad.reshape(-1, proj_grad.shape[-1])).astype(BF16)
        wo_grads[l] = dot_tn(normed_out.reshape(-1, wide), all_grads.reshape(-1, width)).astype(BF16)
        grad_normed = sum_rows(parts).astype(F32)
        rows = inputs[l].astype(F32)
        scale = lax.rsqrt(jnp.mean(rows * rows, axis=-1, keepdims=True) + NORM_EPS)
        scaled = rows * scale
        g_gain = jnp.sum(grad_normed * scaled, axis=0)
        pulled = grad_normed * params[l][0]
        inner = jnp.mean(pulled * scaled, axis=-1, keepdims=True)
        grad = scale * (pulled - scaled * inner) + grad_rows.astype(F32)
        grad_rows = grad.astype(BF16)
        grads_in[l] = grad_rows

        def placed(value, size):
            value = value[..., :size]
            full = jnp.zeros((plan.seq, plan.halves) + value.shape, F32)
            full = lax.dynamic_update_slice(full, value[None, None], (place, half, 0, 0))
            return plan.put(full, 1)

        by_channel = placed(g_ch, channels)
        by_head = placed(g_dt, heads)
        skip = by_channel[5].reshape(HEADS, HEADDIM).sum(-1)
        small_grads[l] = jnp.concatenate(
            [
                g_gain, by_channel[:5].ravel(), g_bc[:5].ravel(), by_head[0], by_head[1], skip, by_channel[6]
            ]
        )

    smalls = lax.psum(jnp.stack(small_grads), ("section", "seq", "fsdp"))
    smalls = lax.dynamic_index_in_dim(smalls, section, 0, False)
    cuts, at = [], 0
    for size in (width, (CONV + 1) * INNER, (CONV + 1) * SHARED, HEADS, HEADS, HEADS):
        at += size
        cuts.append(at)
    g_gain, g_x, g_bc, g_shift, g_rate, g_skip, g_gate = jnp.split(smalls, cuts)
    conv_rows = jnp.concatenate([g_x.reshape(CONV + 1, -1), g_bc.reshape(CONV + 1, -1)], axis=1)

    w_grad = lax.psum_scatter(jnp.stack(w_grads), "section", scatter_dimension=0)
    w_grad = lax.all_to_all(w_grad, "fsdp", 0, 0, tiled=True)
    w_grad = w_grad.reshape(plan.halves, plan.mates, -1, w_grad.shape[-1]).astype(F32).sum(1)
    shared_grad = lax.psum(w_grad[..., 2 * wide : 2 * wide + SHARED].sum(0), "seq")
    head_grads = jnp.concatenate(
        [
            w_grad[..., :channels],
            w_grad[..., wide : wide + channels],
            w_grad[..., 2 * wide + SHARED : 2 * wide + SHARED + heads],
        ],
        axis=-1,
    ).astype(BF16)
    head_grads = lax.all_gather(head_grads, "seq", axis=0)
    grad_w_in = jnp.concatenate(
        [
            plan.put(head_grads[..., :channels], 1),
            plan.put(head_grads[..., channels : 2 * channels], 1),
            shared_grad.astype(BF16),
            plan.put(head_grads[..., 2 * channels :], 1),
        ],
        axis=-1,
    ).astype(F32)
    wo_grad = lax.psum_scatter(jnp.stack(wo_grads)[:, :channels], "section", scatter_dimension=0)
    if plan.pieces == plan.mates:
        wo_grad = lax.psum_scatter(
            wo_grad, "fsdp", scatter_dimension=0, tiled=True, axis_index_groups=plan.mate_groups
        )
        wo_grad = lax.all_gather(wo_grad, "seq", axis=0, tiled=True)
    else:
        full = jnp.zeros((plan.seq, plan.halves) + wo_grad.shape, BF16)
        full = lax.dynamic_update_slice(full, wo_grad[None, None], (place, half, 0, 0))
        full = plan.put(full, 0)
        wo_grad = lax.psum_scatter(full, "fsdp", scatter_dimension=0, tiled=True)
        wo_grad = lax.psum(wo_grad, "seq")

    def home(per_layer):
        return lax.all_to_all(jnp.stack(per_layer), "section", 0, 0, tiled=True)[None, :, None]

    return (
        home(outputs),
        home(grads_in),
        g_gain[None],
        grad_w_in[None],
        conv_rows[None, :CONV],
        conv_rows[CONV:],
        g_shift[None],
        g_rate[None],
        g_skip[None],
        g_gate[None],
        wo_grad.astype(F32)[None],
    )


def solution(mesh):
    shape = tuple(mesh.shape[a] for a in ("section", "seq", "fsdp"))
    return jax.shard_map(
        fast_shards if shape == (2, 4, 4) else shards,
        mesh=mesh,
        in_specs=(
            P(None, "fsdp", "seq", None),
            P(None, "fsdp", "seq", None),
            P("section", None),
            P("section", "fsdp", None),
            P("section", None, None),
            P("section", None),
            P("section", None),
            P("section", None),
            P("section", None),
            P("section", None),
            P("section", "fsdp", None),
        ),
        out_specs=(
            P("section", None, "fsdp", "seq", None),
            P("section", None, "fsdp", "seq", None),
            P("section", None),
            P("section", "fsdp", None),
            P("section", None, None),
            P("section", None),
            P("section", None),
            P("section", None),
            P("section", None),
            P("section", None),
            P("section", "fsdp", None),
        ),
        check_vma=False,
    )
```

```python
from functools import partial

import jax
import jax.numpy as jnp
from jax import lax
from jax.experimental import pallas as pl
from jax.experimental.pallas import tpu as pltpu
from jax.sharding import PartitionSpec as P

HEADS = 48
HEADDIM = 64
STATE = 128
CONV = 4
SPAN = 256
INNER = 3072
XBC = 3328
SHARED = 2 * STATE
LANES = 128
THIRD = 192
PIECE = 256
GAIN_END = 1536
DT_AT = 1536
RATE_AT = DT_AT + LANES
NORM_EPS = 1e-05
HIGHEST = lax.Precision.HIGHEST
BF16 = jnp.bfloat16
F32 = jnp.float32


def take(refs, counts):
    refs = list(refs)
    return [[refs.pop(0) for _ in range(n)] for n in counts]


def dot(left, right, contract=((1,), (0,)), precision=None):
    return lax.dot_general(
        left, right, (contract, ((), ())), preferred_element_type=F32, precision=precision
    )


def dot_nt(left, right):
    return dot(left, right, ((1,), (1,)))


def dot_tn(left, right):
    return dot(left, right, ((0,), (0,)))


def sigmoid(value):
    return 1.0 / (1.0 + jnp.exp(-value))


def shifted(value, distance):
    if distance == 0:
        return value
    length = value.shape[0]
    rows = lax.broadcasted_iota(jnp.int32, value.shape, 0)
    moved = pltpu.roll(value, distance % length, 0)
    if distance > 0:
        return jnp.where(rows >= distance, moved, 0.0)
    return jnp.where(rows < length + distance, moved, 0.0)


def conv_sum(raw, taps):
    total = taps[CONV : CONV + 1]
    for k in range(CONV):
        total = total + taps[k : k + 1] * shifted(raw, CONV - 1 - k)
    return total


def conv_back(grad, raw, taps):
    grad_raw = 0.0
    rows = []
    for k in range(CONV):
        grad_raw = grad_raw + taps[k : k + 1] * shifted(grad, -(CONV - 1 - k))
        rows.append(jnp.sum(grad * shifted(raw, CONV - 1 - k), axis=0, keepdims=True))
    rows.append(jnp.sum(grad, axis=0, keepdims=True))
    return grad_raw, rows


def stacked(rows, count):
    width = rows[0].shape[1]
    short = count - len(rows)
    return jnp.concatenate(rows + [jnp.zeros((short, width), F32)], axis=0)


def triangles():
    row_ids = lax.broadcasted_iota(jnp.int32, (SPAN, SPAN), 0)
    col_ids = lax.broadcasted_iota(jnp.int32, (SPAN, SPAN), 1)
    return row_ids >= col_ids


def step_sizes(dt_raw, dt_row):
    shift = dt_raw + dt_row
    step = jnp.maximum(shift, 0.0) + jnp.log1p(jnp.exp(-jnp.abs(shift)))
    return step, sigmoid(shift)


def low_half():
    return lax.broadcasted_iota(jnp.int32, (SPAN, LANES), 1) < HEADDIM


def head_lanes(h):
    lanes = lax.broadcasted_iota(jnp.int32, (1, LANES), 1)
    return (lanes < HEADDIM) if h % 2 == 0 else (lanes >= HEADDIM)


def split_three(value):
    lanes = lax.broadcasted_iota(jnp.int32, (value.shape[0], LANES), 1)
    result = jnp.zeros((value.shape[0], LANES), F32)
    for k in range(3):
        part = value.astype(BF16).astype(F32)
        result = jnp.where(lanes == k, part, result)
        value = value - part
    return result.astype(BF16)


def selection(ids):
    rows = lax.broadcasted_iota(jnp.int32, (HEADS, LANES), 0)
    columns = lax.broadcasted_iota(jnp.int32, (HEADS, LANES), 1)
    target = jnp.full((HEADS, LANES), -1, jnp.int32)
    for j in range(2):
        here = (columns >= 3 * j) & (columns < 3 * j + 3)
        target = jnp.where(here, columns + 3 * (ids[j] - j), target)
    return (rows == target).astype(F32)


def piece_lanes(ids, j):
    return pl.ds(pl.multiple_of(ids[j] * PIECE, PIECE), PIECE)


def load_params(refs):
    if len(refs) == 2:
        ids, pack_ref = refs
        sel = selection(ids)
        ch = jnp.concatenate([pack_ref[:, piece_lanes(ids, j)][:, :THIRD] for j in range(2)], axis=1)
        rows = [pack_ref[7:8, at : at + HEADS] for at in (DT_AT, RATE_AT)]
        dtp = dot(stacked(rows, 8), sel, precision=HIGHEST)
        return pack_ref[7:8, :GAIN_END], ch, pack_ref[:, -SHARED:], dtp, sel.astype(BF16)
    gain_ref, ch_ref, bc_ref, dtp_ref = refs
    return gain_ref[...], ch_ref[...], bc_ref[...], dtp_ref[...], None


def forward_kernel(heads, *refs):
    u_ref, w_ref, wo_ref, *refs = refs
    forward_rows(heads, load_params(refs[:4]), 0, u_ref, w_ref, wo_ref, None, refs[4:])


def forward_rows(heads, params, i, u_ref, w_ref, wo_ref, h_ref, outs):
    gain, ch, bc, dtp, sel = params
    out_ref, sums_ref, normed_ref, gate_ref, xraw_ref, bcraw_ref, dtraw_ref, mixed_ref = outs
    length, width = u_ref.shape[1:]
    wide = ch.shape[1]
    blocks = length // SPAN
    rows = u_ref[i].astype(F32)
    scale = lax.rsqrt(jnp.mean(rows * rows, axis=-1, keepdims=True) + NORM_EPS)
    normed = (rows * scale * gain).astype(BF16)
    normed_ref[i] = normed
    gate = dot_nt(normed, w_ref[:wide])
    gate_ref[i] = gate
    x_raw = dot_nt(normed, w_ref[wide : 2 * wide]).astype(BF16)
    xraw_ref[i] = x_raw
    rest = dot_nt(normed, w_ref[2 * wide :]).astype(BF16)
    bcraw_ref[i] = rest[:, :SHARED]
    dt_raw = rest[:, SHARED:]
    if sel is not None:
        dt_raw = dot(dt_raw, sel).astype(BF16)
    dtraw_ref[i] = dt_raw
    conv_x = conv_sum(x_raw.astype(F32), ch)
    act_x = (conv_x * sigmoid(conv_x)).astype(BF16)
    conv_bc = conv_sum(rest[:, :SHARED].astype(F32), bc)
    act_bc = (conv_bc * sigmoid(conv_bc)).astype(BF16)
    step, _ = step_sizes(dt_raw.astype(F32), dtp[0:1])
    rate = jnp.exp(dtp[1:2])
    causal = triangles()
    ones = causal.astype(F32)
    lower = low_half()
    carries = [None] * heads
    for b in range(blocks):
        span = slice(b * SPAN, (b + 1) * SPAN)
        step_b = step[span]
        decay = -dot(ones, rate * step_b, precision=HIGHEST)
        decay_t, step_t = decay.T, step_b.T
        b_in, c_out = act_bc[span, :STATE], act_bc[span, STATE:]
        scores = dot_nt(c_out, b_in)
        for first in range(0, heads, 2):
            lanes = slice(first * HEADDIM, first * HEADDIM + LANES)
            x_pair = act_x[span, lanes]
            parts = []
            for h in range(first, min(first + 2, heads)):
                gap = decay[:, h : h + 1] - decay_t[h : h + 1]
                mask = jnp.exp(jnp.where(causal, gap, -1e30))
                weights = (scores * mask * step_t[h : h + 1]).astype(BF16)
                part = dot(weights, x_pair)
                if carries[h] is not None:
                    part += jnp.exp(decay[:, h : h + 1]) * dot(c_out, carries[h].astype(BF16))
                if b + 1 < blocks:
                    last = decay[SPAN - 1 :, h : h + 1]
                    tail = jnp.exp(last - decay[:, h : h + 1]) * step_b[:, h : h + 1]
                    shaped = (b_in.astype(F32) * tail).astype(BF16)
                    fresh = dot_tn(shaped, x_pair)
                    if carries[h] is not None:
                        fresh += jnp.exp(last) * carries[h]
                    carries[h] = fresh
                parts.append(part)
            if len(parts) == 1:
                parts.append(jnp.zeros_like(parts[0]))
            within = jnp.where(lower, parts[0], parts[1])
            mixed = within + ch[5:6, lanes] * x_pair.astype(F32)
            mixed_ref[i, span, lanes] = mixed.astype(BF16)
    gated = mixed_ref[i].astype(F32) * (gate * sigmoid(gate))
    square = jnp.sum(gated * gated, axis=-1, keepdims=True)
    scaled = gated * ch[6:7]
    out_ref[i, :, :width] = dot(scaled.astype(BF16), wo_ref[...]).astype(BF16)
    if sel is None:
        sums_ref[i] = jnp.broadcast_to(square, sums_ref.shape[1:])
        return
    out_ref[i, :, width:] = split_three(square)
    if h_ref is not None:
        grad_no = dot_nt(h_ref[i], wo_ref[...])
        cross = jnp.sum(grad_no * scaled, axis=-1, keepdims=True)
        lane_ids = lax.broadcasted_iota(jnp.int32, (length, LANES), 1)
        both = jnp.where(lane_ids == 0, square, jnp.where(lane_ids == 1, cross, 0.0))
        sums_ref[i] = both.T[:8]


def backward_kernel(heads, *refs):
    h_ref, aux_ref, *refs = refs
    saved, (w_ref, wo_ref), params, outs, sum_refs, scratch = take(refs, (5, 2, 4, 3, 3, 4))
    params = load_params(params)
    aux = aux_ref[0, :, 0:1], aux_ref[0, :, 1:2]
    sums = backward_rows(heads, params, 0, h_ref, aux, saved, w_ref, wo_ref, outs, scratch)
    for ref, value in zip(sum_refs, sums):

        @pl.when(pl.program_id(0) == 0)
        def _(ref=ref, value=value):
            ref[...] = value

        @pl.when(pl.program_id(0) > 0)
        def _(ref=ref, value=value):
            ref[...] += value


def aux_of_columns(h_ref, i, width):
    aux = h_ref[i, :, width:].astype(F32)
    return aux[:, 0:1] + aux[:, 1:2] + aux[:, 2:3], aux[:, 3:4] + aux[:, 4:5] + aux[:, 5:6]


def aux_of_rows(sums):
    aux = jnp.concatenate([sums, jnp.zeros((LANES - 8, sums.shape[1]), F32)], axis=0).T
    scale = lax.rsqrt(aux[:, 0:1] * (1.0 / INNER) + NORM_EPS)
    return scale, aux[:, 1:2] * scale


def backward_rows(heads, params, i, h_ref, aux, saved, w_ref, wo_ref, outs, scratch):
    _, ch, bc, dtp, sel = params
    gate_ref, xraw_ref, bcraw_ref, dtraw_ref, mixed_ref = saved
    dn_ref, pg_ref, no_ref = outs
    dmix_s, dx_s, dbc_s, ddt_s = scratch
    length, width = dn_ref.shape[1:]
    wide = ch.shape[1]
    blocks = length // SPAN
    h_rows = h_ref[i, :, :width]
    scale, rdot = aux
    gate = gate_ref[i]
    mixed = mixed_ref[i].astype(F32)
    sig = sigmoid(gate)
    silu = gate * sig
    gated = mixed * silu
    gain = ch[6:7]
    grad_no = dot_nt(h_rows, wo_ref[...])
    grad_g = scale * (gain * grad_no) - gated * (scale * scale * (1.0 / INNER) * rdot)
    scaled = gated * scale
    no_ref[i] = (scaled * gain).astype(BF16)
    gain_row = jnp.sum(grad_no * scaled, axis=0, keepdims=True)
    dmix_s[...] = (grad_g * silu).astype(BF16)
    pg_ref[i, :, :wide] = (grad_g * mixed * (sig * (1.0 + gate * (1.0 - sig)))).astype(BF16)

    x_raw = xraw_ref[i].astype(F32)
    bc_raw = bcraw_ref[i].astype(F32)
    conv_x = conv_sum(x_raw, ch)
    sig_x = sigmoid(conv_x)
    act_x = (conv_x * sig_x).astype(BF16)
    conv_bc = conv_sum(bc_raw, bc)
    sig_bc = sigmoid(conv_bc)
    act_bc = (conv_bc * sig_bc).astype(BF16)
    step, slope = step_sizes(dtraw_ref[i].astype(F32), dtp[0:1])
    rate = jnp.exp(dtp[1:2])
    causal = triangles()
    ones = causal.astype(F32)
    lower = low_half()
    lane_ids = lax.broadcasted_iota(jnp.int32, (SPAN, LANES), 1)
    last_row = lax.broadcasted_iota(jnp.int32, (SPAN, 1), 0) == SPAN - 1
    decays = []
    for b in range(blocks):
        decays.append(-dot(ones, rate * step[b * SPAN : (b + 1) * SPAN], precision=HIGHEST))
    entering = [[None] * heads for _ in range(blocks)]
    for b in range(blocks - 1):
        span = slice(b * SPAN, (b + 1) * SPAN)
        b_in = act_bc[span, :STATE].astype(F32)
        for h in range(heads):
            lanes = slice(h // 2 * LANES, h // 2 * LANES + LANES)
            column = decays[b][:, h : h + 1]
            last = column[SPAN - 1 :]
            tail = jnp.exp(last - column) * step[span, h : h + 1]
            fresh = dot_tn((b_in * tail).astype(BF16), act_x[span, lanes])
            if entering[b][h] is not None:
                fresh += jnp.exp(last) * entering[b][h]
            entering[b + 1][h] = fresh
    leaving = [None] * heads
    rate_row = jnp.zeros((1, LANES), F32)
    for b in reversed(range(blocks)):
        span = slice(b * SPAN, (b + 1) * SPAN)
        step_b, decay = step[span], decays[b]
        decay_t, step_t = decay.T, step_b.T
        b_in, c_out = act_bc[span, :STATE], act_bc[span, STATE:]
        scores = dot_nt(c_out, b_in)
        grad_scores = jnp.zeros((SPAN, SPAN), F32)
        grad_b = jnp.zeros((SPAN, STATE), F32)
        grad_c = jnp.zeros((SPAN, STATE), F32)
        row_sums = jnp.zeros((SPAN, LANES), F32)
        grad_step = jnp.zeros((SPAN, LANES), F32)
        col_rows = []
        for first in range(0, heads, 2):
            lanes = slice(first * HEADDIM, first * HEADDIM + LANES)
            x_pair = act_x[span, lanes]
            grad_pair = dmix_s[span, lanes]
            parts = []
            for h in range(first, min(first + 2, heads)):
                own = head_lanes(h)
                grad_own = jnp.where(own, grad_pair, jnp.zeros((), BF16))
                column = decay[:, h : h + 1]
                mask = jnp.exp(jnp.where(causal, column - decay_t[h : h + 1], -1e30))
                spread = mask * step_t[h : h + 1]
                weights = (scores * spread).astype(BF16)
                part = dot_tn(weights, grad_pair)
                grad_w = dot_nt(grad_own, x_pair)
                grad_scores += grad_w * spread
                pulled = grad_w * (scores * mask)
                col_rows.append(jnp.sum(pulled, axis=0, keepdims=True))
                row_sum = jnp.sum(pulled * step_t[h : h + 1], axis=1, keepdims=True)
                if entering[b][h] is not None:
                    carry = entering[b][h].astype(BF16)
                    grown = jnp.exp(column)
                    grad_grown = grad_own.astype(F32) * grown
                    grad_c += dot_nt(grad_grown.astype(BF16), carry)
                    grad_carry = dot_tn(c_out, grad_grown.astype(BF16))
                    row_sum += jnp.sum(grad_grown * dot(c_out, carry), axis=1, keepdims=True)
                else:
                    grad_carry = None
                if leaving[h] is not None:
                    last = column[SPAN - 1 :]
                    fade = jnp.exp(last - column)
                    tail = fade * step_b[:, h : h + 1]
                    b_wide = b_in.astype(F32)
                    grad_state = leaving[h].astype(BF16)
                    grad_shaped = dot_nt(x_pair, grad_state)
                    part += dot((b_wide * tail).astype(BF16), grad_state)
                    grad_b += grad_shaped * tail
                    grad_tail = jnp.sum(grad_shaped * b_wide, axis=1, keepdims=True)
                    grad_step += jnp.where(lane_ids == h, grad_tail * fade, 0.0)
                    moved = grad_tail * tail
                    total = jnp.sum(moved, axis=0, keepdims=True)
                    if entering[b][h] is not None:
                        faded = jnp.exp(last) * leaving[h]
                        kept = jnp.sum(faded * entering[b][h], axis=1, keepdims=True)
                        total += jnp.sum(kept, axis=0, keepdims=True)
                        grad_carry += faded
                    row_sum += jnp.where(last_row, total, 0.0) - moved
                leaving[h] = grad_carry
                row_sums += jnp.where(lane_ids == h, row_sum, 0.0)
                parts.append(part)
            if len(parts) == 1:
                parts.append(jnp.zeros_like(parts[0]))
            grad_x = jnp.where(lower, parts[0], parts[1])
            dx_s[span, lanes] = grad_x + ch[5:6, lanes] * grad_pair.astype(F32)
        col_sums = stacked(col_rows, LANES).T
        low_scores = grad_scores.astype(BF16)
        dbc_s[span, :STATE] = grad_b + dot_tn(low_scores, c_out)
        dbc_s[span, STATE:] = grad_c + dot(low_scores, b_in)
        grad_decay = dot(
            ones, row_sums - step_b * col_sums, ((0,), (0,)), precision=HIGHEST
        )
        ddt_s[span] = col_sums + grad_step - rate * grad_decay
        rate_row -= jnp.sum(grad_decay * step_b, axis=0, keepdims=True)

    skip_row = jnp.sum(dmix_s[...].astype(F32) * act_x.astype(F32), axis=0, keepdims=True)
    grad_conv = dx_s[...] * (sig_x * (1.0 + conv_x * (1.0 - sig_x)))
    grad_raw, ch_rows = conv_back(grad_conv, x_raw, ch)
    pg_ref[i, :, wide : 2 * wide] = grad_raw.astype(BF16)
    grad_conv = dbc_s[...] * (sig_bc * (1.0 + conv_bc * (1.0 - sig_bc)))
    grad_raw, bc_rows = conv_back(grad_conv, bc_raw, bc)
    pg_ref[i, :, 2 * wide : 2 * wide + SHARED] = grad_raw.astype(BF16)
    grad_dt = ddt_s[...] * slope
    low_dt = grad_dt.astype(BF16)
    if sel is not None:
        low_dt = dot_nt(low_dt, sel).astype(BF16)
    pg_ref[i, :, 2 * wide + SHARED :] = low_dt
    dn_ref[i] = dot(pg_ref[i], w_ref[...]).astype(BF16)
    by_channel = stacked(ch_rows + [skip_row, gain_row], 8)
    by_shared = stacked(bc_rows, 8)
    by_head = stacked([jnp.sum(grad_dt, axis=0, keepdims=True), rate_row * rate], 8)
    if sel is not None:
        by_head = lax.dot_general(
            by_head, sel.astype(F32), (((1,), (1,)), ((), ())),
            preferred_element_type=F32, precision=HIGHEST,
        )
    return by_channel, by_shared, by_head


def add_small(small, by_channel, by_shared, by_head):
    for j in range(2):
        part = by_channel[:, j * THIRD : (j + 1) * THIRD]
        small[:, j * PIECE : j * PIECE + THIRD] += part
    small[:, 2 * PIECE : 3 * PIECE] += by_shared
    small[7:8, 2 * PIECE : 2 * PIECE + HEADS] += by_head[0:1]
    small[7:8, 2 * PIECE + LANES : 2 * PIECE + LANES + HEADS] += by_head[1:2]


def add_gain(small, row):
    for r in range(8):
        small[r : r + 1, 3 * PIECE : 3 * PIECE + THIRD] = row[:, r * THIRD : (r + 1) * THIRD]


def whole_spec(array):
    return pl.BlockSpec(array.shape, lambda i: (0,) * array.ndim)


def row_spec(length, width):
    return pl.BlockSpec((1, length, width), lambda i: (i, 0, 0))


def block_spec(array):
    return pl.BlockSpec((1,) + array.shape[1:], lambda i: (i, 0, 0))


PARAMS = dict(vmem_limit_bytes=60 * 1024 * 1024)


def run_forward(heads, wide, rows, w, wo, params):
    count, length, width = rows.shape
    constants = [w, wo, *params]
    outs = [
        (width, BF16), (LANES, F32), (width, BF16), (wide, F32),
        (wide, BF16), (SHARED, BF16), (LANES, BF16), (wide, BF16),
    ]
    return pl.pallas_call(
        partial(forward_kernel, heads),
        grid=(count,),
        out_shape=[jax.ShapeDtypeStruct((count, length, n), t) for n, t in outs],
        in_specs=[block_spec(rows)] + [whole_spec(c) for c in constants],
        out_specs=[row_spec(length, n) for n, _ in outs],
        compiler_params=pltpu.CompilerParams(**PARAMS),
        name="forward",
    )(rows, *constants)


def run_backward(heads, wide, grad_rows, aux, saved, w, wo, params):
    count, length, _ = grad_rows.shape
    columns, width = w.shape
    given = [grad_rows, aux, *saved]
    constants = [w, wo, *params]
    outs = [(width, BF16), (columns, BF16), (wide, BF16)]
    sums = [(8, wide), (8, SHARED), (8, LANES)]
    return pl.pallas_call(
        partial(backward_kernel, heads),
        grid=(count,),
        out_shape=[jax.ShapeDtypeStruct((count, length, n), t) for n, t in outs]
        + [jax.ShapeDtypeStruct(s, F32) for s in sums],
        in_specs=[block_spec(g) for g in given] + [whole_spec(c) for c in constants],
        out_specs=[row_spec(length, n) for n, _ in outs]
        + [pl.BlockSpec(s, lambda i: (0, 0)) for s in sums],
        scratch_shapes=backward_scratch(length, wide),
        compiler_params=pltpu.CompilerParams(**PARAMS),
        name="backward",
    )(*given, *constants)


def backward_scratch(length, wide):
    return [
        pltpu.VMEM((length, wide), BF16),
        pltpu.VMEM((length, wide), F32),
        pltpu.VMEM((length, SHARED), F32),
        pltpu.VMEM((length, LANES), F32),
    ]


class Plan:
    def __init__(self, seq, fsdp):
        self.seq, self.fsdp = seq, fsdp
        halves = 2
        if fsdp % 2 or HEADS % (seq * 2) or (HEADS // fsdp) % seq:
            halves = 1
        self.halves, self.mates = halves, fsdp // halves
        self.heads = HEADS // (seq * halves)
        self.pieces = self.mates if (HEADS // fsdp) % seq == 0 else 1
        channels = self.heads * HEADDIM
        self.channels = channels
        self.wide = -(-channels // LANES) * LANES
        self.peer_groups = [[lo + self.mates * h for h in range(halves)] for lo in range(self.mates)]
        self.mate_groups = [[h * self.mates + j for j in range(self.mates)] for h in range(halves)]

    def split(self, array, axis):
        size = array.shape[axis] // (self.halves * self.pieces * self.seq)
        shape = array.shape[:axis] + (self.halves, self.pieces, self.seq, size) + array.shape[axis + 1 :]
        return array.reshape(shape)

    def take(self, array, axis, place):
        array = lax.dynamic_index_in_dim(self.split(array, axis), place, axis + 2, False)
        shape = array.shape[: axis + 1] + (-1,) + array.shape[axis + 3 :]
        return jnp.moveaxis(array.reshape(shape), axis, 0)

    def put(self, parts, axis):
        size = parts.shape[axis + 2] // self.pieces
        shape = parts.shape[: axis + 2] + (self.pieces, size) + parts.shape[axis + 3 :]
        parts = jnp.moveaxis(parts.reshape(shape), (1, axis + 2, 0), (axis, axis + 1, axis + 2))
        shape = parts.shape[:axis] + (-1,) + parts.shape[axis + 4 :]
        return parts.reshape(shape)


def widened(array, axis, size):
    pads = [(0, 0)] * array.ndim
    pads[axis] = (0, size - array.shape[axis])
    return jnp.pad(array, pads)


MESH = pl.DeviceIdType.MESH
ANY = pl.BlockSpec(memory_space=pl.ANY)
VMEM = pl.BlockSpec(memory_space=pltpu.VMEM)
DMA = pltpu.SemaphoreType.DMA


class Spot:
    def __init__(self):
        self.s, self.q, self.z = (lax.axis_index(a) for a in ("section", "seq", "fsdp"))
        self.half, self.lo = self.z // 2, self.z % 2
        self.mate, self.twin = self.z + 1 - 2 * self.lo, (self.z + 2) % 4
        self.around = [None, self.q + 1 - 2 * (self.q % 2), (self.q + 2) % 4, 3 - self.q]
        self.sibling = (1 - self.s, self.q, self.z)
        self.at_mate, self.at_twin = (self.s, self.q, self.mate), (self.s, self.q, self.twin)

    def plane(self, k):
        return (self.s, self.around[k], self.z)

    def column(self, z):
        return (self.s, self.q, z)

    def piece(self, half, j):
        return 8 * half + 4 * j + self.q


def greet(places):
    barrier = pltpu.get_barrier_semaphore()
    for place in places:
        pl.semaphore_signal(barrier, inc=1, device_id=place, device_id_type=MESH)
    pl.semaphore_wait(barrier, len(places))


def remote(src, dst, send_sem, recv_sem, place):
    return pltpu.make_async_remote_copy(
        src_ref=src, dst_ref=dst, send_sem=send_sem, recv_sem=recv_sem, device_id=place, device_id_type=MESH
    )


class Home:
    def __init__(self, src, buffer, dst, sems):
        self.load = pltpu.make_async_copy(src, buffer, sems[0])
        self.store = pltpu.make_async_copy(buffer, dst, sems[1])

    def begin(self):
        self.load.start()

    def go_on(self):
        self.load.wait()
        self.store.start()

    def end(self):
        self.store.wait()


class Spread:
    SEMS = [DMA((7,)), DMA((7,)), DMA]

    def __init__(self, spot, own, all_rows, sems):
        self.spot, self.own, self.all = spot, own, all_rows
        self.send, self.recv, self.local = sems

    def slot(self, half):
        rows = self.own.shape[0]
        return self.all.at[half, pl.ds(pl.multiple_of(self.spot.q * rows, rows), rows)]

    def copy(self, j):
        spot = self.spot
        slot = self.slot(spot.half)
        if j == 3:
            return remote(self.own, slot, self.send.at[3], self.recv.at[3], spot.at_twin)
        if j < 3:
            return remote(self.own, slot, self.send.at[j], self.recv.at[j], spot.plane(j + 1))
        slot = self.slot(1 - spot.half)
        return remote(slot, slot, self.send.at[j], self.recv.at[j], spot.plane(j - 3))

    def here(self):
        return pltpu.make_async_copy(self.own, self.slot(self.spot.half), self.local)

    def start(self):
        for j in (3, 0, 1, 2):
            self.copy(j).start()
        self.here().start()

    def forward(self):
        self.copy(3).wait_recv()
        for j in (4, 5, 6):
            self.copy(j).start()

    def own_half(self):
        for j in (0, 1, 2):
            self.copy(j).wait_recv()
        self.here().wait()

    def other_half(self):
        for j in (4, 5, 6):
            self.copy(j).wait_recv()

    def close(self):
        for j in range(7):
            self.copy(j).wait_send()

    def finish(self):
        self.own_half()
        self.other_half()
        self.close()


class Sum:
    @staticmethod
    def scratch(rows, columns):
        return [
            pltpu.VMEM((2, 4 * rows, columns), BF16),
            pltpu.VMEM((3, 2, rows, columns), BF16),
            pltpu.VMEM((2, rows, columns), BF16),
            DMA((7,)),
            DMA((7,)),
        ]

    def __init__(self, spot, width, scratch):
        self.spot, self.width = spot, width
        self.parts, self.recv_rows, self.twin_rows, self.send, self.recv = scratch
        self.rows = self.twin_rows.shape[1]

    def half(self, i):
        return 1 - self.spot.half + i * (2 * self.spot.half - 1)

    def block(self, q):
        return pl.ds(pl.multiple_of(q * self.rows, self.rows), self.rows)

    def copy(self, k, i):
        spot = self.spot
        j = 3 * i + k - 1
        return remote(
            self.parts.at[self.half(i), self.block(spot.around[k])], self.recv_rows.at[k - 1, i],
            self.send.at[j], self.recv.at[j], spot.plane(k),
        )

    def across(self):
        return remote(
            self.twin_rows.at[0], self.twin_rows.at[1], self.send.at[6], self.recv.at[6], self.spot.at_twin
        )

    def start(self, i):
        for k in (1, 2, 3):
            self.copy(k, i).start()

    def plane_total(self, i):
        total = self.parts[self.half(i), self.block(self.spot.q), :].astype(F32)
        for k in (1, 2, 3):
            self.copy(k, i).wait_recv()
            total += self.recv_rows[k - 1, i].astype(F32)
        return total

    def forward(self):
        total = self.plane_total(0)
        width = self.width
        self.twin_rows[0, :, :width] = total[:, :width].astype(BF16)
        if total.shape[1] > width:
            column = jnp.sum(total[:, width:], axis=1, keepdims=True)
            self.twin_rows[0, :, width:] = split_three(column)
        self.across().start()

    def finish(self):
        total = self.plane_total(1)
        self.across().wait_recv()
        total += self.twin_rows[1].astype(F32)
        return total

    def close(self):
        for i in range(2):
            for k in (1, 2, 3):
                self.copy(k, i).wait_send()
        self.across().wait_send()


def tile_parts(spot, half):
    parts = []
    for part in range(2):
        for j in range(2):
            at = part * INNER + THIRD * spot.piece(half, j)
            parts.append((pl.multiple_of(at, 64), (2 * part + j) * THIRD, THIRD))
    return parts + [(2 * INNER, 4 * THIRD, SHARED + HEADS)]


class Weights:
    PARTS = 5

    @staticmethod
    def scratch(columns, shard, width):
        buffers = [pltpu.VMEM((columns, shard), BF16), pltpu.VMEM((THIRD, width), BF16)]
        return buffers + [DMA((4,)), DMA((43,)), DMA((43,))]

    def __init__(self, spot, layer, w_in, w_out, tile, tile_out, scratch):
        self.spot, self.layer = spot, layer
        self.w_in, self.w_out, self.tile, self.tile_out = w_in, w_out, tile, tile_out
        self.buffer, self.out_buffer, self.local, self.send, self.recv = scratch
        self.shard = w_in.shape[1]
        self.others = 2 * (1 - spot.half)
        self.gateway = 2 - spot.half
        self.is_gateway = (spot.z == 1) | (spot.z == 2)

    def at_source(self, step):
        pl.when(self.spot.s == self.layer)(step)

    def source(self, half, n):
        first, _, size = tile_parts(self.spot, half)[n]
        return self.w_in.at[pl.ds(first, size)]

    def target(self, z, n):
        _, first, size = tile_parts(self.spot, 0)[n]
        columns = pl.ds(pl.multiple_of(z * self.shard, LANES), self.shard)
        return self.tile.at[pl.ds(first, size), columns]

    def load(self, n):
        part = self.buffer.at[pl.ds(*tile_parts(self.spot, 0)[n][1:])]
        return pltpu.make_async_copy(self.source(self.spot.half, n), part, self.send.at[n])

    def store(self):
        columns = pl.ds(pl.multiple_of(self.spot.z * self.shard, LANES), self.shard)
        return pltpu.make_async_copy(self.buffer, self.tile.at[:, columns], self.local.at[0])

    def out_home(self):
        return Home(
            self.out_source(), self.out_buffer, self.out_part(self.spot.lo),
            (self.local.at[1], self.local.at[2]),
        )

    def to_mate(self, n):
        source, target = self.source(self.spot.half, n), self.target(self.spot.z, n)
        return remote(source, target, self.send.at[n], self.recv.at[n], self.spot.at_mate)

    def to_gateway(self, n):
        source, target = self.source(1 - self.spot.half, n), self.target(self.spot.z, n)
        j = 5 + 5 * self.spot.lo + n
        return remote(source, target, self.send.at[5 + n], self.recv.at[j], self.spot.column(self.gateway))

    def passed(self, c, n):
        part = self.target(self.others + c, n)
        j = 5 * c + n
        return remote(part, part, self.send.at[10 + j], self.recv.at[5 + j], self.spot.at_mate)

    def to_sibling(self, b, n):
        j = 20 + 5 * b + n
        part = self.target([self.spot.z, self.spot.mate, self.others, self.others + 1][b], n)
        source = self.source(self.spot.half, n) if b == 0 else part
        return remote(source, part, self.send.at[j], self.recv.at[j], self.spot.sibling)

    def out_part(self, lo):
        return self.tile_out.at[pl.ds(pl.multiple_of(lo * THIRD, 64), THIRD)]

    def out_source(self):
        return self.w_out.at[pl.ds(pl.multiple_of(self.spot.q * THIRD, 64), THIRD)]

    def out_to(self, n):
        part = self.out_part(self.spot.lo if n < 2 else 1 - self.spot.lo)
        place = self.spot.sibling if n else self.spot.at_mate
        source = self.out_source() if n < 2 else part
        return remote(source, part, self.send.at[40 + n], self.recv.at[40 + n], place)

    def send_part(self, n):
        if n < self.PARTS:
            self.to_gateway(n).start()
            self.to_mate(n).start()
        elif n == self.PARTS:
            self.out_to(0).start()

    def begin(self):
        @self.at_source
        def _():
            for n in range(self.PARTS):
                self.load(n).start()
            self.out_home().begin()

    def start(self):
        @self.at_source
        def _():
            for n in range(self.PARTS):
                self.load(n).wait()
            for n in range(self.PARTS):
                self.to_gateway(n).start()
                self.to_mate(n).start()
            self.out_to(0).start()
            for n in range(self.PARTS):
                self.to_sibling(0, n).start()
            self.out_to(1).start()
            self.store().start()
            self.out_home().go_on()

    def step(self, n):
        @self.at_source
        def _():
            for b in range(2):
                self.passed(b, n).wait_recv()
                pl.when(self.is_gateway)(lambda b=b: self.passed(b, n).start())
                self.to_sibling(2 + b, n).start()
            self.to_mate(n).wait_recv()
            self.to_sibling(1, n).start()

    def finish(self):
        @self.at_source
        def _():
            self.out_to(0).wait_recv()
            self.out_to(2).start()
            for n in range(self.PARTS):
                self.to_gateway(n).wait_send()
                self.to_mate(n).wait_send()
                for c in range(2):
                    pl.when(self.is_gateway)(lambda c=c, n=n: self.passed(c, n).wait_send())
                for b in range(4):
                    self.to_sibling(b, n).wait_send()
            self.store().wait()
            self.out_home().end()
            for n in range(3):
                self.out_to(n).wait_send()

        @pl.when(self.spot.s != self.layer)
        def _():
            for b in range(4):
                for n in range(self.PARTS):
                    self.to_sibling(b, n).wait_recv()
            for n in (1, 2):
                self.out_to(n).wait_recv()


def all_places(spot):
    places = [spot.plane(k) for k in (1, 2, 3)]
    places += [spot.column((spot.z + k) % 4) for k in (1, 2, 3)]
    return places + [spot.sibling]


def open_kernel(*refs):
    ins, outs, weight_s, spread_a, spread_b, (own_tokens, own_cot, own_pack, load, *pack_sems) = take(
        refs, (11, 5, 5, 3, 3, 7)
    )
    w_in, w_out, tokens, cotangent, *raw = ins
    tile, tile_out, packs, all_tokens, all_cot = outs
    spot = Spot()
    weights = Weights(spot, 0, w_in, w_out, tile, tile_out, weight_s)
    rows = Spread(spot, own_tokens, all_tokens, spread_a)
    grads = Spread(spot, own_cot, all_cot, spread_b)
    loads = [
        pltpu.make_async_copy(src, dst, load.at[n])
        for n, (src, dst) in enumerate(
            ((tokens.at[spot.s], own_tokens), (cotangent.at[spot.s], own_cot))
        )
    ]
    pack_here = pltpu.make_async_copy(own_pack, packs.at[spot.s], pack_sems[0])
    pack_there = remote(own_pack, packs.at[spot.s], pack_sems[1], pack_sems[2], spot.sibling)
    for copy in loads:
        copy.start()
    weights.begin()
    greet(all_places(spot))
    for copy in loads:
        copy.wait()
    rows.start()
    weights.start()
    pack_params(own_pack, *raw)
    pack_here.start()
    pack_there.start()
    rows.forward()
    grads.start()
    weights.step(0)
    weights.step(1)
    weights.step(2)
    grads.forward()
    weights.step(3)
    weights.step(4)
    rows.finish()
    grads.finish()
    weights.finish()
    pack_here.wait()
    pack_there.wait()


def pack_params(pack, conv_weight, conv_bias, gate_gain, skip_gain, norm_gain, dt_bias, a_log):
    pack[...] = jnp.zeros_like(pack)
    for p in range(INNER // THIRD):
        source, target = slice(p * THIRD, (p + 1) * THIRD), slice(p * PIECE, p * PIECE + THIRD)
        pack[0:CONV, target] = conv_weight[:, source]
        pack[CONV : CONV + 1, target] = conv_bias[:, source]
        skips = [jnp.broadcast_to(skip_gain[:, 3 * p + h : 3 * p + h + 1], (1, HEADDIM)) for h in range(3)]
        pack[5:6, target] = jnp.concatenate(skips, axis=1)
        pack[6:7, target] = gate_gain[:, source]
    pack[0:CONV, -SHARED:] = conv_weight[:, INNER:]
    pack[CONV : CONV + 1, -SHARED:] = conv_bias[:, INNER:]
    pack[7:8, :GAIN_END] = norm_gain[...]
    pack[7:8, DT_AT : DT_AT + HEADS] = dt_bias[...]
    pack[7:8, RATE_AT : RATE_AT + HEADS] = a_log[...]


def layer_rows(total, rows_in, branch, scales, rows_out):
    width = rows_in.shape[1]
    square = jnp.sum(total[:, width:], axis=1, keepdims=True)
    scale = lax.rsqrt(square * (1.0 / INNER) + NORM_EPS)
    part = total[:, :width] * scale
    rows_out[...] = (rows_in[...].astype(F32) + part).astype(BF16)
    if branch is not None:
        branch[...] = part
        scales[...] = jnp.broadcast_to(scale, scales.shape)


def norm_back(total, rows_in, gain, grad_out):
    rows = rows_in[...].astype(F32)
    scale = lax.rsqrt(jnp.mean(rows * rows, axis=-1, keepdims=True) + NORM_EPS)
    scaled = rows * scale
    pulled = total * gain
    inner = jnp.mean(pulled * scaled, axis=-1, keepdims=True)
    grad = scale * (pulled - scaled * inner) + grad_out[...].astype(F32)
    return grad, jnp.sum(total * scaled, axis=0, keepdims=True)


def add_rows(target, sources, chunk=64):
    @pl.loop(0, target.shape[0] // chunk)
    def _(n):
        rows = pl.ds(pl.multiple_of(n * chunk, chunk), chunk)
        total = sources[0][rows, :].astype(F32)
        for source in sources[1:]:
            total += source[rows, :].astype(F32)
        target[rows, :] = total.astype(target.dtype)


class Grads:
    ORDER = (4, 0, 1, 2, 3, 5)

    @staticmethod
    def scratch(shard, columns, wide, width):
        return [
            pltpu.VMEM((3, columns, width), BF16),
            pltpu.VMEM((3, wide, width), BF16),
            pltpu.VMEM((2, columns, shard), BF16),
            pltpu.VMEM((2, columns, shard), BF16),
            pltpu.VMEM((THIRD, width), BF16),
            DMA((22,)),
            DMA((27,)),
        ]

    @staticmethod
    def results(shard, width):
        return [((2, 4 * THIRD, shard), BF16), ((SHARED + HEADS, shard), BF16), ((THIRD, width), BF16)]

    def __init__(self, spot, results, scratch):
        self.spot = spot
        self.reduced, self.shared, self.out = results
        self.cores, self.cores_out, self.planes, self.relay, self.mate_out, self.send, self.recv = scratch
        self.shard = self.planes.shape[2]
        self.others = 2 * (1 - spot.half)
        self.is_gateway = (spot.z == 1) | (spot.z == 2)

    def rows(self, n):
        _, first, size = tile_parts(self.spot, 0)[n]
        return pl.ds(first, size)

    def columns(self, z):
        return pl.ds(pl.multiple_of(z * self.shard, LANES), self.shard)

    def core_copy(self, n):
        buffer, rows = (self.cores_out, pl.ds(0, self.cores_out.shape[1])) if n == 5 else (self.cores, self.rows(n))
        return remote(
            buffer.at[2, rows], buffer.at[1, rows], self.send.at[n], self.recv.at[n], self.spot.sibling
        )

    def product(self, layer, n, proj_grad, normed, normed_out, h_rows):
        def flat(value):
            return value.reshape(-1, value.shape[-1])

        width = self.cores.shape[2]
        slot = 2 * (self.spot.s - layer) * (self.spot.s - layer)
        if n == 5:
            total = dot_tn(flat(normed_out[...]), flat(h_rows[:, :, :width]))
            self.cores_out[slot] = total.astype(BF16)
        else:
            _, first, size = tile_parts(self.spot, 0)[n]
            total = dot_tn(flat(proj_grad[:, :, first : first + size]), flat(normed[...]))
            self.cores[slot, first : first + size, :] = total.astype(BF16)
        pl.when(self.spot.s != layer)(lambda: self.core_copy(n).start())

    def far_part(self, c, n):
        return self.cores.at[0, self.rows(n), self.columns(self.others + c)]

    def to_mate(self, n):
        source = self.cores.at[0, self.rows(n), self.columns(self.spot.mate)]
        target = self.planes.at[1, self.rows(n)]
        return remote(source, target, self.send.at[6 + n], self.recv.at[11 + n], self.spot.at_mate)

    def to_relay(self, c, n):
        j = 2 * n + c
        target = self.relay.at[c, self.rows(n)]
        return remote(
            self.far_part(c, n), target, self.send.at[11 + j], self.recv.at[16 + j], self.spot.at_mate
        )

    def to_far(self, c, n):
        target = self.planes.at[0, self.rows(n)]
        place = self.spot.column(self.others + c)
        return remote(
            self.far_part(c, n), target, self.send.at[11 + 2 * n + c], self.recv.at[6 + n], place
        )

    def out_rows(self, lo):
        return pl.ds(pl.multiple_of(lo * THIRD, 64), THIRD)

    def mate_copy(self):
        source = self.cores_out.at[0, self.out_rows(1 - self.spot.lo)]
        return remote(source, self.mate_out, self.send.at[21], self.recv.at[26], self.spot.at_mate)

    def sent(self, n):
        self.to_mate(n).wait_send()
        for c in range(2):
            self.to_relay(c, n).wait_send()

    def to_planes(self, n):
        self.core_copy(n).wait_recv()
        if n == 5:
            add_rows(self.cores_out.at[0], [self.cores_out.at[0], self.cores_out.at[1]])
            self.mate_copy().start()
            return
        own, sibling = self.cores.at[0, self.rows(n)], self.cores.at[1, self.rows(n)]
        add_rows(own, [own, sibling], 48 if n < 4 else 16)

        @pl.when(jnp.logical_not(self.is_gateway))
        def _():
            for c in range(2):
                self.to_relay(c, n).start()

        self.to_mate(n).start()

    def pass_on(self, n):
        @pl.when(self.is_gateway)
        def _():
            for c in range(2):
                self.to_relay(c, n).wait_recv()
                target, relay = self.far_part(c, n), self.relay.at[c, self.rows(n)]
                add_rows(target, [target, relay], 48 if n < 4 else 16)
                self.to_far(c, n).start()

    def gather(self, n):
        if n == 5:
            self.mate_copy().wait_recv()
            add_rows(self.out, [self.cores_out.at[0, self.out_rows(self.spot.lo)], self.mate_out], 48)
            return
        self.to_mate(n).wait_recv()
        self.to_far(0, n).wait_recv()
        _, first, size = tile_parts(self.spot, 0)[n]
        mine = self.columns(self.spot.z)
        chunk = 48 if n < 4 else 16

        @pl.loop(0, size // chunk)
        def _(r):
            rows = pl.ds(pl.multiple_of(first + r * chunk, 16), chunk)
            own = self.cores[0, rows, mine].astype(F32) + self.planes[1, rows, :].astype(F32)
            other = self.planes[0, rows, :]
            if n < 4:
                self.reduced[0, rows, :] = own.astype(BF16)
                self.reduced[1, rows, :] = other
            else:
                rows = pl.ds(pl.multiple_of(r * chunk, 16), chunk)
                self.shared[rows, :] = (own + other.astype(F32)).astype(BF16)

    def finish(self):
        self.mate_copy().wait_send()
        for n in self.ORDER:
            self.core_copy(n).wait_send()


class GradsAround:
    @staticmethod
    def scratch(shard):
        return [
            pltpu.VMEM((4, SHARED + HEADS, shard), BF16),
            DMA((11,)),
            DMA((34,)),
            DMA((34,)),
        ]

    def __init__(self, spot, results, final, final_out, scratch):
        self.spot, self.final, self.final_out = spot, final, final_out
        self.reduced, self.shared, self.out = results
        self.sums, self.local, self.send, self.recv = scratch

    def region(self, k, i, n):
        q = self.spot.q if k == 0 else self.spot.around[k]
        half = self.spot.half if i == 0 else 1 - self.spot.half
        at = n // 2 * INNER + THIRD * (8 * half + 4 * (n % 2) + q)
        return self.final.at[pl.ds(pl.multiple_of(at, 64), THIRD)]

    def copy(self, k, i, n):
        source = self.reduced.at[i, pl.ds(n * THIRD, THIRD)]
        target = self.region(0, i, n)
        j = 4 * i + n
        if k == 0:
            return pltpu.make_async_copy(source, target, self.local.at[j])
        if k < 3:
            j += 8 * (k - 1)
            return remote(source, target, self.send.at[j], self.recv.at[j], self.spot.plane(k))
        source = target = self.region(1 if i == 0 else 2, i, n)
        place = self.spot.plane(2 if i == 0 else 1)
        return remote(source, target, self.send.at[16 + j], self.recv.at[16 + j], place)

    def send_part(self, n):
        for i in range(2):
            for k in (1, 2, 0):
                self.copy(k, i, n).start()

    def pass_part(self, n):
        for i in range(2):
            self.copy(1 + i, i, n).wait_recv()
            self.copy(3, i, n).start()

    def out_region(self, k, i):
        q = self.spot.q if k == 0 else self.spot.around[k]
        size = THIRD if i is None else THIRD // 2
        at = q * THIRD + (0 if i is None else i * size)
        return self.final_out.at[pl.ds(pl.multiple_of(at, 32), size)]

    def out_copy(self, k, i=None):
        target = self.out_region(0, None)
        if k == 0:
            return pltpu.make_async_copy(self.out, target, self.local.at[8])
        if k < 3:
            return remote(self.out, target, self.send.at[23 + k], self.recv.at[23 + k], self.spot.plane(k))
        part = self.out_region(1 + i, i)
        return remote(part, part, self.send.at[26 + i], self.recv.at[26 + i], self.spot.plane(2 - i))

    def send_out(self):
        for k in (1, 2, 0):
            self.out_copy(k).start()

    def pass_out(self):
        for i in range(2):
            self.out_copy(1 + i).wait_recv()
            self.out_copy(3, i).start()

    def shared_copy(self, k):
        source = self.shared if k == 1 else self.sums.at[1]
        target = self.sums.at[0 if k == 1 else 2]
        return remote(source, target, self.send.at[27 + k], self.recv.at[27 + k], self.spot.plane(k))

    def shared_home(self):
        tail = self.final.at[pl.ds(2 * INNER, SHARED + HEADS)]
        return pltpu.make_async_copy(self.sums.at[3], tail, self.local.at[9])

    def shared_step(self, n):
        if n > 0:
            self.shared_copy(n).wait_recv()
            sources = [self.shared, self.sums.at[0]] if n == 1 else [self.sums.at[1], self.sums.at[2]]
            add_rows(self.sums.at[1 if n == 1 else 3], sources, 16)
        if n < 2:
            self.shared_copy(n + 1).start()
        else:
            self.shared_home().start()

    def finish(self):
        for i in range(2):
            for n in range(4):
                self.copy(2 - i, i, n).wait_recv()
                self.copy(3, i, n).wait_recv()
                for k in (1, 2, 3):
                    self.copy(k, i, n).wait_send()
                self.copy(0, i, n).wait()
            self.out_copy(3, i).wait_recv()
            self.out_copy(3, i).wait_send()
        for k in (1, 2):
            self.out_copy(k).wait_send()
            self.shared_copy(k).wait_send()
        self.out_copy(0).wait()
        self.shared_home().wait()


class SmallSum:
    SHAPE = (8, 4 * PIECE)

    @staticmethod
    def scratch():
        return [
            pltpu.VMEM((4,) + SmallSum.SHAPE, F32),
            pltpu.VMEM((8,) + SmallSum.SHAPE, F32),
            DMA((9,)),
            DMA((9,)),
        ]

    def __init__(self, spot, scratch):
        self.spot = spot
        self.small, self.group, self.send, self.recv = scratch

    def to_sibling(self):
        return remote(
            self.small.at[0], self.small.at[1], self.send.at[0], self.recv.at[0], self.spot.sibling
        )

    def to_mate(self):
        return remote(
            self.small.at[2], self.small.at[3], self.send.at[1], self.recv.at[1], self.spot.at_mate
        )

    def to_group(self, j):
        spot = self.spot
        part = self.group.at[4 * spot.half + spot.q]
        places = [spot.plane(k) for k in (1, 2, 3)] + [spot.at_twin]
        places += [(spot.s, spot.around[k], spot.twin) for k in (1, 2, 3)]
        return remote(part, part, self.send.at[2 + j], self.recv.at[2 + j], places[j])

    def begin(self, value):
        self.small[0] = value
        self.to_sibling().start()

    def step(self, n, value=None):
        if n == 0:
            self.to_sibling().wait_recv()
            self.small[2] = value + self.small[1]
            self.to_mate().start()
        else:
            self.to_mate().wait_recv()
            self.group[4 * self.spot.half + self.spot.q] = self.small[2] + self.small[3]
            for j in range(7):
                self.to_group(j).start()

    def finish(self, out):
        for j in range(7):
            self.to_group(j).wait_recv()
        total = self.group[0, :, 2 * PIECE :]
        for n in range(1, 8):
            total += self.group[n, :, 2 * PIECE :]
        for half in range(2):
            for j in range(2):
                for q in range(4):
                    at = (8 * half + 4 * j + q) * PIECE
                    out[:, at : at + PIECE] = self.group[4 * half + q, :, j * PIECE : (j + 1) * PIECE]
        out[:, -SHARED:] = total[:, :SHARED]
        out[7:8, DT_AT : DT_AT + HEADS] = total[7:8, :HEADS]
        out[7:8, RATE_AT : RATE_AT + HEADS] = total[7:8, LANES : LANES + HEADS]
        for r in range(8):
            out[7:8, r * THIRD : (r + 1) * THIRD] = total[r : r + 1, PIECE : PIECE + THIRD]
        self.to_sibling().wait_send()
        self.to_mate().wait_send()
        for j in range(7):
            self.to_group(j).wait_send()


def loading(sources, targets, sems):
    return [pltpu.make_async_copy(a, b, sems.at[n]) for n, (a, b) in enumerate(zip(sources, targets))]


def saved_shapes(length, width, wide):
    columns = ((width, BF16), (wide, F32), (wide, BF16), (SHARED, BF16), (LANES, BF16), (wide, BF16))
    return [((2, length, n), t) for n, t in columns]


def middle_kernel(heads, *refs):
    ins, outs, kept, weight_s, sum_s, spread_s, layer_s, (store,) = take(refs, (7, 6, 6, 5, 5, 3, 11, 1))
    w_in, w_out, *layer_ins, rows_in = ins
    tile, tile_out, all_rows, branch, scales, rows_out = outs
    u, w, wo, pack, *saved, load = layer_s
    spot = Spot()
    rows_in = rows_in.at[spot.s]
    weights = Weights(spot, 1, w_in, w_out, tile, tile_out, weight_s)
    total = Sum(spot, rows_in.shape[1], sum_s)
    spread = Spread(spot, rows_out, all_rows, spread_s)
    loads = loading(layer_ins[:3] + [layer_ins[3].at[0]], layer_s[:4], load)
    for copy in loads:
        copy.start()
    weights.begin()
    greet(all_places(spot))
    weights.start()
    for copy in loads:
        copy.wait()
    params = load_params(([spot.piece(spot.half, j) for j in range(2)], pack))

    @pl.loop(0, 2)
    def _(i):
        forward_rows(heads, params, total.half(i), u, w, wo, None, [total.parts, None, *saved])
        total.start(i)

    stores = loading(saved, kept, store)
    for copy in stores:
        copy.start()
    weights.step(0)
    total.forward()
    weights.step(1)
    layer_rows(total.finish(), rows_in, branch, scales, rows_out)
    spread.start()
    weights.step(2)
    spread.forward()
    weights.step(3)
    weights.step(4)
    spread.finish()
    total.close()
    weights.finish()
    for copy in stores:
        copy.wait()


class RowSums:
    @staticmethod
    def scratch(length):
        shape = (2, 8, length)
        return [pltpu.VMEM(shape, F32), pltpu.VMEM((7,) + shape, F32), DMA((14,)), DMA((14,))]

    def __init__(self, spot, scratch):
        self.mine, self.others, self.send, self.recv = scratch
        self.places = [spot.plane(k) for k in (1, 2, 3)] + [spot.at_twin]
        self.places += [(spot.s, spot.around[k], spot.twin) for k in (1, 2, 3)]

    def copies(self, seq):
        return [
            remote(
                self.mine.at[seq], self.others.at[j, seq],
                self.send.at[2 * j + seq], self.recv.at[2 * j + seq], place,
            )
            for j, place in enumerate(self.places)
        ]

    def start(self, seq):
        for copy in self.copies(seq):
            copy.start()

    def finish(self, seq):
        total = self.mine[seq]
        for j, copy in enumerate(self.copies(seq)):
            copy.wait_recv()
            total += self.others[j, seq]
        for copy in self.copies(seq):
            copy.wait_send()
        self.mine[seq] = total


def back_kernel(heads, *refs):
    ins, outs, first_s, last_s, second_s, spread_s, row_s, back_s, layer_s, grads_s, results, around_s, own_s, rest = take(
        refs, (18, 5, 5, 5, 5, 3, 4, 6, 11, 7, 3, 4, 4, 10)
    )
    (all_rows, all_cot, packs), tiles, kept, own_ins = take(ins, (3, 4, 6, 5))
    first_rows, tokens, grad_out, branch, scales = own_ins
    home_rows, home_grads, final, final_out, small_out = outs
    u, w, wo, pack, *saved, load = layer_s
    h_rows, h_next, payload, last_rows, last_grad, first_grad, small, send, recv, local = rest
    proj_grad, normed_out, *scratch = back_s
    spot = Spot()
    tokens, grad_out = tokens.at[spot.s], grad_out.at[spot.s]
    width = first_rows.shape[1]
    total = Sum(spot, width, first_s)
    last = Sum(spot, width, last_s)
    second = Sum(spot, width, second_s)
    spread = Spread(spot, payload, h_next, spread_s)
    sums = RowSums(spot, row_s)
    grads = Grads(spot, results, grads_s)
    around = GradsAround(spot, results, final, final_out, around_s)
    own = SmallSum(spot, own_s)
    first_core, last_core = pl.when(spot.s == 0), pl.when(spot.s == 1)
    loads = loading([all_rows, *tiles[2:], packs, all_cot], [u, w, wo, pack, h_rows], load)
    reloads = loading([*tiles[:2], *kept], [w, wo, *saved], load)
    for copy in loads:
        copy.start()
    places = [spot.plane(k) for k in (1, 2, 3)] + [spot.column((spot.z + k) % 4) for k in (1, 2, 3)]
    places += [(spot.s, spot.around[k], spot.twin) for k in (1, 2, 3)] + [spot.sibling]
    greet(places)
    for copy in loads:
        copy.wait()
    ids = [spot.piece(spot.half, j) for j in range(2)]
    params = load_params((ids, pack.at[1]))

    @pl.loop(0, 2)
    def _(i):
        seq = last.half(i)
        forward_rows(heads, params, seq, u, w, wo, h_rows, [last.parts, sums.mine, *saved])
        sums.start(seq)
        pl.when(i == 0)(lambda: last.start(0))

    def backward(layer, params, total, h_ref, aux_of, order):
        small[layer] = jnp.zeros(small.shape[1:], F32)

        @pl.loop(0, 2)
        def _(n):
            i = order(n)
            seq = total.half(i)
            aux = aux_of(n, seq)
            outs = (total.parts, proj_grad, normed_out)
            parts = backward_rows(heads, params, seq, h_ref, aux, saved[1:], w, wo, outs, scratch)
            add_small(small.at[layer], *parts)
            total.start(i)

    def row_aux(n, seq):
        pl.when(n == 1)(last.forward)
        sums.finish(seq)
        return aux_of_rows(sums.mine[seq])

    def column_aux(n, seq):
        pl.when(n == 0)(spread.own_half)

        @pl.when((n == 1) & (spot.s == 1))
        def _():
            own.step(1)
            grads.to_planes(5)
            grads.pass_on(1)
            grads.gather(4)
            around.shared_step(0)

        pl.when(n == 1)(spread.other_half)
        return aux_of_columns(h_next, seq, width)

    backward(1, params, total, h_rows, row_aux, lambda n: n)

    def product(layer, n):
        grads.product(layer, n, proj_grad, saved[0], normed_out, h_rows if layer else h_next)

    product(1, 4)
    product(1, 0)
    total.forward()
    last_core(lambda: grads.to_planes(4))
    for n in (1, 2, 3, 5):
        product(1, n)
    last_core(lambda: grads.to_planes(0))
    for copy in reloads:
        copy.start()
    grad, last_gain = norm_back(total.finish(), first_rows, pack[1, 7:8, :width], grad_out)
    low = grad.astype(BF16)
    last_grad[...] = low
    cross = jnp.sum(low.astype(F32) * branch[...], axis=1, keepdims=True)
    payload[:, :width] = low
    lanes = lax.broadcasted_iota(jnp.int32, (payload.shape[0], LANES), 1)
    scale_part = split_three(scales[:, 0:1]).astype(F32)
    cross_part = pltpu.roll(split_three(cross).astype(F32), 3, 1)
    payload[:, width:] = jnp.where(lanes < 3, scale_part, cross_part).astype(BF16)
    spread.start()
    add_gain(small.at[1], last_gain)
    first_core(lambda: own.begin(small[1]))

    @last_core
    def _():
        grads.pass_on(4)
        grads.to_planes(1)

    spread.forward()

    @last_core
    def _():
        own.step(0, small[1])
        grads.pass_on(0)
        for n in (2, 3):
            grads.to_planes(n)

    last.start(1)
    for copy in reloads:
        copy.wait()
    params = load_params((ids, pack.at[0]))
    backward(0, params, second, h_next, column_aux, lambda n: 1 - n)

    @last_core
    def _():
        grads.gather(0)
        around.send_part(0)
        grads.pass_on(2)

    for n in Grads.ORDER:
        product(0, n)

    @first_core
    def _():
        for n in (4, 0, 1):
            grads.to_planes(n)
        grads.pass_on(4)
        for n in (5, 2):
            grads.to_planes(n)
        grads.pass_on(0)
        grads.gather(4)
        around.shared_step(0)
        grads.to_planes(3)
        grads.pass_on(1)
        grads.gather(0)
        around.send_part(0)

    @last_core
    def _():
        grads.gather(1)
        around.send_part(1)
        grads.pass_on(3)
        around.shared_step(1)

    second.forward()

    @first_core
    def _():
        grads.pass_on(2)
        grads.gather(5)
        around.send_out()
        grads.gather(1)
        around.send_part(1)
        around.shared_step(1)
        around.pass_part(0)
        grads.pass_on(3)

    @last_core
    def _():
        grads.gather(5)
        around.send_out()
        grads.gather(2)
        around.send_part(2)
        around.pass_part(0)
        grads.gather(3)
        around.send_part(3)
        around.pass_part(1)

    grad, first_gain = norm_back(second.finish(), tokens, pack[0, 7:8, :width], last_grad)
    first_grad[...] = grad.astype(BF16)
    layers = ((first_rows, first_grad), (last_rows, last_grad))

    def home_copies(s):
        copies = []
        for n, target in enumerate((home_rows, home_grads)):
            copies.append(remote(layers[1 - s][n], target.at[s], send.at[n], recv.at[n], spot.sibling))
            copies.append(pltpu.make_async_copy(layers[s][n], target.at[s], local.at[n]))
        return copies

    add_gain(small.at[0], first_gain)
    last_core(lambda: own.begin(small[0]))

    @first_core
    def _():
        grads.gather(2)
        around.send_part(2)
        around.pass_out()
        around.pass_part(1)
        own.step(0, small[0])
        grads.gather(3)
        around.send_part(3)
        around.shared_step(2)
        own.step(1)

    layer_rows(last.finish(), first_rows, None, None, last_rows)
    for s in range(2):

        @pl.when(spot.s == s)
        def _(s=s):
            for copy in home_copies(s):
                copy.start()

    @first_core
    def _():
        for n in (2, 3):
            around.pass_part(n)

    @last_core
    def _():
        around.shared_step(2)
        around.pass_out()
        for n in (2, 3):
            around.pass_part(n)

    own.finish(small_out)
    around.finish()
    for n in range(5):
        grads.sent(n)
    grads.finish()
    for s in range(2):

        @pl.when(spot.s == s)
        def _(s=s):
            for copy in home_copies(s):
                copy.wait()

    total.close()
    last.close()
    second.close()
    spread.close()


def comm_call(kernel, collective, ins, in_specs, outs, out_specs, scratch, name):
    return pl.pallas_call(
        kernel,
        out_shape=[jax.ShapeDtypeStruct(s, t) for s, t in outs],
        in_specs=in_specs,
        out_specs=out_specs,
        scratch_shapes=scratch,
        compiler_params=pltpu.CompilerParams(
            collective_id=collective, has_side_effects=True, vmem_limit_bytes=60 * 1024 * 1024
        ),
        name=name,
    )(*ins)


def fast_shards(
    tokens, cotangent, norm_gain, w_in, conv_weight, conv_bias, dt_bias, a_log, skip_gain, gate_gain, w_out
):
    span, width = tokens.shape[2:]
    heads = HEADS // 8
    wide = heads * HEADDIM
    columns = 2 * wide + SHARED + HEADS
    shard = w_in.shape[1]
    rows_in = w_in[0].T
    pack_shape = (8, INNER // THIRD * PIECE + SHARED)
    group = (2, 4 * span, width)
    weight_outs = [((columns, width), BF16), ((wide, width), BF16)]
    weight_s = Weights.scratch(columns, shard, width)
    payload = width + LANES
    tile, tile_out, packs, all_rows, all_cot = comm_call(
        open_kernel, 1,
        [
            rows_in, w_out[0], tokens[:, 0], cotangent[:, 0], conv_weight[0], conv_bias, gate_gain, skip_gain,
            norm_gain, dt_bias, a_log,
        ],
        [ANY] * 4 + [VMEM] * 7,
        weight_outs + [((2,) + pack_shape, F32), (group, BF16), (group, BF16)], [ANY] * 5,
        weight_s + Spread.SEMS + Spread.SEMS
        + [pltpu.VMEM((span, width), BF16)] * 2 + [pltpu.VMEM(pack_shape, F32), DMA((2,)), DMA, DMA, DMA],
        "open",
    )
    length = 4 * span
    rows_spec = ((span, width), BF16)
    layer_s = [
        pltpu.VMEM((2, length, width), BF16), pltpu.VMEM((columns, width), BF16),
        pltpu.VMEM((wide, width), BF16), pltpu.VMEM(pack_shape, F32),
    ]
    kept_shapes = saved_shapes(length, width, wide)
    kept_s = [pltpu.VMEM(*k) for k in kept_shapes]
    back_s = [pltpu.VMEM((2, length, columns), BF16), pltpu.VMEM((2, length, wide), BF16)]
    back_s += backward_scratch(length, wide)
    results = Grads.results(shard, width)
    sum_s = Sum.scratch(span, width)
    first_tiles = [tile, tile_out]
    tile, tile_out, all_rows, branch, scales, rows, *kept = comm_call(
        partial(middle_kernel, heads), 2,
        [rows_in, w_out[0], all_rows, tile, tile_out, packs, tokens[:, 0]], [ANY] * 6 + [VMEM],
        weight_outs + [(group, BF16), ((span, width), F32), ((span, LANES), F32), rows_spec] + kept_shapes,
        [ANY] * 3 + [VMEM] * 3 + [ANY] * 6,
        weight_s + Sum.scratch(span, payload) + Spread.SEMS + layer_s + kept_s + [DMA((4,)), DMA((6,))],
        "middle",
    )
    home_rows, home_grads, final, final_out, small = comm_call(
        partial(back_kernel, heads), 3,
        [
            all_rows, all_cot, packs, *first_tiles, tile, tile_out, *kept,
            rows, tokens[:, 0], cotangent[:, 0], branch, scales,
        ],
        [ANY] * 13 + [VMEM] * 5,
        [
            ((2, span, width), BF16), ((2, span, width), BF16),
            ((2 * INNER + SHARED + HEADS, shard), BF16), (w_out.shape[1:], BF16), (pack_shape, F32),
        ],
        [ANY] * 4 + [VMEM],
        sum_s + Sum.scratch(span, payload) + sum_s + Spread.SEMS + RowSums.scratch(length) + back_s
        + layer_s[:3] + [pltpu.VMEM((2,) + pack_shape, F32)] + kept_s + [DMA((8,))]
        + Grads.scratch(shard, columns, wide, width) + [pltpu.VMEM(*r) for r in results]
        + GradsAround.scratch(shard) + SmallSum.scratch()
        + [
            pltpu.VMEM((2, length, width), BF16), pltpu.VMEM((2, length, payload), BF16),
            pltpu.VMEM((span, payload), BF16), *[pltpu.VMEM((span, width), BF16)] * 3,
            pltpu.VMEM((2,) + SmallSum.SHAPE, F32), DMA((2,)), DMA((2,)), DMA((2,)),
        ],
        "back",
    )
    grad_in, grad_out, gain, conv, bias, shift, rate, skip, gate = finish_call(final, final_out, small)
    return (
        home_rows[None, :, None], home_grads[None, :, None], gain, grad_in.T[None], conv[None],
        bias, shift, rate, skip, gate, grad_out[None],
    )


def finish_kernel(final, final_out, small, grad_in, grad_out, gain, conv, bias, shift, rate, skip, gate):
    grad_in[...] = final[...].astype(F32)
    step = pl.program_id(0)
    grad_out[...] = final_out[...].astype(F32)

    @pl.when(step == 0)
    def _():
        gain[...] = small[7:8, :GAIN_END]
        shift[...] = small[7:8, DT_AT : DT_AT + HEADS]
        rate[...] = small[7:8, RATE_AT : RATE_AT + HEADS]
        heads = []
        for p in range(INNER // THIRD):
            source, target = slice(p * PIECE, p * PIECE + THIRD), slice(p * THIRD, (p + 1) * THIRD)
            conv[:, target] = small[0:CONV, source]
            bias[:, target] = small[CONV : CONV + 1, source]
            gate[:, target] = small[6:7, source]
            for h in range(3):
                part = small[5:6, p * PIECE + h * HEADDIM : p * PIECE + (h + 1) * HEADDIM]
                heads.append(jnp.sum(part, axis=1, keepdims=True))
        skip[...] = jnp.concatenate(heads, axis=1)
        conv[:, INNER:] = small[0:CONV, -SHARED:]
        bias[:, INNER:] = small[CONV : CONV + 1, -SHARED:]


def finish_call(final, final_out, small):
    rows, shard = final.shape
    out_rows, width = final_out.shape
    steps = 3
    block, out_block = -(-rows // (16 * steps)) * 16, out_rows // steps
    smalls = [(1, GAIN_END), (CONV, XBC), (1, XBC), (1, HEADS), (1, HEADS), (1, HEADS), (1, INNER)]

    def in_block(i):
        return (i, 0)

    def same(i):
        return (0, 0)

    return pl.pallas_call(
        finish_kernel,
        grid=(steps,),
        out_shape=[jax.ShapeDtypeStruct(s, F32) for s in [final.shape, final_out.shape] + smalls],
        in_specs=[
            pl.BlockSpec((block, shard), in_block),
            pl.BlockSpec((out_block, width), in_block),
            pl.BlockSpec(small.shape, same),
        ],
        out_specs=[
            pl.BlockSpec((block, shard), in_block),
            pl.BlockSpec((out_block, width), in_block),
        ]
        + [pl.BlockSpec(s, same) for s in smalls],
        compiler_params=pltpu.CompilerParams(**PARAMS),
        name="finish",
    )(final, final_out, small)


def shards(
    tokens, cotangent, norm_gain, w_in, conv_weight, conv_bias, dt_bias, a_log, skip_gain, gate_gain, w_out
):
    section = lax.axis_index("section")
    place = lax.axis_index("seq")
    depth = lax.axis_index("fsdp")
    plan = Plan(lax.axis_size("seq"), lax.axis_size("fsdp"))
    half = depth // plan.mates
    micro, _, span, width = tokens.shape
    layers = lax.axis_size("section")
    wide, channels, heads = plan.wide, plan.channels, plan.heads

    shard = w_in[0]
    gate_part = widened(plan.take(shard[:, :INNER], 1, place), 2, wide)
    x_part = widened(plan.take(shard[:, INNER : 2 * INNER], 1, place), 2, wide)
    shared_part = jnp.broadcast_to(
        shard[:, 2 * INNER : INNER + XBC], (plan.halves, shard.shape[0], SHARED)
    )
    dt_part = widened(plan.take(shard[:, INNER + XBC :], 1, place), 2, LANES)
    tile = jnp.concatenate([gate_part, x_part, shared_part, dt_part], axis=2)
    tile = jnp.repeat(tile, plan.mates, axis=0)
    tile = lax.all_to_all(tile, "fsdp", 0, 0, tiled=True).reshape(width, -1).T
    w_tiles = lax.all_gather(tile, "section", axis=0)
    if plan.pieces == plan.mates:
        piece = w_out[0].reshape(plan.seq, -1, width)
        piece = lax.dynamic_index_in_dim(piece, place, 0, False)
        rows_out = lax.all_gather(
            piece, "fsdp", axis=0, tiled=True, axis_index_groups=plan.mate_groups
        )
    else:
        rows_out = lax.all_gather(w_out[0], "fsdp", axis=0, tiled=True)
        rows_out = lax.dynamic_index_in_dim(plan.take(rows_out, 0, place), half, 0, False)
    wo_tiles = lax.all_gather(widened(rows_out, 0, wide), "section", axis=0)

    def own(array, axis, size):
        part = lax.dynamic_index_in_dim(plan.take(array, axis, place), half, 0, False)
        return widened(part, axis, size)

    skip_wide = jnp.repeat(skip_gain[0], HEADDIM)[None]
    by_channel = jnp.concatenate(
        [conv_weight[0, :, :INNER], conv_bias[:, :INNER], skip_wide, gate_gain, jnp.zeros((1, INNER))], 0
    )
    by_channel = own(by_channel, 1, wide)
    by_shared = jnp.concatenate(
        [conv_weight[0, :, INNER:], conv_bias[:, INNER:], jnp.zeros((3, SHARED))], 0
    )
    by_head = jnp.concatenate([dt_bias, a_log, jnp.zeros((6, HEADS))], 0)
    by_head = own(by_head, 1, LANES)
    smalls = jnp.concatenate(
        [by_channel.ravel(), by_shared.ravel(), by_head.ravel(), norm_gain[0]]
    )
    smalls = lax.all_gather(smalls, "section", axis=0)
    cuts = [8 * wide, 8 * (wide + SHARED), 8 * (wide + SHARED + LANES)]
    params = []
    for l in range(layers):
        ch, bc, dtp, gain = jnp.split(smalls[l], cuts)
        params.append((gain[None], ch.reshape(8, -1), bc.reshape(8, -1), dtp.reshape(8, -1)))

    def gather_rows(own_rows):
        rows = lax.all_gather(own_rows, "seq", axis=0, tiled=True)
        if plan.halves == 1:
            return rows[None]
        return lax.all_gather(rows, "fsdp", axis=0, axis_index_groups=plan.peer_groups)

    def sum_rows(parts):
        if plan.halves == 1:
            rows = parts[0]
        else:
            rows = lax.psum_scatter(
                parts, "fsdp", scatter_dimension=0, axis_index_groups=plan.peer_groups
            )
        return lax.psum_scatter(rows, "seq", scatter_dimension=0, tiled=True)

    own_tokens = lax.dynamic_index_in_dim(tokens, section, 0, False)[0]
    own_cot = lax.dynamic_index_in_dim(cotangent, section, 0, False)[0]
    inputs, outputs, branch, saved, scales = [own_tokens], [], [], [], []
    for l in range(layers):
        rows = gather_rows(inputs[l])
        parts, square, normed, *kept = run_forward(
            heads, wide, rows, w_tiles[l], wo_tiles[l], params[l]
        )
        saved.append((normed, kept))
        total = sum_rows(parts).astype(F32)
        square = sum_rows(square)[:, :1]
        scale = lax.rsqrt(square / INNER + NORM_EPS)
        branch.append(total * scale)
        scales.append(scale)
        outputs.append((inputs[l].astype(F32) + branch[l]).astype(BF16))
        inputs.append(outputs[l])
    grads_in, small_grads = [None] * layers, [None] * layers
    w_grads, wo_grads = [None] * layers, [None] * layers
    grad_rows = own_cot
    for l in reversed(range(layers)):
        rdot = jnp.sum(grad_rows.astype(F32) * branch[l], axis=-1, keepdims=True)
        aux = widened(jnp.concatenate([scales[l], rdot], axis=1), 1, LANES)
        all_grads = gather_rows(grad_rows)
        aux = gather_rows(aux)
        normed, kept = saved[l]
        parts, proj_grad, normed_out, g_ch, g_bc, g_dt = run_backward(
            heads, wide, all_grads, aux, kept, w_tiles[l], wo_tiles[l], params[l]
        )
        w_grads[l] = dot_tn(normed.reshape(-1, width), proj_grad.reshape(-1, proj_grad.shape[-1])).astype(BF16)
        wo_grads[l] = dot_tn(normed_out.reshape(-1, wide), all_grads.reshape(-1, width)).astype(BF16)
        grad_normed = sum_rows(parts).astype(F32)
        rows = inputs[l].astype(F32)
        scale = lax.rsqrt(jnp.mean(rows * rows, axis=-1, keepdims=True) + NORM_EPS)
        scaled = rows * scale
        g_gain = jnp.sum(grad_normed * scaled, axis=0)
        pulled = grad_normed * params[l][0]
        inner = jnp.mean(pulled * scaled, axis=-1, keepdims=True)
        grad = scale * (pulled - scaled * inner) + grad_rows.astype(F32)
        grad_rows = grad.astype(BF16)
        grads_in[l] = grad_rows

        def placed(value, size):
            value = value[..., :size]
            full = jnp.zeros((plan.seq, plan.halves) + value.shape, F32)
            full = lax.dynamic_update_slice(full, value[None, None], (place, half, 0, 0))
            return plan.put(full, 1)

        by_channel = placed(g_ch, channels)
        by_head = placed(g_dt, heads)
        skip = by_channel[5].reshape(HEADS, HEADDIM).sum(-1)
        small_grads[l] = jnp.concatenate(
            [
                g_gain, by_channel[:5].ravel(), g_bc[:5].ravel(), by_head[0], by_head[1], skip, by_channel[6]
            ]
        )

    smalls = lax.psum(jnp.stack(small_grads), ("section", "seq", "fsdp"))
    smalls = lax.dynamic_index_in_dim(smalls, section, 0, False)
    cuts, at = [], 0
    for size in (width, (CONV + 1) * INNER, (CONV + 1) * SHARED, HEADS, HEADS, HEADS):
        at += size
        cuts.append(at)
    g_gain, g_x, g_bc, g_shift, g_rate, g_skip, g_gate = jnp.split(smalls, cuts)
    conv_rows = jnp.concatenate([g_x.reshape(CONV + 1, -1), g_bc.reshape(CONV + 1, -1)], axis=1)

    w_grad = lax.psum_scatter(jnp.stack(w_grads), "section", scatter_dimension=0)
    w_grad = lax.all_to_all(w_grad, "fsdp", 0, 0, tiled=True)
    w_grad = w_grad.reshape(plan.halves, plan.mates, -1, w_grad.shape[-1]).astype(F32).sum(1)
    shared_grad = lax.psum(w_grad[..., 2 * wide : 2 * wide + SHARED].sum(0), "seq")
    head_grads = jnp.concatenate(
        [
            w_grad[..., :channels],
            w_grad[..., wide : wide + channels],
            w_grad[..., 2 * wide + SHARED : 2 * wide + SHARED + heads],
        ],
        axis=-1,
    ).astype(BF16)
    head_grads = lax.all_gather(head_grads, "seq", axis=0)
    grad_w_in = jnp.concatenate(
        [
            plan.put(head_grads[..., :channels], 1),
            plan.put(head_grads[..., channels : 2 * channels], 1),
            shared_grad.astype(BF16),
            plan.put(head_grads[..., 2 * channels :], 1),
        ],
        axis=-1,
    ).astype(F32)
    wo_grad = lax.psum_scatter(jnp.stack(wo_grads)[:, :channels], "section", scatter_dimension=0)
    if plan.pieces == plan.mates:
        wo_grad = lax.psum_scatter(
            wo_grad, "fsdp", scatter_dimension=0, tiled=True, axis_index_groups=plan.mate_groups
        )
        wo_grad = lax.all_gather(wo_grad, "seq", axis=0, tiled=True)
    else:
        full = jnp.zeros((plan.seq, plan.halves) + wo_grad.shape, BF16)
        full = lax.dynamic_update_slice(full, wo_grad[None, None], (place, half, 0, 0))
        full = plan.put(full, 0)
        wo_grad = lax.psum_scatter(full, "fsdp", scatter_dimension=0, tiled=True)
        wo_grad = lax.psum(wo_grad, "seq")

    def home(per_layer):
        return lax.all_to_all(jnp.stack(per_layer), "section", 0, 0, tiled=True)[None, :, None]

    return (
        home(outputs),
        home(grads_in),
        g_gain[None],
        grad_w_in[None],
        conv_rows[None, :CONV],
        conv_rows[CONV:],
        g_shift[None],
        g_rate[None],
        g_skip[None],
        g_gate[None],
        wo_grad.astype(F32)[None],
    )


def solution(mesh):
    shape = tuple(mesh.shape[a] for a in ("section", "seq", "fsdp"))
    return jax.shard_map(
        fast_shards if shape == (2, 4, 4) else shards,
        mesh=mesh,
        in_specs=(
            P(None, "fsdp", "seq", None),
            P(None, "fsdp", "seq", None),
            P("section", None),
            P("section", "fsdp", None),
            P("section", None, None),
            P("section", None),
            P("section", None),
            P("section", None),
            P("section", None),
            P("section", None),
            P("section", "fsdp", None),
        ),
        out_specs=(
            P("section", None, "fsdp", "seq", None),
            P("section", None, "fsdp", "seq", None),
            P("section", None),
            P("section", "fsdp", None),
            P("section", None, None),
            P("section", None),
            P("section", None),
            P("section", None),
            P("section", None),
            P("section", None),
            P("section", "fsdp", None),
        ),
        check_vma=False,
    )
```

```python
from functools import partial

import jax
import jax.numpy as jnp
from jax import lax
from jax.experimental import pallas as pl
from jax.experimental.pallas import tpu as pltpu
from jax.sharding import PartitionSpec as P

HEADS = 48
HEADDIM = 64
STATE = 128
CONV = 4
SPAN = 256
INNER = 3072
XBC = 3328
SHARED = 2 * STATE
LANES = 128
THIRD = 192
PIECE = 256
GAIN_END = 1536
DT_AT = 1536
RATE_AT = DT_AT + LANES
NORM_EPS = 1e-05
HIGHEST = lax.Precision.HIGHEST
BF16 = jnp.bfloat16
F32 = jnp.float32


def take(refs, counts):
    refs = list(refs)
    return [[refs.pop(0) for _ in range(n)] for n in counts]


def dot(left, right, contract=((1,), (0,)), precision=None):
    return lax.dot_general(
        left, right, (contract, ((), ())), preferred_element_type=F32, precision=precision
    )


def dot_nt(left, right):
    return dot(left, right, ((1,), (1,)))


def dot_tn(left, right):
    return dot(left, right, ((0,), (0,)))


def sigmoid(value):
    return 1.0 / (1.0 + jnp.exp(-value))


def shifted(value, distance):
    if distance == 0:
        return value
    length = value.shape[0]
    rows = lax.broadcasted_iota(jnp.int32, value.shape, 0)
    moved = pltpu.roll(value, distance % length, 0)
    if distance > 0:
        return jnp.where(rows >= distance, moved, 0.0)
    return jnp.where(rows < length + distance, moved, 0.0)


def conv_sum(raw, taps):
    total = taps[CONV : CONV + 1]
    for k in range(CONV):
        total = total + taps[k : k + 1] * shifted(raw, CONV - 1 - k)
    return total


def conv_back(grad, raw, taps):
    grad_raw = 0.0
    rows = []
    for k in range(CONV):
        grad_raw = grad_raw + taps[k : k + 1] * shifted(grad, -(CONV - 1 - k))
        rows.append(jnp.sum(grad * shifted(raw, CONV - 1 - k), axis=0, keepdims=True))
    rows.append(jnp.sum(grad, axis=0, keepdims=True))
    return grad_raw, rows


def stacked(rows, count):
    width = rows[0].shape[1]
    short = count - len(rows)
    return jnp.concatenate(rows + [jnp.zeros((short, width), F32)], axis=0)


def triangles():
    row_ids = lax.broadcasted_iota(jnp.int32, (SPAN, SPAN), 0)
    col_ids = lax.broadcasted_iota(jnp.int32, (SPAN, SPAN), 1)
    return row_ids >= col_ids


def step_sizes(dt_raw, dt_row):
    shift = dt_raw + dt_row
    step = jnp.maximum(shift, 0.0) + jnp.log1p(jnp.exp(-jnp.abs(shift)))
    return step, sigmoid(shift)


def low_half():
    return lax.broadcasted_iota(jnp.int32, (SPAN, LANES), 1) < HEADDIM


def head_lanes(h):
    lanes = lax.broadcasted_iota(jnp.int32, (1, LANES), 1)
    return (lanes < HEADDIM) if h % 2 == 0 else (lanes >= HEADDIM)


def split_three(value):
    lanes = lax.broadcasted_iota(jnp.int32, (value.shape[0], LANES), 1)
    result = jnp.zeros((value.shape[0], LANES), F32)
    for k in range(3):
        part = value.astype(BF16).astype(F32)
        result = jnp.where(lanes == k, part, result)
        value = value - part
    return result.astype(BF16)


def selection(ids):
    rows = lax.broadcasted_iota(jnp.int32, (HEADS, LANES), 0)
    columns = lax.broadcasted_iota(jnp.int32, (HEADS, LANES), 1)
    target = jnp.full((HEADS, LANES), -1, jnp.int32)
    for j in range(2):
        here = (columns >= 3 * j) & (columns < 3 * j + 3)
        target = jnp.where(here, columns + 3 * (ids[j] - j), target)
    return (rows == target).astype(F32)


def piece_lanes(ids, j):
    return pl.ds(pl.multiple_of(ids[j] * PIECE, PIECE), PIECE)


def load_params(refs):
    if len(refs) == 2:
        ids, pack_ref = refs
        sel = selection(ids)
        ch = jnp.concatenate([pack_ref[:, piece_lanes(ids, j)][:, :THIRD] for j in range(2)], axis=1)
        rows = [pack_ref[7:8, at : at + HEADS] for at in (DT_AT, RATE_AT)]
        dtp = dot(stacked(rows, 8), sel, precision=HIGHEST)
        return pack_ref[7:8, :GAIN_END], ch, pack_ref[:, -SHARED:], dtp, sel.astype(BF16)
    gain_ref, ch_ref, bc_ref, dtp_ref = refs
    return gain_ref[...], ch_ref[...], bc_ref[...], dtp_ref[...], None


def forward_kernel(heads, *refs):
    u_ref, w_ref, wo_ref, *refs = refs
    forward_rows(heads, load_params(refs[:4]), 0, u_ref, w_ref, wo_ref, None, refs[4:])


def forward_rows(heads, params, i, u_ref, w_ref, wo_ref, h_ref, outs):
    gain, ch, bc, dtp, sel = params
    out_ref, sums_ref, normed_ref, gate_ref, xraw_ref, bcraw_ref, dtraw_ref, mixed_ref = outs
    length, width = u_ref.shape[1:]
    wide = ch.shape[1]
    blocks = length // SPAN
    rows = u_ref[i].astype(F32)
    scale = lax.rsqrt(jnp.mean(rows * rows, axis=-1, keepdims=True) + NORM_EPS)
    normed = (rows * scale * gain).astype(BF16)
    normed_ref[i] = normed
    gate = dot_nt(normed, w_ref[:wide])
    gate_ref[i] = gate
    x_raw = dot_nt(normed, w_ref[wide : 2 * wide]).astype(BF16)
    xraw_ref[i] = x_raw
    rest = dot_nt(normed, w_ref[2 * wide :]).astype(BF16)
    bcraw_ref[i] = rest[:, :SHARED]
    dt_raw = rest[:, SHARED:]
    if sel is not None:
        dt_raw = dot(dt_raw, sel).astype(BF16)
    dtraw_ref[i] = dt_raw
    conv_x = conv_sum(x_raw.astype(F32), ch)
    act_x = (conv_x * sigmoid(conv_x)).astype(BF16)
    conv_bc = conv_sum(rest[:, :SHARED].astype(F32), bc)
    act_bc = (conv_bc * sigmoid(conv_bc)).astype(BF16)
    step, _ = step_sizes(dt_raw.astype(F32), dtp[0:1])
    rate = jnp.exp(dtp[1:2])
    causal = triangles()
    ones = causal.astype(F32)
    lower = low_half()
    carries = [None] * heads
    for b in range(blocks):
        span = slice(b * SPAN, (b + 1) * SPAN)
        step_b = step[span]
        decay = -dot(ones, rate * step_b, precision=HIGHEST)
        decay_t, step_t = decay.T, step_b.T
        b_in, c_out = act_bc[span, :STATE], act_bc[span, STATE:]
        scores = dot_nt(c_out, b_in)
        for first in range(0, heads, 2):
            lanes = slice(first * HEADDIM, first * HEADDIM + LANES)
            x_pair = act_x[span, lanes]
            parts = []
            for h in range(first, min(first + 2, heads)):
                gap = decay[:, h : h + 1] - decay_t[h : h + 1]
                mask = jnp.exp(jnp.where(causal, gap, -1e30))
                weights = (scores * mask * step_t[h : h + 1]).astype(BF16)
                part = dot(weights, x_pair)
                if carries[h] is not None:
                    part += jnp.exp(decay[:, h : h + 1]) * dot(c_out, carries[h].astype(BF16))
                if b + 1 < blocks:
                    last = decay[SPAN - 1 :, h : h + 1]
                    tail = jnp.exp(last - decay[:, h : h + 1]) * step_b[:, h : h + 1]
                    shaped = (b_in.astype(F32) * tail).astype(BF16)
                    fresh = dot_tn(shaped, x_pair)
                    if carries[h] is not None:
                        fresh += jnp.exp(last) * carries[h]
                    carries[h] = fresh
                parts.append(part)
            if len(parts) == 1:
                parts.append(jnp.zeros_like(parts[0]))
            within = jnp.where(lower, parts[0], parts[1])
            mixed = within + ch[5:6, lanes] * x_pair.astype(F32)
            mixed_ref[i, span, lanes] = mixed.astype(BF16)
    gated = mixed_ref[i].astype(F32) * (gate * sigmoid(gate))
    square = jnp.sum(gated * gated, axis=-1, keepdims=True)
    scaled = gated * ch[6:7]
    out_ref[i, :, :width] = dot(scaled.astype(BF16), wo_ref[...]).astype(BF16)
    if sel is None:
        sums_ref[i] = jnp.broadcast_to(square, sums_ref.shape[1:])
        return
    out_ref[i, :, width:] = split_three(square)
    if h_ref is not None:
        grad_no = dot_nt(h_ref[i], wo_ref[...])
        cross = jnp.sum(grad_no * scaled, axis=-1, keepdims=True)
        lane_ids = lax.broadcasted_iota(jnp.int32, (length, LANES), 1)
        both = jnp.where(lane_ids == 0, square, jnp.where(lane_ids == 1, cross, 0.0))
        sums_ref[i] = both.T[:8]


def backward_kernel(heads, *refs):
    h_ref, aux_ref, *refs = refs
    saved, (w_ref, wo_ref), params, outs, sum_refs, scratch = take(refs, (5, 2, 4, 3, 3, 4))
    params = load_params(params)
    aux = aux_ref[0, :, 0:1], aux_ref[0, :, 1:2]
    sums = backward_rows(heads, params, 0, h_ref, aux, saved, w_ref, wo_ref, outs, scratch)
    for ref, value in zip(sum_refs, sums):

        @pl.when(pl.program_id(0) == 0)
        def _(ref=ref, value=value):
            ref[...] = value

        @pl.when(pl.program_id(0) > 0)
        def _(ref=ref, value=value):
            ref[...] += value


def aux_of_columns(h_ref, i, width):
    aux = h_ref[i, :, width:].astype(F32)
    return aux[:, 0:1] + aux[:, 1:2] + aux[:, 2:3], aux[:, 3:4] + aux[:, 4:5] + aux[:, 5:6]


def aux_of_rows(sums):
    aux = jnp.concatenate([sums, jnp.zeros((LANES - 8, sums.shape[1]), F32)], axis=0).T
    scale = lax.rsqrt(aux[:, 0:1] * (1.0 / INNER) + NORM_EPS)
    return scale, aux[:, 1:2] * scale


def backward_rows(heads, params, i, h_ref, aux, saved, w_ref, wo_ref, outs, scratch):
    _, ch, bc, dtp, sel = params
    gate_ref, xraw_ref, bcraw_ref, dtraw_ref, mixed_ref = saved
    dn_ref, pg_ref, no_ref = outs
    dmix_s, dx_s, dbc_s, ddt_s = scratch
    length, width = dn_ref.shape[1:]
    wide = ch.shape[1]
    blocks = length // SPAN
    h_rows = h_ref[i, :, :width]
    scale, rdot = aux
    gate = gate_ref[i]
    mixed = mixed_ref[i].astype(F32)
    sig = sigmoid(gate)
    silu = gate * sig
    gated = mixed * silu
    gain = ch[6:7]
    grad_no = dot_nt(h_rows, wo_ref[...])
    grad_g = scale * (gain * grad_no) - gated * (scale * scale * (1.0 / INNER) * rdot)
    scaled = gated * scale
    no_ref[i] = (scaled * gain).astype(BF16)
    gain_row = jnp.sum(grad_no * scaled, axis=0, keepdims=True)
    dmix_s[...] = (grad_g * silu).astype(BF16)
    pg_ref[i, :, :wide] = (grad_g * mixed * (sig * (1.0 + gate * (1.0 - sig)))).astype(BF16)

    x_raw = xraw_ref[i].astype(F32)
    bc_raw = bcraw_ref[i].astype(F32)
    conv_x = conv_sum(x_raw, ch)
    sig_x = sigmoid(conv_x)
    act_x = (conv_x * sig_x).astype(BF16)
    conv_bc = conv_sum(bc_raw, bc)
    sig_bc = sigmoid(conv_bc)
    act_bc = (conv_bc * sig_bc).astype(BF16)
    step, slope = step_sizes(dtraw_ref[i].astype(F32), dtp[0:1])
    rate = jnp.exp(dtp[1:2])
    causal = triangles()
    ones = causal.astype(F32)
    lower = low_half()
    lane_ids = lax.broadcasted_iota(jnp.int32, (SPAN, LANES), 1)
    last_row = lax.broadcasted_iota(jnp.int32, (SPAN, 1), 0) == SPAN - 1
    decays = []
    for b in range(blocks):
        decays.append(-dot(ones, rate * step[b * SPAN : (b + 1) * SPAN], precision=HIGHEST))
    entering = [[None] * heads for _ in range(blocks)]
    for b in range(blocks - 1):
        span = slice(b * SPAN, (b + 1) * SPAN)
        b_in = act_bc[span, :STATE].astype(F32)
        for h in range(heads):
            lanes = slice(h // 2 * LANES, h // 2 * LANES + LANES)
            column = decays[b][:, h : h + 1]
            last = column[SPAN - 1 :]
            tail = jnp.exp(last - column) * step[span, h : h + 1]
            fresh = dot_tn((b_in * tail).astype(BF16), act_x[span, lanes])
            if entering[b][h] is not None:
                fresh += jnp.exp(last) * entering[b][h]
            entering[b + 1][h] = fresh
    leaving = [None] * heads
    rate_row = jnp.zeros((1, LANES), F32)
    for b in reversed(range(blocks)):
        span = slice(b * SPAN, (b + 1) * SPAN)
        step_b, decay = step[span], decays[b]
        decay_t, step_t = decay.T, step_b.T
        b_in, c_out = act_bc[span, :STATE], act_bc[span, STATE:]
        scores = dot_nt(c_out, b_in)
        grad_scores = jnp.zeros((SPAN, SPAN), F32)
        grad_b = jnp.zeros((SPAN, STATE), F32)
        grad_c = jnp.zeros((SPAN, STATE), F32)
        row_sums = jnp.zeros((SPAN, LANES), F32)
        grad_step = jnp.zeros((SPAN, LANES), F32)
        col_rows = []
        for first in range(0, heads, 2):
            lanes = slice(first * HEADDIM, first * HEADDIM + LANES)
            x_pair = act_x[span, lanes]
            grad_pair = dmix_s[span, lanes]
            parts = []
            for h in range(first, min(first + 2, heads)):
                own = head_lanes(h)
                grad_own = jnp.where(own, grad_pair, jnp.zeros((), BF16))
                column = decay[:, h : h + 1]
                mask = jnp.exp(jnp.where(causal, column - decay_t[h : h + 1], -1e30))
                spread = mask * step_t[h : h + 1]
                weights = (scores * spread).astype(BF16)
                part = dot_tn(weights, grad_pair)
                grad_w = dot_nt(grad_own, x_pair)
                grad_scores += grad_w * spread
                pulled = grad_w * (scores * mask)
                col_rows.append(jnp.sum(pulled, axis=0, keepdims=True))
                row_sum = jnp.sum(pulled * step_t[h : h + 1], axis=1, keepdims=True)
                if entering[b][h] is not None:
                    carry = entering[b][h].astype(BF16)
                    grown = jnp.exp(column)
                    grad_grown = grad_own.astype(F32) * grown
                    grad_c += dot_nt(grad_grown.astype(BF16), carry)
                    grad_carry = dot_tn(c_out, grad_grown.astype(BF16))
                    row_sum += jnp.sum(grad_grown * dot(c_out, carry), axis=1, keepdims=True)
                else:
                    grad_carry = None
                if leaving[h] is not None:
                    last = column[SPAN - 1 :]
                    fade = jnp.exp(last - column)
                    tail = fade * step_b[:, h : h + 1]
                    b_wide = b_in.astype(F32)
                    grad_state = leaving[h].astype(BF16)
                    grad_shaped = dot_nt(x_pair, grad_state)
                    part += dot((b_wide * tail).astype(BF16), grad_state)
                    grad_b += grad_shaped * tail
                    grad_tail = jnp.sum(grad_shaped * b_wide, axis=1, keepdims=True)
                    grad_step += jnp.where(lane_ids == h, grad_tail * fade, 0.0)
                    moved = grad_tail * tail
                    total = jnp.sum(moved, axis=0, keepdims=True)
                    if entering[b][h] is not None:
                        faded = jnp.exp(last) * leaving[h]
                        kept = jnp.sum(faded * entering[b][h], axis=1, keepdims=True)
                        total += jnp.sum(kept, axis=0, keepdims=True)
                        grad_carry += faded
                    row_sum += jnp.where(last_row, total, 0.0) - moved
                leaving[h] = grad_carry
                row_sums += jnp.where(lane_ids == h, row_sum, 0.0)
                parts.append(part)
            if len(parts) == 1:
                parts.append(jnp.zeros_like(parts[0]))
            grad_x = jnp.where(lower, parts[0], parts[1])
            dx_s[span, lanes] = grad_x + ch[5:6, lanes] * grad_pair.astype(F32)
        col_sums = stacked(col_rows, LANES).T
        low_scores = grad_scores.astype(BF16)
        dbc_s[span, :STATE] = grad_b + dot_tn(low_scores, c_out)
        dbc_s[span, STATE:] = grad_c + dot(low_scores, b_in)
        grad_decay = dot(
            ones, row_sums - step_b * col_sums, ((0,), (0,)), precision=HIGHEST
        )
        ddt_s[span] = col_sums + grad_step - rate * grad_decay
        rate_row -= jnp.sum(grad_decay * step_b, axis=0, keepdims=True)

    skip_row = jnp.sum(dmix_s[...].astype(F32) * act_x.astype(F32), axis=0, keepdims=True)
    grad_conv = dx_s[...] * (sig_x * (1.0 + conv_x * (1.0 - sig_x)))
    grad_raw, ch_rows = conv_back(grad_conv, x_raw, ch)
    pg_ref[i, :, wide : 2 * wide] = grad_raw.astype(BF16)
    grad_conv = dbc_s[...] * (sig_bc * (1.0 + conv_bc * (1.0 - sig_bc)))
    grad_raw, bc_rows = conv_back(grad_conv, bc_raw, bc)
    pg_ref[i, :, 2 * wide : 2 * wide + SHARED] = grad_raw.astype(BF16)
    grad_dt = ddt_s[...] * slope
    low_dt = grad_dt.astype(BF16)
    if sel is not None:
        low_dt = dot_nt(low_dt, sel).astype(BF16)
    pg_ref[i, :, 2 * wide + SHARED :] = low_dt
    dn_ref[i] = dot(pg_ref[i], w_ref[...]).astype(BF16)
    by_channel = stacked(ch_rows + [skip_row, gain_row], 8)
    by_shared = stacked(bc_rows, 8)
    by_head = stacked([jnp.sum(grad_dt, axis=0, keepdims=True), rate_row * rate], 8)
    if sel is not None:
        by_head = lax.dot_general(
            by_head, sel.astype(F32), (((1,), (1,)), ((), ())),
            preferred_element_type=F32, precision=HIGHEST,
        )
    return by_channel, by_shared, by_head


def add_small(small, by_channel, by_shared, by_head):
    for j in range(2):
        part = by_channel[:, j * THIRD : (j + 1) * THIRD]
        small[:, j * PIECE : j * PIECE + THIRD] += part
    small[:, 2 * PIECE : 3 * PIECE] += by_shared
    small[7:8, 2 * PIECE : 2 * PIECE + HEADS] += by_head[0:1]
    small[7:8, 2 * PIECE + LANES : 2 * PIECE + LANES + HEADS] += by_head[1:2]


def add_gain(small, row):
    for r in range(8):
        small[r : r + 1, 3 * PIECE : 3 * PIECE + THIRD] = row[:, r * THIRD : (r + 1) * THIRD]


def whole_spec(array):
    return pl.BlockSpec(array.shape, lambda i: (0,) * array.ndim)


def row_spec(length, width):
    return pl.BlockSpec((1, length, width), lambda i: (i, 0, 0))


def block_spec(array):
    return pl.BlockSpec((1,) + array.shape[1:], lambda i: (i, 0, 0))


PARAMS = dict(vmem_limit_bytes=60 * 1024 * 1024)


def run_forward(heads, wide, rows, w, wo, params):
    count, length, width = rows.shape
    constants = [w, wo, *params]
    outs = [
        (width, BF16), (LANES, F32), (width, BF16), (wide, F32),
        (wide, BF16), (SHARED, BF16), (LANES, BF16), (wide, BF16),
    ]
    return pl.pallas_call(
        partial(forward_kernel, heads),
        grid=(count,),
        out_shape=[jax.ShapeDtypeStruct((count, length, n), t) for n, t in outs],
        in_specs=[block_spec(rows)] + [whole_spec(c) for c in constants],
        out_specs=[row_spec(length, n) for n, _ in outs],
        compiler_params=pltpu.CompilerParams(**PARAMS),
        name="forward",
    )(rows, *constants)


def run_backward(heads, wide, grad_rows, aux, saved, w, wo, params):
    count, length, _ = grad_rows.shape
    columns, width = w.shape
    given = [grad_rows, aux, *saved]
    constants = [w, wo, *params]
    outs = [(width, BF16), (columns, BF16), (wide, BF16)]
    sums = [(8, wide), (8, SHARED), (8, LANES)]
    return pl.pallas_call(
        partial(backward_kernel, heads),
        grid=(count,),
        out_shape=[jax.ShapeDtypeStruct((count, length, n), t) for n, t in outs]
        + [jax.ShapeDtypeStruct(s, F32) for s in sums],
        in_specs=[block_spec(g) for g in given] + [whole_spec(c) for c in constants],
        out_specs=[row_spec(length, n) for n, _ in outs]
        + [pl.BlockSpec(s, lambda i: (0, 0)) for s in sums],
        scratch_shapes=backward_scratch(length, wide),
        compiler_params=pltpu.CompilerParams(**PARAMS),
        name="backward",
    )(*given, *constants)


def backward_scratch(length, wide):
    return [
        pltpu.VMEM((length, wide), BF16),
        pltpu.VMEM((length, wide), F32),
        pltpu.VMEM((length, SHARED), F32),
        pltpu.VMEM((length, LANES), F32),
    ]


class Plan:
    def __init__(self, seq, fsdp):
        self.seq, self.fsdp = seq, fsdp
        halves = 2
        if fsdp % 2 or HEADS % (seq * 2) or (HEADS // fsdp) % seq:
            halves = 1
        self.halves, self.mates = halves, fsdp // halves
        self.heads = HEADS // (seq * halves)
        self.pieces = self.mates if (HEADS // fsdp) % seq == 0 else 1
        channels = self.heads * HEADDIM
        self.channels = channels
        self.wide = -(-channels // LANES) * LANES
        self.peer_groups = [[lo + self.mates * h for h in range(halves)] for lo in range(self.mates)]
        self.mate_groups = [[h * self.mates + j for j in range(self.mates)] for h in range(halves)]

    def split(self, array, axis):
        size = array.shape[axis] // (self.halves * self.pieces * self.seq)
        shape = array.shape[:axis] + (self.halves, self.pieces, self.seq, size) + array.shape[axis + 1 :]
        return array.reshape(shape)

    def take(self, array, axis, place):
        array = lax.dynamic_index_in_dim(self.split(array, axis), place, axis + 2, False)
        shape = array.shape[: axis + 1] + (-1,) + array.shape[axis + 3 :]
        return jnp.moveaxis(array.reshape(shape), axis, 0)

    def put(self, parts, axis):
        size = parts.shape[axis + 2] // self.pieces
        shape = parts.shape[: axis + 2] + (self.pieces, size) + parts.shape[axis + 3 :]
        parts = jnp.moveaxis(parts.reshape(shape), (1, axis + 2, 0), (axis, axis + 1, axis + 2))
        shape = parts.shape[:axis] + (-1,) + parts.shape[axis + 4 :]
        return parts.reshape(shape)


def widened(array, axis, size):
    pads = [(0, 0)] * array.ndim
    pads[axis] = (0, size - array.shape[axis])
    return jnp.pad(array, pads)


MESH = pl.DeviceIdType.MESH
ANY = pl.BlockSpec(memory_space=pl.ANY)
VMEM = pl.BlockSpec(memory_space=pltpu.VMEM)
DMA = pltpu.SemaphoreType.DMA


class Spot:
    def __init__(self):
        self.s, self.q, self.z = (lax.axis_index(a) for a in ("section", "seq", "fsdp"))
        self.half, self.lo = self.z // 2, self.z % 2
        self.mate, self.twin = self.z + 1 - 2 * self.lo, (self.z + 2) % 4
        self.around = [None, self.q + 1 - 2 * (self.q % 2), (self.q + 2) % 4, 3 - self.q]
        self.sibling = (1 - self.s, self.q, self.z)
        self.at_mate, self.at_twin = (self.s, self.q, self.mate), (self.s, self.q, self.twin)

    def plane(self, k):
        return (self.s, self.around[k], self.z)

    def column(self, z):
        return (self.s, self.q, z)

    def piece(self, half, j):
        return 8 * half + 4 * j + self.q


def greet(places):
    barrier = pltpu.get_barrier_semaphore()
    for place in places:
        pl.semaphore_signal(barrier, inc=1, device_id=place, device_id_type=MESH)
    pl.semaphore_wait(barrier, len(places))


def remote(src, dst, send_sem, recv_sem, place):
    return pltpu.make_async_remote_copy(
        src_ref=src, dst_ref=dst, send_sem=send_sem, recv_sem=recv_sem, device_id=place, device_id_type=MESH
    )


class Home:
    def __init__(self, src, buffer, dst, sems):
        self.load = pltpu.make_async_copy(src, buffer, sems[0])
        self.store = pltpu.make_async_copy(buffer, dst, sems[1])

    def begin(self):
        self.load.start()

    def go_on(self):
        self.load.wait()
        self.store.start()

    def end(self):
        self.store.wait()


class Spread:
    SEMS = [DMA((7,)), DMA((7,)), DMA]

    def __init__(self, spot, own, all_rows, sems):
        self.spot, self.own, self.all = spot, own, all_rows
        self.send, self.recv, self.local = sems

    def slot(self, half):
        rows = self.own.shape[0]
        return self.all.at[half, pl.ds(pl.multiple_of(self.spot.q * rows, rows), rows)]

    def copy(self, j):
        spot = self.spot
        slot = self.slot(spot.half)
        if j == 3:
            return remote(self.own, slot, self.send.at[3], self.recv.at[3], spot.at_twin)
        if j < 3:
            return remote(self.own, slot, self.send.at[j], self.recv.at[j], spot.plane(j + 1))
        slot = self.slot(1 - spot.half)
        return remote(slot, slot, self.send.at[j], self.recv.at[j], spot.plane(j - 3))

    def here(self):
        return pltpu.make_async_copy(self.own, self.slot(self.spot.half), self.local)

    def start(self):
        for j in (3, 0, 1, 2):
            self.copy(j).start()
        self.here().start()

    def forward(self):
        self.copy(3).wait_recv()
        for j in (4, 5, 6):
            self.copy(j).start()

    def own_half(self):
        for j in (0, 1, 2):
            self.copy(j).wait_recv()
        self.here().wait()

    def other_half(self):
        for j in (4, 5, 6):
            self.copy(j).wait_recv()

    def close(self):
        for j in range(7):
            self.copy(j).wait_send()

    def finish(self):
        self.own_half()
        self.other_half()
        self.close()


class Sum:
    @staticmethod
    def scratch(rows, columns):
        return [
            pltpu.VMEM((2, 4 * rows, columns), BF16),
            pltpu.VMEM((3, 2, rows, columns), BF16),
            pltpu.VMEM((2, rows, columns), BF16),
            DMA((7,)),
            DMA((7,)),
        ]

    def __init__(self, spot, width, scratch):
        self.spot, self.width = spot, width
        self.parts, self.recv_rows, self.twin_rows, self.send, self.recv = scratch
        self.rows = self.twin_rows.shape[1]

    def half(self, i):
        return 1 - self.spot.half + i * (2 * self.spot.half - 1)

    def block(self, q):
        return pl.ds(pl.multiple_of(q * self.rows, self.rows), self.rows)

    def copy(self, k, i):
        spot = self.spot
        j = 3 * i + k - 1
        return remote(
            self.parts.at[self.half(i), self.block(spot.around[k])], self.recv_rows.at[k - 1, i],
            self.send.at[j], self.recv.at[j], spot.plane(k),
        )

    def across(self):
        return remote(
            self.twin_rows.at[0], self.twin_rows.at[1], self.send.at[6], self.recv.at[6], self.spot.at_twin
        )

    def start(self, i):
        for k in (1, 2, 3):
            self.copy(k, i).start()

    def plane_total(self, i):
        total = self.parts[self.half(i), self.block(self.spot.q), :].astype(F32)
        for k in (1, 2, 3):
            self.copy(k, i).wait_recv()
            total += self.recv_rows[k - 1, i].astype(F32)
        return total

    def forward(self):
        total = self.plane_total(0)
        width = self.width
        self.twin_rows[0, :, :width] = total[:, :width].astype(BF16)
        if total.shape[1] > width:
            column = jnp.sum(total[:, width:], axis=1, keepdims=True)
            self.twin_rows[0, :, width:] = split_three(column)
        self.across().start()

    def finish(self):
        total = self.plane_total(1)
        self.across().wait_recv()
        total += self.twin_rows[1].astype(F32)
        return total

    def close(self):
        for i in range(2):
            for k in (1, 2, 3):
                self.copy(k, i).wait_send()
        self.across().wait_send()


class RelaySum(Sum):
    @staticmethod
    def scratch(rows, columns):
        return [
            pltpu.VMEM((2, 4 * rows, columns), BF16),
            pltpu.VMEM((2, 2, rows, columns), BF16),
            pltpu.VMEM((2, rows, columns), BF16),
            DMA((9,)),
            DMA((9,)),
            pltpu.VMEM((2, rows, columns), BF16),
        ]

    def __init__(self, spot, width, scratch):
        super().__init__(spot, width, scratch[:5])
        self.relays = scratch[5]
        columns = self.relays.shape[2]
        cut = columns // 2 // LANES * LANES
        self.cuts = [(0, cut), (cut, columns - cut)]

    def relay(self, k, i):
        spot = self.spot
        columns = pl.ds(*self.cuts[k - 1])
        return remote(
            self.parts.at[self.half(i), self.block(spot.around[3]), columns], self.relays.at[i, :, columns],
            self.send.at[5 + 2 * i + k - 1], self.recv.at[5 + 2 * i + k - 1], spot.plane(k),
        )

    def copy(self, k, i):
        spot = self.spot
        j = 2 * i + k - 1
        return remote(
            self.parts.at[self.half(i), self.block(spot.around[k])], self.recv_rows.at[k - 1, i],
            self.send.at[j], self.recv.at[j], spot.plane(k),
        )

    def across(self):
        return remote(
            self.twin_rows.at[0], self.twin_rows.at[1], self.send.at[4], self.recv.at[4], self.spot.at_twin
        )

    def start(self, i):
        for k in (1, 2):
            self.relay(k, i).start()

    def go_on(self, i):
        for k in (1, 2):
            self.relay(k, i).wait_recv()
            at, size = self.cuts[k - 1]
            rows = self.block(self.spot.around[3 - k])
            half = self.half(i)
            own = self.parts[half, rows, at : at + size].astype(F32)
            total = own + self.relays[i, :, at : at + size].astype(F32)
            self.parts[half, rows, at : at + size] = total.astype(BF16)
        for k in (1, 2):
            self.copy(k, i).start()

    def plane_total(self, i):
        total = self.parts[self.half(i), self.block(self.spot.q), :].astype(F32)
        for k in (1, 2):
            self.copy(k, i).wait_recv()
            total += self.recv_rows[k - 1, i].astype(F32)
        return total

    def close(self):
        for i in range(2):
            for k in (1, 2):
                self.copy(k, i).wait_send()
                self.relay(k, i).wait_send()
        self.across().wait_send()


def tile_parts(spot, half):
    parts = []
    for part in range(2):
        for j in range(2):
            at = part * INNER + THIRD * spot.piece(half, j)
            parts.append((pl.multiple_of(at, 64), (2 * part + j) * THIRD, THIRD))
    return parts + [(2 * INNER, 4 * THIRD, SHARED + HEADS)]


class Weights:
    PARTS = 6
    ORDER = (4, 5, 0, 1, 2, 3)
    QUARTER = SHARED // 4

    @staticmethod
    def scratch(columns, shard, width):
        buffers = [pltpu.VMEM((columns, shard), BF16), pltpu.VMEM((THIRD, width), BF16)]
        return buffers + [DMA((9,)), DMA((57,)), DMA((57,))]

    def __init__(self, spot, layer, w_in, w_out, tile, tile_out, scratch):
        self.spot, self.layer = spot, layer
        self.w_in, self.w_out, self.tile, self.tile_out = w_in, w_out, tile, tile_out
        self.buffer, self.out_buffer, self.local, self.send, self.recv = scratch
        self.shard = w_in.shape[1]
        self.others = 2 * (1 - spot.half)
        self.gateway = 2 - spot.half
        self.is_gateway = (spot.z == 1) | (spot.z == 2)

    def at_source(self, step):
        pl.when(self.spot.s == self.layer)(step)

    def at_relay(self, step):
        pl.when(self.spot.s != self.layer)(step)

    def parts(self, half, n):
        if n < 4:
            return tile_parts(self.spot, half)[n]
        if n == 5:
            return 2 * INNER + SHARED, 4 * THIRD + SHARED, HEADS
        at = self.QUARTER * self.spot.q
        return (
            pl.multiple_of(2 * INNER + at, 64), pl.multiple_of(4 * THIRD + at, 64), self.QUARTER
        )

    def source(self, half, n):
        first, _, size = self.parts(half, n)
        return self.w_in.at[pl.ds(first, size)]

    def target(self, z, n):
        _, first, size = self.parts(0, n)
        columns = pl.ds(pl.multiple_of(z * self.shard, LANES), self.shard)
        return self.tile.at[pl.ds(first, size), columns]

    def buffered(self, n):
        _, first, size = self.parts(0, n)
        return self.buffer.at[pl.ds(first, size)]

    def load(self, n):
        return pltpu.make_async_copy(self.source(self.spot.half, n), self.buffered(n), self.send.at[n])

    def store(self, n):
        return pltpu.make_async_copy(self.buffered(n), self.target(self.spot.z, n), self.local.at[3 + n])

    def out_home(self):
        return Home(
            self.out_source(), self.out_buffer, self.out_part(self.spot.lo),
            (self.local.at[1], self.local.at[2]),
        )

    def to_mate(self, n):
        source, target = self.source(self.spot.half, n), self.target(self.spot.z, n)
        return remote(source, target, self.send.at[n], self.recv.at[n], self.spot.at_mate)

    def to_gateway(self, n):
        source, target = self.source(1 - self.spot.half, n), self.target(self.spot.z, n)
        j = 6 + 6 * self.spot.lo + n
        place = (1 - self.spot.s, self.spot.q, self.gateway)
        return remote(source, target, self.send.at[6 + n], self.recv.at[j], place)

    def passed(self, c, n):
        part = self.target(self.others + c, n)
        j = 6 * c + n
        return remote(part, part, self.send.at[12 + j], self.recv.at[6 + j], self.spot.at_mate)

    def to_sibling(self, b, n):
        j = 24 + 6 * b + n
        part = self.target([self.spot.z, self.spot.mate, self.others, self.others + 1][b], n)
        source = self.source(self.spot.half, n) if b == 0 else part
        return remote(source, part, self.send.at[j], self.recv.at[j], self.spot.sibling)

    def out_part(self, lo):
        return self.tile_out.at[pl.ds(pl.multiple_of(lo * THIRD, 64), THIRD)]

    def out_source(self):
        return self.w_out.at[pl.ds(pl.multiple_of(self.spot.q * THIRD, 64), THIRD)]

    def out_to(self, n):
        part = self.out_part(self.spot.lo if n < 2 else 1 - self.spot.lo)
        place = self.spot.sibling if n else self.spot.at_mate
        source = self.out_source() if n < 2 else part
        return remote(source, part, self.send.at[48 + n], self.recv.at[48 + n], place)

    def send_part(self, n):
        if n < self.PARTS:
            self.to_gateway(n).start()
            self.to_mate(n).start()
        elif n == self.PARTS:
            self.out_to(0).start()

    def begin(self):
        @self.at_source
        def _():
            for n in range(self.PARTS):
                self.load(n).start()
            self.out_home().begin()

    def quarter(self, q):
        at = 4 * THIRD + self.QUARTER * q
        return self.tile.at[pl.ds(pl.multiple_of(at, 64), self.QUARTER)]

    def to_plane(self, k):
        part = self.quarter(self.spot.q)
        return remote(part, part, self.send.at[50 + k], self.recv.at[50 + k], self.spot.plane(k))

    def quarter_to_sibling(self, k):
        part = self.quarter(self.spot.around[k])
        return remote(part, part, self.send.at[53 + k], self.recv.at[53 + k], self.spot.sibling)

    def mates(self):
        for n in self.ORDER:
            self.to_mate(n).start()
        self.out_to(0).start()

    def start(self, window):
        @self.at_source
        def _():
            for n in self.ORDER:
                self.load(n).wait()
            for n in self.ORDER[:window]:
                self.to_gateway(n).start()
            pl.when(self.is_gateway)(self.mates)
            for n in self.ORDER:
                self.to_sibling(0, n).start()
                self.store(n).start()
            self.out_to(1).start()
            self.out_home().go_on()

    def more(self, at, window):
        @self.at_source
        def _():
            self.to_gateway(self.ORDER[at - window]).wait_send()
            self.to_gateway(self.ORDER[at]).start()
            if at == self.PARTS - 1:
                pl.when(jnp.logical_not(self.is_gateway))(self.mates)

    def relay(self, at):
        n = self.ORDER[at]

        @self.at_relay
        def _():
            for c in range(2):
                self.passed(c, n).wait_recv()
                pl.when(self.is_gateway)(lambda c=c: self.passed(c, n).start())
                self.to_sibling(2 + c, n).start()

    def share(self):
        @self.at_source
        def _():
            self.store(4).wait()
            self.to_mate(4).wait_recv()
            self.to_sibling(1, 4).start()
            for c in range(2):
                self.to_sibling(2 + c, 4).wait_recv()
            for k in (1, 2, 3):
                self.to_plane(k).start()

    def shared(self):
        @self.at_source
        def _():
            for k in (1, 2, 3):
                self.to_plane(k).wait_recv()
                self.quarter_to_sibling(k).start()

    def relay_mate(self):
        @self.at_source
        def _():
            for n in self.ORDER[1:]:
                self.to_mate(n).wait_recv()
                self.to_sibling(1, n).start()
            self.out_to(0).wait_recv()
            self.out_to(2).start()

    def finish(self, window):
        @self.at_source
        def _():
            for n in self.ORDER[-window:]:
                self.to_gateway(n).wait_send()
            for n in self.ORDER:
                self.to_mate(n).wait_send()
                for b in range(2):
                    if n != 4:
                        self.to_sibling(2 + b, n).wait_recv()
                    self.to_sibling(b, n).wait_send()
                if n != 4:
                    self.store(n).wait()
            for k in (1, 2, 3):
                self.to_plane(k).wait_send()
                self.quarter_to_sibling(k).wait_send()
            self.out_home().end()
            for n in range(3):
                self.out_to(n).wait_send()

        @self.at_relay
        def _():
            for n in self.ORDER:
                for c in range(2):
                    self.to_sibling(c, n).wait_recv()
                    self.to_sibling(2 + c, n).wait_send()
                    pl.when(self.is_gateway)(lambda c=c, n=n: self.passed(c, n).wait_send())
            for k in (1, 2, 3):
                self.quarter_to_sibling(k).wait_recv()
            for n in (1, 2):
                self.out_to(n).wait_recv()


def all_places(spot):
    places = [spot.plane(k) for k in (1, 2, 3)]
    places += [(s, spot.q, (spot.z + k) % 4) for k in (1, 2, 3) for s in range(2)]
    return places + [spot.sibling]


def open_kernel(*refs):
    ins, outs, weight_s, spread_a, spread_b, (own_tokens, own_cot, own_pack, load, *pack_sems) = take(
        refs, (11, 5, 5, 3, 3, 7)
    )
    w_in, w_out, tokens, cotangent, *raw = ins
    tile, tile_out, packs, all_tokens, all_cot = outs
    spot = Spot()
    weights = Weights(spot, 0, w_in, w_out, tile, tile_out, weight_s)
    rows = Spread(spot, own_tokens, all_tokens, spread_a)
    grads = Spread(spot, own_cot, all_cot, spread_b)
    loads = [
        pltpu.make_async_copy(src, dst, load.at[n])
        for n, (src, dst) in enumerate(
            ((tokens.at[spot.s], own_tokens), (cotangent.at[spot.s], own_cot))
        )
    ]
    pack_here = pltpu.make_async_copy(own_pack, packs.at[spot.s], pack_sems[0])
    pack_there = remote(own_pack, packs.at[spot.s], pack_sems[1], pack_sems[2], spot.sibling)
    for copy in loads:
        copy.start()
    weights.begin()
    greet(all_places(spot))
    for copy in loads:
        copy.wait()
    few = 2
    rows.start()
    weights.start(few)
    pack_params(own_pack, *raw)
    pack_here.start()
    pack_there.start()
    weights.more(2, few)
    rows.forward()
    for at in (3, 4, 5):
        weights.more(at, few)
    weights.relay(0)
    weights.relay(1)
    weights.share()
    grads.start()
    weights.relay(2)
    weights.relay(3)
    weights.shared()
    grads.forward()
    weights.relay(4)
    weights.relay(5)
    weights.relay_mate()
    rows.finish()
    grads.finish()
    weights.finish(few)
    pack_here.wait()
    pack_there.wait()


def pack_params(pack, conv_weight, conv_bias, gate_gain, skip_gain, norm_gain, dt_bias, a_log):
    pack[...] = jnp.zeros_like(pack)
    for p in range(INNER // THIRD):
        source, target = slice(p * THIRD, (p + 1) * THIRD), slice(p * PIECE, p * PIECE + THIRD)
        pack[0:CONV, target] = conv_weight[:, source]
        pack[CONV : CONV + 1, target] = conv_bias[:, source]
        skips = [jnp.broadcast_to(skip_gain[:, 3 * p + h : 3 * p + h + 1], (1, HEADDIM)) for h in range(3)]
        pack[5:6, target] = jnp.concatenate(skips, axis=1)
        pack[6:7, target] = gate_gain[:, source]
    pack[0:CONV, -SHARED:] = conv_weight[:, INNER:]
    pack[CONV : CONV + 1, -SHARED:] = conv_bias[:, INNER:]
    pack[7:8, :GAIN_END] = norm_gain[...]
    pack[7:8, DT_AT : DT_AT + HEADS] = dt_bias[...]
    pack[7:8, RATE_AT : RATE_AT + HEADS] = a_log[...]


def layer_rows(total, rows_in, branch, scales, rows_out):
    width = rows_in.shape[1]
    square = jnp.sum(total[:, width:], axis=1, keepdims=True)
    scale = lax.rsqrt(square * (1.0 / INNER) + NORM_EPS)
    part = total[:, :width] * scale
    rows_out[...] = (rows_in[...].astype(F32) + part).astype(BF16)
    if branch is not None:
        branch[...] = part
        scales[...] = jnp.broadcast_to(scale, scales.shape)


def norm_back(total, rows_in, gain, grad_out):
    rows = rows_in[...].astype(F32)
    scale = lax.rsqrt(jnp.mean(rows * rows, axis=-1, keepdims=True) + NORM_EPS)
    scaled = rows * scale
    pulled = total * gain
    inner = jnp.mean(pulled * scaled, axis=-1, keepdims=True)
    grad = scale * (pulled - scaled * inner) + grad_out[...].astype(F32)
    return grad, jnp.sum(total * scaled, axis=0, keepdims=True)


def add_rows(target, sources, chunk=64):
    @pl.loop(0, target.shape[0] // chunk)
    def _(n):
        rows = pl.ds(pl.multiple_of(n * chunk, chunk), chunk)
        total = sources[0][rows, :].astype(F32)
        for source in sources[1:]:
            total += source[rows, :].astype(F32)
        target[rows, :] = total.astype(target.dtype)


class Grads:
    ORDER = (4, 0, 1, 2, 3, 5)

    @staticmethod
    def scratch(shard, columns, wide, width):
        return [
            pltpu.VMEM((3, columns, width), BF16),
            pltpu.VMEM((3, wide, width), BF16),
            pltpu.VMEM((2, columns, shard), BF16),
            pltpu.VMEM((2, columns, shard), BF16),
            pltpu.VMEM((THIRD, width), BF16),
            DMA((22,)),
            DMA((27,)),
        ]

    @staticmethod
    def results(shard, width):
        return [((2, 4 * THIRD, shard), BF16), ((SHARED + HEADS, shard), BF16), ((THIRD, width), BF16)]

    def __init__(self, spot, results, scratch):
        self.spot = spot
        self.reduced, self.shared, self.out = results
        self.cores, self.cores_out, self.planes, self.relay, self.mate_out, self.send, self.recv = scratch
        self.shard = self.planes.shape[2]
        self.others = 2 * (1 - spot.half)
        self.is_gateway = (spot.z == 1) | (spot.z == 2)

    def rows(self, n):
        _, first, size = tile_parts(self.spot, 0)[n]
        return pl.ds(first, size)

    def columns(self, z):
        return pl.ds(pl.multiple_of(z * self.shard, LANES), self.shard)

    def core_copy(self, n):
        buffer, rows = (self.cores_out, pl.ds(0, self.cores_out.shape[1])) if n == 5 else (self.cores, self.rows(n))
        return remote(
            buffer.at[2, rows], buffer.at[1, rows], self.send.at[n], self.recv.at[n], self.spot.sibling
        )

    def product(self, layer, n, proj_grad, normed, normed_out, h_rows):
        def flat(value):
            return value.reshape(-1, value.shape[-1])

        width = self.cores.shape[2]
        slot = 2 * (self.spot.s - layer) * (self.spot.s - layer)
        if n == 5:
            total = dot_tn(flat(normed_out[...]), flat(h_rows[:, :, :width]))
            self.cores_out[slot] = total.astype(BF16)
        else:
            _, first, size = tile_parts(self.spot, 0)[n]
            total = dot_tn(flat(proj_grad[:, :, first : first + size]), flat(normed[...]))
            self.cores[slot, first : first + size, :] = total.astype(BF16)
        pl.when(self.spot.s != layer)(lambda: self.core_copy(n).start())

    def far_part(self, c, n):
        return self.cores.at[0, self.rows(n), self.columns(self.others + c)]

    def to_mate(self, n):
        source = self.cores.at[0, self.rows(n), self.columns(self.spot.mate)]
        target = self.planes.at[1, self.rows(n)]
        return remote(source, target, self.send.at[6 + n], self.recv.at[11 + n], self.spot.at_mate)

    def to_relay(self, c, n):
        j = 2 * n + c
        target = self.relay.at[c, self.rows(n)]
        return remote(
            self.far_part(c, n), target, self.send.at[11 + j], self.recv.at[16 + j], self.spot.at_mate
        )

    def to_far(self, c, n):
        target = self.planes.at[0, self.rows(n)]
        place = self.spot.column(self.others + c)
        return remote(
            self.far_part(c, n), target, self.send.at[11 + 2 * n + c], self.recv.at[6 + n], place
        )

    def out_rows(self, lo):
        return pl.ds(pl.multiple_of(lo * THIRD, 64), THIRD)

    def mate_copy(self):
        source = self.cores_out.at[0, self.out_rows(1 - self.spot.lo)]
        return remote(source, self.mate_out, self.send.at[21], self.recv.at[26], self.spot.at_mate)

    def sent(self, n):
        self.to_mate(n).wait_send()
        for c in range(2):
            self.to_relay(c, n).wait_send()

    def to_planes(self, n):
        self.core_copy(n).wait_recv()
        if n == 5:
            add_rows(self.cores_out.at[0], [self.cores_out.at[0], self.cores_out.at[1]])
            self.mate_copy().start()
            return
        own, sibling = self.cores.at[0, self.rows(n)], self.cores.at[1, self.rows(n)]
        add_rows(own, [own, sibling], 48 if n < 4 else 16)

        @pl.when(jnp.logical_not(self.is_gateway))
        def _():
            for c in range(2):
                self.to_relay(c, n).start()

        self.to_mate(n).start()

    def pass_on(self, n):
        @pl.when(self.is_gateway)
        def _():
            for c in range(2):
                self.to_relay(c, n).wait_recv()
                target, relay = self.far_part(c, n), self.relay.at[c, self.rows(n)]
                add_rows(target, [target, relay], 48 if n < 4 else 16)
                self.to_far(c, n).start()

    def gather(self, n):
        if n == 5:
            self.mate_copy().wait_recv()
            add_rows(self.out, [self.cores_out.at[0, self.out_rows(self.spot.lo)], self.mate_out], 48)
            return
        self.to_mate(n).wait_recv()
        self.to_far(0, n).wait_recv()
        _, first, size = tile_parts(self.spot, 0)[n]
        mine = self.columns(self.spot.z)
        chunk = 48 if n < 4 else 16

        @pl.loop(0, size // chunk)
        def _(r):
            rows = pl.ds(pl.multiple_of(first + r * chunk, 16), chunk)
            own = self.cores[0, rows, mine].astype(F32) + self.planes[1, rows, :].astype(F32)
            other = self.planes[0, rows, :]
            if n < 4:
                self.reduced[0, rows, :] = own.astype(BF16)
                self.reduced[1, rows, :] = other
            else:
                rows = pl.ds(pl.multiple_of(r * chunk, 16), chunk)
                self.shared[rows, :] = (own + other.astype(F32)).astype(BF16)

    def finish(self):
        self.mate_copy().wait_send()
        for n in self.ORDER:
            self.core_copy(n).wait_send()


class GradsAround:
    @staticmethod
    def scratch(shard):
        return [
            pltpu.VMEM((4, SHARED + HEADS, shard), BF16),
            DMA((11,)),
            DMA((34,)),
            DMA((34,)),
        ]

    def __init__(self, spot, results, final, final_out, scratch):
        self.spot, self.final, self.final_out = spot, final, final_out
        self.reduced, self.shared, self.out = results
        self.sums, self.local, self.send, self.recv = scratch

    def region(self, k, i, n):
        q = self.spot.q if k == 0 else self.spot.around[k]
        half = self.spot.half if i == 0 else 1 - self.spot.half
        at = n // 2 * INNER + THIRD * (8 * half + 4 * (n % 2) + q)
        return self.final.at[pl.ds(pl.multiple_of(at, 64), THIRD)]

    def copy(self, k, i, n):
        source = self.reduced.at[i, pl.ds(n * THIRD, THIRD)]
        target = self.region(0, i, n)
        j = 4 * i + n
        if k == 0:
            return pltpu.make_async_copy(source, target, self.local.at[j])
        if k < 3:
            j += 8 * (k - 1)
            return remote(source, target, self.send.at[j], self.recv.at[j], self.spot.plane(k))
        source = target = self.region(1 if i == 0 else 2, i, n)
        place = self.spot.plane(2 if i == 0 else 1)
        return remote(source, target, self.send.at[16 + j], self.recv.at[16 + j], place)

    def send_part(self, n):
        for i in range(2):
            for k in (1, 2, 0):
                self.copy(k, i, n).start()

    def pass_part(self, n):
        for i in range(2):
            self.copy(1 + i, i, n).wait_recv()
            self.copy(3, i, n).start()

    def out_region(self, k, i):
        q = self.spot.q if k == 0 else self.spot.around[k]
        size = THIRD if i is None else THIRD // 2
        at = q * THIRD + (0 if i is None else i * size)
        return self.final_out.at[pl.ds(pl.multiple_of(at, 32), size)]

    def out_copy(self, k, i=None):
        target = self.out_region(0, None)
        if k == 0:
            return pltpu.make_async_copy(self.out, target, self.local.at[8])
        if k < 3:
            return remote(self.out, target, self.send.at[23 + k], self.recv.at[23 + k], self.spot.plane(k))
        part = self.out_region(1 + i, i)
        return remote(part, part, self.send.at[26 + i], self.recv.at[26 + i], self.spot.plane(2 - i))

    def send_out(self):
        for k in (1, 2, 0):
            self.out_copy(k).start()

    def pass_out(self):
        for i in range(2):
            self.out_copy(1 + i).wait_recv()
            self.out_copy(3, i).start()

    def shared_copy(self, k):
        source = self.shared if k == 1 else self.sums.at[1]
        target = self.sums.at[0 if k == 1 else 2]
        return remote(source, target, self.send.at[27 + k], self.recv.at[27 + k], self.spot.plane(k))

    def shared_home(self):
        tail = self.final.at[pl.ds(2 * INNER, SHARED + HEADS)]
        return pltpu.make_async_copy(self.sums.at[3], tail, self.local.at[9])

    def shared_step(self, n):
        if n > 0:
            self.shared_copy(n).wait_recv()
            sources = [self.shared, self.sums.at[0]] if n == 1 else [self.sums.at[1], self.sums.at[2]]
            add_rows(self.sums.at[1 if n == 1 else 3], sources, 16)
        if n < 2:
            self.shared_copy(n + 1).start()
        else:
            self.shared_home().start()

    def finish(self):
        for i in range(2):
            for n in range(4):
                self.copy(2 - i, i, n).wait_recv()
                self.copy(3, i, n).wait_recv()
                for k in (1, 2, 3):
                    self.copy(k, i, n).wait_send()
                self.copy(0, i, n).wait()
            self.out_copy(3, i).wait_recv()
            self.out_copy(3, i).wait_send()
        for k in (1, 2):
            self.out_copy(k).wait_send()
            self.shared_copy(k).wait_send()
        self.out_copy(0).wait()
        self.shared_home().wait()


class SmallSum:
    SHAPE = (8, 4 * PIECE)

    @staticmethod
    def scratch():
        return [
            pltpu.VMEM((4,) + SmallSum.SHAPE, F32),
            pltpu.VMEM((8,) + SmallSum.SHAPE, F32),
            DMA((9,)),
            DMA((9,)),
        ]

    def __init__(self, spot, scratch):
        self.spot = spot
        self.small, self.group, self.send, self.recv = scratch

    def to_sibling(self):
        return remote(
            self.small.at[0], self.small.at[1], self.send.at[0], self.recv.at[0], self.spot.sibling
        )

    def to_mate(self):
        return remote(
            self.small.at[2], self.small.at[3], self.send.at[1], self.recv.at[1], self.spot.at_mate
        )

    def to_group(self, j):
        spot = self.spot
        part = self.group.at[4 * spot.half + spot.q]
        places = [spot.plane(k) for k in (1, 2, 3)] + [spot.at_twin]
        places += [(spot.s, spot.around[k], spot.twin) for k in (1, 2, 3)]
        return remote(part, part, self.send.at[2 + j], self.recv.at[2 + j], places[j])

    def begin(self, value):
        self.small[0] = value
        self.to_sibling().start()

    def step(self, n, value=None):
        if n == 0:
            self.to_sibling().wait_recv()
            self.small[2] = value + self.small[1]
            self.to_mate().start()
        else:
            self.to_mate().wait_recv()
            self.group[4 * self.spot.half + self.spot.q] = self.small[2] + self.small[3]
            for j in range(7):
                self.to_group(j).start()

    def finish(self, out):
        for j in range(7):
            self.to_group(j).wait_recv()
        total = self.group[0, :, 2 * PIECE :]
        for n in range(1, 8):
            total += self.group[n, :, 2 * PIECE :]
        for half in range(2):
            for j in range(2):
                for q in range(4):
                    at = (8 * half + 4 * j + q) * PIECE
                    out[:, at : at + PIECE] = self.group[4 * half + q, :, j * PIECE : (j + 1) * PIECE]
        out[:, -SHARED:] = total[:, :SHARED]
        out[7:8, DT_AT : DT_AT + HEADS] = total[7:8, :HEADS]
        out[7:8, RATE_AT : RATE_AT + HEADS] = total[7:8, LANES : LANES + HEADS]
        for r in range(8):
            out[7:8, r * THIRD : (r + 1) * THIRD] = total[r : r + 1, PIECE : PIECE + THIRD]
        self.to_sibling().wait_send()
        self.to_mate().wait_send()
        for j in range(7):
            self.to_group(j).wait_send()


def loading(sources, targets, sems):
    return [pltpu.make_async_copy(a, b, sems.at[n]) for n, (a, b) in enumerate(zip(sources, targets))]


def saved_shapes(length, width, wide):
    columns = ((width, BF16), (wide, F32), (wide, BF16), (SHARED, BF16), (LANES, BF16), (wide, BF16))
    return [((2, length, n), t) for n, t in columns]


def middle_kernel(heads, *refs):
    ins, outs, kept, weight_s, sum_s, spread_s, layer_s, (store,) = take(refs, (7, 6, 6, 5, 5, 3, 11, 1))
    w_in, w_out, *layer_ins, rows_in = ins
    tile, tile_out, all_rows, branch, scales, rows_out = outs
    u, w, wo, pack, *saved, load = layer_s
    spot = Spot()
    rows_in = rows_in.at[spot.s]
    weights = Weights(spot, 1, w_in, w_out, tile, tile_out, weight_s)
    total = Sum(spot, rows_in.shape[1], sum_s)
    spread = Spread(spot, rows_out, all_rows, spread_s)
    loads = loading(layer_ins[:3] + [layer_ins[3].at[0]], layer_s[:4], load)
    for copy in loads:
        copy.start()
    weights.begin()
    greet(all_places(spot))
    few = 3
    weights.start(few)
    for copy in loads:
        copy.wait()
    params = load_params(([spot.piece(spot.half, j) for j in range(2)], pack))

    @pl.loop(0, 2)
    def _(i):
        forward_rows(heads, params, total.half(i), u, w, wo, None, [total.parts, None, *saved])
        total.start(i)


        @pl.when(i == 0)
        def _():
            weights.more(3, few)
            weights.more(4, few)

    stores = loading(saved, kept, store)
    for copy in stores:
        copy.start()
    weights.more(5, few)
    total.forward()
    weights.relay(0)
    weights.relay(1)
    weights.relay(2)
    weights.share()
    layer_rows(total.finish(), rows_in, branch, scales, rows_out)
    spread.start()
    weights.shared()
    weights.relay(3)
    spread.forward()
    weights.relay(4)
    weights.relay(5)
    weights.relay_mate()
    spread.finish()
    total.close()
    weights.finish(few)
    for copy in stores:
        copy.wait()


class RowSums:
    @staticmethod
    def scratch(length):
        shape = (2, 8, length)
        return [pltpu.VMEM(shape, F32), pltpu.VMEM((7,) + shape, F32), DMA((14,)), DMA((14,))]

    def __init__(self, spot, scratch):
        self.mine, self.others, self.send, self.recv = scratch
        self.places = [spot.plane(k) for k in (1, 2, 3)] + [spot.at_twin]
        self.places += [(spot.s, spot.around[k], spot.twin) for k in (1, 2, 3)]

    def copies(self, seq):
        return [
            remote(
                self.mine.at[seq], self.others.at[j, seq],
                self.send.at[2 * j + seq], self.recv.at[2 * j + seq], place,
            )
            for j, place in enumerate(self.places)
        ]

    def start(self, seq):
        for copy in self.copies(seq):
            copy.start()

    def finish(self, seq):
        total = self.mine[seq]
        for j, copy in enumerate(self.copies(seq)):
            copy.wait_recv()
            total += self.others[j, seq]
        for copy in self.copies(seq):
            copy.wait_send()
        self.mine[seq] = total


def back_kernel(heads, *refs):
    ins, outs, first_s, last_s, second_s, spread_s, row_s, back_s, layer_s, grads_s, results, around_s, own_s, rest = take(
        refs, (18, 5, 5, 6, 6, 3, 4, 6, 11, 7, 3, 4, 4, 10)
    )
    (all_rows, all_cot, packs), tiles, kept, own_ins = take(ins, (3, 4, 6, 5))
    first_rows, tokens, grad_out, branch, scales = own_ins
    home_rows, home_grads, final, final_out, small_out = outs
    u, w, wo, pack, *saved, load = layer_s
    h_rows, h_next, payload, last_rows, last_grad, first_grad, small, send, recv, local = rest
    proj_grad, normed_out, *scratch = back_s
    spot = Spot()
    tokens, grad_out = tokens.at[spot.s], grad_out.at[spot.s]
    width = first_rows.shape[1]
    total = Sum(spot, width, first_s)
    last = RelaySum(spot, width, last_s)
    second = RelaySum(spot, width, second_s)
    spread = Spread(spot, payload, h_next, spread_s)
    sums = RowSums(spot, row_s)
    grads = Grads(spot, results, grads_s)
    around = GradsAround(spot, results, final, final_out, around_s)
    own = SmallSum(spot, own_s)
    first_core, last_core = pl.when(spot.s == 0), pl.when(spot.s == 1)
    loads = loading([all_rows, *tiles[2:], packs, all_cot], [u, w, wo, pack, h_rows], load)
    reloads = loading([*tiles[:2], *kept], [w, wo, *saved], load)
    for copy in loads:
        copy.start()
    places = [spot.plane(k) for k in (1, 2, 3)] + [spot.column((spot.z + k) % 4) for k in (1, 2, 3)]
    places += [(spot.s, spot.around[k], spot.twin) for k in (1, 2, 3)] + [spot.sibling]
    greet(places)
    for copy in loads:
        copy.wait()
    ids = [spot.piece(spot.half, j) for j in range(2)]
    params = load_params((ids, pack.at[1]))

    @pl.loop(0, 2)
    def _(i):
        seq = last.half(i)
        forward_rows(heads, params, seq, u, w, wo, h_rows, [last.parts, sums.mine, *saved])
        sums.start(seq)
        pl.when(i == 0)(lambda: last.start(0))

    last.go_on(0)

    def backward(layer, params, total, h_ref, aux_of, order):
        small[layer] = jnp.zeros(small.shape[1:], F32)

        @pl.loop(0, 2)
        def _(n):
            i = order(n)
            seq = total.half(i)
            aux = aux_of(n, seq)
            outs = (total.parts, proj_grad, normed_out)
            parts = backward_rows(heads, params, seq, h_ref, aux, saved[1:], w, wo, outs, scratch)
            add_small(small.at[layer], *parts)
            total.start(i)

    def row_aux(n, seq):
        pl.when(n == 1)(last.forward)
        sums.finish(seq)
        return aux_of_rows(sums.mine[seq])

    def column_aux(n, seq):
        pl.when(n == 0)(spread.own_half)

        @pl.when((n == 1) & (spot.s == 1))
        def _():
            own.step(1)
            grads.to_planes(5)
            grads.pass_on(1)
            grads.gather(4)
            around.shared_step(0)

        pl.when(n == 1)(spread.other_half)
        return aux_of_columns(h_next, seq, width)

    backward(1, params, total, h_rows, row_aux, lambda n: n)

    def product(layer, n):
        grads.product(layer, n, proj_grad, saved[0], normed_out, h_rows if layer else h_next)

    product(1, 4)
    product(1, 0)
    total.forward()
    last_core(lambda: grads.to_planes(4))
    for n in (1, 2, 3, 5):
        product(1, n)
    last_core(lambda: grads.to_planes(0))
    for copy in reloads:
        copy.start()
    grad, last_gain = norm_back(total.finish(), first_rows, pack[1, 7:8, :width], grad_out)
    low = grad.astype(BF16)
    last_grad[...] = low
    cross = jnp.sum(low.astype(F32) * branch[...], axis=1, keepdims=True)
    payload[:, :width] = low
    lanes = lax.broadcasted_iota(jnp.int32, (payload.shape[0], LANES), 1)
    scale_part = split_three(scales[:, 0:1]).astype(F32)
    cross_part = pltpu.roll(split_three(cross).astype(F32), 3, 1)
    payload[:, width:] = jnp.where(lanes < 3, scale_part, cross_part).astype(BF16)
    spread.start()
    add_gain(small.at[1], last_gain)
    first_core(lambda: own.begin(small[1]))

    @last_core
    def _():
        grads.pass_on(4)
        grads.to_planes(1)

    spread.forward()

    @last_core
    def _():
        own.step(0, small[1])
        grads.pass_on(0)
        for n in (2, 3):
            grads.to_planes(n)

    last.start(1)
    for copy in reloads:
        copy.wait()
    params = load_params((ids, pack.at[0]))
    backward(0, params, second, h_next, column_aux, lambda n: 1 - n)

    @last_core
    def _():
        grads.gather(0)
        around.send_part(0)
        grads.pass_on(2)

    for n in Grads.ORDER:
        product(0, n)
    second.go_on(1)
    second.go_on(0)
    last.go_on(1)

    @first_core
    def _():
        for n in (4, 0, 1):
            grads.to_planes(n)
        grads.pass_on(4)
        for n in (5, 2):
            grads.to_planes(n)
        grads.pass_on(0)
        grads.gather(4)
        around.shared_step(0)
        grads.to_planes(3)
        grads.pass_on(1)
        grads.gather(0)
        around.send_part(0)

    @last_core
    def _():
        grads.gather(1)
        around.send_part(1)
        grads.pass_on(3)

    second.forward()

    @first_core
    def _():
        grads.pass_on(2)
        grads.gather(5)
        around.send_out()
        grads.gather(1)
        around.send_part(1)
        around.shared_step(1)
        around.pass_part(0)
        grads.pass_on(3)

    @last_core
    def _():
        grads.gather(5)
        around.send_out()
        grads.gather(2)
        around.send_part(2)
        around.pass_part(0)
        grads.gather(3)
        around.send_part(3)
        around.shared_step(1)
        around.pass_part(1)

    grad, first_gain = norm_back(second.finish(), tokens, pack[0, 7:8, :width], last_grad)
    first_grad[...] = grad.astype(BF16)
    layers = ((first_rows, first_grad), (last_rows, last_grad))

    def home_copies(s):
        copies = []
        for n, target in enumerate((home_rows, home_grads)):
            copies.append(remote(layers[1 - s][n], target.at[s], send.at[n], recv.at[n], spot.sibling))
            copies.append(pltpu.make_async_copy(layers[s][n], target.at[s], local.at[n]))
        return copies

    add_gain(small.at[0], first_gain)
    last_core(lambda: own.begin(small[0]))

    @first_core
    def _():
        grads.gather(2)
        around.send_part(2)
        own.step(0, small[0])
        grads.gather(3)
        around.send_part(3)
        around.pass_out()
        around.pass_part(1)
        own.step(1)
        around.pass_part(2)
        around.shared_step(2)

    layer_rows(last.finish(), first_rows, None, None, last_rows)
    for s in range(2):

        @pl.when(spot.s == s)
        def _(s=s):
            for copy in home_copies(s):
                copy.start()

    first_core(lambda: around.pass_part(3))

    @last_core
    def _():
        around.pass_out()
        for n in (2, 3):
            around.pass_part(n)
        around.shared_step(2)

    own.finish(small_out)
    around.finish()
    for n in range(5):
        grads.sent(n)
    grads.finish()
    for s in range(2):

        @pl.when(spot.s == s)
        def _(s=s):
            for copy in home_copies(s):
                copy.wait()

    total.close()
    last.close()
    second.close()
    spread.close()


def comm_call(kernel, collective, ins, in_specs, outs, out_specs, scratch, name):
    return pl.pallas_call(
        kernel,
        out_shape=[jax.ShapeDtypeStruct(s, t) for s, t in outs],
        in_specs=in_specs,
        out_specs=out_specs,
        scratch_shapes=scratch,
        compiler_params=pltpu.CompilerParams(
            collective_id=collective, has_side_effects=True, vmem_limit_bytes=60 * 1024 * 1024
        ),
        name=name,
    )(*ins)


def fast_shards(
    tokens, cotangent, norm_gain, w_in, conv_weight, conv_bias, dt_bias, a_log, skip_gain, gate_gain, w_out
):
    span, width = tokens.shape[2:]
    heads = HEADS // 8
    wide = heads * HEADDIM
    columns = 2 * wide + SHARED + HEADS
    shard = w_in.shape[1]
    rows_in = w_in[0].T
    pack_shape = (8, INNER // THIRD * PIECE + SHARED)
    group = (2, 4 * span, width)
    weight_outs = [((columns, width), BF16), ((wide, width), BF16)]
    weight_s = Weights.scratch(columns, shard, width)
    payload = width + LANES
    tile, tile_out, packs, all_rows, all_cot = comm_call(
        open_kernel, 1,
        [
            rows_in, w_out[0], tokens[:, 0], cotangent[:, 0], conv_weight[0], conv_bias, gate_gain, skip_gain,
            norm_gain, dt_bias, a_log,
        ],
        [ANY] * 4 + [VMEM] * 7,
        weight_outs + [((2,) + pack_shape, F32), (group, BF16), (group, BF16)], [ANY] * 5,
        weight_s + Spread.SEMS + Spread.SEMS
        + [pltpu.VMEM((span, width), BF16)] * 2 + [pltpu.VMEM(pack_shape, F32), DMA((2,)), DMA, DMA, DMA],
        "open",
    )
    length = 4 * span
    rows_spec = ((span, width), BF16)
    layer_s = [
        pltpu.VMEM((2, length, width), BF16), pltpu.VMEM((columns, width), BF16),
        pltpu.VMEM((wide, width), BF16), pltpu.VMEM(pack_shape, F32),
    ]
    kept_shapes = saved_shapes(length, width, wide)
    kept_s = [pltpu.VMEM(*k) for k in kept_shapes]
    back_s = [pltpu.VMEM((2, length, columns), BF16), pltpu.VMEM((2, length, wide), BF16)]
    back_s += backward_scratch(length, wide)
    results = Grads.results(shard, width)
    sum_s = Sum.scratch(span, width)
    first_tiles = [tile, tile_out]
    tile, tile_out, all_rows, branch, scales, rows, *kept = comm_call(
        partial(middle_kernel, heads), 2,
        [rows_in, w_out[0], all_rows, tile, tile_out, packs, tokens[:, 0]], [ANY] * 6 + [VMEM],
        weight_outs + [(group, BF16), ((span, width), F32), ((span, LANES), F32), rows_spec] + kept_shapes,
        [ANY] * 3 + [VMEM] * 3 + [ANY] * 6,
        weight_s + Sum.scratch(span, payload) + Spread.SEMS + layer_s + kept_s + [DMA((4,)), DMA((6,))],
        "middle",
    )
    home_rows, home_grads, final, final_out, small = comm_call(
        partial(back_kernel, heads), 3,
        [
            all_rows, all_cot, packs, *first_tiles, tile, tile_out, *kept,
            rows, tokens[:, 0], cotangent[:, 0], branch, scales,
        ],
        [ANY] * 13 + [VMEM] * 5,
        [
            ((2, span, width), BF16), ((2, span, width), BF16),
            ((2 * INNER + SHARED + HEADS, shard), BF16), (w_out.shape[1:], BF16), (pack_shape, F32),
        ],
        [ANY] * 4 + [VMEM],
        sum_s + RelaySum.scratch(span, payload) + RelaySum.scratch(span, width) + Spread.SEMS + RowSums.scratch(length) + back_s
        + layer_s[:3] + [pltpu.VMEM((2,) + pack_shape, F32)] + kept_s + [DMA((8,))]
        + Grads.scratch(shard, columns, wide, width) + [pltpu.VMEM(*r) for r in results]
        + GradsAround.scratch(shard) + SmallSum.scratch()
        + [
            pltpu.VMEM((2, length, width), BF16), pltpu.VMEM((2, length, payload), BF16),
            pltpu.VMEM((span, payload), BF16), *[pltpu.VMEM((span, width), BF16)] * 3,
            pltpu.VMEM((2,) + SmallSum.SHAPE, F32), DMA((2,)), DMA((2,)), DMA((2,)),
        ],
        "back",
    )
    grad_in, grad_out, gain, conv, bias, shift, rate, skip, gate = finish_call(final, final_out, small)
    return (
        home_rows[None, :, None], home_grads[None, :, None], gain, grad_in.T[None], conv[None],
        bias, shift, rate, skip, gate, grad_out[None],
    )


def finish_kernel(final, final_out, small, grad_in, grad_out, gain, conv, bias, shift, rate, skip, gate):
    grad_in[...] = final[...].astype(F32)
    step = pl.program_id(0)
    grad_out[...] = final_out[...].astype(F32)

    @pl.when(step == 0)
    def _():
        gain[...] = small[7:8, :GAIN_END]
        shift[...] = small[7:8, DT_AT : DT_AT + HEADS]
        rate[...] = small[7:8, RATE_AT : RATE_AT + HEADS]
        heads = []
        for p in range(INNER // THIRD):
            source, target = slice(p * PIECE, p * PIECE + THIRD), slice(p * THIRD, (p + 1) * THIRD)
            conv[:, target] = small[0:CONV, source]
            bias[:, target] = small[CONV : CONV + 1, source]
            gate[:, target] = small[6:7, source]
            for h in range(3):
                part = small[5:6, p * PIECE + h * HEADDIM : p * PIECE + (h + 1) * HEADDIM]
                heads.append(jnp.sum(part, axis=1, keepdims=True))
        skip[...] = jnp.concatenate(heads, axis=1)
        conv[:, INNER:] = small[0:CONV, -SHARED:]
        bias[:, INNER:] = small[CONV : CONV + 1, -SHARED:]


def finish_call(final, final_out, small):
    rows, shard = final.shape
    out_rows, width = final_out.shape
    steps = 3
    block, out_block = -(-rows // (16 * steps)) * 16, out_rows // steps
    smalls = [(1, GAIN_END), (CONV, XBC), (1, XBC), (1, HEADS), (1, HEADS), (1, HEADS), (1, INNER)]

    def in_block(i):
        return (i, 0)

    def same(i):
        return (0, 0)

    return pl.pallas_call(
        finish_kernel,
        grid=(steps,),
        out_shape=[jax.ShapeDtypeStruct(s, F32) for s in [final.shape, final_out.shape] + smalls],
        in_specs=[
            pl.BlockSpec((block, shard), in_block),
            pl.BlockSpec((out_block, width), in_block),
            pl.BlockSpec(small.shape, same),
        ],
        out_specs=[
            pl.BlockSpec((block, shard), in_block),
            pl.BlockSpec((out_block, width), in_block),
        ]
        + [pl.BlockSpec(s, same) for s in smalls],
        compiler_params=pltpu.CompilerParams(**PARAMS),
        name="finish",
    )(final, final_out, small)


def shards(
    tokens, cotangent, norm_gain, w_in, conv_weight, conv_bias, dt_bias, a_log, skip_gain, gate_gain, w_out
):
    section = lax.axis_index("section")
    place = lax.axis_index("seq")
    depth = lax.axis_index("fsdp")
    plan = Plan(lax.axis_size("seq"), lax.axis_size("fsdp"))
    half = depth // plan.mates
    micro, _, span, width = tokens.shape
    layers = lax.axis_size("section")
    wide, channels, heads = plan.wide, plan.channels, plan.heads

    shard = w_in[0]
    gate_part = widened(plan.take(shard[:, :INNER], 1, place), 2, wide)
    x_part = widened(plan.take(shard[:, INNER : 2 * INNER], 1, place), 2, wide)
    shared_part = jnp.broadcast_to(
        shard[:, 2 * INNER : INNER + XBC], (plan.halves, shard.shape[0], SHARED)
    )
    dt_part = widened(plan.take(shard[:, INNER + XBC :], 1, place), 2, LANES)
    tile = jnp.concatenate([gate_part, x_part, shared_part, dt_part], axis=2)
    tile = jnp.repeat(tile, plan.mates, axis=0)
    tile = lax.all_to_all(tile, "fsdp", 0, 0, tiled=True).reshape(width, -1).T
    w_tiles = lax.all_gather(tile, "section", axis=0)
    if plan.pieces == plan.mates:
        piece = w_out[0].reshape(plan.seq, -1, width)
        piece = lax.dynamic_index_in_dim(piece, place, 0, False)
        rows_out = lax.all_gather(
            piece, "fsdp", axis=0, tiled=True, axis_index_groups=plan.mate_groups
        )
    else:
        rows_out = lax.all_gather(w_out[0], "fsdp", axis=0, tiled=True)
        rows_out = lax.dynamic_index_in_dim(plan.take(rows_out, 0, place), half, 0, False)
    wo_tiles = lax.all_gather(widened(rows_out, 0, wide), "section", axis=0)

    def own(array, axis, size):
        part = lax.dynamic_index_in_dim(plan.take(array, axis, place), half, 0, False)
        return widened(part, axis, size)

    skip_wide = jnp.repeat(skip_gain[0], HEADDIM)[None]
    by_channel = jnp.concatenate(
        [conv_weight[0, :, :INNER], conv_bias[:, :INNER], skip_wide, gate_gain, jnp.zeros((1, INNER))], 0
    )
    by_channel = own(by_channel, 1, wide)
    by_shared = jnp.concatenate(
        [conv_weight[0, :, INNER:], conv_bias[:, INNER:], jnp.zeros((3, SHARED))], 0
    )
    by_head = jnp.concatenate([dt_bias, a_log, jnp.zeros((6, HEADS))], 0)
    by_head = own(by_head, 1, LANES)
    smalls = jnp.concatenate(
        [by_channel.ravel(), by_shared.ravel(), by_head.ravel(), norm_gain[0]]
    )
    smalls = lax.all_gather(smalls, "section", axis=0)
    cuts = [8 * wide, 8 * (wide + SHARED), 8 * (wide + SHARED + LANES)]
    params = []
    for l in range(layers):
        ch, bc, dtp, gain = jnp.split(smalls[l], cuts)
        params.append((gain[None], ch.reshape(8, -1), bc.reshape(8, -1), dtp.reshape(8, -1)))

    def gather_rows(own_rows):
        rows = lax.all_gather(own_rows, "seq", axis=0, tiled=True)
        if plan.halves == 1:
            return rows[None]
        return lax.all_gather(rows, "fsdp", axis=0, axis_index_groups=plan.peer_groups)

    def sum_rows(parts):
        if plan.halves == 1:
            rows = parts[0]
        else:
            rows = lax.psum_scatter(
                parts, "fsdp", scatter_dimension=0, axis_index_groups=plan.peer_groups
            )
        return lax.psum_scatter(rows, "seq", scatter_dimension=0, tiled=True)

    own_tokens = lax.dynamic_index_in_dim(tokens, section, 0, False)[0]
    own_cot = lax.dynamic_index_in_dim(cotangent, section, 0, False)[0]
    inputs, outputs, branch, saved, scales = [own_tokens], [], [], [], []
    for l in range(layers):
        rows = gather_rows(inputs[l])
        parts, square, normed, *kept = run_forward(
            heads, wide, rows, w_tiles[l], wo_tiles[l], params[l]
        )
        saved.append((normed, kept))
        total = sum_rows(parts).astype(F32)
        square = sum_rows(square)[:, :1]
        scale = lax.rsqrt(square / INNER + NORM_EPS)
        branch.append(total * scale)
        scales.append(scale)
        outputs.append((inputs[l].astype(F32) + branch[l]).astype(BF16))
        inputs.append(outputs[l])
    grads_in, small_grads = [None] * layers, [None] * layers
    w_grads, wo_grads = [None] * layers, [None] * layers
    grad_rows = own_cot
    for l in reversed(range(layers)):
        rdot = jnp.sum(grad_rows.astype(F32) * branch[l], axis=-1, keepdims=True)
        aux = widened(jnp.concatenate([scales[l], rdot], axis=1), 1, LANES)
        all_grads = gather_rows(grad_rows)
        aux = gather_rows(aux)
        normed, kept = saved[l]
        parts, proj_grad, normed_out, g_ch, g_bc, g_dt = run_backward(
            heads, wide, all_grads, aux, kept, w_tiles[l], wo_tiles[l], params[l]
        )
        w_grads[l] = dot_tn(normed.reshape(-1, width), proj_grad.reshape(-1, proj_grad.shape[-1])).astype(BF16)
        wo_grads[l] = dot_tn(normed_out.reshape(-1, wide), all_grads.reshape(-1, width)).astype(BF16)
        grad_normed = sum_rows(parts).astype(F32)
        rows = inputs[l].astype(F32)
        scale = lax.rsqrt(jnp.mean(rows * rows, axis=-1, keepdims=True) + NORM_EPS)
        scaled = rows * scale
        g_gain = jnp.sum(grad_normed * scaled, axis=0)
        pulled = grad_normed * params[l][0]
        inner = jnp.mean(pulled * scaled, axis=-1, keepdims=True)
        grad = scale * (pulled - scaled * inner) + grad_rows.astype(F32)
        grad_rows = grad.astype(BF16)
        grads_in[l] = grad_rows

        def placed(value, size):
            value = value[..., :size]
            full = jnp.zeros((plan.seq, plan.halves) + value.shape, F32)
            full = lax.dynamic_update_slice(full, value[None, None], (place, half, 0, 0))
            return plan.put(full, 1)

        by_channel = placed(g_ch, channels)
        by_head = placed(g_dt, heads)
        skip = by_channel[5].reshape(HEADS, HEADDIM).sum(-1)
        small_grads[l] = jnp.concatenate(
            [
                g_gain, by_channel[:5].ravel(), g_bc[:5].ravel(), by_head[0], by_head[1], skip, by_channel[6]
            ]
        )

    smalls = lax.psum(jnp.stack(small_grads), ("section", "seq", "fsdp"))
    smalls = lax.dynamic_index_in_dim(smalls, section, 0, False)
    cuts, at = [], 0
    for size in (width, (CONV + 1) * INNER, (CONV + 1) * SHARED, HEADS, HEADS, HEADS):
        at += size
        cuts.append(at)
    g_gain, g_x, g_bc, g_shift, g_rate, g_skip, g_gate = jnp.split(smalls, cuts)
    conv_rows = jnp.concatenate([g_x.reshape(CONV + 1, -1), g_bc.reshape(CONV + 1, -1)], axis=1)

    w_grad = lax.psum_scatter(jnp.stack(w_grads), "section", scatter_dimension=0)
    w_grad = lax.all_to_all(w_grad, "fsdp", 0, 0, tiled=True)
    w_grad = w_grad.reshape(plan.halves, plan.mates, -1, w_grad.shape[-1]).astype(F32).sum(1)
    shared_grad = lax.psum(w_grad[..., 2 * wide : 2 * wide + SHARED].sum(0), "seq")
    head_grads = jnp.concatenate(
        [
            w_grad[..., :channels],
            w_grad[..., wide : wide + channels],
            w_grad[..., 2 * wide + SHARED : 2 * wide + SHARED + heads],
        ],
        axis=-1,
    ).astype(BF16)
    head_grads = lax.all_gather(head_grads, "seq", axis=0)
    grad_w_in = jnp.concatenate(
        [
            plan.put(head_grads[..., :channels], 1),
            plan.put(head_grads[..., channels : 2 * channels], 1),
            shared_grad.astype(BF16),
            plan.put(head_grads[..., 2 * channels :], 1),
        ],
        axis=-1,
    ).astype(F32)
    wo_grad = lax.psum_scatter(jnp.stack(wo_grads)[:, :channels], "section", scatter_dimension=0)
    if plan.pieces == plan.mates:
        wo_grad = lax.psum_scatter(
            wo_grad, "fsdp", scatter_dimension=0, tiled=True, axis_index_groups=plan.mate_groups
        )
        wo_grad = lax.all_gather(wo_grad, "seq", axis=0, tiled=True)
    else:
        full = jnp.zeros((plan.seq, plan.halves) + wo_grad.shape, BF16)
        full = lax.dynamic_update_slice(full, wo_grad[None, None], (place, half, 0, 0))
        full = plan.put(full, 0)
        wo_grad = lax.psum_scatter(full, "fsdp", scatter_dimension=0, tiled=True)
        wo_grad = lax.psum(wo_grad, "seq")

    def home(per_layer):
        return lax.all_to_all(jnp.stack(per_layer), "section", 0, 0, tiled=True)[None, :, None]

    return (
        home(outputs),
        home(grads_in),
        g_gain[None],
        grad_w_in[None],
        conv_rows[None, :CONV],
        conv_rows[CONV:],
        g_shift[None],
        g_rate[None],
        g_skip[None],
        g_gate[None],
        wo_grad.astype(F32)[None],
    )


def solution(mesh):
    shape = tuple(mesh.shape[a] for a in ("section", "seq", "fsdp"))
    return jax.shard_map(
        fast_shards if shape == (2, 4, 4) else shards,
        mesh=mesh,
        in_specs=(
            P(None, "fsdp", "seq", None),
            P(None, "fsdp", "seq", None),
            P("section", None),
            P("section", "fsdp", None),
            P("section", None, None),
            P("section", None),
            P("section", None),
            P("section", None),
            P("section", None),
            P("section", None),
            P("section", "fsdp", None),
        ),
        out_specs=(
            P("section", None, "fsdp", "seq", None),
            P("section", None, "fsdp", "seq", None),
            P("section", None),
            P("section", "fsdp", None),
            P("section", None, None),
            P("section", None),
            P("section", None),
            P("section", None),
            P("section", None),
            P("section", None),
            P("section", "fsdp", None),
        ),
        check_vma=False,
    )
```

```python
from functools import partial

import jax
import jax.numpy as jnp
from jax import lax
from jax.experimental import pallas as pl
from jax.experimental.pallas import tpu as pltpu
from jax.sharding import PartitionSpec as P

HEADS = 48
HEADDIM = 64
STATE = 128
CONV = 4
SPAN = 256
INNER = 3072
XBC = 3328
SHARED = 2 * STATE
LANES = 128
THIRD = 192
PIECE = 256
GAIN_END = 1536
DT_AT = 1536
RATE_AT = DT_AT + LANES
NORM_EPS = 1e-05
HIGHEST = lax.Precision.HIGHEST
BF16 = jnp.bfloat16
F32 = jnp.float32


def take(refs, counts):
    refs = list(refs)
    return [[refs.pop(0) for _ in range(n)] for n in counts]


def dot(left, right, contract=((1,), (0,)), precision=None):
    return lax.dot_general(
        left, right, (contract, ((), ())), preferred_element_type=F32, precision=precision
    )


def dot_nt(left, right):
    return dot(left, right, ((1,), (1,)))


def dot_tn(left, right):
    return dot(left, right, ((0,), (0,)))


def sigmoid(value):
    return 1.0 / (1.0 + jnp.exp(-value))


def shifted(value, distance):
    if distance == 0:
        return value
    length = value.shape[0]
    rows = lax.broadcasted_iota(jnp.int32, value.shape, 0)
    moved = pltpu.roll(value, distance % length, 0)
    if distance > 0:
        return jnp.where(rows >= distance, moved, 0.0)
    return jnp.where(rows < length + distance, moved, 0.0)


def conv_sum(raw, taps):
    total = taps[CONV : CONV + 1]
    for k in range(CONV):
        total = total + taps[k : k + 1] * shifted(raw, CONV - 1 - k)
    return total


def conv_back(grad, raw, taps):
    grad_raw = 0.0
    rows = []
    for k in range(CONV):
        grad_raw = grad_raw + taps[k : k + 1] * shifted(grad, -(CONV - 1 - k))
        rows.append(jnp.sum(grad * shifted(raw, CONV - 1 - k), axis=0, keepdims=True))
    rows.append(jnp.sum(grad, axis=0, keepdims=True))
    return grad_raw, rows


def stacked(rows, count):
    width = rows[0].shape[1]
    short = count - len(rows)
    return jnp.concatenate(rows + [jnp.zeros((short, width), F32)], axis=0)


def triangles():
    row_ids = lax.broadcasted_iota(jnp.int32, (SPAN, SPAN), 0)
    col_ids = lax.broadcasted_iota(jnp.int32, (SPAN, SPAN), 1)
    return row_ids >= col_ids


def step_sizes(dt_raw, dt_row):
    shift = dt_raw + dt_row
    step = jnp.maximum(shift, 0.0) + jnp.log1p(jnp.exp(-jnp.abs(shift)))
    return step, sigmoid(shift)


def low_half():
    return lax.broadcasted_iota(jnp.int32, (SPAN, LANES), 1) < HEADDIM


def head_lanes(h):
    lanes = lax.broadcasted_iota(jnp.int32, (1, LANES), 1)
    return (lanes < HEADDIM) if h % 2 == 0 else (lanes >= HEADDIM)


def split_three(value):
    lanes = lax.broadcasted_iota(jnp.int32, (value.shape[0], LANES), 1)
    result = jnp.zeros((value.shape[0], LANES), F32)
    for k in range(3):
        part = value.astype(BF16).astype(F32)
        result = jnp.where(lanes == k, part, result)
        value = value - part
    return result.astype(BF16)


def selection(ids):
    rows = lax.broadcasted_iota(jnp.int32, (HEADS, LANES), 0)
    columns = lax.broadcasted_iota(jnp.int32, (HEADS, LANES), 1)
    target = jnp.full((HEADS, LANES), -1, jnp.int32)
    for j in range(2):
        here = (columns >= 3 * j) & (columns < 3 * j + 3)
        target = jnp.where(here, columns + 3 * (ids[j] - j), target)
    return (rows == target).astype(F32)


def piece_lanes(ids, j):
    return pl.ds(pl.multiple_of(ids[j] * PIECE, PIECE), PIECE)


def load_params(refs):
    if len(refs) == 2:
        ids, pack_ref = refs
        sel = selection(ids)
        ch = jnp.concatenate([pack_ref[:, piece_lanes(ids, j)][:, :THIRD] for j in range(2)], axis=1)
        rows = [pack_ref[7:8, at : at + HEADS] for at in (DT_AT, RATE_AT)]
        dtp = dot(stacked(rows, 8), sel, precision=HIGHEST)
        return pack_ref[7:8, :GAIN_END], ch, pack_ref[:, -SHARED:], dtp, sel.astype(BF16)
    gain_ref, ch_ref, bc_ref, dtp_ref = refs
    return gain_ref[...], ch_ref[...], bc_ref[...], dtp_ref[...], None


def forward_kernel(heads, *refs):
    u_ref, w_ref, wo_ref, *refs = refs
    forward_rows(heads, load_params(refs[:4]), 0, u_ref, w_ref, wo_ref, None, refs[4:])


def forward_rows(heads, params, i, u_ref, w_ref, wo_ref, h_ref, outs):
    gain, ch, bc, dtp, sel = params
    out_ref, sums_ref, normed_ref, gate_ref, xraw_ref, bcraw_ref, dtraw_ref, mixed_ref = outs
    length, width = u_ref.shape[1:]
    wide = ch.shape[1]
    blocks = length // SPAN
    rows = u_ref[i].astype(F32)
    scale = lax.rsqrt(jnp.mean(rows * rows, axis=-1, keepdims=True) + NORM_EPS)
    normed = (rows * scale * gain).astype(BF16)
    normed_ref[i] = normed
    gate = dot_nt(normed, w_ref[:wide])
    gate_ref[i] = gate
    x_raw = dot_nt(normed, w_ref[wide : 2 * wide]).astype(BF16)
    xraw_ref[i] = x_raw
    rest = dot_nt(normed, w_ref[2 * wide :]).astype(BF16)
    bcraw_ref[i] = rest[:, :SHARED]
    dt_raw = rest[:, SHARED:]
    if sel is not None:
        dt_raw = dot(dt_raw, sel).astype(BF16)
    dtraw_ref[i] = dt_raw
    conv_x = conv_sum(x_raw.astype(F32), ch)
    act_x = (conv_x * sigmoid(conv_x)).astype(BF16)
    conv_bc = conv_sum(rest[:, :SHARED].astype(F32), bc)
    act_bc = (conv_bc * sigmoid(conv_bc)).astype(BF16)
    step, _ = step_sizes(dt_raw.astype(F32), dtp[0:1])
    rate = jnp.exp(dtp[1:2])
    causal = triangles()
    ones = causal.astype(F32)
    lower = low_half()
    carries = [None] * heads
    for b in range(blocks):
        span = slice(b * SPAN, (b + 1) * SPAN)
        step_b = step[span]
        decay = -dot(ones, rate * step_b, precision=HIGHEST)
        decay_t, step_t = decay.T, step_b.T
        b_in, c_out = act_bc[span, :STATE], act_bc[span, STATE:]
        scores = dot_nt(c_out, b_in)
        for first in range(0, heads, 2):
            lanes = slice(first * HEADDIM, first * HEADDIM + LANES)
            x_pair = act_x[span, lanes]
            parts = []
            for h in range(first, min(first + 2, heads)):
                gap = decay[:, h : h + 1] - decay_t[h : h + 1]
                mask = jnp.exp(jnp.where(causal, gap, -1e30))
                weights = (scores * mask * step_t[h : h + 1]).astype(BF16)
                part = dot(weights, x_pair)
                if carries[h] is not None:
                    part += jnp.exp(decay[:, h : h + 1]) * dot(c_out, carries[h].astype(BF16))
                if b + 1 < blocks:
                    last = decay[SPAN - 1 :, h : h + 1]
                    tail = jnp.exp(last - decay[:, h : h + 1]) * step_b[:, h : h + 1]
                    shaped = (b_in.astype(F32) * tail).astype(BF16)
                    fresh = dot_tn(shaped, x_pair)
                    if carries[h] is not None:
                        fresh += jnp.exp(last) * carries[h]
                    carries[h] = fresh
                parts.append(part)
            if len(parts) == 1:
                parts.append(jnp.zeros_like(parts[0]))
            within = jnp.where(lower, parts[0], parts[1])
            mixed = within + ch[5:6, lanes] * x_pair.astype(F32)
            mixed_ref[i, span, lanes] = mixed.astype(BF16)
    gated = mixed_ref[i].astype(F32) * (gate * sigmoid(gate))
    square = jnp.sum(gated * gated, axis=-1, keepdims=True)
    scaled = gated * ch[6:7]
    out_ref[i, :, :width] = dot(scaled.astype(BF16), wo_ref[...]).astype(BF16)
    if sel is None:
        sums_ref[i] = jnp.broadcast_to(square, sums_ref.shape[1:])
        return
    out_ref[i, :, width:] = split_three(square)
    if h_ref is not None:
        grad_no = dot_nt(h_ref[i], wo_ref[...])
        cross = jnp.sum(grad_no * scaled, axis=-1, keepdims=True)
        lane_ids = lax.broadcasted_iota(jnp.int32, (length, LANES), 1)
        both = jnp.where(lane_ids == 0, square, jnp.where(lane_ids == 1, cross, 0.0))
        sums_ref[i] = both.T[:8]


def backward_kernel(heads, *refs):
    h_ref, aux_ref, *refs = refs
    saved, (w_ref, wo_ref), params, outs, sum_refs, scratch = take(refs, (5, 2, 4, 3, 3, 4))
    params = load_params(params)

    def aux():
        return aux_ref[0, :, 0:1], aux_ref[0, :, 1:2]

    sums = backward_rows(heads, params, 0, h_ref, aux, saved, w_ref, wo_ref, outs, scratch)
    for ref, value in zip(sum_refs, sums):

        @pl.when(pl.program_id(0) == 0)
        def _(ref=ref, value=value):
            ref[...] = value

        @pl.when(pl.program_id(0) > 0)
        def _(ref=ref, value=value):
            ref[...] += value


def aux_of_columns(h_ref, i, width):
    aux = h_ref[i, :, width:].astype(F32)
    return aux[:, 0:1] + aux[:, 1:2] + aux[:, 2:3], aux[:, 3:4] + aux[:, 4:5] + aux[:, 5:6]


def aux_of_rows(sums):
    aux = jnp.concatenate([sums, jnp.zeros((LANES - 8, sums.shape[1]), F32)], axis=0).T
    scale = lax.rsqrt(aux[:, 0:1] * (1.0 / INNER) + NORM_EPS)
    return scale, aux[:, 1:2] * scale


def backward_rows(heads, params, i, h_ref, aux, saved, w_ref, wo_ref, outs, scratch):
    _, ch, bc, dtp, sel = params
    gate_ref, xraw_ref, bcraw_ref, dtraw_ref, mixed_ref = saved
    dn_ref, pg_ref, no_ref = outs
    dmix_s, dx_s, dbc_s, ddt_s = scratch
    length, width = dn_ref.shape[1:]
    wide = ch.shape[1]
    blocks = length // SPAN
    x_raw = xraw_ref[i].astype(F32)
    bc_raw = bcraw_ref[i].astype(F32)
    conv_x = conv_sum(x_raw, ch)
    sig_x = sigmoid(conv_x)
    act_x = (conv_x * sig_x).astype(BF16)
    conv_bc = conv_sum(bc_raw, bc)
    sig_bc = sigmoid(conv_bc)
    act_bc = (conv_bc * sig_bc).astype(BF16)
    step, slope = step_sizes(dtraw_ref[i].astype(F32), dtp[0:1])
    rate = jnp.exp(dtp[1:2])
    causal = triangles()
    ones = causal.astype(F32)
    lower = low_half()
    lane_ids = lax.broadcasted_iota(jnp.int32, (SPAN, LANES), 1)
    last_row = lax.broadcasted_iota(jnp.int32, (SPAN, 1), 0) == SPAN - 1
    decays = []
    for b in range(blocks):
        decays.append(-dot(ones, rate * step[b * SPAN : (b + 1) * SPAN], precision=HIGHEST))
    entering = [[None] * heads for _ in range(blocks)]
    for b in range(blocks - 1):
        span = slice(b * SPAN, (b + 1) * SPAN)
        b_in = act_bc[span, :STATE].astype(F32)
        for h in range(heads):
            lanes = slice(h // 2 * LANES, h // 2 * LANES + LANES)
            column = decays[b][:, h : h + 1]
            last = column[SPAN - 1 :]
            tail = jnp.exp(last - column) * step[span, h : h + 1]
            fresh = dot_tn((b_in * tail).astype(BF16), act_x[span, lanes])
            if entering[b][h] is not None:
                fresh += jnp.exp(last) * entering[b][h]
            entering[b + 1][h] = fresh

    scale, rdot = aux()
    h_rows = h_ref[i, :, :width]
    gate = gate_ref[i]
    mixed = mixed_ref[i].astype(F32)
    sig = sigmoid(gate)
    silu = gate * sig
    gated = mixed * silu
    gain = ch[6:7]
    grad_no = dot_nt(h_rows, wo_ref[...])
    grad_g = scale * (gain * grad_no) - gated * (scale * scale * (1.0 / INNER) * rdot)
    scaled = gated * scale
    no_ref[i] = (scaled * gain).astype(BF16)
    gain_row = jnp.sum(grad_no * scaled, axis=0, keepdims=True)
    dmix_s[...] = (grad_g * silu).astype(BF16)
    pg_ref[i, :, :wide] = (grad_g * mixed * (sig * (1.0 + gate * (1.0 - sig)))).astype(BF16)

    leaving = [None] * heads
    rate_row = jnp.zeros((1, LANES), F32)
    for b in reversed(range(blocks)):
        span = slice(b * SPAN, (b + 1) * SPAN)
        step_b, decay = step[span], decays[b]
        decay_t, step_t = decay.T, step_b.T
        b_in, c_out = act_bc[span, :STATE], act_bc[span, STATE:]
        scores = dot_nt(c_out, b_in)
        grad_scores = jnp.zeros((SPAN, SPAN), F32)
        grad_b = jnp.zeros((SPAN, STATE), F32)
        grad_c = jnp.zeros((SPAN, STATE), F32)
        row_sums = jnp.zeros((SPAN, LANES), F32)
        grad_step = jnp.zeros((SPAN, LANES), F32)
        col_rows = []
        for first in range(0, heads, 2):
            lanes = slice(first * HEADDIM, first * HEADDIM + LANES)
            x_pair = act_x[span, lanes]
            grad_pair = dmix_s[span, lanes]
            parts = []
            for h in range(first, min(first + 2, heads)):
                own = head_lanes(h)
                grad_own = jnp.where(own, grad_pair, jnp.zeros((), BF16))
                column = decay[:, h : h + 1]
                mask = jnp.exp(jnp.where(causal, column - decay_t[h : h + 1], -1e30))
                spread = mask * step_t[h : h + 1]
                weights = (scores * spread).astype(BF16)
                part = dot_tn(weights, grad_pair)
                grad_w = dot_nt(grad_own, x_pair)
                grad_scores += grad_w * spread
                pulled = grad_w * (scores * mask)
                col_rows.append(jnp.sum(pulled, axis=0, keepdims=True))
                row_sum = jnp.sum(pulled * step_t[h : h + 1], axis=1, keepdims=True)
                if entering[b][h] is not None:
                    carry = entering[b][h].astype(BF16)
                    grown = jnp.exp(column)
                    grad_grown = grad_own.astype(F32) * grown
                    grad_c += dot_nt(grad_grown.astype(BF16), carry)
                    grad_carry = dot_tn(c_out, grad_grown.astype(BF16))
                    row_sum += jnp.sum(grad_grown * dot(c_out, carry), axis=1, keepdims=True)
                else:
                    grad_carry = None
                if leaving[h] is not None:
                    last = column[SPAN - 1 :]
                    fade = jnp.exp(last - column)
                    tail = fade * step_b[:, h : h + 1]
                    b_wide = b_in.astype(F32)
                    grad_state = leaving[h].astype(BF16)
                    grad_shaped = dot_nt(x_pair, grad_state)
                    part += dot((b_wide * tail).astype(BF16), grad_state)
                    grad_b += grad_shaped * tail
                    grad_tail = jnp.sum(grad_shaped * b_wide, axis=1, keepdims=True)
                    grad_step += jnp.where(lane_ids == h, grad_tail * fade, 0.0)
                    moved = grad_tail * tail
                    total = jnp.sum(moved, axis=0, keepdims=True)
                    if entering[b][h] is not None:
                        faded = jnp.exp(last) * leaving[h]
                        kept = jnp.sum(faded * entering[b][h], axis=1, keepdims=True)
                        total += jnp.sum(kept, axis=0, keepdims=True)
                        grad_carry += faded
                    row_sum += jnp.where(last_row, total, 0.0) - moved
                leaving[h] = grad_carry
                row_sums += jnp.where(lane_ids == h, row_sum, 0.0)
                parts.append(part)
            if len(parts) == 1:
                parts.append(jnp.zeros_like(parts[0]))
            grad_x = jnp.where(lower, parts[0], parts[1])
            dx_s[span, lanes] = grad_x + ch[5:6, lanes] * grad_pair.astype(F32)
        col_sums = stacked(col_rows, LANES).T
        low_scores = grad_scores.astype(BF16)
        dbc_s[span, :STATE] = grad_b + dot_tn(low_scores, c_out)
        dbc_s[span, STATE:] = grad_c + dot(low_scores, b_in)
        grad_decay = dot(
            ones, row_sums - step_b * col_sums, ((0,), (0,)), precision=HIGHEST
        )
        ddt_s[span] = col_sums + grad_step - rate * grad_decay
        rate_row -= jnp.sum(grad_decay * step_b, axis=0, keepdims=True)

    skip_row = jnp.sum(dmix_s[...].astype(F32) * act_x.astype(F32), axis=0, keepdims=True)
    grad_conv = dx_s[...] * (sig_x * (1.0 + conv_x * (1.0 - sig_x)))
    grad_raw, ch_rows = conv_back(grad_conv, x_raw, ch)
    pg_ref[i, :, wide : 2 * wide] = grad_raw.astype(BF16)
    grad_conv = dbc_s[...] * (sig_bc * (1.0 + conv_bc * (1.0 - sig_bc)))
    grad_raw, bc_rows = conv_back(grad_conv, bc_raw, bc)
    pg_ref[i, :, 2 * wide : 2 * wide + SHARED] = grad_raw.astype(BF16)
    grad_dt = ddt_s[...] * slope
    low_dt = grad_dt.astype(BF16)
    if sel is not None:
        low_dt = dot_nt(low_dt, sel).astype(BF16)
    pg_ref[i, :, 2 * wide + SHARED :] = low_dt
    dn_ref[i] = dot(pg_ref[i], w_ref[...]).astype(BF16)
    by_channel = stacked(ch_rows + [skip_row, gain_row], 8)
    by_shared = stacked(bc_rows, 8)
    by_head = stacked([jnp.sum(grad_dt, axis=0, keepdims=True), rate_row * rate], 8)
    if sel is not None:
        by_head = lax.dot_general(
            by_head, sel.astype(F32), (((1,), (1,)), ((), ())),
            preferred_element_type=F32, precision=HIGHEST,
        )
    return by_channel, by_shared, by_head


def add_small(small, by_channel, by_shared, by_head):
    for j in range(2):
        part = by_channel[:, j * THIRD : (j + 1) * THIRD]
        small[:, j * PIECE : j * PIECE + THIRD] += part
    small[:, 2 * PIECE : 3 * PIECE] += by_shared
    small[7:8, 2 * PIECE : 2 * PIECE + HEADS] += by_head[0:1]
    small[7:8, 2 * PIECE + LANES : 2 * PIECE + LANES + HEADS] += by_head[1:2]


def add_gain(small, row):
    for r in range(8):
        small[r : r + 1, 3 * PIECE : 3 * PIECE + THIRD] = row[:, r * THIRD : (r + 1) * THIRD]


def whole_spec(array):
    return pl.BlockSpec(array.shape, lambda i: (0,) * array.ndim)


def row_spec(length, width):
    return pl.BlockSpec((1, length, width), lambda i: (i, 0, 0))


def block_spec(array):
    return pl.BlockSpec((1,) + array.shape[1:], lambda i: (i, 0, 0))


PARAMS = dict(vmem_limit_bytes=60 * 1024 * 1024)


def run_forward(heads, wide, rows, w, wo, params):
    count, length, width = rows.shape
    constants = [w, wo, *params]
    outs = [
        (width, BF16), (LANES, F32), (width, BF16), (wide, F32),
        (wide, BF16), (SHARED, BF16), (LANES, BF16), (wide, BF16),
    ]
    return pl.pallas_call(
        partial(forward_kernel, heads),
        grid=(count,),
        out_shape=[jax.ShapeDtypeStruct((count, length, n), t) for n, t in outs],
        in_specs=[block_spec(rows)] + [whole_spec(c) for c in constants],
        out_specs=[row_spec(length, n) for n, _ in outs],
        compiler_params=pltpu.CompilerParams(**PARAMS),
        name="forward",
    )(rows, *constants)


def run_backward(heads, wide, grad_rows, aux, saved, w, wo, params):
    count, length, _ = grad_rows.shape
    columns, width = w.shape
    given = [grad_rows, aux, *saved]
    constants = [w, wo, *params]
    outs = [(width, BF16), (columns, BF16), (wide, BF16)]
    sums = [(8, wide), (8, SHARED), (8, LANES)]
    return pl.pallas_call(
        partial(backward_kernel, heads),
        grid=(count,),
        out_shape=[jax.ShapeDtypeStruct((count, length, n), t) for n, t in outs]
        + [jax.ShapeDtypeStruct(s, F32) for s in sums],
        in_specs=[block_spec(g) for g in given] + [whole_spec(c) for c in constants],
        out_specs=[row_spec(length, n) for n, _ in outs]
        + [pl.BlockSpec(s, lambda i: (0, 0)) for s in sums],
        scratch_shapes=backward_scratch(length, wide),
        compiler_params=pltpu.CompilerParams(**PARAMS),
        name="backward",
    )(*given, *constants)


def backward_scratch(length, wide):
    return [
        pltpu.VMEM((length, wide), BF16),
        pltpu.VMEM((length, wide), F32),
        pltpu.VMEM((length, SHARED), F32),
        pltpu.VMEM((length, LANES), F32),
    ]


class Plan:
    def __init__(self, seq, fsdp):
        self.seq, self.fsdp = seq, fsdp
        halves = 2
        if fsdp % 2 or HEADS % (seq * 2) or (HEADS // fsdp) % seq:
            halves = 1
        self.halves, self.mates = halves, fsdp // halves
        self.heads = HEADS // (seq * halves)
        self.pieces = self.mates if (HEADS // fsdp) % seq == 0 else 1
        channels = self.heads * HEADDIM
        self.channels = channels
        self.wide = -(-channels // LANES) * LANES
        self.peer_groups = [[lo + self.mates * h for h in range(halves)] for lo in range(self.mates)]
        self.mate_groups = [[h * self.mates + j for j in range(self.mates)] for h in range(halves)]

    def split(self, array, axis):
        size = array.shape[axis] // (self.halves * self.pieces * self.seq)
        shape = array.shape[:axis] + (self.halves, self.pieces, self.seq, size) + array.shape[axis + 1 :]
        return array.reshape(shape)

    def take(self, array, axis, place):
        array = lax.dynamic_index_in_dim(self.split(array, axis), place, axis + 2, False)
        shape = array.shape[: axis + 1] + (-1,) + array.shape[axis + 3 :]
        return jnp.moveaxis(array.reshape(shape), axis, 0)

    def put(self, parts, axis):
        size = parts.shape[axis + 2] // self.pieces
        shape = parts.shape[: axis + 2] + (self.pieces, size) + parts.shape[axis + 3 :]
        parts = jnp.moveaxis(parts.reshape(shape), (1, axis + 2, 0), (axis, axis + 1, axis + 2))
        shape = parts.shape[:axis] + (-1,) + parts.shape[axis + 4 :]
        return parts.reshape(shape)


def widened(array, axis, size):
    pads = [(0, 0)] * array.ndim
    pads[axis] = (0, size - array.shape[axis])
    return jnp.pad(array, pads)


MESH = pl.DeviceIdType.MESH
ANY = pl.BlockSpec(memory_space=pl.ANY)
VMEM = pl.BlockSpec(memory_space=pltpu.VMEM)
DMA = pltpu.SemaphoreType.DMA


class Spot:
    def __init__(self):
        self.s, self.q, self.z = (lax.axis_index(a) for a in ("section", "seq", "fsdp"))
        self.half, self.lo = self.z // 2, self.z % 2
        self.mate, self.twin = self.z + 1 - 2 * self.lo, (self.z + 2) % 4
        self.around = [None, self.q + 1 - 2 * (self.q % 2), (self.q + 2) % 4, 3 - self.q]
        self.sibling = (1 - self.s, self.q, self.z)
        self.at_mate, self.at_twin = (self.s, self.q, self.mate), (self.s, self.q, self.twin)

    def plane(self, k):
        return (self.s, self.around[k], self.z)

    def column(self, z):
        return (self.s, self.q, z)

    def piece(self, half, j):
        return 8 * half + 4 * j + self.q


def greet(places):
    barrier = pltpu.get_barrier_semaphore()
    for place in places:
        pl.semaphore_signal(barrier, inc=1, device_id=place, device_id_type=MESH)
    pl.semaphore_wait(barrier, len(places))


def remote(src, dst, send_sem, recv_sem, place):
    return pltpu.make_async_remote_copy(
        src_ref=src, dst_ref=dst, send_sem=send_sem, recv_sem=recv_sem, device_id=place, device_id_type=MESH
    )


class Home:
    def __init__(self, src, buffer, dst, sems):
        self.load = pltpu.make_async_copy(src, buffer, sems[0])
        self.store = pltpu.make_async_copy(buffer, dst, sems[1])

    def begin(self):
        self.load.start()

    def go_on(self):
        self.load.wait()
        self.store.start()

    def end(self):
        self.store.wait()


class Spread:
    SEMS = [DMA((7,)), DMA((7,)), DMA]

    def __init__(self, spot, own, all_rows, sems):
        self.spot, self.own, self.all = spot, own, all_rows
        self.send, self.recv, self.local = sems

    def slot(self, half):
        rows = self.own.shape[0]
        return self.all.at[half, pl.ds(pl.multiple_of(self.spot.q * rows, rows), rows)]

    def copy(self, j):
        spot = self.spot
        slot = self.slot(spot.half)
        if j == 3:
            return remote(self.own, slot, self.send.at[3], self.recv.at[3], spot.at_twin)
        if j < 3:
            return remote(self.own, slot, self.send.at[j], self.recv.at[j], spot.plane(j + 1))
        slot = self.slot(1 - spot.half)
        return remote(slot, slot, self.send.at[j], self.recv.at[j], spot.plane(j - 3))

    def here(self):
        return pltpu.make_async_copy(self.own, self.slot(self.spot.half), self.local)

    def start(self):
        for j in (3, 0, 1, 2):
            self.copy(j).start()
        self.here().start()

    def forward(self):
        self.copy(3).wait_recv()
        for j in (4, 5, 6):
            self.copy(j).start()

    def own_half(self):
        for j in (0, 1, 2):
            self.copy(j).wait_recv()
        self.here().wait()

    def other_half(self):
        for j in (4, 5, 6):
            self.copy(j).wait_recv()

    def close(self):
        for j in range(7):
            self.copy(j).wait_send()

    def finish(self):
        self.own_half()
        self.other_half()
        self.close()


class Sum:
    @staticmethod
    def scratch(rows, columns):
        return [
            pltpu.VMEM((2, 4 * rows, columns), BF16),
            pltpu.VMEM((3, 2, rows, columns), BF16),
            pltpu.VMEM((2, rows, columns), BF16),
            DMA((7,)),
            DMA((7,)),
        ]

    def __init__(self, spot, width, scratch):
        self.spot, self.width = spot, width
        self.parts, self.recv_rows, self.twin_rows, self.send, self.recv = scratch
        self.rows = self.twin_rows.shape[1]

    def half(self, i):
        return 1 - self.spot.half + i * (2 * self.spot.half - 1)

    def block(self, q):
        return pl.ds(pl.multiple_of(q * self.rows, self.rows), self.rows)

    def copy(self, k, i):
        spot = self.spot
        j = 3 * i + k - 1
        return remote(
            self.parts.at[self.half(i), self.block(spot.around[k])], self.recv_rows.at[k - 1, i],
            self.send.at[j], self.recv.at[j], spot.plane(k),
        )

    def across(self):
        return remote(
            self.twin_rows.at[0], self.twin_rows.at[1], self.send.at[6], self.recv.at[6], self.spot.at_twin
        )

    def start(self, i):
        for k in (1, 2, 3):
            self.copy(k, i).start()

    def plane_total(self, i):
        total = self.parts[self.half(i), self.block(self.spot.q), :].astype(F32)
        for k in (1, 2, 3):
            self.copy(k, i).wait_recv()
            total += self.recv_rows[k - 1, i].astype(F32)
        return total

    def forward(self):
        total = self.plane_total(0)
        width = self.width
        self.twin_rows[0, :, :width] = total[:, :width].astype(BF16)
        if total.shape[1] > width:
            column = jnp.sum(total[:, width:], axis=1, keepdims=True)
            self.twin_rows[0, :, width:] = split_three(column)
        self.across().start()

    def finish(self):
        total = self.plane_total(1)
        self.across().wait_recv()
        total += self.twin_rows[1].astype(F32)
        return total

    def close(self):
        for i in range(2):
            for k in (1, 2, 3):
                self.copy(k, i).wait_send()
        self.across().wait_send()


class RelaySum(Sum):
    @staticmethod
    def scratch(rows, columns):
        return [
            pltpu.VMEM((2, 4 * rows, columns), BF16),
            pltpu.VMEM((2, 2, rows, columns), BF16),
            pltpu.VMEM((2, rows, columns), BF16),
            DMA((9,)),
            DMA((9,)),
            pltpu.VMEM((2, rows, columns), BF16),
        ]

    def __init__(self, spot, width, scratch):
        super().__init__(spot, width, scratch[:5])
        self.relays = scratch[5]
        columns = self.relays.shape[2]
        cut = columns // 2 // LANES * LANES
        self.cuts = [(0, cut), (cut, columns - cut)]

    def relay(self, k, i):
        spot = self.spot
        columns = pl.ds(*self.cuts[k - 1])
        return remote(
            self.parts.at[self.half(i), self.block(spot.around[3]), columns], self.relays.at[i, :, columns],
            self.send.at[5 + 2 * i + k - 1], self.recv.at[5 + 2 * i + k - 1], spot.plane(k),
        )

    def copy(self, k, i):
        spot = self.spot
        j = 2 * i + k - 1
        return remote(
            self.parts.at[self.half(i), self.block(spot.around[k])], self.recv_rows.at[k - 1, i],
            self.send.at[j], self.recv.at[j], spot.plane(k),
        )

    def across(self):
        return remote(
            self.twin_rows.at[0], self.twin_rows.at[1], self.send.at[4], self.recv.at[4], self.spot.at_twin
        )

    def start(self, i):
        for k in (1, 2):
            self.relay(k, i).start()

    def go_on(self, i):
        for k in (1, 2):
            self.relay(k, i).wait_recv()
            at, size = self.cuts[k - 1]
            rows = self.block(self.spot.around[3 - k])
            half = self.half(i)
            own = self.parts[half, rows, at : at + size].astype(F32)
            total = own + self.relays[i, :, at : at + size].astype(F32)
            self.parts[half, rows, at : at + size] = total.astype(BF16)
        for k in (1, 2):
            self.copy(k, i).start()

    def plane_total(self, i):
        total = self.parts[self.half(i), self.block(self.spot.q), :].astype(F32)
        for k in (1, 2):
            self.copy(k, i).wait_recv()
            total += self.recv_rows[k - 1, i].astype(F32)
        return total

    def close(self):
        for i in range(2):
            for k in (1, 2):
                self.copy(k, i).wait_send()
                self.relay(k, i).wait_send()
        self.across().wait_send()


def tile_parts(spot, half):
    parts = []
    for part in range(2):
        for j in range(2):
            at = part * INNER + THIRD * spot.piece(half, j)
            parts.append((pl.multiple_of(at, 64), (2 * part + j) * THIRD, THIRD))
    return parts + [(2 * INNER, 4 * THIRD, SHARED + HEADS)]


class Weights:
    PARTS = 6
    ORDER = (4, 5, 0, 1, 2, 3)
    QUARTER = SHARED // 4

    @staticmethod
    def scratch(columns, shard, width):
        buffers = [pltpu.VMEM((columns, shard), BF16), pltpu.VMEM((THIRD, width), BF16)]
        return buffers + [DMA((9,)), DMA((57,)), DMA((57,))]

    def __init__(self, spot, layer, w_in, w_out, tile, tile_out, scratch):
        self.spot, self.layer = spot, layer
        self.w_in, self.w_out, self.tile, self.tile_out = w_in, w_out, tile, tile_out
        self.buffer, self.out_buffer, self.local, self.send, self.recv = scratch
        self.shard = w_in.shape[1]
        self.others = 2 * (1 - spot.half)
        self.gateway = 2 - spot.half
        self.is_gateway = (spot.z == 1) | (spot.z == 2)

    def at_source(self, step):
        pl.when(self.spot.s == self.layer)(step)

    def at_relay(self, step):
        pl.when(self.spot.s != self.layer)(step)

    def parts(self, half, n):
        if n < 4:
            return tile_parts(self.spot, half)[n]
        if n == 5:
            return 2 * INNER + SHARED, 4 * THIRD + SHARED, HEADS
        at = self.QUARTER * self.spot.q
        return (
            pl.multiple_of(2 * INNER + at, 64), pl.multiple_of(4 * THIRD + at, 64), self.QUARTER
        )

    def source(self, half, n):
        first, _, size = self.parts(half, n)
        return self.w_in.at[pl.ds(first, size)]

    def target(self, z, n):
        _, first, size = self.parts(0, n)
        columns = pl.ds(pl.multiple_of(z * self.shard, LANES), self.shard)
        return self.tile.at[pl.ds(first, size), columns]

    def buffered(self, n):
        _, first, size = self.parts(0, n)
        return self.buffer.at[pl.ds(first, size)]

    def load(self, n):
        return pltpu.make_async_copy(self.source(self.spot.half, n), self.buffered(n), self.send.at[n])

    def store(self, n):
        return pltpu.make_async_copy(self.buffered(n), self.target(self.spot.z, n), self.local.at[3 + n])

    def out_home(self):
        return Home(
            self.out_source(), self.out_buffer, self.out_part(self.spot.lo),
            (self.local.at[1], self.local.at[2]),
        )

    def to_mate(self, n):
        source, target = self.source(self.spot.half, n), self.target(self.spot.z, n)
        return remote(source, target, self.send.at[n], self.recv.at[n], self.spot.at_mate)

    def to_gateway(self, n):
        source, target = self.source(1 - self.spot.half, n), self.target(self.spot.z, n)
        j = 6 + 6 * self.spot.lo + n
        place = (1 - self.spot.s, self.spot.q, self.gateway)
        return remote(source, target, self.send.at[6 + n], self.recv.at[j], place)

    def passed(self, c, n):
        part = self.target(self.others + c, n)
        j = 6 * c + n
        return remote(part, part, self.send.at[12 + j], self.recv.at[6 + j], self.spot.at_mate)

    def to_sibling(self, b, n):
        j = 24 + 6 * b + n
        part = self.target([self.spot.z, self.spot.mate, self.others, self.others + 1][b], n)
        source = self.source(self.spot.half, n) if b == 0 else part
        return remote(source, part, self.send.at[j], self.recv.at[j], self.spot.sibling)

    def out_part(self, lo):
        return self.tile_out.at[pl.ds(pl.multiple_of(lo * THIRD, 64), THIRD)]

    def out_source(self):
        return self.w_out.at[pl.ds(pl.multiple_of(self.spot.q * THIRD, 64), THIRD)]

    def out_to(self, n):
        part = self.out_part(self.spot.lo if n < 2 else 1 - self.spot.lo)
        place = self.spot.sibling if n else self.spot.at_mate
        source = self.out_source() if n < 2 else part
        return remote(source, part, self.send.at[48 + n], self.recv.at[48 + n], place)

    def send_part(self, n):
        if n < self.PARTS:
            self.to_gateway(n).start()
            self.to_mate(n).start()
        elif n == self.PARTS:
            self.out_to(0).start()

    def begin(self):
        @self.at_source
        def _():
            for n in range(self.PARTS):
                self.load(n).start()
            self.out_home().begin()

    def quarter(self, q):
        at = 4 * THIRD + self.QUARTER * q
        return self.tile.at[pl.ds(pl.multiple_of(at, 64), self.QUARTER)]

    def to_plane(self, k):
        part = self.quarter(self.spot.q)
        return remote(part, part, self.send.at[50 + k], self.recv.at[50 + k], self.spot.plane(k))

    def quarter_to_sibling(self, k):
        part = self.quarter(self.spot.around[k])
        return remote(part, part, self.send.at[53 + k], self.recv.at[53 + k], self.spot.sibling)

    def mates(self):
        for n in self.ORDER:
            self.to_mate(n).start()
        self.out_to(0).start()

    def start(self, window):
        @self.at_source
        def _():
            for n in self.ORDER:
                self.load(n).wait()
            for n in self.ORDER[:window]:
                self.to_gateway(n).start()
            pl.when(self.is_gateway)(self.mates)
            for n in self.ORDER:
                self.to_sibling(0, n).start()
                self.store(n).start()
            self.out_to(1).start()
            self.out_home().go_on()

    def more(self, at, window):
        @self.at_source
        def _():
            self.to_gateway(self.ORDER[at - window]).wait_send()
            self.to_gateway(self.ORDER[at]).start()
            if at == self.PARTS - 1:
                pl.when(jnp.logical_not(self.is_gateway))(self.mates)

    def relay(self, at):
        n = self.ORDER[at]

        @self.at_relay
        def _():
            for c in range(2):
                self.passed(c, n).wait_recv()
                pl.when(self.is_gateway)(lambda c=c: self.passed(c, n).start())
                self.to_sibling(2 + c, n).start()

    def share(self):
        @self.at_source
        def _():
            self.store(4).wait()
            self.to_mate(4).wait_recv()
            self.to_sibling(1, 4).start()
            for c in range(2):
                self.to_sibling(2 + c, 4).wait_recv()
            for k in (1, 2, 3):
                self.to_plane(k).start()

    def shared(self):
        @self.at_source
        def _():
            for k in (1, 2, 3):
                self.to_plane(k).wait_recv()
                self.quarter_to_sibling(k).start()

    def relay_mate(self):
        @self.at_source
        def _():
            for n in self.ORDER[1:]:
                self.to_mate(n).wait_recv()
                self.to_sibling(1, n).start()
            self.out_to(0).wait_recv()
            self.out_to(2).start()

    def finish(self, window):
        @self.at_source
        def _():
            for n in self.ORDER[-window:]:
                self.to_gateway(n).wait_send()
            for n in self.ORDER:
                self.to_mate(n).wait_send()
                for b in range(2):
                    if n != 4:
                        self.to_sibling(2 + b, n).wait_recv()
                    self.to_sibling(b, n).wait_send()
                if n != 4:
                    self.store(n).wait()
            for k in (1, 2, 3):
                self.to_plane(k).wait_send()
                self.quarter_to_sibling(k).wait_send()
            self.out_home().end()
            for n in range(3):
                self.out_to(n).wait_send()

        @self.at_relay
        def _():
            for n in self.ORDER:
                for c in range(2):
                    self.to_sibling(c, n).wait_recv()
                    self.to_sibling(2 + c, n).wait_send()
                    pl.when(self.is_gateway)(lambda c=c, n=n: self.passed(c, n).wait_send())
            for k in (1, 2, 3):
                self.quarter_to_sibling(k).wait_recv()
            for n in (1, 2):
                self.out_to(n).wait_recv()


def all_places(spot):
    places = [spot.plane(k) for k in (1, 2, 3)]
    places += [(s, spot.q, (spot.z + k) % 4) for k in (1, 2, 3) for s in range(2)]
    return places + [spot.sibling]


def open_kernel(*refs):
    ins, outs, weight_s, spread_a, spread_b, (own_tokens, own_cot, own_pack, load, *pack_sems) = take(
        refs, (11, 5, 5, 3, 3, 7)
    )
    w_in, w_out, tokens, cotangent, *raw = ins
    tile, tile_out, packs, all_tokens, all_cot = outs
    spot = Spot()
    weights = Weights(spot, 0, w_in, w_out, tile, tile_out, weight_s)
    rows = Spread(spot, own_tokens, all_tokens, spread_a)
    grads = Spread(spot, own_cot, all_cot, spread_b)
    loads = [
        pltpu.make_async_copy(src, dst, load.at[n])
        for n, (src, dst) in enumerate(
            ((tokens.at[spot.s], own_tokens), (cotangent.at[spot.s], own_cot))
        )
    ]
    pack_here = pltpu.make_async_copy(own_pack, packs.at[spot.s], pack_sems[0])
    pack_there = remote(own_pack, packs.at[spot.s], pack_sems[1], pack_sems[2], spot.sibling)
    for copy in loads:
        copy.start()
    weights.begin()
    greet(all_places(spot))
    for copy in loads:
        copy.wait()
    few = 2
    rows.start()
    weights.start(few)
    pack_params(own_pack, *raw)
    pack_here.start()
    pack_there.start()
    weights.more(2, few)
    rows.forward()
    grads.start()
    for at in (3, 4, 5):
        weights.more(at, few)
    weights.relay(0)
    weights.relay(1)
    weights.share()
    weights.relay(2)
    grads.forward()
    weights.relay(3)
    weights.shared()
    weights.relay(4)
    weights.relay(5)
    weights.relay_mate()
    rows.finish()
    grads.finish()
    weights.finish(few)
    pack_here.wait()
    pack_there.wait()


def pack_params(pack, conv_weight, conv_bias, gate_gain, skip_gain, norm_gain, dt_bias, a_log):
    pack[...] = jnp.zeros_like(pack)
    for p in range(INNER // THIRD):
        source, target = slice(p * THIRD, (p + 1) * THIRD), slice(p * PIECE, p * PIECE + THIRD)
        pack[0:CONV, target] = conv_weight[:, source]
        pack[CONV : CONV + 1, target] = conv_bias[:, source]
        skips = [jnp.broadcast_to(skip_gain[:, 3 * p + h : 3 * p + h + 1], (1, HEADDIM)) for h in range(3)]
        pack[5:6, target] = jnp.concatenate(skips, axis=1)
        pack[6:7, target] = gate_gain[:, source]
    pack[0:CONV, -SHARED:] = conv_weight[:, INNER:]
    pack[CONV : CONV + 1, -SHARED:] = conv_bias[:, INNER:]
    pack[7:8, :GAIN_END] = norm_gain[...]
    pack[7:8, DT_AT : DT_AT + HEADS] = dt_bias[...]
    pack[7:8, RATE_AT : RATE_AT + HEADS] = a_log[...]


def layer_rows(total, rows_in, branch, scales, rows_out):
    width = rows_in.shape[1]
    square = jnp.sum(total[:, width:], axis=1, keepdims=True)
    scale = lax.rsqrt(square * (1.0 / INNER) + NORM_EPS)
    part = total[:, :width] * scale
    rows_out[...] = (rows_in[...].astype(F32) + part).astype(BF16)
    if branch is not None:
        branch[...] = part
        scales[...] = jnp.broadcast_to(scale, scales.shape)


def norm_back(total, rows_in, gain, grad_out):
    rows = rows_in[...].astype(F32)
    scale = lax.rsqrt(jnp.mean(rows * rows, axis=-1, keepdims=True) + NORM_EPS)
    scaled = rows * scale
    pulled = total * gain
    inner = jnp.mean(pulled * scaled, axis=-1, keepdims=True)
    grad = scale * (pulled - scaled * inner) + grad_out[...].astype(F32)
    return grad, jnp.sum(total * scaled, axis=0, keepdims=True)


def add_rows(target, sources, chunk=64):
    @pl.loop(0, target.shape[0] // chunk)
    def _(n):
        rows = pl.ds(pl.multiple_of(n * chunk, chunk), chunk)
        total = sources[0][rows, :].astype(F32)
        for source in sources[1:]:
            total += source[rows, :].astype(F32)
        target[rows, :] = total.astype(target.dtype)


class Grads:
    ORDER = (4, 0, 1, 2, 3, 5)

    @staticmethod
    def scratch(shard, columns, wide, width):
        return [
            pltpu.VMEM((3, columns, width), BF16),
            pltpu.VMEM((3, wide, width), BF16),
            pltpu.VMEM((2, columns, shard), BF16),
            pltpu.VMEM((2, columns, shard), BF16),
            pltpu.VMEM((THIRD, width), BF16),
            DMA((22,)),
            DMA((27,)),
        ]

    @staticmethod
    def results(shard, width):
        return [((2, 4 * THIRD, shard), BF16), ((SHARED + HEADS, shard), BF16), ((THIRD, width), BF16)]

    def __init__(self, spot, results, scratch):
        self.spot = spot
        self.reduced, self.shared, self.out = results
        self.cores, self.cores_out, self.planes, self.relay, self.mate_out, self.send, self.recv = scratch
        self.shard = self.planes.shape[2]
        self.others = 2 * (1 - spot.half)
        self.is_gateway = (spot.z == 1) | (spot.z == 2)

    def rows(self, n):
        _, first, size = tile_parts(self.spot, 0)[n]
        return pl.ds(first, size)

    def columns(self, z):
        return pl.ds(pl.multiple_of(z * self.shard, LANES), self.shard)

    def core_copy(self, n):
        buffer, rows = (self.cores_out, pl.ds(0, self.cores_out.shape[1])) if n == 5 else (self.cores, self.rows(n))
        return remote(
            buffer.at[2, rows], buffer.at[1, rows], self.send.at[n], self.recv.at[n], self.spot.sibling
        )

    def product(self, layer, n, proj_grad, normed, normed_out, h_rows):
        def flat(value):
            return value.reshape(-1, value.shape[-1])

        width = self.cores.shape[2]
        slot = 2 * (self.spot.s - layer) * (self.spot.s - layer)
        if n == 5:
            total = dot_tn(flat(normed_out[...]), flat(h_rows[:, :, :width]))
            self.cores_out[slot] = total.astype(BF16)
        else:
            _, first, size = tile_parts(self.spot, 0)[n]
            total = dot_tn(flat(proj_grad[:, :, first : first + size]), flat(normed[...]))
            self.cores[slot, first : first + size, :] = total.astype(BF16)
        pl.when(self.spot.s != layer)(lambda: self.core_copy(n).start())

    def far_part(self, c, n):
        return self.cores.at[0, self.rows(n), self.columns(self.others + c)]

    def to_mate(self, n):
        source = self.cores.at[0, self.rows(n), self.columns(self.spot.mate)]
        target = self.planes.at[1, self.rows(n)]
        return remote(source, target, self.send.at[6 + n], self.recv.at[11 + n], self.spot.at_mate)

    def to_relay(self, c, n):
        j = 2 * n + c
        target = self.relay.at[c, self.rows(n)]
        return remote(
            self.far_part(c, n), target, self.send.at[11 + j], self.recv.at[16 + j], self.spot.at_mate
        )

    def to_far(self, c, n):
        target = self.planes.at[0, self.rows(n)]
        place = self.spot.column(self.others + c)
        return remote(
            self.far_part(c, n), target, self.send.at[11 + 2 * n + c], self.recv.at[6 + n], place
        )

    def out_rows(self, lo):
        return pl.ds(pl.multiple_of(lo * THIRD, 64), THIRD)

    def mate_copy(self):
        source = self.cores_out.at[0, self.out_rows(1 - self.spot.lo)]
        return remote(source, self.mate_out, self.send.at[21], self.recv.at[26], self.spot.at_mate)

    def sent(self, n):
        self.to_mate(n).wait_send()
        for c in range(2):
            self.to_relay(c, n).wait_send()

    def to_planes(self, n):
        self.core_copy(n).wait_recv()
        if n == 5:
            add_rows(self.cores_out.at[0], [self.cores_out.at[0], self.cores_out.at[1]])
            self.mate_copy().start()
            return
        own, sibling = self.cores.at[0, self.rows(n)], self.cores.at[1, self.rows(n)]
        add_rows(own, [own, sibling], 48 if n < 4 else 16)

        @pl.when(jnp.logical_not(self.is_gateway))
        def _():
            for c in range(2):
                self.to_relay(c, n).start()

        self.to_mate(n).start()

    def pass_on(self, n):
        @pl.when(self.is_gateway)
        def _():
            for c in range(2):
                self.to_relay(c, n).wait_recv()
                target, relay = self.far_part(c, n), self.relay.at[c, self.rows(n)]
                add_rows(target, [target, relay], 48 if n < 4 else 16)
                self.to_far(c, n).start()

    def gather(self, n):
        if n == 5:
            self.mate_copy().wait_recv()
            add_rows(self.out, [self.cores_out.at[0, self.out_rows(self.spot.lo)], self.mate_out], 48)
            return
        self.to_mate(n).wait_recv()
        self.to_far(0, n).wait_recv()
        _, first, size = tile_parts(self.spot, 0)[n]
        mine = self.columns(self.spot.z)
        chunk = 48 if n < 4 else 16

        @pl.loop(0, size // chunk)
        def _(r):
            rows = pl.ds(pl.multiple_of(first + r * chunk, 16), chunk)
            own = self.cores[0, rows, mine].astype(F32) + self.planes[1, rows, :].astype(F32)
            other = self.planes[0, rows, :]
            if n < 4:
                self.reduced[0, rows, :] = own.astype(BF16)
                self.reduced[1, rows, :] = other
            else:
                rows = pl.ds(pl.multiple_of(r * chunk, 16), chunk)
                self.shared[rows, :] = (own + other.astype(F32)).astype(BF16)

    def finish(self):
        self.mate_copy().wait_send()
        for n in self.ORDER:
            self.core_copy(n).wait_send()


class GradsAround:
    @staticmethod
    def scratch(shard):
        return [
            pltpu.VMEM((4, SHARED + HEADS, shard), BF16),
            DMA((11,)),
            DMA((34,)),
            DMA((34,)),
        ]

    def __init__(self, spot, results, final, final_out, scratch):
        self.spot, self.final, self.final_out = spot, final, final_out
        self.reduced, self.shared, self.out = results
        self.sums, self.local, self.send, self.recv = scratch

    def region(self, k, i, n):
        q = self.spot.q if k == 0 else self.spot.around[k]
        half = self.spot.half if i == 0 else 1 - self.spot.half
        at = n // 2 * INNER + THIRD * (8 * half + 4 * (n % 2) + q)
        return self.final.at[pl.ds(pl.multiple_of(at, 64), THIRD)]

    def copy(self, k, i, n):
        source = self.reduced.at[i, pl.ds(n * THIRD, THIRD)]
        target = self.region(0, i, n)
        j = 4 * i + n
        if k == 0:
            return pltpu.make_async_copy(source, target, self.local.at[j])
        if k < 3:
            j += 8 * (k - 1)
            return remote(source, target, self.send.at[j], self.recv.at[j], self.spot.plane(k))
        source = target = self.region(1 if i == 0 else 2, i, n)
        place = self.spot.plane(2 if i == 0 else 1)
        return remote(source, target, self.send.at[16 + j], self.recv.at[16 + j], place)

    def send_part(self, n):
        for i in range(2):
            for k in (1, 2, 0):
                self.copy(k, i, n).start()

    def pass_part(self, n):
        for i in range(2):
            self.copy(1 + i, i, n).wait_recv()
            self.copy(3, i, n).start()

    def out_region(self, k, i):
        q = self.spot.q if k == 0 else self.spot.around[k]
        size = THIRD if i is None else THIRD // 2
        at = q * THIRD + (0 if i is None else i * size)
        return self.final_out.at[pl.ds(pl.multiple_of(at, 32), size)]

    def out_copy(self, k, i=None):
        target = self.out_region(0, None)
        if k == 0:
            return pltpu.make_async_copy(self.out, target, self.local.at[8])
        if k < 3:
            return remote(self.out, target, self.send.at[23 + k], self.recv.at[23 + k], self.spot.plane(k))
        part = self.out_region(1 + i, i)
        return remote(part, part, self.send.at[26 + i], self.recv.at[26 + i], self.spot.plane(2 - i))

    def send_out(self):
        for k in (1, 2, 0):
            self.out_copy(k).start()

    def pass_out(self):
        for i in range(2):
            self.out_copy(1 + i).wait_recv()
            self.out_copy(3, i).start()

    def shared_copy(self, k):
        source = self.shared if k == 1 else self.sums.at[1]
        target = self.sums.at[0 if k == 1 else 2]
        return remote(source, target, self.send.at[27 + k], self.recv.at[27 + k], self.spot.plane(k))

    def shared_home(self):
        tail = self.final.at[pl.ds(2 * INNER, SHARED + HEADS)]
        return pltpu.make_async_copy(self.sums.at[3], tail, self.local.at[9])

    def shared_step(self, n):
        if n > 0:
            self.shared_copy(n).wait_recv()
            sources = [self.shared, self.sums.at[0]] if n == 1 else [self.sums.at[1], self.sums.at[2]]
            add_rows(self.sums.at[1 if n == 1 else 3], sources, 16)
        if n < 2:
            self.shared_copy(n + 1).start()
        else:
            self.shared_home().start()

    def finish(self):
        for i in range(2):
            for n in range(4):
                self.copy(2 - i, i, n).wait_recv()
                self.copy(3, i, n).wait_recv()
                for k in (1, 2, 3):
                    self.copy(k, i, n).wait_send()
                self.copy(0, i, n).wait()
            self.out_copy(3, i).wait_recv()
            self.out_copy(3, i).wait_send()
        for k in (1, 2):
            self.out_copy(k).wait_send()
            self.shared_copy(k).wait_send()
        self.out_copy(0).wait()
        self.shared_home().wait()


class SmallSum:
    SHAPE = (8, 4 * PIECE)

    @staticmethod
    def scratch():
        return [
            pltpu.VMEM((4,) + SmallSum.SHAPE, F32),
            pltpu.VMEM((8,) + SmallSum.SHAPE, F32),
            DMA((9,)),
            DMA((9,)),
        ]

    def __init__(self, spot, scratch):
        self.spot = spot
        self.small, self.group, self.send, self.recv = scratch

    def to_sibling(self):
        return remote(
            self.small.at[0], self.small.at[1], self.send.at[0], self.recv.at[0], self.spot.sibling
        )

    def to_mate(self):
        return remote(
            self.small.at[2], self.small.at[3], self.send.at[1], self.recv.at[1], self.spot.at_mate
        )

    def to_group(self, j):
        spot = self.spot
        part = self.group.at[4 * spot.half + spot.q]
        places = [spot.plane(k) for k in (1, 2, 3)] + [spot.at_twin]
        places += [(spot.s, spot.around[k], spot.twin) for k in (1, 2, 3)]
        return remote(part, part, self.send.at[2 + j], self.recv.at[2 + j], places[j])

    def begin(self, value):
        self.small[0] = value
        self.to_sibling().start()

    def step(self, n, value=None):
        if n == 0:
            self.to_sibling().wait_recv()
            self.small[2] = value + self.small[1]
            self.to_mate().start()
        else:
            self.to_mate().wait_recv()
            self.group[4 * self.spot.half + self.spot.q] = self.small[2] + self.small[3]
            for j in range(7):
                self.to_group(j).start()

    def finish(self, out):
        for j in range(7):
            self.to_group(j).wait_recv()
        total = self.group[0, :, 2 * PIECE :]
        for n in range(1, 8):
            total += self.group[n, :, 2 * PIECE :]
        for half in range(2):
            for j in range(2):
                for q in range(4):
                    at = (8 * half + 4 * j + q) * PIECE
                    out[:, at : at + PIECE] = self.group[4 * half + q, :, j * PIECE : (j + 1) * PIECE]
        out[:, -SHARED:] = total[:, :SHARED]
        out[7:8, DT_AT : DT_AT + HEADS] = total[7:8, :HEADS]
        out[7:8, RATE_AT : RATE_AT + HEADS] = total[7:8, LANES : LANES + HEADS]
        for r in range(8):
            out[7:8, r * THIRD : (r + 1) * THIRD] = total[r : r + 1, PIECE : PIECE + THIRD]
        self.to_sibling().wait_send()
        self.to_mate().wait_send()
        for j in range(7):
            self.to_group(j).wait_send()


def loading(sources, targets, sems):
    return [pltpu.make_async_copy(a, b, sems.at[n]) for n, (a, b) in enumerate(zip(sources, targets))]


def saved_shapes(length, width, wide):
    columns = ((width, BF16), (wide, F32), (wide, BF16), (SHARED, BF16), (LANES, BF16), (wide, BF16))
    return [((2, length, n), t) for n, t in columns]


def middle_kernel(heads, *refs):
    ins, outs, kept, weight_s, sum_s, spread_s, layer_s, (store,) = take(refs, (7, 6, 6, 5, 5, 3, 11, 1))
    w_in, w_out, *layer_ins, rows_in = ins
    tile, tile_out, all_rows, branch, scales, rows_out = outs
    u, w, wo, pack, *saved, load = layer_s
    spot = Spot()
    rows_in = rows_in.at[spot.s]
    weights = Weights(spot, 1, w_in, w_out, tile, tile_out, weight_s)
    total = Sum(spot, rows_in.shape[1], sum_s)
    spread = Spread(spot, rows_out, all_rows, spread_s)
    loads = loading(layer_ins[:3] + [layer_ins[3].at[0]], layer_s[:4], load)
    for copy in loads:
        copy.start()
    weights.begin()
    greet(all_places(spot))
    few = 3
    weights.start(few)
    for copy in loads:
        copy.wait()
    params = load_params(([spot.piece(spot.half, j) for j in range(2)], pack))

    @pl.loop(0, 2)
    def _(i):
        forward_rows(heads, params, total.half(i), u, w, wo, None, [total.parts, None, *saved])
        total.start(i)


        @pl.when(i == 0)
        def _():
            weights.more(3, few)
            weights.more(4, few)

    stores = loading(saved, kept, store)
    for copy in stores:
        copy.start()
    weights.more(5, few)
    total.forward()
    weights.relay(0)
    weights.relay(1)
    weights.relay(2)
    weights.share()
    layer_rows(total.finish(), rows_in, branch, scales, rows_out)
    spread.start()
    weights.shared()
    weights.relay(3)
    spread.forward()
    weights.relay(4)
    weights.relay(5)
    weights.relay_mate()
    spread.finish()
    total.close()
    weights.finish(few)
    for copy in stores:
        copy.wait()


class RowSums:
    @staticmethod
    def scratch(length):
        shape = (2, 8, length)
        return [pltpu.VMEM(shape, F32), pltpu.VMEM((7,) + shape, F32), DMA((14,)), DMA((14,))]

    def __init__(self, spot, scratch):
        self.mine, self.others, self.send, self.recv = scratch
        self.places = [spot.plane(k) for k in (1, 2, 3)] + [spot.at_twin]
        self.places += [(spot.s, spot.around[k], spot.twin) for k in (1, 2, 3)]

    def copies(self, seq):
        return [
            remote(
                self.mine.at[seq], self.others.at[j, seq],
                self.send.at[2 * j + seq], self.recv.at[2 * j + seq], place,
            )
            for j, place in enumerate(self.places)
        ]

    def start(self, seq):
        for copy in self.copies(seq):
            copy.start()

    def finish(self, seq):
        total = self.mine[seq]
        for j, copy in enumerate(self.copies(seq)):
            copy.wait_recv()
            total += self.others[j, seq]
        for copy in self.copies(seq):
            copy.wait_send()
        self.mine[seq] = total


def back_kernel(heads, *refs):
    ins, outs, first_s, last_s, second_s, spread_s, row_s, back_s, layer_s, grads_s, results, around_s, own_s, rest = take(
        refs, (18, 5, 5, 6, 6, 3, 4, 6, 11, 7, 3, 4, 4, 10)
    )
    (all_rows, all_cot, packs), tiles, kept, own_ins = take(ins, (3, 4, 6, 5))
    first_rows, tokens, grad_out, branch, scales = own_ins
    home_rows, home_grads, final, final_out, small_out = outs
    u, w, wo, pack, *saved, load = layer_s
    h_rows, h_next, payload, last_rows, last_grad, first_grad, small, send, recv, local = rest
    proj_grad, normed_out, *scratch = back_s
    spot = Spot()
    tokens, grad_out = tokens.at[spot.s], grad_out.at[spot.s]
    width = first_rows.shape[1]
    total = Sum(spot, width, first_s)
    last = RelaySum(spot, width, last_s)
    second = RelaySum(spot, width, second_s)
    spread = Spread(spot, payload, h_next, spread_s)
    sums = RowSums(spot, row_s)
    grads = Grads(spot, results, grads_s)
    around = GradsAround(spot, results, final, final_out, around_s)
    own = SmallSum(spot, own_s)
    first_core, last_core = pl.when(spot.s == 0), pl.when(spot.s == 1)
    loads = loading([all_rows, *tiles[2:], packs, all_cot], [u, w, wo, pack, h_rows], load)
    reloads = loading([*tiles[:2], *kept], [w, wo, *saved], load)
    for copy in loads:
        copy.start()
    places = [spot.plane(k) for k in (1, 2, 3)] + [spot.column((spot.z + k) % 4) for k in (1, 2, 3)]
    places += [(spot.s, spot.around[k], spot.twin) for k in (1, 2, 3)] + [spot.sibling]
    greet(places)
    for copy in loads:
        copy.wait()
    ids = [spot.piece(spot.half, j) for j in range(2)]
    params = load_params((ids, pack.at[1]))

    @pl.loop(0, 2)
    def _(i):
        seq = last.half(i)
        forward_rows(heads, params, seq, u, w, wo, h_rows, [last.parts, sums.mine, *saved])
        sums.start(seq)
        last.start(i)

    last.go_on(0)

    def backward(layer, params, total, h_ref, aux_of, order):
        small[layer] = jnp.zeros(small.shape[1:], F32)

        @pl.loop(0, 2)
        def _(n):
            i = order(n)
            seq = total.half(i)
            outs = (total.parts, proj_grad, normed_out)
            parts = backward_rows(
                heads, params, seq, h_ref, lambda: aux_of(n, seq), saved[1:], w, wo, outs, scratch
            )
            add_small(small.at[layer], *parts)
            total.start(i)

    def row_aux(n, seq):

        @pl.when(n == 1)
        def _():
            last.go_on(1)
            last.forward()

        sums.finish(seq)
        return aux_of_rows(sums.mine[seq])

    def column_aux(n, seq):
        pl.when(n == 0)(spread.own_half)

        @pl.when((n == 1) & (spot.s == 1))
        def _():
            own.step(1)
            grads.to_planes(5)
            grads.pass_on(1)
            grads.gather(4)
            around.shared_step(0)

        pl.when(n == 1)(spread.other_half)
        return aux_of_columns(h_next, seq, width)

    backward(1, params, total, h_rows, row_aux, lambda n: n)

    def product(layer, n):
        grads.product(layer, n, proj_grad, saved[0], normed_out, h_rows if layer else h_next)

    product(1, 4)
    product(1, 0)
    total.forward()
    last_core(lambda: grads.to_planes(4))
    for n in (1, 2, 3, 5):
        product(1, n)
    last_core(lambda: grads.to_planes(0))
    for copy in reloads:
        copy.start()
    grad, last_gain = norm_back(total.finish(), first_rows, pack[1, 7:8, :width], grad_out)
    low = grad.astype(BF16)
    last_grad[...] = low
    cross = jnp.sum(low.astype(F32) * branch[...], axis=1, keepdims=True)
    payload[:, :width] = low
    lanes = lax.broadcasted_iota(jnp.int32, (payload.shape[0], LANES), 1)
    scale_part = split_three(scales[:, 0:1]).astype(F32)
    cross_part = pltpu.roll(split_three(cross).astype(F32), 3, 1)
    payload[:, width:] = jnp.where(lanes < 3, scale_part, cross_part).astype(BF16)
    spread.start()
    add_gain(small.at[1], last_gain)
    first_core(lambda: own.begin(small[1]))

    @last_core
    def _():
        grads.pass_on(4)
        grads.to_planes(1)

    spread.forward()

    @last_core
    def _():
        own.step(0, small[1])
        grads.pass_on(0)
        for n in (2, 3):
            grads.to_planes(n)

    for copy in reloads:
        copy.wait()
    params = load_params((ids, pack.at[0]))
    backward(0, params, second, h_next, column_aux, lambda n: 1 - n)

    @last_core
    def _():
        grads.gather(0)
        around.send_part(0)
        grads.pass_on(2)

    for n in Grads.ORDER:
        product(0, n)
    second.go_on(1)
    second.go_on(0)

    @first_core
    def _():
        for n in (4, 0, 1):
            grads.to_planes(n)
        grads.pass_on(4)
        for n in (5, 2):
            grads.to_planes(n)
        grads.pass_on(0)
        grads.gather(4)
        around.shared_step(0)
        grads.to_planes(3)
        grads.pass_on(1)
        grads.gather(0)
        around.send_part(0)

    @last_core
    def _():
        grads.gather(1)
        around.send_part(1)
        grads.pass_on(3)

    second.forward()

    @first_core
    def _():
        grads.pass_on(2)
        grads.gather(5)
        around.send_out()
        grads.gather(1)
        around.send_part(1)
        around.shared_step(1)
        around.pass_part(0)
        grads.pass_on(3)

    @last_core
    def _():
        grads.gather(5)
        around.send_out()
        grads.gather(2)
        around.send_part(2)
        around.pass_part(0)
        grads.gather(3)
        around.send_part(3)
        around.shared_step(1)
        around.pass_part(1)

    grad, first_gain = norm_back(second.finish(), tokens, pack[0, 7:8, :width], last_grad)
    first_grad[...] = grad.astype(BF16)
    layers = ((first_rows, first_grad), (last_rows, last_grad))

    def home_copies(s):
        copies = []
        for n, target in enumerate((home_rows, home_grads)):
            copies.append(remote(layers[1 - s][n], target.at[s], send.at[n], recv.at[n], spot.sibling))
            copies.append(pltpu.make_async_copy(layers[s][n], target.at[s], local.at[n]))
        return copies

    add_gain(small.at[0], first_gain)
    last_core(lambda: own.begin(small[0]))

    @first_core
    def _():
        grads.gather(2)
        around.send_part(2)
        own.step(0, small[0])
        grads.gather(3)
        around.send_part(3)
        around.pass_out()
        around.pass_part(1)
        own.step(1)
        around.pass_part(2)
        around.shared_step(2)

    layer_rows(last.finish(), first_rows, None, None, last_rows)
    for s in range(2):

        @pl.when(spot.s == s)
        def _(s=s):
            for copy in home_copies(s):
                copy.start()

    first_core(lambda: around.pass_part(3))

    @last_core
    def _():
        around.pass_out()
        for n in (2, 3):
            around.pass_part(n)
        around.shared_step(2)

    own.finish(small_out)
    around.finish()
    for n in range(5):
        grads.sent(n)
    grads.finish()
    for s in range(2):

        @pl.when(spot.s == s)
        def _(s=s):
            for copy in home_copies(s):
                copy.wait()

    total.close()
    last.close()
    second.close()
    spread.close()


def comm_call(kernel, collective, ins, in_specs, outs, out_specs, scratch, name):
    return pl.pallas_call(
        kernel,
        out_shape=[jax.ShapeDtypeStruct(s, t) for s, t in outs],
        in_specs=in_specs,
        out_specs=out_specs,
        scratch_shapes=scratch,
        compiler_params=pltpu.CompilerParams(
            collective_id=collective, has_side_effects=True, vmem_limit_bytes=60 * 1024 * 1024
        ),
        name=name,
    )(*ins)


def fast_shards(
    tokens, cotangent, norm_gain, w_in, conv_weight, conv_bias, dt_bias, a_log, skip_gain, gate_gain, w_out
):
    span, width = tokens.shape[2:]
    heads = HEADS // 8
    wide = heads * HEADDIM
    columns = 2 * wide + SHARED + HEADS
    shard = w_in.shape[1]
    rows_in = w_in[0].T
    pack_shape = (8, INNER // THIRD * PIECE + SHARED)
    group = (2, 4 * span, width)
    weight_outs = [((columns, width), BF16), ((wide, width), BF16)]
    weight_s = Weights.scratch(columns, shard, width)
    payload = width + LANES
    tile, tile_out, packs, all_rows, all_cot = comm_call(
        open_kernel, 1,
        [
            rows_in, w_out[0], tokens[:, 0], cotangent[:, 0], conv_weight[0], conv_bias, gate_gain, skip_gain,
            norm_gain, dt_bias, a_log,
        ],
        [ANY] * 4 + [VMEM] * 7,
        weight_outs + [((2,) + pack_shape, F32), (group, BF16), (group, BF16)], [ANY] * 5,
        weight_s + Spread.SEMS + Spread.SEMS
        + [pltpu.VMEM((span, width), BF16)] * 2 + [pltpu.VMEM(pack_shape, F32), DMA((2,)), DMA, DMA, DMA],
        "open",
    )
    length = 4 * span
    rows_spec = ((span, width), BF16)
    layer_s = [
        pltpu.VMEM((2, length, width), BF16), pltpu.VMEM((columns, width), BF16),
        pltpu.VMEM((wide, width), BF16), pltpu.VMEM(pack_shape, F32),
    ]
    kept_shapes = saved_shapes(length, width, wide)
    kept_s = [pltpu.VMEM(*k) for k in kept_shapes]
    back_s = [pltpu.VMEM((2, length, columns), BF16), pltpu.VMEM((2, length, wide), BF16)]
    back_s += backward_scratch(length, wide)
    results = Grads.results(shard, width)
    sum_s = Sum.scratch(span, width)
    first_tiles = [tile, tile_out]
    tile, tile_out, all_rows, branch, scales, rows, *kept = comm_call(
        partial(middle_kernel, heads), 2,
        [rows_in, w_out[0], all_rows, tile, tile_out, packs, tokens[:, 0]], [ANY] * 6 + [VMEM],
        weight_outs + [(group, BF16), ((span, width), F32), ((span, LANES), F32), rows_spec] + kept_shapes,
        [ANY] * 3 + [VMEM] * 3 + [ANY] * 6,
        weight_s + Sum.scratch(span, payload) + Spread.SEMS + layer_s + kept_s + [DMA((4,)), DMA((6,))],
        "middle",
    )
    home_rows, home_grads, final, final_out, small = comm_call(
        partial(back_kernel, heads), 3,
        [
            all_rows, all_cot, packs, *first_tiles, tile, tile_out, *kept,
            rows, tokens[:, 0], cotangent[:, 0], branch, scales,
        ],
        [ANY] * 13 + [VMEM] * 5,
        [
            ((2, span, width), BF16), ((2, span, width), BF16),
            ((2 * INNER + SHARED + HEADS, shard), BF16), (w_out.shape[1:], BF16), (pack_shape, F32),
        ],
        [ANY] * 4 + [VMEM],
        sum_s + RelaySum.scratch(span, payload) + RelaySum.scratch(span, width) + Spread.SEMS + RowSums.scratch(length) + back_s
        + layer_s[:3] + [pltpu.VMEM((2,) + pack_shape, F32)] + kept_s + [DMA((8,))]
        + Grads.scratch(shard, columns, wide, width) + [pltpu.VMEM(*r) for r in results]
        + GradsAround.scratch(shard) + SmallSum.scratch()
        + [
            pltpu.VMEM((2, length, width), BF16), pltpu.VMEM((2, length, payload), BF16),
            pltpu.VMEM((span, payload), BF16), *[pltpu.VMEM((span, width), BF16)] * 3,
            pltpu.VMEM((2,) + SmallSum.SHAPE, F32), DMA((2,)), DMA((2,)), DMA((2,)),
        ],
        "back",
    )
    grad_in, grad_out, gain, conv, bias, shift, rate, skip, gate = finish_call(final, final_out, small)
    return (
        home_rows[None, :, None], home_grads[None, :, None], gain, grad_in.T[None], conv[None],
        bias, shift, rate, skip, gate, grad_out[None],
    )


def finish_kernel(final, final_out, small, grad_in, grad_out, gain, conv, bias, shift, rate, skip, gate):
    grad_in[...] = final[...].astype(F32)
    step = pl.program_id(0)
    grad_out[...] = final_out[...].astype(F32)

    @pl.when(step == 0)
    def _():
        gain[...] = small[7:8, :GAIN_END]
        shift[...] = small[7:8, DT_AT : DT_AT + HEADS]
        rate[...] = small[7:8, RATE_AT : RATE_AT + HEADS]
        heads = []
        for p in range(INNER // THIRD):
            source, target = slice(p * PIECE, p * PIECE + THIRD), slice(p * THIRD, (p + 1) * THIRD)
            conv[:, target] = small[0:CONV, source]
            bias[:, target] = small[CONV : CONV + 1, source]
            gate[:, target] = small[6:7, source]
            for h in range(3):
                part = small[5:6, p * PIECE + h * HEADDIM : p * PIECE + (h + 1) * HEADDIM]
                heads.append(jnp.sum(part, axis=1, keepdims=True))
        skip[...] = jnp.concatenate(heads, axis=1)
        conv[:, INNER:] = small[0:CONV, -SHARED:]
        bias[:, INNER:] = small[CONV : CONV + 1, -SHARED:]


def finish_call(final, final_out, small):
    rows, shard = final.shape
    out_rows, width = final_out.shape
    steps = 3
    block, out_block = -(-rows // (16 * steps)) * 16, out_rows // steps
    smalls = [(1, GAIN_END), (CONV, XBC), (1, XBC), (1, HEADS), (1, HEADS), (1, HEADS), (1, INNER)]

    def in_block(i):
        return (i, 0)

    def same(i):
        return (0, 0)

    return pl.pallas_call(
        finish_kernel,
        grid=(steps,),
        out_shape=[jax.ShapeDtypeStruct(s, F32) for s in [final.shape, final_out.shape] + smalls],
        in_specs=[
            pl.BlockSpec((block, shard), in_block),
            pl.BlockSpec((out_block, width), in_block),
            pl.BlockSpec(small.shape, same),
        ],
        out_specs=[
            pl.BlockSpec((block, shard), in_block),
            pl.BlockSpec((out_block, width), in_block),
        ]
        + [pl.BlockSpec(s, same) for s in smalls],
        compiler_params=pltpu.CompilerParams(**PARAMS),
        name="finish",
    )(final, final_out, small)


def shards(
    tokens, cotangent, norm_gain, w_in, conv_weight, conv_bias, dt_bias, a_log, skip_gain, gate_gain, w_out
):
    section = lax.axis_index("section")
    place = lax.axis_index("seq")
    depth = lax.axis_index("fsdp")
    plan = Plan(lax.axis_size("seq"), lax.axis_size("fsdp"))
    half = depth // plan.mates
    micro, _, span, width = tokens.shape
    layers = lax.axis_size("section")
    wide, channels, heads = plan.wide, plan.channels, plan.heads

    shard = w_in[0]
    gate_part = widened(plan.take(shard[:, :INNER], 1, place), 2, wide)
    x_part = widened(plan.take(shard[:, INNER : 2 * INNER], 1, place), 2, wide)
    shared_part = jnp.broadcast_to(
        shard[:, 2 * INNER : INNER + XBC], (plan.halves, shard.shape[0], SHARED)
    )
    dt_part = widened(plan.take(shard[:, INNER + XBC :], 1, place), 2, LANES)
    tile = jnp.concatenate([gate_part, x_part, shared_part, dt_part], axis=2)
    tile = jnp.repeat(tile, plan.mates, axis=0)
    tile = lax.all_to_all(tile, "fsdp", 0, 0, tiled=True).reshape(width, -1).T
    w_tiles = lax.all_gather(tile, "section", axis=0)
    if plan.pieces == plan.mates:
        piece = w_out[0].reshape(plan.seq, -1, width)
        piece = lax.dynamic_index_in_dim(piece, place, 0, False)
        rows_out = lax.all_gather(
            piece, "fsdp", axis=0, tiled=True, axis_index_groups=plan.mate_groups
        )
    else:
        rows_out = lax.all_gather(w_out[0], "fsdp", axis=0, tiled=True)
        rows_out = lax.dynamic_index_in_dim(plan.take(rows_out, 0, place), half, 0, False)
    wo_tiles = lax.all_gather(widened(rows_out, 0, wide), "section", axis=0)

    def own(array, axis, size):
        part = lax.dynamic_index_in_dim(plan.take(array, axis, place), half, 0, False)
        return widened(part, axis, size)

    skip_wide = jnp.repeat(skip_gain[0], HEADDIM)[None]
    by_channel = jnp.concatenate(
        [conv_weight[0, :, :INNER], conv_bias[:, :INNER], skip_wide, gate_gain, jnp.zeros((1, INNER))], 0
    )
    by_channel = own(by_channel, 1, wide)
    by_shared = jnp.concatenate(
        [conv_weight[0, :, INNER:], conv_bias[:, INNER:], jnp.zeros((3, SHARED))], 0
    )
    by_head = jnp.concatenate([dt_bias, a_log, jnp.zeros((6, HEADS))], 0)
    by_head = own(by_head, 1, LANES)
    smalls = jnp.concatenate(
        [by_channel.ravel(), by_shared.ravel(), by_head.ravel(), norm_gain[0]]
    )
    smalls = lax.all_gather(smalls, "section", axis=0)
    cuts = [8 * wide, 8 * (wide + SHARED), 8 * (wide + SHARED + LANES)]
    params = []
    for l in range(layers):
        ch, bc, dtp, gain = jnp.split(smalls[l], cuts)
        params.append((gain[None], ch.reshape(8, -1), bc.reshape(8, -1), dtp.reshape(8, -1)))

    def gather_rows(own_rows):
        rows = lax.all_gather(own_rows, "seq", axis=0, tiled=True)
        if plan.halves == 1:
            return rows[None]
        return lax.all_gather(rows, "fsdp", axis=0, axis_index_groups=plan.peer_groups)

    def sum_rows(parts):
        if plan.halves == 1:
            rows = parts[0]
        else:
            rows = lax.psum_scatter(
                parts, "fsdp", scatter_dimension=0, axis_index_groups=plan.peer_groups
            )
        return lax.psum_scatter(rows, "seq", scatter_dimension=0, tiled=True)

    own_tokens = lax.dynamic_index_in_dim(tokens, section, 0, False)[0]
    own_cot = lax.dynamic_index_in_dim(cotangent, section, 0, False)[0]
    inputs, outputs, branch, saved, scales = [own_tokens], [], [], [], []
    for l in range(layers):
        rows = gather_rows(inputs[l])
        parts, square, normed, *kept = run_forward(
            heads, wide, rows, w_tiles[l], wo_tiles[l], params[l]
        )
        saved.append((normed, kept))
        total = sum_rows(parts).astype(F32)
        square = sum_rows(square)[:, :1]
        scale = lax.rsqrt(square / INNER + NORM_EPS)
        branch.append(total * scale)
        scales.append(scale)
        outputs.append((inputs[l].astype(F32) + branch[l]).astype(BF16))
        inputs.append(outputs[l])
    grads_in, small_grads = [None] * layers, [None] * layers
    w_grads, wo_grads = [None] * layers, [None] * layers
    grad_rows = own_cot
    for l in reversed(range(layers)):
        rdot = jnp.sum(grad_rows.astype(F32) * branch[l], axis=-1, keepdims=True)
        aux = widened(jnp.concatenate([scales[l], rdot], axis=1), 1, LANES)
        all_grads = gather_rows(grad_rows)
        aux = gather_rows(aux)
        normed, kept = saved[l]
        parts, proj_grad, normed_out, g_ch, g_bc, g_dt = run_backward(
            heads, wide, all_grads, aux, kept, w_tiles[l], wo_tiles[l], params[l]
        )
        w_grads[l] = dot_tn(normed.reshape(-1, width), proj_grad.reshape(-1, proj_grad.shape[-1])).astype(BF16)
        wo_grads[l] = dot_tn(normed_out.reshape(-1, wide), all_grads.reshape(-1, width)).astype(BF16)
        grad_normed = sum_rows(parts).astype(F32)
        rows = inputs[l].astype(F32)
        scale = lax.rsqrt(jnp.mean(rows * rows, axis=-1, keepdims=True) + NORM_EPS)
        scaled = rows * scale
        g_gain = jnp.sum(grad_normed * scaled, axis=0)
        pulled = grad_normed * params[l][0]
        inner = jnp.mean(pulled * scaled, axis=-1, keepdims=True)
        grad = scale * (pulled - scaled * inner) + grad_rows.astype(F32)
        grad_rows = grad.astype(BF16)
        grads_in[l] = grad_rows

        def placed(value, size):
            value = value[..., :size]
            full = jnp.zeros((plan.seq, plan.halves) + value.shape, F32)
            full = lax.dynamic_update_slice(full, value[None, None], (place, half, 0, 0))
            return plan.put(full, 1)

        by_channel = placed(g_ch, channels)
        by_head = placed(g_dt, heads)
        skip = by_channel[5].reshape(HEADS, HEADDIM).sum(-1)
        small_grads[l] = jnp.concatenate(
            [
                g_gain, by_channel[:5].ravel(), g_bc[:5].ravel(), by_head[0], by_head[1], skip, by_channel[6]
            ]
        )

    smalls = lax.psum(jnp.stack(small_grads), ("section", "seq", "fsdp"))
    smalls = lax.dynamic_index_in_dim(smalls, section, 0, False)
    cuts, at = [], 0
    for size in (width, (CONV + 1) * INNER, (CONV + 1) * SHARED, HEADS, HEADS, HEADS):
        at += size
        cuts.append(at)
    g_gain, g_x, g_bc, g_shift, g_rate, g_skip, g_gate = jnp.split(smalls, cuts)
    conv_rows = jnp.concatenate([g_x.reshape(CONV + 1, -1), g_bc.reshape(CONV + 1, -1)], axis=1)

    w_grad = lax.psum_scatter(jnp.stack(w_grads), "section", scatter_dimension=0)
    w_grad = lax.all_to_all(w_grad, "fsdp", 0, 0, tiled=True)
    w_grad = w_grad.reshape(plan.halves, plan.mates, -1, w_grad.shape[-1]).astype(F32).sum(1)
    shared_grad = lax.psum(w_grad[..., 2 * wide : 2 * wide + SHARED].sum(0), "seq")
    head_grads = jnp.concatenate(
        [
            w_grad[..., :channels],
            w_grad[..., wide : wide + channels],
            w_grad[..., 2 * wide + SHARED : 2 * wide + SHARED + heads],
        ],
        axis=-1,
    ).astype(BF16)
    head_grads = lax.all_gather(head_grads, "seq", axis=0)
    grad_w_in = jnp.concatenate(
        [
            plan.put(head_grads[..., :channels], 1),
            plan.put(head_grads[..., channels : 2 * channels], 1),
            shared_grad.astype(BF16),
            plan.put(head_grads[..., 2 * channels :], 1),
        ],
        axis=-1,
    ).astype(F32)
    wo_grad = lax.psum_scatter(jnp.stack(wo_grads)[:, :channels], "section", scatter_dimension=0)
    if plan.pieces == plan.mates:
        wo_grad = lax.psum_scatter(
            wo_grad, "fsdp", scatter_dimension=0, tiled=True, axis_index_groups=plan.mate_groups
        )
        wo_grad = lax.all_gather(wo_grad, "seq", axis=0, tiled=True)
    else:
        full = jnp.zeros((plan.seq, plan.halves) + wo_grad.shape, BF16)
        full = lax.dynamic_update_slice(full, wo_grad[None, None], (place, half, 0, 0))
        full = plan.put(full, 0)
        wo_grad = lax.psum_scatter(full, "fsdp", scatter_dimension=0, tiled=True)
        wo_grad = lax.psum(wo_grad, "seq")

    def home(per_layer):
        return lax.all_to_all(jnp.stack(per_layer), "section", 0, 0, tiled=True)[None, :, None]

    return (
        home(outputs),
        home(grads_in),
        g_gain[None],
        grad_w_in[None],
        conv_rows[None, :CONV],
        conv_rows[CONV:],
        g_shift[None],
        g_rate[None],
        g_skip[None],
        g_gate[None],
        wo_grad.astype(F32)[None],
    )


def solution(mesh):
    shape = tuple(mesh.shape[a] for a in ("section", "seq", "fsdp"))
    return jax.shard_map(
        fast_shards if shape == (2, 4, 4) else shards,
        mesh=mesh,
        in_specs=(
            P(None, "fsdp", "seq", None),
            P(None, "fsdp", "seq", None),
            P("section", None),
            P("section", "fsdp", None),
            P("section", None, None),
            P("section", None),
            P("section", None),
            P("section", None),
            P("section", None),
            P("section", None),
            P("section", "fsdp", None),
        ),
        out_specs=(
            P("section", None, "fsdp", "seq", None),
            P("section", None, "fsdp", "seq", None),
            P("section", None),
            P("section", "fsdp", None),
            P("section", None, None),
            P("section", None),
            P("section", None),
            P("section", None),
            P("section", None),
            P("section", None),
            P("section", "fsdp", None),
        ),
        check_vma=False,
    )
```

```python
from functools import partial

import jax
import jax.numpy as jnp
from jax import lax
from jax.experimental import pallas as pl
from jax.experimental.pallas import tpu as pltpu
from jax.sharding import PartitionSpec as P

HEADS = 48
HEADDIM = 64
STATE = 128
CONV = 4
SPAN = 256
INNER = 3072
XBC = 3328
SHARED = 2 * STATE
LANES = 128
THIRD = 192
PIECE = 256
GAIN_END = 1536
DT_AT = 1536
RATE_AT = DT_AT + LANES
NORM_EPS = 1e-05
HIGHEST = lax.Precision.HIGHEST
BF16 = jnp.bfloat16
F32 = jnp.float32


def take(refs, counts):
    refs = list(refs)
    return [[refs.pop(0) for _ in range(n)] for n in counts]


def dot(left, right, contract=((1,), (0,)), precision=None):
    return lax.dot_general(
        left, right, (contract, ((), ())), preferred_element_type=F32, precision=precision
    )


def dot_nt(left, right):
    return dot(left, right, ((1,), (1,)))


def dot_tn(left, right):
    return dot(left, right, ((0,), (0,)))


def sigmoid(value):
    return 1.0 / (1.0 + jnp.exp(-value))


def shifted(value, distance):
    if distance == 0:
        return value
    length = value.shape[0]
    rows = lax.broadcasted_iota(jnp.int32, value.shape, 0)
    moved = pltpu.roll(value, distance % length, 0)
    if distance > 0:
        return jnp.where(rows >= distance, moved, 0.0)
    return jnp.where(rows < length + distance, moved, 0.0)


def conv_sum(raw, taps):
    total = taps[CONV : CONV + 1]
    for k in range(CONV):
        total = total + taps[k : k + 1] * shifted(raw, CONV - 1 - k)
    return total


def conv_back(grad, raw, taps):
    grad_raw = 0.0
    rows = []
    for k in range(CONV):
        grad_raw = grad_raw + taps[k : k + 1] * shifted(grad, -(CONV - 1 - k))
        rows.append(jnp.sum(grad * shifted(raw, CONV - 1 - k), axis=0, keepdims=True))
    rows.append(jnp.sum(grad, axis=0, keepdims=True))
    return grad_raw, rows


def stacked(rows, count):
    width = rows[0].shape[1]
    short = count - len(rows)
    return jnp.concatenate(rows + [jnp.zeros((short, width), F32)], axis=0)


def triangles():
    row_ids = lax.broadcasted_iota(jnp.int32, (SPAN, SPAN), 0)
    col_ids = lax.broadcasted_iota(jnp.int32, (SPAN, SPAN), 1)
    return row_ids >= col_ids


def step_sizes(dt_raw, dt_row):
    shift = dt_raw + dt_row
    step = jnp.maximum(shift, 0.0) + jnp.log1p(jnp.exp(-jnp.abs(shift)))
    return step, sigmoid(shift)


def low_half():
    return lax.broadcasted_iota(jnp.int32, (SPAN, LANES), 1) < HEADDIM


def head_lanes(h):
    lanes = lax.broadcasted_iota(jnp.int32, (1, LANES), 1)
    return (lanes < HEADDIM) if h % 2 == 0 else (lanes >= HEADDIM)


def split_three(value):
    lanes = lax.broadcasted_iota(jnp.int32, (value.shape[0], LANES), 1)
    result = jnp.zeros((value.shape[0], LANES), F32)
    for k in range(3):
        part = value.astype(BF16).astype(F32)
        result = jnp.where(lanes == k, part, result)
        value = value - part
    return result.astype(BF16)


def selection(ids):
    rows = lax.broadcasted_iota(jnp.int32, (HEADS, LANES), 0)
    columns = lax.broadcasted_iota(jnp.int32, (HEADS, LANES), 1)
    target = jnp.full((HEADS, LANES), -1, jnp.int32)
    for j in range(2):
        here = (columns >= 3 * j) & (columns < 3 * j + 3)
        target = jnp.where(here, columns + 3 * (ids[j] - j), target)
    return (rows == target).astype(F32)


def piece_lanes(ids, j):
    return pl.ds(pl.multiple_of(ids[j] * PIECE, PIECE), PIECE)


def load_params(refs):
    if len(refs) == 2:
        ids, pack_ref = refs
        sel = selection(ids)
        ch = jnp.concatenate([pack_ref[:, piece_lanes(ids, j)][:, :THIRD] for j in range(2)], axis=1)
        rows = [pack_ref[7:8, at : at + HEADS] for at in (DT_AT, RATE_AT)]
        dtp = dot(stacked(rows, 8), sel, precision=HIGHEST)
        return pack_ref[7:8, :GAIN_END], ch, pack_ref[:, -SHARED:], dtp, sel.astype(BF16)
    gain_ref, ch_ref, bc_ref, dtp_ref = refs
    return gain_ref[...], ch_ref[...], bc_ref[...], dtp_ref[...], None


def forward_kernel(heads, *refs):
    u_ref, w_ref, wo_ref, *refs = refs
    forward_rows(heads, load_params(refs[:4]), 0, u_ref, w_ref, wo_ref, None, refs[4:])


def forward_rows(heads, params, i, u_ref, w_ref, wo_ref, h_ref, outs):
    gain, ch, bc, dtp, sel = params
    out_ref, sums_ref, normed_ref, gate_ref, xraw_ref, bcraw_ref, dtraw_ref, mixed_ref = outs
    length, width = u_ref.shape[1:]
    wide = ch.shape[1]
    blocks = length // SPAN
    rows = u_ref[i].astype(F32)
    scale = lax.rsqrt(jnp.mean(rows * rows, axis=-1, keepdims=True) + NORM_EPS)
    normed = (rows * scale * gain).astype(BF16)
    normed_ref[i] = normed
    gate = dot_nt(normed, w_ref[:wide])
    gate_ref[i] = gate
    x_raw = dot_nt(normed, w_ref[wide : 2 * wide]).astype(BF16)
    xraw_ref[i] = x_raw
    rest = dot_nt(normed, w_ref[2 * wide :]).astype(BF16)
    bcraw_ref[i] = rest[:, :SHARED]
    dt_raw = rest[:, SHARED:]
    if sel is not None:
        dt_raw = dot(dt_raw, sel).astype(BF16)
    dtraw_ref[i] = dt_raw
    conv_x = conv_sum(x_raw.astype(F32), ch)
    act_x = (conv_x * sigmoid(conv_x)).astype(BF16)
    conv_bc = conv_sum(rest[:, :SHARED].astype(F32), bc)
    act_bc = (conv_bc * sigmoid(conv_bc)).astype(BF16)
    step, _ = step_sizes(dt_raw.astype(F32), dtp[0:1])
    rate = jnp.exp(dtp[1:2])
    causal = triangles()
    ones = causal.astype(F32)
    lower = low_half()
    carries = [None] * heads
    for b in range(blocks):
        span = slice(b * SPAN, (b + 1) * SPAN)
        step_b = step[span]
        decay = -dot(ones, rate * step_b, precision=HIGHEST)
        decay_t, step_t = decay.T, step_b.T
        b_in, c_out = act_bc[span, :STATE], act_bc[span, STATE:]
        scores = dot_nt(c_out, b_in)
        for first in range(0, heads, 2):
            lanes = slice(first * HEADDIM, first * HEADDIM + LANES)
            x_pair = act_x[span, lanes]
            parts = []
            for h in range(first, min(first + 2, heads)):
                gap = decay[:, h : h + 1] - decay_t[h : h + 1]
                mask = jnp.exp(jnp.where(causal, gap, -1e30))
                weights = (scores * mask * step_t[h : h + 1]).astype(BF16)
                part = dot(weights, x_pair)
                if carries[h] is not None:
                    part += jnp.exp(decay[:, h : h + 1]) * dot(c_out, carries[h].astype(BF16))
                if b + 1 < blocks:
                    last = decay[SPAN - 1 :, h : h + 1]
                    tail = jnp.exp(last - decay[:, h : h + 1]) * step_b[:, h : h + 1]
                    shaped = (b_in.astype(F32) * tail).astype(BF16)
                    fresh = dot_tn(shaped, x_pair)
                    if carries[h] is not None:
                        fresh += jnp.exp(last) * carries[h]
                    carries[h] = fresh
                parts.append(part)
            if len(parts) == 1:
                parts.append(jnp.zeros_like(parts[0]))
            within = jnp.where(lower, parts[0], parts[1])
            mixed = within + ch[5:6, lanes] * x_pair.astype(F32)
            mixed_ref[i, span, lanes] = mixed.astype(BF16)
    gated = mixed_ref[i].astype(F32) * (gate * sigmoid(gate))
    square = jnp.sum(gated * gated, axis=-1, keepdims=True)
    scaled = gated * ch[6:7]
    out_ref[i, :, :width] = dot(scaled.astype(BF16), wo_ref[...]).astype(BF16)
    if sel is None:
        sums_ref[i] = jnp.broadcast_to(square, sums_ref.shape[1:])
        return
    out_ref[i, :, width:] = split_three(square)
    if h_ref is not None:
        grad_no = dot_nt(h_ref[i], wo_ref[...])
        cross = jnp.sum(grad_no * scaled, axis=-1, keepdims=True)
        lane_ids = lax.broadcasted_iota(jnp.int32, (length, LANES), 1)
        both = jnp.where(lane_ids == 0, square, jnp.where(lane_ids == 1, cross, 0.0))
        sums_ref[i] = both.T[:8]


def backward_kernel(heads, *refs):
    h_ref, aux_ref, *refs = refs
    saved, (w_ref, wo_ref), params, outs, sum_refs, scratch = take(refs, (5, 2, 4, 3, 3, 4))
    params = load_params(params)

    def aux():
        return aux_ref[0, :, 0:1], aux_ref[0, :, 1:2]

    sums = backward_rows(heads, params, 0, h_ref, aux, saved, w_ref, wo_ref, outs, scratch)
    for ref, value in zip(sum_refs, sums):

        @pl.when(pl.program_id(0) == 0)
        def _(ref=ref, value=value):
            ref[...] = value

        @pl.when(pl.program_id(0) > 0)
        def _(ref=ref, value=value):
            ref[...] += value


def aux_of_columns(h_ref, i, width):
    aux = h_ref[i, :, width:].astype(F32)
    return aux[:, 0:1] + aux[:, 1:2] + aux[:, 2:3], aux[:, 3:4] + aux[:, 4:5] + aux[:, 5:6]


def aux_of_rows(sums):
    aux = jnp.concatenate([sums, jnp.zeros((LANES - 8, sums.shape[1]), F32)], axis=0).T
    scale = lax.rsqrt(aux[:, 0:1] * (1.0 / INNER) + NORM_EPS)
    return scale, aux[:, 1:2] * scale


def backward_rows(heads, params, i, h_ref, aux, saved, w_ref, wo_ref, outs, scratch):
    _, ch, bc, dtp, sel = params
    gate_ref, xraw_ref, bcraw_ref, dtraw_ref, mixed_ref = saved
    dn_ref, pg_ref, no_ref = outs
    dmix_s, dx_s, dbc_s, ddt_s = scratch
    length, width = dn_ref.shape[1:]
    wide = ch.shape[1]
    blocks = length // SPAN
    x_raw = xraw_ref[i].astype(F32)
    bc_raw = bcraw_ref[i].astype(F32)
    conv_x = conv_sum(x_raw, ch)
    sig_x = sigmoid(conv_x)
    act_x = (conv_x * sig_x).astype(BF16)
    conv_bc = conv_sum(bc_raw, bc)
    sig_bc = sigmoid(conv_bc)
    act_bc = (conv_bc * sig_bc).astype(BF16)
    step, slope = step_sizes(dtraw_ref[i].astype(F32), dtp[0:1])
    rate = jnp.exp(dtp[1:2])
    causal = triangles()
    ones = causal.astype(F32)
    lower = low_half()
    lane_ids = lax.broadcasted_iota(jnp.int32, (SPAN, LANES), 1)
    last_row = lax.broadcasted_iota(jnp.int32, (SPAN, 1), 0) == SPAN - 1
    decays = []
    for b in range(blocks):
        decays.append(-dot(ones, rate * step[b * SPAN : (b + 1) * SPAN], precision=HIGHEST))
    entering = [[None] * heads for _ in range(blocks)]
    for b in range(blocks - 1):
        span = slice(b * SPAN, (b + 1) * SPAN)
        b_in = act_bc[span, :STATE].astype(F32)
        for h in range(heads):
            lanes = slice(h // 2 * LANES, h // 2 * LANES + LANES)
            column = decays[b][:, h : h + 1]
            last = column[SPAN - 1 :]
            tail = jnp.exp(last - column) * step[span, h : h + 1]
            fresh = dot_tn((b_in * tail).astype(BF16), act_x[span, lanes])
            if entering[b][h] is not None:
                fresh += jnp.exp(last) * entering[b][h]
            entering[b + 1][h] = fresh

    scale, rdot = aux()
    h_rows = h_ref[i, :, :width]
    gate = gate_ref[i]
    mixed = mixed_ref[i].astype(F32)
    sig = sigmoid(gate)
    silu = gate * sig
    gated = mixed * silu
    gain = ch[6:7]
    grad_no = dot_nt(h_rows, wo_ref[...])
    grad_g = scale * (gain * grad_no) - gated * (scale * scale * (1.0 / INNER) * rdot)
    scaled = gated * scale
    no_ref[i] = (scaled * gain).astype(BF16)
    gain_row = jnp.sum(grad_no * scaled, axis=0, keepdims=True)
    dmix_s[...] = (grad_g * silu).astype(BF16)
    pg_ref[i, :, :wide] = (grad_g * mixed * (sig * (1.0 + gate * (1.0 - sig)))).astype(BF16)

    leaving = [None] * heads
    rate_row = jnp.zeros((1, LANES), F32)
    for b in reversed(range(blocks)):
        span = slice(b * SPAN, (b + 1) * SPAN)
        step_b, decay = step[span], decays[b]
        decay_t, step_t = decay.T, step_b.T
        b_in, c_out = act_bc[span, :STATE], act_bc[span, STATE:]
        scores = dot_nt(c_out, b_in)
        grad_scores = jnp.zeros((SPAN, SPAN), F32)
        grad_b = jnp.zeros((SPAN, STATE), F32)
        grad_c = jnp.zeros((SPAN, STATE), F32)
        row_sums = jnp.zeros((SPAN, LANES), F32)
        grad_step = jnp.zeros((SPAN, LANES), F32)
        col_rows = []
        for first in range(0, heads, 2):
            lanes = slice(first * HEADDIM, first * HEADDIM + LANES)
            x_pair = act_x[span, lanes]
            grad_pair = dmix_s[span, lanes]
            parts = []
            for h in range(first, min(first + 2, heads)):
                own = head_lanes(h)
                grad_own = jnp.where(own, grad_pair, jnp.zeros((), BF16))
                column = decay[:, h : h + 1]
                mask = jnp.exp(jnp.where(causal, column - decay_t[h : h + 1], -1e30))
                spread = mask * step_t[h : h + 1]
                weights = (scores * spread).astype(BF16)
                part = dot_tn(weights, grad_pair)
                grad_w = dot_nt(grad_own, x_pair)
                grad_scores += grad_w * spread
                pulled = grad_w * (scores * mask)
                col_rows.append(jnp.sum(pulled, axis=0, keepdims=True))
                row_sum = jnp.sum(pulled * step_t[h : h + 1], axis=1, keepdims=True)
                if entering[b][h] is not None:
                    carry = entering[b][h].astype(BF16)
                    grown = jnp.exp(column)
                    grad_grown = grad_own.astype(F32) * grown
                    grad_c += dot_nt(grad_grown.astype(BF16), carry)
                    grad_carry = dot_tn(c_out, grad_grown.astype(BF16))
                    row_sum += jnp.sum(grad_grown * dot(c_out, carry), axis=1, keepdims=True)
                else:
                    grad_carry = None
                if leaving[h] is not None:
                    last = column[SPAN - 1 :]
                    fade = jnp.exp(last - column)
                    tail = fade * step_b[:, h : h + 1]
                    b_wide = b_in.astype(F32)
                    grad_state = leaving[h].astype(BF16)
                    grad_shaped = dot_nt(x_pair, grad_state)
                    part += dot((b_wide * tail).astype(BF16), grad_state)
                    grad_b += grad_shaped * tail
                    grad_tail = jnp.sum(grad_shaped * b_wide, axis=1, keepdims=True)
                    grad_step += jnp.where(lane_ids == h, grad_tail * fade, 0.0)
                    moved = grad_tail * tail
                    total = jnp.sum(moved, axis=0, keepdims=True)
                    if entering[b][h] is not None:
                        faded = jnp.exp(last) * leaving[h]
                        kept = jnp.sum(faded * entering[b][h], axis=1, keepdims=True)
                        total += jnp.sum(kept, axis=0, keepdims=True)
                        grad_carry += faded
                    row_sum += jnp.where(last_row, total, 0.0) - moved
                leaving[h] = grad_carry
                row_sums += jnp.where(lane_ids == h, row_sum, 0.0)
                parts.append(part)
            if len(parts) == 1:
                parts.append(jnp.zeros_like(parts[0]))
            grad_x = jnp.where(lower, parts[0], parts[1])
            dx_s[span, lanes] = grad_x + ch[5:6, lanes] * grad_pair.astype(F32)
        col_sums = stacked(col_rows, LANES).T
        low_scores = grad_scores.astype(BF16)
        dbc_s[span, :STATE] = grad_b + dot_tn(low_scores, c_out)
        dbc_s[span, STATE:] = grad_c + dot(low_scores, b_in)
        grad_decay = dot(
            ones, row_sums - step_b * col_sums, ((0,), (0,)), precision=HIGHEST
        )
        ddt_s[span] = col_sums + grad_step - rate * grad_decay
        rate_row -= jnp.sum(grad_decay * step_b, axis=0, keepdims=True)

    skip_row = jnp.sum(dmix_s[...].astype(F32) * act_x.astype(F32), axis=0, keepdims=True)
    grad_conv = dx_s[...] * (sig_x * (1.0 + conv_x * (1.0 - sig_x)))
    grad_raw, ch_rows = conv_back(grad_conv, x_raw, ch)
    pg_ref[i, :, wide : 2 * wide] = grad_raw.astype(BF16)
    grad_conv = dbc_s[...] * (sig_bc * (1.0 + conv_bc * (1.0 - sig_bc)))
    grad_raw, bc_rows = conv_back(grad_conv, bc_raw, bc)
    pg_ref[i, :, 2 * wide : 2 * wide + SHARED] = grad_raw.astype(BF16)
    grad_dt = ddt_s[...] * slope
    low_dt = grad_dt.astype(BF16)
    if sel is not None:
        low_dt = dot_nt(low_dt, sel).astype(BF16)
    pg_ref[i, :, 2 * wide + SHARED :] = low_dt
    dn_ref[i] = dot(pg_ref[i], w_ref[...]).astype(BF16)
    by_channel = stacked(ch_rows + [skip_row, gain_row], 8)
    by_shared = stacked(bc_rows, 8)
    by_head = stacked([jnp.sum(grad_dt, axis=0, keepdims=True), rate_row * rate], 8)
    if sel is not None:
        by_head = lax.dot_general(
            by_head, sel.astype(F32), (((1,), (1,)), ((), ())),
            preferred_element_type=F32, precision=HIGHEST,
        )
    return by_channel, by_shared, by_head


def add_small(small, by_channel, by_shared, by_head):
    for j in range(2):
        part = by_channel[:, j * THIRD : (j + 1) * THIRD]
        small[:, j * PIECE : j * PIECE + THIRD] += part
    small[:, 2 * PIECE : 3 * PIECE] += by_shared
    small[7:8, 2 * PIECE : 2 * PIECE + HEADS] += by_head[0:1]
    small[7:8, 2 * PIECE + LANES : 2 * PIECE + LANES + HEADS] += by_head[1:2]


def add_gain(small, row):
    for r in range(8):
        small[r : r + 1, 3 * PIECE : 3 * PIECE + THIRD] = row[:, r * THIRD : (r + 1) * THIRD]


def whole_spec(array):
    return pl.BlockSpec(array.shape, lambda i: (0,) * array.ndim)


def row_spec(length, width):
    return pl.BlockSpec((1, length, width), lambda i: (i, 0, 0))


def block_spec(array):
    return pl.BlockSpec((1,) + array.shape[1:], lambda i: (i, 0, 0))


PARAMS = dict(vmem_limit_bytes=60 * 1024 * 1024)


def run_forward(heads, wide, rows, w, wo, params):
    count, length, width = rows.shape
    constants = [w, wo, *params]
    outs = [
        (width, BF16), (LANES, F32), (width, BF16), (wide, F32),
        (wide, BF16), (SHARED, BF16), (LANES, BF16), (wide, BF16),
    ]
    return pl.pallas_call(
        partial(forward_kernel, heads),
        grid=(count,),
        out_shape=[jax.ShapeDtypeStruct((count, length, n), t) for n, t in outs],
        in_specs=[block_spec(rows)] + [whole_spec(c) for c in constants],
        out_specs=[row_spec(length, n) for n, _ in outs],
        compiler_params=pltpu.CompilerParams(**PARAMS),
        name="forward",
    )(rows, *constants)


def run_backward(heads, wide, grad_rows, aux, saved, w, wo, params):
    count, length, _ = grad_rows.shape
    columns, width = w.shape
    given = [grad_rows, aux, *saved]
    constants = [w, wo, *params]
    outs = [(width, BF16), (columns, BF16), (wide, BF16)]
    sums = [(8, wide), (8, SHARED), (8, LANES)]
    return pl.pallas_call(
        partial(backward_kernel, heads),
        grid=(count,),
        out_shape=[jax.ShapeDtypeStruct((count, length, n), t) for n, t in outs]
        + [jax.ShapeDtypeStruct(s, F32) for s in sums],
        in_specs=[block_spec(g) for g in given] + [whole_spec(c) for c in constants],
        out_specs=[row_spec(length, n) for n, _ in outs]
        + [pl.BlockSpec(s, lambda i: (0, 0)) for s in sums],
        scratch_shapes=backward_scratch(length, wide),
        compiler_params=pltpu.CompilerParams(**PARAMS),
        name="backward",
    )(*given, *constants)


def backward_scratch(length, wide):
    return [
        pltpu.VMEM((length, wide), BF16),
        pltpu.VMEM((length, wide), F32),
        pltpu.VMEM((length, SHARED), F32),
        pltpu.VMEM((length, LANES), F32),
    ]


class Plan:
    def __init__(self, seq, fsdp):
        self.seq, self.fsdp = seq, fsdp
        halves = 2
        if fsdp % 2 or HEADS % (seq * 2) or (HEADS // fsdp) % seq:
            halves = 1
        self.halves, self.mates = halves, fsdp // halves
        self.heads = HEADS // (seq * halves)
        self.pieces = self.mates if (HEADS // fsdp) % seq == 0 else 1
        channels = self.heads * HEADDIM
        self.channels = channels
        self.wide = -(-channels // LANES) * LANES
        self.peer_groups = [[lo + self.mates * h for h in range(halves)] for lo in range(self.mates)]
        self.mate_groups = [[h * self.mates + j for j in range(self.mates)] for h in range(halves)]

    def split(self, array, axis):
        size = array.shape[axis] // (self.halves * self.pieces * self.seq)
        shape = array.shape[:axis] + (self.halves, self.pieces, self.seq, size) + array.shape[axis + 1 :]
        return array.reshape(shape)

    def take(self, array, axis, place):
        array = lax.dynamic_index_in_dim(self.split(array, axis), place, axis + 2, False)
        shape = array.shape[: axis + 1] + (-1,) + array.shape[axis + 3 :]
        return jnp.moveaxis(array.reshape(shape), axis, 0)

    def put(self, parts, axis):
        size = parts.shape[axis + 2] // self.pieces
        shape = parts.shape[: axis + 2] + (self.pieces, size) + parts.shape[axis + 3 :]
        parts = jnp.moveaxis(parts.reshape(shape), (1, axis + 2, 0), (axis, axis + 1, axis + 2))
        shape = parts.shape[:axis] + (-1,) + parts.shape[axis + 4 :]
        return parts.reshape(shape)


def widened(array, axis, size):
    pads = [(0, 0)] * array.ndim
    pads[axis] = (0, size - array.shape[axis])
    return jnp.pad(array, pads)


MESH = pl.DeviceIdType.MESH
ANY = pl.BlockSpec(memory_space=pl.ANY)
VMEM = pl.BlockSpec(memory_space=pltpu.VMEM)
DMA = pltpu.SemaphoreType.DMA


class Spot:
    def __init__(self):
        self.s, self.q, self.z = (lax.axis_index(a) for a in ("section", "seq", "fsdp"))
        self.half, self.lo = self.z // 2, self.z % 2
        self.mate, self.twin = self.z + 1 - 2 * self.lo, (self.z + 2) % 4
        self.around = [None, self.q + 1 - 2 * (self.q % 2), (self.q + 2) % 4, 3 - self.q]
        self.sibling = (1 - self.s, self.q, self.z)
        self.at_mate, self.at_twin = (self.s, self.q, self.mate), (self.s, self.q, self.twin)

    def plane(self, k):
        return (self.s, self.around[k], self.z)

    def column(self, z):
        return (self.s, self.q, z)

    def piece(self, half, j):
        return 8 * half + 4 * j + self.q


def greet(places):
    barrier = pltpu.get_barrier_semaphore()
    for place in places:
        pl.semaphore_signal(barrier, inc=1, device_id=place, device_id_type=MESH)
    pl.semaphore_wait(barrier, len(places))


def remote(src, dst, send_sem, recv_sem, place):
    return pltpu.make_async_remote_copy(
        src_ref=src, dst_ref=dst, send_sem=send_sem, recv_sem=recv_sem, device_id=place, device_id_type=MESH
    )


class Home:
    def __init__(self, src, buffer, dst, sems):
        self.load = pltpu.make_async_copy(src, buffer, sems[0])
        self.store = pltpu.make_async_copy(buffer, dst, sems[1])

    def begin(self):
        self.load.start()

    def go_on(self):
        self.load.wait()
        self.store.start()

    def end(self):
        self.store.wait()


class Spread:
    SEMS = [DMA((7,)), DMA((7,)), DMA]

    def __init__(self, spot, own, all_rows, sems):
        self.spot, self.own, self.all = spot, own, all_rows
        self.send, self.recv, self.local = sems

    def slot(self, half):
        rows = self.own.shape[0]
        return self.all.at[half, pl.ds(pl.multiple_of(self.spot.q * rows, rows), rows)]

    def copy(self, j):
        spot = self.spot
        slot = self.slot(spot.half)
        if j == 3:
            return remote(self.own, slot, self.send.at[3], self.recv.at[3], spot.at_twin)
        if j < 3:
            return remote(self.own, slot, self.send.at[j], self.recv.at[j], spot.plane(j + 1))
        slot = self.slot(1 - spot.half)
        return remote(slot, slot, self.send.at[j], self.recv.at[j], spot.plane(j - 3))

    def here(self):
        return pltpu.make_async_copy(self.own, self.slot(self.spot.half), self.local)

    def start(self):
        for j in (3, 0, 1, 2):
            self.copy(j).start()
        self.here().start()

    def forward(self):
        self.copy(3).wait_recv()
        for j in (4, 5, 6):
            self.copy(j).start()

    def own_half(self):
        for j in (0, 1, 2):
            self.copy(j).wait_recv()
        self.here().wait()

    def other_half(self):
        for j in (4, 5, 6):
            self.copy(j).wait_recv()

    def close(self):
        for j in range(7):
            self.copy(j).wait_send()

    def finish(self):
        self.own_half()
        self.other_half()
        self.close()


class Sum:
    @staticmethod
    def scratch(rows, columns):
        return [
            pltpu.VMEM((2, 4 * rows, columns), BF16),
            pltpu.VMEM((3, 2, rows, columns), BF16),
            pltpu.VMEM((2, rows, columns), BF16),
            DMA((7,)),
            DMA((7,)),
        ]

    def __init__(self, spot, width, scratch):
        self.spot, self.width = spot, width
        self.parts, self.recv_rows, self.twin_rows, self.send, self.recv = scratch
        self.rows = self.twin_rows.shape[1]

    def half(self, i):
        return 1 - self.spot.half + i * (2 * self.spot.half - 1)

    def block(self, q):
        return pl.ds(pl.multiple_of(q * self.rows, self.rows), self.rows)

    def copy(self, k, i):
        spot = self.spot
        j = 3 * i + k - 1
        return remote(
            self.parts.at[self.half(i), self.block(spot.around[k])], self.recv_rows.at[k - 1, i],
            self.send.at[j], self.recv.at[j], spot.plane(k),
        )

    def across(self):
        return remote(
            self.twin_rows.at[0], self.twin_rows.at[1], self.send.at[6], self.recv.at[6], self.spot.at_twin
        )

    def start(self, i):
        for k in (1, 2, 3):
            self.copy(k, i).start()

    def plane_total(self, i):
        total = self.parts[self.half(i), self.block(self.spot.q), :].astype(F32)
        for k in (1, 2, 3):
            self.copy(k, i).wait_recv()
            total += self.recv_rows[k - 1, i].astype(F32)
        return total

    def forward(self):
        total = self.plane_total(0)
        width = self.width
        self.twin_rows[0, :, :width] = total[:, :width].astype(BF16)
        if total.shape[1] > width:
            column = jnp.sum(total[:, width:], axis=1, keepdims=True)
            self.twin_rows[0, :, width:] = split_three(column)
        self.across().start()

    def finish(self):
        total = self.plane_total(1)
        self.across().wait_recv()
        total += self.twin_rows[1].astype(F32)
        return total

    def close(self):
        for i in range(2):
            for k in (1, 2, 3):
                self.copy(k, i).wait_send()
        self.across().wait_send()


class RelaySum(Sum):
    @staticmethod
    def scratch(rows, columns):
        return [
            pltpu.VMEM((2, 4 * rows, columns), BF16),
            pltpu.VMEM((2, 2, rows, columns), BF16),
            pltpu.VMEM((2, rows, columns), BF16),
            DMA((9,)),
            DMA((9,)),
            pltpu.VMEM((2, rows, columns), BF16),
        ]

    def __init__(self, spot, width, scratch):
        super().__init__(spot, width, scratch[:5])
        self.relays = scratch[5]
        columns = self.relays.shape[2]
        cut = columns // 2 // LANES * LANES
        self.cuts = [(0, cut), (cut, columns - cut)]

    def relay(self, k, i):
        spot = self.spot
        columns = pl.ds(*self.cuts[k - 1])
        return remote(
            self.parts.at[self.half(i), self.block(spot.around[3]), columns], self.relays.at[i, :, columns],
            self.send.at[5 + 2 * i + k - 1], self.recv.at[5 + 2 * i + k - 1], spot.plane(k),
        )

    def copy(self, k, i):
        spot = self.spot
        j = 2 * i + k - 1
        return remote(
            self.parts.at[self.half(i), self.block(spot.around[k])], self.recv_rows.at[k - 1, i],
            self.send.at[j], self.recv.at[j], spot.plane(k),
        )

    def across(self):
        return remote(
            self.twin_rows.at[0], self.twin_rows.at[1], self.send.at[4], self.recv.at[4], self.spot.at_twin
        )

    def start(self, i):
        for k in (1, 2):
            self.relay(k, i).start()

    def go_on(self, i):
        for k in (1, 2):
            self.relay(k, i).wait_recv()
            at, size = self.cuts[k - 1]
            rows = self.block(self.spot.around[3 - k])
            half = self.half(i)
            own = self.parts[half, rows, at : at + size].astype(F32)
            total = own + self.relays[i, :, at : at + size].astype(F32)
            self.parts[half, rows, at : at + size] = total.astype(BF16)
        for k in (1, 2):
            self.copy(k, i).start()

    def plane_total(self, i):
        total = self.parts[self.half(i), self.block(self.spot.q), :].astype(F32)
        for k in (1, 2):
            self.copy(k, i).wait_recv()
            total += self.recv_rows[k - 1, i].astype(F32)
        return total

    def close(self):
        for i in range(2):
            for k in (1, 2):
                self.copy(k, i).wait_send()
                self.relay(k, i).wait_send()
        self.across().wait_send()


def tile_parts(spot, half):
    parts = []
    for part in range(2):
        for j in range(2):
            at = part * INNER + THIRD * spot.piece(half, j)
            parts.append((pl.multiple_of(at, 64), (2 * part + j) * THIRD, THIRD))
    return parts + [(2 * INNER, 4 * THIRD, SHARED + HEADS)]


class Weights:
    PARTS = 6
    ORDER = (4, 5, 0, 1, 2, 3)
    QUARTER = SHARED // 4

    @staticmethod
    def scratch(columns, shard, width):
        buffers = [pltpu.VMEM((columns, shard), BF16), pltpu.VMEM((THIRD, width), BF16)]
        return buffers + [DMA((9,)), DMA((57,)), DMA((57,))]

    def __init__(self, spot, layer, w_in, w_out, tile, tile_out, scratch):
        self.spot, self.layer = spot, layer
        self.w_in, self.w_out, self.tile, self.tile_out = w_in, w_out, tile, tile_out
        self.buffer, self.out_buffer, self.local, self.send, self.recv = scratch
        self.shard = w_in.shape[1]
        self.others = 2 * (1 - spot.half)
        self.gateway = 2 - spot.half
        self.is_gateway = (spot.z == 1) | (spot.z == 2)

    def at_source(self, step):
        pl.when(self.spot.s == self.layer)(step)

    def at_relay(self, step):
        pl.when(self.spot.s != self.layer)(step)

    def parts(self, half, n):
        if n < 4:
            return tile_parts(self.spot, half)[n]
        if n == 5:
            return 2 * INNER + SHARED, 4 * THIRD + SHARED, HEADS
        at = self.QUARTER * self.spot.q
        return (
            pl.multiple_of(2 * INNER + at, 64), pl.multiple_of(4 * THIRD + at, 64), self.QUARTER
        )

    def source(self, half, n):
        first, _, size = self.parts(half, n)
        return self.w_in.at[pl.ds(first, size)]

    def target(self, z, n):
        _, first, size = self.parts(0, n)
        columns = pl.ds(pl.multiple_of(z * self.shard, LANES), self.shard)
        return self.tile.at[pl.ds(first, size), columns]

    def buffered(self, n):
        _, first, size = self.parts(0, n)
        return self.buffer.at[pl.ds(first, size)]

    def load(self, n):
        return pltpu.make_async_copy(self.source(self.spot.half, n), self.buffered(n), self.send.at[n])

    def store(self, n):
        return pltpu.make_async_copy(self.buffered(n), self.target(self.spot.z, n), self.local.at[3 + n])

    def out_home(self):
        return Home(
            self.out_source(), self.out_buffer, self.out_part(self.spot.lo),
            (self.local.at[1], self.local.at[2]),
        )

    def to_mate(self, n):
        source, target = self.source(self.spot.half, n), self.target(self.spot.z, n)
        return remote(source, target, self.send.at[n], self.recv.at[n], self.spot.at_mate)

    def to_gateway(self, n):
        source, target = self.source(1 - self.spot.half, n), self.target(self.spot.z, n)
        j = 6 + 6 * self.spot.lo + n
        place = (1 - self.spot.s, self.spot.q, self.gateway)
        return remote(source, target, self.send.at[6 + n], self.recv.at[j], place)

    def passed(self, c, n):
        part = self.target(self.others + c, n)
        j = 6 * c + n
        return remote(part, part, self.send.at[12 + j], self.recv.at[6 + j], self.spot.at_mate)

    def to_sibling(self, b, n):
        j = 24 + 6 * b + n
        part = self.target([self.spot.z, self.spot.mate, self.others, self.others + 1][b], n)
        source = self.source(self.spot.half, n) if b == 0 else part
        return remote(source, part, self.send.at[j], self.recv.at[j], self.spot.sibling)

    def out_part(self, lo):
        return self.tile_out.at[pl.ds(pl.multiple_of(lo * THIRD, 64), THIRD)]

    def out_source(self):
        return self.w_out.at[pl.ds(pl.multiple_of(self.spot.q * THIRD, 64), THIRD)]

    def out_to(self, n):
        part = self.out_part(self.spot.lo if n < 2 else 1 - self.spot.lo)
        place = self.spot.sibling if n else self.spot.at_mate
        source = self.out_source() if n < 2 else part
        return remote(source, part, self.send.at[48 + n], self.recv.at[48 + n], place)

    def send_part(self, n):
        if n < self.PARTS:
            self.to_gateway(n).start()
            self.to_mate(n).start()
        elif n == self.PARTS:
            self.out_to(0).start()

    def begin(self):
        @self.at_source
        def _():
            for n in range(self.PARTS):
                self.load(n).start()
            self.out_home().begin()

    def quarter(self, q):
        at = 4 * THIRD + self.QUARTER * q
        return self.tile.at[pl.ds(pl.multiple_of(at, 64), self.QUARTER)]

    def to_plane(self, k):
        part = self.quarter(self.spot.q)
        return remote(part, part, self.send.at[50 + k], self.recv.at[50 + k], self.spot.plane(k))

    def quarter_to_sibling(self, k):
        part = self.quarter(self.spot.around[k])
        return remote(part, part, self.send.at[53 + k], self.recv.at[53 + k], self.spot.sibling)

    def mates(self):
        for n in self.ORDER:
            self.to_mate(n).start()
        self.out_to(0).start()

    def start(self, window):
        @self.at_source
        def _():
            for n in self.ORDER:
                self.load(n).wait()
            for n in self.ORDER[:window]:
                self.to_gateway(n).start()
            pl.when(self.is_gateway)(self.mates)
            for n in self.ORDER:
                self.to_sibling(0, n).start()
                self.store(n).start()
            self.out_to(1).start()
            self.out_home().go_on()

    def more(self, at, window):
        @self.at_source
        def _():
            self.to_gateway(self.ORDER[at - window]).wait_send()
            self.to_gateway(self.ORDER[at]).start()
            if at == self.PARTS - 1:
                pl.when(jnp.logical_not(self.is_gateway))(self.mates)

    def relay(self, at):
        n = self.ORDER[at]

        @self.at_relay
        def _():
            for c in range(2):
                self.passed(c, n).wait_recv()
                pl.when(self.is_gateway)(lambda c=c: self.passed(c, n).start())
                self.to_sibling(2 + c, n).start()

    def share(self):
        @self.at_source
        def _():
            self.store(4).wait()
            self.to_mate(4).wait_recv()
            self.to_sibling(1, 4).start()
            for c in range(2):
                self.to_sibling(2 + c, 4).wait_recv()
            for k in (1, 2, 3):
                self.to_plane(k).start()

    def shared(self):
        @self.at_source
        def _():
            for k in (1, 2, 3):
                self.to_plane(k).wait_recv()
                self.quarter_to_sibling(k).start()

    def relay_mate(self):
        @self.at_source
        def _():
            for n in self.ORDER[1:]:
                self.to_mate(n).wait_recv()
                self.to_sibling(1, n).start()
            self.out_to(0).wait_recv()
            self.out_to(2).start()

    def finish(self, window):
        @self.at_source
        def _():
            for n in self.ORDER[-window:]:
                self.to_gateway(n).wait_send()
            for n in self.ORDER:
                self.to_mate(n).wait_send()
                for b in range(2):
                    if n != 4:
                        self.to_sibling(2 + b, n).wait_recv()
                    self.to_sibling(b, n).wait_send()
                if n != 4:
                    self.store(n).wait()
            for k in (1, 2, 3):
                self.to_plane(k).wait_send()
                self.quarter_to_sibling(k).wait_send()
            self.out_home().end()
            for n in range(3):
                self.out_to(n).wait_send()

        @self.at_relay
        def _():
            for n in self.ORDER:
                for c in range(2):
                    self.to_sibling(c, n).wait_recv()
                    self.to_sibling(2 + c, n).wait_send()
                    pl.when(self.is_gateway)(lambda c=c, n=n: self.passed(c, n).wait_send())
            for k in (1, 2, 3):
                self.quarter_to_sibling(k).wait_recv()
            for n in (1, 2):
                self.out_to(n).wait_recv()


def all_places(spot):
    places = [spot.plane(k) for k in (1, 2, 3)]
    places += [(s, spot.q, (spot.z + k) % 4) for k in (1, 2, 3) for s in range(2)]
    return places + [spot.sibling]


def open_kernel(*refs):
    ins, outs, weight_s, spread_a, spread_b, (own_tokens, own_cot, own_pack, load, *pack_sems) = take(
        refs, (11, 5, 5, 3, 3, 7)
    )
    w_in, w_out, tokens, cotangent, *raw = ins
    tile, tile_out, packs, all_tokens, all_cot = outs
    spot = Spot()
    weights = Weights(spot, 0, w_in, w_out, tile, tile_out, weight_s)
    rows = Spread(spot, own_tokens, all_tokens, spread_a)
    grads = Spread(spot, own_cot, all_cot, spread_b)
    loads = [
        pltpu.make_async_copy(src, dst, load.at[n])
        for n, (src, dst) in enumerate(
            ((tokens.at[spot.s], own_tokens), (cotangent.at[spot.s], own_cot))
        )
    ]
    pack_here = pltpu.make_async_copy(own_pack, packs.at[spot.s], pack_sems[0])
    pack_there = remote(own_pack, packs.at[spot.s], pack_sems[1], pack_sems[2], spot.sibling)
    for copy in loads:
        copy.start()
    weights.begin()
    greet(all_places(spot))
    for copy in loads:
        copy.wait()
    few = 2
    rows.start()
    weights.start(few)
    pack_params(own_pack, *raw)
    pack_here.start()
    pack_there.start()
    weights.more(2, few)
    rows.forward()
    grads.start()
    for at in (3, 4, 5):
        weights.more(at, few)
    weights.relay(0)
    weights.relay(1)
    weights.share()
    weights.relay(2)
    grads.forward()
    weights.relay(3)
    weights.shared()
    weights.relay(4)
    weights.relay(5)
    weights.relay_mate()
    rows.finish()
    grads.finish()
    weights.finish(few)
    pack_here.wait()
    pack_there.wait()


def pack_params(pack, conv_weight, conv_bias, gate_gain, skip_gain, norm_gain, dt_bias, a_log):
    pack[...] = jnp.zeros_like(pack)
    for p in range(INNER // THIRD):
        source, target = slice(p * THIRD, (p + 1) * THIRD), slice(p * PIECE, p * PIECE + THIRD)
        pack[0:CONV, target] = conv_weight[:, source]
        pack[CONV : CONV + 1, target] = conv_bias[:, source]
        skips = [jnp.broadcast_to(skip_gain[:, 3 * p + h : 3 * p + h + 1], (1, HEADDIM)) for h in range(3)]
        pack[5:6, target] = jnp.concatenate(skips, axis=1)
        pack[6:7, target] = gate_gain[:, source]
    pack[0:CONV, -SHARED:] = conv_weight[:, INNER:]
    pack[CONV : CONV + 1, -SHARED:] = conv_bias[:, INNER:]
    pack[7:8, :GAIN_END] = norm_gain[...]
    pack[7:8, DT_AT : DT_AT + HEADS] = dt_bias[...]
    pack[7:8, RATE_AT : RATE_AT + HEADS] = a_log[...]


def layer_rows(total, rows_in, branch, scales, rows_out):
    width = rows_in.shape[1]
    square = jnp.sum(total[:, width:], axis=1, keepdims=True)
    scale = lax.rsqrt(square * (1.0 / INNER) + NORM_EPS)
    part = total[:, :width] * scale
    rows_out[...] = (rows_in[...].astype(F32) + part).astype(BF16)
    if branch is not None:
        branch[...] = part
        scales[...] = jnp.broadcast_to(scale, scales.shape)


def norm_back(total, rows_in, gain, grad_out):
    rows = rows_in[...].astype(F32)
    scale = lax.rsqrt(jnp.mean(rows * rows, axis=-1, keepdims=True) + NORM_EPS)
    scaled = rows * scale
    pulled = total * gain
    inner = jnp.mean(pulled * scaled, axis=-1, keepdims=True)
    grad = scale * (pulled - scaled * inner) + grad_out[...].astype(F32)
    return grad, jnp.sum(total * scaled, axis=0, keepdims=True)


def add_rows(target, sources, chunk=64):
    @pl.loop(0, target.shape[0] // chunk)
    def _(n):
        rows = pl.ds(pl.multiple_of(n * chunk, chunk), chunk)
        total = sources[0][rows, :].astype(F32)
        for source in sources[1:]:
            total += source[rows, :].astype(F32)
        target[rows, :] = total.astype(target.dtype)


class Grads:
    ORDER = (4, 0, 1, 2, 3, 5)

    @staticmethod
    def scratch(shard, columns, wide, width):
        return [
            pltpu.VMEM((3, columns, width), BF16),
            pltpu.VMEM((3, wide, width), BF16),
            pltpu.VMEM((2, columns, shard), BF16),
            pltpu.VMEM((2, columns, shard), BF16),
            pltpu.VMEM((THIRD, width), BF16),
            DMA((22,)),
            DMA((27,)),
        ]

    @staticmethod
    def results(shard, width):
        return [((2, 4 * THIRD, shard), BF16), ((SHARED + HEADS, shard), BF16), ((THIRD, width), BF16)]

    def __init__(self, spot, results, scratch):
        self.spot = spot
        self.reduced, self.shared, self.out = results
        self.cores, self.cores_out, self.planes, self.relay, self.mate_out, self.send, self.recv = scratch
        self.shard = self.planes.shape[2]
        self.others = 2 * (1 - spot.half)
        self.is_gateway = (spot.z == 1) | (spot.z == 2)

    def rows(self, n):
        _, first, size = tile_parts(self.spot, 0)[n]
        return pl.ds(first, size)

    def columns(self, z):
        return pl.ds(pl.multiple_of(z * self.shard, LANES), self.shard)

    def core_copy(self, n):
        buffer, rows = (self.cores_out, pl.ds(0, self.cores_out.shape[1])) if n == 5 else (self.cores, self.rows(n))
        return remote(
            buffer.at[2, rows], buffer.at[1, rows], self.send.at[n], self.recv.at[n], self.spot.sibling
        )

    def product(self, layer, n, proj_grad, normed, normed_out, h_rows):
        def flat(value):
            return value.reshape(-1, value.shape[-1])

        width = self.cores.shape[2]
        slot = 2 * (self.spot.s - layer) * (self.spot.s - layer)
        if n == 5:
            total = dot_tn(flat(normed_out[...]), flat(h_rows[:, :, :width]))
            self.cores_out[slot] = total.astype(BF16)
        else:
            _, first, size = tile_parts(self.spot, 0)[n]
            total = dot_tn(flat(proj_grad[:, :, first : first + size]), flat(normed[...]))
            self.cores[slot, first : first + size, :] = total.astype(BF16)
        pl.when(self.spot.s != layer)(lambda: self.core_copy(n).start())

    def far_part(self, c, n):
        return self.cores.at[0, self.rows(n), self.columns(self.others + c)]

    def to_mate(self, n):
        source = self.cores.at[0, self.rows(n), self.columns(self.spot.mate)]
        target = self.planes.at[1, self.rows(n)]
        return remote(source, target, self.send.at[6 + n], self.recv.at[11 + n], self.spot.at_mate)

    def to_relay(self, c, n):
        j = 2 * n + c
        target = self.relay.at[c, self.rows(n)]
        return remote(
            self.far_part(c, n), target, self.send.at[11 + j], self.recv.at[16 + j], self.spot.at_mate
        )

    def to_far(self, c, n):
        target = self.planes.at[0, self.rows(n)]
        place = self.spot.column(self.others + c)
        return remote(
            self.far_part(c, n), target, self.send.at[11 + 2 * n + c], self.recv.at[6 + n], place
        )

    def out_rows(self, lo):
        return pl.ds(pl.multiple_of(lo * THIRD, 64), THIRD)

    def mate_copy(self):
        source = self.cores_out.at[0, self.out_rows(1 - self.spot.lo)]
        return remote(source, self.mate_out, self.send.at[21], self.recv.at[26], self.spot.at_mate)

    def sent(self, n):
        self.to_mate(n).wait_send()
        for c in range(2):
            self.to_relay(c, n).wait_send()

    def to_planes(self, n):
        self.core_copy(n).wait_recv()
        if n == 5:
            add_rows(self.cores_out.at[0], [self.cores_out.at[0], self.cores_out.at[1]])
            self.mate_copy().start()
            return
        own, sibling = self.cores.at[0, self.rows(n)], self.cores.at[1, self.rows(n)]
        add_rows(own, [own, sibling], 48 if n < 4 else 16)

        @pl.when(jnp.logical_not(self.is_gateway))
        def _():
            for c in range(2):
                self.to_relay(c, n).start()

        self.to_mate(n).start()

    def pass_on(self, n):
        @pl.when(self.is_gateway)
        def _():
            for c in range(2):
                self.to_relay(c, n).wait_recv()
                target, relay = self.far_part(c, n), self.relay.at[c, self.rows(n)]
                add_rows(target, [target, relay], 48 if n < 4 else 16)
                self.to_far(c, n).start()

    def gather(self, n):
        if n == 5:
            self.mate_copy().wait_recv()
            add_rows(self.out, [self.cores_out.at[0, self.out_rows(self.spot.lo)], self.mate_out], 48)
            return
        self.to_mate(n).wait_recv()
        self.to_far(0, n).wait_recv()
        _, first, size = tile_parts(self.spot, 0)[n]
        mine = self.columns(self.spot.z)
        chunk = 48 if n < 4 else 16

        @pl.loop(0, size // chunk)
        def _(r):
            rows = pl.ds(pl.multiple_of(first + r * chunk, 16), chunk)
            own = self.cores[0, rows, mine].astype(F32) + self.planes[1, rows, :].astype(F32)
            other = self.planes[0, rows, :]
            if n < 4:
                self.reduced[0, rows, :] = own.astype(BF16)
                self.reduced[1, rows, :] = other
            else:
                rows = pl.ds(pl.multiple_of(r * chunk, 16), chunk)
                self.shared[rows, :] = (own + other.astype(F32)).astype(BF16)

    def finish(self):
        self.mate_copy().wait_send()
        for n in self.ORDER:
            self.core_copy(n).wait_send()


class GradsAround:
    @staticmethod
    def scratch(shard):
        return [
            pltpu.VMEM((4, SHARED + HEADS, shard), BF16),
            DMA((11,)),
            DMA((34,)),
            DMA((34,)),
        ]

    def __init__(self, spot, results, final, final_out, scratch):
        self.spot, self.final, self.final_out = spot, final, final_out
        self.reduced, self.shared, self.out = results
        self.sums, self.local, self.send, self.recv = scratch

    def region(self, k, i, n):
        q = self.spot.q if k == 0 else self.spot.around[k]
        half = self.spot.half if i == 0 else 1 - self.spot.half
        at = n // 2 * INNER + THIRD * (8 * half + 4 * (n % 2) + q)
        return self.final.at[pl.ds(pl.multiple_of(at, 64), THIRD)]

    def copy(self, k, i, n):
        source = self.reduced.at[i, pl.ds(n * THIRD, THIRD)]
        target = self.region(0, i, n)
        j = 4 * i + n
        if k == 0:
            return pltpu.make_async_copy(source, target, self.local.at[j])
        if k < 3:
            j += 8 * (k - 1)
            return remote(source, target, self.send.at[j], self.recv.at[j], self.spot.plane(k))
        source = target = self.region(1 if i == 0 else 2, i, n)
        place = self.spot.plane(2 if i == 0 else 1)
        return remote(source, target, self.send.at[16 + j], self.recv.at[16 + j], place)

    def send_part(self, n):
        for i in range(2):
            for k in (1, 2, 0):
                self.copy(k, i, n).start()

    def pass_part(self, n):
        for i in range(2):
            self.copy(1 + i, i, n).wait_recv()
            self.copy(3, i, n).start()

    def out_region(self, k, i):
        q = self.spot.q if k == 0 else self.spot.around[k]
        size = THIRD if i is None else THIRD // 2
        at = q * THIRD + (0 if i is None else i * size)
        return self.final_out.at[pl.ds(pl.multiple_of(at, 32), size)]

    def out_copy(self, k, i=None):
        target = self.out_region(0, None)
        if k == 0:
            return pltpu.make_async_copy(self.out, target, self.local.at[8])
        if k < 3:
            return remote(self.out, target, self.send.at[23 + k], self.recv.at[23 + k], self.spot.plane(k))
        part = self.out_region(1 + i, i)
        return remote(part, part, self.send.at[26 + i], self.recv.at[26 + i], self.spot.plane(2 - i))

    def send_out(self):
        for k in (1, 2, 0):
            self.out_copy(k).start()

    def pass_out(self):
        for i in range(2):
            self.out_copy(1 + i).wait_recv()
            self.out_copy(3, i).start()

    def shared_copy(self, k):
        source = self.shared if k == 1 else self.sums.at[1]
        target = self.sums.at[0 if k == 1 else 2]
        return remote(source, target, self.send.at[27 + k], self.recv.at[27 + k], self.spot.plane(k))

    def shared_home(self):
        tail = self.final.at[pl.ds(2 * INNER, SHARED + HEADS)]
        return pltpu.make_async_copy(self.sums.at[3], tail, self.local.at[9])

    def shared_step(self, n):
        if n > 0:
            self.shared_copy(n).wait_recv()
            sources = [self.shared, self.sums.at[0]] if n == 1 else [self.sums.at[1], self.sums.at[2]]
            add_rows(self.sums.at[1 if n == 1 else 3], sources, 16)
        if n < 2:
            self.shared_copy(n + 1).start()
        else:
            self.shared_home().start()

    def finish(self):
        for i in range(2):
            for n in range(4):
                self.copy(2 - i, i, n).wait_recv()
                self.copy(3, i, n).wait_recv()
                for k in (1, 2, 3):
                    self.copy(k, i, n).wait_send()
                self.copy(0, i, n).wait()
            self.out_copy(3, i).wait_recv()
            self.out_copy(3, i).wait_send()
        for k in (1, 2):
            self.out_copy(k).wait_send()
            self.shared_copy(k).wait_send()
        self.out_copy(0).wait()
        self.shared_home().wait()


class SmallSum:
    SHAPE = (8, 4 * PIECE)

    @staticmethod
    def scratch():
        return [
            pltpu.VMEM((4,) + SmallSum.SHAPE, F32),
            pltpu.VMEM((8,) + SmallSum.SHAPE, F32),
            DMA((9,)),
            DMA((9,)),
        ]

    def __init__(self, spot, scratch):
        self.spot = spot
        self.small, self.group, self.send, self.recv = scratch

    def to_sibling(self):
        return remote(
            self.small.at[0], self.small.at[1], self.send.at[0], self.recv.at[0], self.spot.sibling
        )

    def to_mate(self):
        return remote(
            self.small.at[2], self.small.at[3], self.send.at[1], self.recv.at[1], self.spot.at_mate
        )

    def to_group(self, j):
        spot = self.spot
        part = self.group.at[4 * spot.half + spot.q]
        places = [spot.plane(k) for k in (1, 2, 3)] + [spot.at_twin]
        places += [(spot.s, spot.around[k], spot.twin) for k in (1, 2, 3)]
        return remote(part, part, self.send.at[2 + j], self.recv.at[2 + j], places[j])

    def begin(self, value):
        self.small[0] = value
        self.to_sibling().start()

    def step(self, n, value=None):
        if n == 0:
            self.to_sibling().wait_recv()
            self.small[2] = value + self.small[1]
            self.to_mate().start()
        else:
            self.to_mate().wait_recv()
            self.group[4 * self.spot.half + self.spot.q] = self.small[2] + self.small[3]
            for j in range(7):
                self.to_group(j).start()

    def finish(self, out):
        for j in range(7):
            self.to_group(j).wait_recv()
        total = self.group[0, :, 2 * PIECE :]
        for n in range(1, 8):
            total += self.group[n, :, 2 * PIECE :]
        for half in range(2):
            for j in range(2):
                for q in range(4):
                    at = (8 * half + 4 * j + q) * PIECE
                    out[:, at : at + PIECE] = self.group[4 * half + q, :, j * PIECE : (j + 1) * PIECE]
        out[:, -SHARED:] = total[:, :SHARED]
        out[7:8, DT_AT : DT_AT + HEADS] = total[7:8, :HEADS]
        out[7:8, RATE_AT : RATE_AT + HEADS] = total[7:8, LANES : LANES + HEADS]
        for r in range(8):
            out[7:8, r * THIRD : (r + 1) * THIRD] = total[r : r + 1, PIECE : PIECE + THIRD]
        self.to_sibling().wait_send()
        self.to_mate().wait_send()
        for j in range(7):
            self.to_group(j).wait_send()


def loading(sources, targets, sems):
    return [pltpu.make_async_copy(a, b, sems.at[n]) for n, (a, b) in enumerate(zip(sources, targets))]


def saved_shapes(length, width, wide):
    columns = ((width, BF16), (wide, F32), (wide, BF16), (SHARED, BF16), (LANES, BF16), (wide, BF16))
    return [((2, length, n), t) for n, t in columns]


def middle_kernel(heads, *refs):
    ins, outs, kept, weight_s, sum_s, spread_s, layer_s, (store,) = take(refs, (7, 6, 6, 5, 5, 3, 11, 1))
    w_in, w_out, *layer_ins, rows_in = ins
    tile, tile_out, all_rows, branch, scales, rows_out = outs
    u, w, wo, pack, *saved, load = layer_s
    spot = Spot()
    rows_in = rows_in.at[spot.s]
    weights = Weights(spot, 1, w_in, w_out, tile, tile_out, weight_s)
    total = Sum(spot, rows_in.shape[1], sum_s)
    spread = Spread(spot, rows_out, all_rows, spread_s)
    loads = loading(layer_ins[:3] + [layer_ins[3].at[0]], layer_s[:4], load)
    for copy in loads:
        copy.start()
    weights.begin()
    greet(all_places(spot))
    few = 3
    weights.start(few)
    for copy in loads:
        copy.wait()
    params = load_params(([spot.piece(spot.half, j) for j in range(2)], pack))

    @pl.loop(0, 2)
    def _(i):
        forward_rows(heads, params, total.half(i), u, w, wo, None, [total.parts, None, *saved])
        total.start(i)


        @pl.when(i == 0)
        def _():
            weights.more(3, few)
            weights.more(4, few)

    stores = loading(saved, kept, store)
    for copy in stores:
        copy.start()
    weights.more(5, few)
    total.forward()
    weights.relay(0)
    weights.relay(1)
    weights.relay(2)
    weights.share()
    layer_rows(total.finish(), rows_in, branch, scales, rows_out)
    spread.start()
    weights.shared()
    weights.relay(3)
    spread.forward()
    weights.relay(4)
    weights.relay(5)
    weights.relay_mate()
    spread.finish()
    total.close()
    weights.finish(few)
    for copy in stores:
        copy.wait()


class RowSums:
    @staticmethod
    def scratch(length):
        shape = (2, 8, length)
        return [pltpu.VMEM(shape, F32), pltpu.VMEM((7,) + shape, F32), DMA((14,)), DMA((14,))]

    def __init__(self, spot, scratch):
        self.mine, self.others, self.send, self.recv = scratch
        self.places = [spot.plane(k) for k in (1, 2, 3)] + [spot.at_twin]
        self.places += [(spot.s, spot.around[k], spot.twin) for k in (1, 2, 3)]

    def copies(self, seq):
        return [
            remote(
                self.mine.at[seq], self.others.at[j, seq],
                self.send.at[2 * j + seq], self.recv.at[2 * j + seq], place,
            )
            for j, place in enumerate(self.places)
        ]

    def start(self, seq):
        for copy in self.copies(seq):
            copy.start()

    def finish(self, seq):
        total = self.mine[seq]
        for j, copy in enumerate(self.copies(seq)):
            copy.wait_recv()
            total += self.others[j, seq]
        for copy in self.copies(seq):
            copy.wait_send()
        self.mine[seq] = total


def back_kernel(heads, *refs):
    ins, outs, first_s, last_s, second_s, spread_s, row_s, back_s, layer_s, grads_s, results, around_s, own_s, rest = take(
        refs, (18, 5, 5, 6, 6, 3, 4, 6, 11, 7, 3, 4, 4, 10)
    )
    (all_rows, all_cot, packs), tiles, kept, own_ins = take(ins, (3, 4, 6, 5))
    first_rows, tokens, grad_out, branch, scales = own_ins
    home_rows, home_grads, final, final_out, small_out = outs
    u, w, wo, pack, *saved, load = layer_s
    h_rows, h_next, payload, last_rows, last_grad, first_grad, small, send, recv, local = rest
    proj_grad, normed_out, *scratch = back_s
    spot = Spot()
    tokens, grad_out = tokens.at[spot.s], grad_out.at[spot.s]
    width = first_rows.shape[1]
    total = Sum(spot, width, first_s)
    last = RelaySum(spot, width, last_s)
    second = RelaySum(spot, width, second_s)
    spread = Spread(spot, payload, h_next, spread_s)
    sums = RowSums(spot, row_s)
    grads = Grads(spot, results, grads_s)
    around = GradsAround(spot, results, final, final_out, around_s)
    own = SmallSum(spot, own_s)
    first_core, last_core = pl.when(spot.s == 0), pl.when(spot.s == 1)
    loads = loading([all_rows, *tiles[2:], packs, all_cot], [u, w, wo, pack, h_rows], load)
    reloads = loading([*tiles[:2], *kept], [w, wo, *saved], load)
    for copy in loads:
        copy.start()
    places = [spot.plane(k) for k in (1, 2, 3)] + [spot.column((spot.z + k) % 4) for k in (1, 2, 3)]
    places += [(spot.s, spot.around[k], spot.twin) for k in (1, 2, 3)] + [spot.sibling]
    greet(places)
    for copy in loads:
        copy.wait()
    ids = [spot.piece(spot.half, j) for j in range(2)]
    params = load_params((ids, pack.at[1]))

    @pl.loop(0, 2)
    def _(i):
        seq = last.half(i)
        forward_rows(heads, params, seq, u, w, wo, h_rows, [last.parts, sums.mine, *saved])
        sums.start(seq)
        last.start(i)

    last.go_on(0)

    def backward(layer, params, total, h_ref, aux_of, order):
        small[layer] = jnp.zeros(small.shape[1:], F32)

        @pl.loop(0, 2)
        def _(n):
            i = order(n)
            seq = total.half(i)
            outs = (total.parts, proj_grad, normed_out)
            parts = backward_rows(
                heads, params, seq, h_ref, lambda: aux_of(n, seq), saved[1:], w, wo, outs, scratch
            )
            add_small(small.at[layer], *parts)
            total.start(i)

    def row_aux(n, seq):

        @pl.when(n == 1)
        def _():
            last.go_on(1)
            last.forward()

        sums.finish(seq)
        return aux_of_rows(sums.mine[seq])

    def column_aux(n, seq):
        pl.when(n == 0)(spread.own_half)

        @pl.when((n == 1) & (spot.s == 1))
        def _():
            own.step(1)
            grads.to_planes(5)
            grads.pass_on(1)
            grads.gather(4)
            around.shared_step(0)

        pl.when(n == 1)(spread.other_half)
        return aux_of_columns(h_next, seq, width)

    backward(1, params, total, h_rows, row_aux, lambda n: n)

    def product(layer, n):
        grads.product(layer, n, proj_grad, saved[0], normed_out, h_rows if layer else h_next)

    product(1, 4)
    product(1, 0)
    total.forward()
    last_core(lambda: grads.to_planes(4))
    for n in (1, 2, 3, 5):
        product(1, n)
    last_core(lambda: grads.to_planes(0))
    for copy in reloads:
        copy.start()
    grad, last_gain = norm_back(total.finish(), first_rows, pack[1, 7:8, :width], grad_out)
    low = grad.astype(BF16)
    last_grad[...] = low
    cross = jnp.sum(low.astype(F32) * branch[...], axis=1, keepdims=True)
    payload[:, :width] = low
    lanes = lax.broadcasted_iota(jnp.int32, (payload.shape[0], LANES), 1)
    scale_part = split_three(scales[:, 0:1]).astype(F32)
    cross_part = pltpu.roll(split_three(cross).astype(F32), 3, 1)
    payload[:, width:] = jnp.where(lanes < 3, scale_part, cross_part).astype(BF16)
    spread.start()
    add_gain(small.at[1], last_gain)
    first_core(lambda: own.begin(small[1]))

    @last_core
    def _():
        grads.pass_on(4)
        grads.to_planes(1)

    spread.forward()

    @last_core
    def _():
        own.step(0, small[1])
        grads.pass_on(0)
        for n in (2, 3):
            grads.to_planes(n)

    for copy in reloads:
        copy.wait()
    params = load_params((ids, pack.at[0]))
    backward(0, params, second, h_next, column_aux, lambda n: 1 - n)

    @last_core
    def _():
        grads.gather(0)
        around.send_part(0)
        grads.pass_on(2)

    for n in Grads.ORDER:
        product(0, n)
    second.go_on(1)
    second.go_on(0)

    @first_core
    def _():
        for n in (4, 0, 1):
            grads.to_planes(n)
        grads.pass_on(4)
        for n in (5, 2):
            grads.to_planes(n)
        grads.pass_on(0)
        grads.gather(4)
        around.shared_step(0)
        grads.to_planes(3)
        grads.pass_on(1)
        grads.gather(0)
        around.send_part(0)

    @last_core
    def _():
        grads.gather(1)
        around.send_part(1)
        grads.pass_on(3)

    second.forward()

    @first_core
    def _():
        grads.pass_on(2)
        grads.gather(5)
        around.send_out()
        grads.gather(1)
        around.send_part(1)
        around.shared_step(1)
        around.pass_part(0)
        grads.pass_on(3)

    @last_core
    def _():
        grads.gather(5)
        around.send_out()
        grads.gather(2)
        around.send_part(2)
        around.pass_part(0)
        grads.gather(3)
        around.send_part(3)
        around.shared_step(1)
        around.pass_part(1)

    grad, first_gain = norm_back(second.finish(), tokens, pack[0, 7:8, :width], last_grad)
    first_grad[...] = grad.astype(BF16)
    layers = ((first_rows, first_grad), (last_rows, last_grad))

    def home_copies(s):
        copies = []
        for n, target in enumerate((home_rows, home_grads)):
            copies.append(remote(layers[1 - s][n], target.at[s], send.at[n], recv.at[n], spot.sibling))
            copies.append(pltpu.make_async_copy(layers[s][n], target.at[s], local.at[n]))
        return copies

    add_gain(small.at[0], first_gain)
    last_core(lambda: own.begin(small[0]))

    @first_core
    def _():
        grads.gather(2)
        around.send_part(2)
        own.step(0, small[0])
        grads.gather(3)
        around.send_part(3)
        around.pass_out()
        around.pass_part(1)
        own.step(1)
        around.pass_part(2)
        around.shared_step(2)

    layer_rows(last.finish(), first_rows, None, None, last_rows)
    for s in range(2):

        @pl.when(spot.s == s)
        def _(s=s):
            for copy in home_copies(s):
                copy.start()

    first_core(lambda: around.pass_part(3))

    @last_core
    def _():
        around.pass_out()
        for n in (2, 3):
            around.pass_part(n)
        around.shared_step(2)

    own.finish(small_out)
    around.finish()
    for n in range(5):
        grads.sent(n)
    grads.finish()
    for s in range(2):

        @pl.when(spot.s == s)
        def _(s=s):
            for copy in home_copies(s):
                copy.wait()

    total.close()
    last.close()
    second.close()
    spread.close()


def comm_call(kernel, collective, ins, in_specs, outs, out_specs, scratch, name):
    return pl.pallas_call(
        kernel,
        out_shape=[jax.ShapeDtypeStruct(s, t) for s, t in outs],
        in_specs=in_specs,
        out_specs=out_specs,
        scratch_shapes=scratch,
        compiler_params=pltpu.CompilerParams(
            collective_id=collective, has_side_effects=True, vmem_limit_bytes=60 * 1024 * 1024
        ),
        name=name,
    )(*ins)


def fast_shards(
    tokens, cotangent, norm_gain, w_in, conv_weight, conv_bias, dt_bias, a_log, skip_gain, gate_gain, w_out
):
    span, width = tokens.shape[2:]
    heads = HEADS // 8
    wide = heads * HEADDIM
    columns = 2 * wide + SHARED + HEADS
    shard = w_in.shape[1]
    rows_in = w_in[0].T
    pack_shape = (8, INNER // THIRD * PIECE + SHARED)
    group = (2, 4 * span, width)
    weight_outs = [((columns, width), BF16), ((wide, width), BF16)]
    weight_s = Weights.scratch(columns, shard, width)
    payload = width + LANES
    tile, tile_out, packs, all_rows, all_cot = comm_call(
        open_kernel, 1,
        [
            rows_in, w_out[0], tokens[:, 0], cotangent[:, 0], conv_weight[0], conv_bias, gate_gain, skip_gain,
            norm_gain, dt_bias, a_log,
        ],
        [ANY] * 4 + [VMEM] * 7,
        weight_outs + [((2,) + pack_shape, F32), (group, BF16), (group, BF16)], [ANY] * 5,
        weight_s + Spread.SEMS + Spread.SEMS
        + [pltpu.VMEM((span, width), BF16)] * 2 + [pltpu.VMEM(pack_shape, F32), DMA((2,)), DMA, DMA, DMA],
        "open",
    )
    length = 4 * span
    rows_spec = ((span, width), BF16)
    layer_s = [
        pltpu.VMEM((2, length, width), BF16), pltpu.VMEM((columns, width), BF16),
        pltpu.VMEM((wide, width), BF16), pltpu.VMEM(pack_shape, F32),
    ]
    kept_shapes = saved_shapes(length, width, wide)
    kept_s = [pltpu.VMEM(*k) for k in kept_shapes]
    back_s = [pltpu.VMEM((2, length, columns), BF16), pltpu.VMEM((2, length, wide), BF16)]
    back_s += backward_scratch(length, wide)
    results = Grads.results(shard, width)
    sum_s = Sum.scratch(span, width)
    first_tiles = [tile, tile_out]
    tile, tile_out, all_rows, branch, scales, rows, *kept = comm_call(
        partial(middle_kernel, heads), 2,
        [rows_in, w_out[0], all_rows, tile, tile_out, packs, tokens[:, 0]], [ANY] * 6 + [VMEM],
        weight_outs + [(group, BF16), ((span, width), F32), ((span, LANES), F32), rows_spec] + kept_shapes,
        [ANY] * 3 + [VMEM] * 3 + [ANY] * 6,
        weight_s + Sum.scratch(span, payload) + Spread.SEMS + layer_s + kept_s + [DMA((4,)), DMA((6,))],
        "middle",
    )
    home_rows, home_grads, final, final_out, small = comm_call(
        partial(back_kernel, heads), 3,
        [
            all_rows, all_cot, packs, *first_tiles, tile, tile_out, *kept,
            rows, tokens[:, 0], cotangent[:, 0], branch, scales,
        ],
        [ANY] * 13 + [VMEM] * 5,
        [
            ((2, span, width), BF16), ((2, span, width), BF16),
            ((2 * INNER + SHARED + HEADS, shard), BF16), (w_out.shape[1:], BF16), (pack_shape, F32),
        ],
        [ANY] * 4 + [VMEM],
        sum_s + RelaySum.scratch(span, payload) + RelaySum.scratch(span, width) + Spread.SEMS + RowSums.scratch(length) + back_s
        + layer_s[:3] + [pltpu.VMEM((2,) + pack_shape, F32)] + kept_s + [DMA((8,))]
        + Grads.scratch(shard, columns, wide, width) + [pltpu.VMEM(*r) for r in results]
        + GradsAround.scratch(shard) + SmallSum.scratch()
        + [
            pltpu.VMEM((2, length, width), BF16), pltpu.VMEM((2, length, payload), BF16),
            pltpu.VMEM((span, payload), BF16), *[pltpu.VMEM((span, width), BF16)] * 3,
            pltpu.VMEM((2,) + SmallSum.SHAPE, F32), DMA((2,)), DMA((2,)), DMA((2,)),
        ],
        "back",
    )
    home_rows, home_grads, grad_in, grad_out, gain, conv, bias, shift, rate, skip, gate = finish_call(
        home_rows, home_grads, final, final_out, small
    )
    return (
        home_rows[None, :, None], home_grads[None, :, None], gain, grad_in.T[None], conv[None],
        bias, shift, rate, skip, gate, grad_out[None],
    )


def finish_kernel(
    rows_in, grads_in, final, final_out, small, rows_out, grads_out, grad_in, grad_out, gain, conv, bias, shift, rate, skip, gate
):
    grad_in[...] = final[...].astype(F32)
    step = pl.program_id(0)
    grad_out[...] = final_out[...].astype(F32)

    @pl.when(step == 0)
    def _():
        rows_out[...] = rows_in[...]
        grads_out[...] = grads_in[...]
        gain[...] = small[7:8, :GAIN_END]
        shift[...] = small[7:8, DT_AT : DT_AT + HEADS]
        rate[...] = small[7:8, RATE_AT : RATE_AT + HEADS]
        heads = []
        for p in range(INNER // THIRD):
            source, target = slice(p * PIECE, p * PIECE + THIRD), slice(p * THIRD, (p + 1) * THIRD)
            conv[:, target] = small[0:CONV, source]
            bias[:, target] = small[CONV : CONV + 1, source]
            gate[:, target] = small[6:7, source]
            for h in range(3):
                part = small[5:6, p * PIECE + h * HEADDIM : p * PIECE + (h + 1) * HEADDIM]
                heads.append(jnp.sum(part, axis=1, keepdims=True))
        skip[...] = jnp.concatenate(heads, axis=1)
        conv[:, INNER:] = small[0:CONV, -SHARED:]
        bias[:, INNER:] = small[CONV : CONV + 1, -SHARED:]


def finish_call(home_rows, home_grads, final, final_out, small):
    rows, shard = final.shape
    out_rows, width = final_out.shape
    steps = 3
    block, out_block = -(-rows // (16 * steps)) * 16, out_rows // steps
    smalls = [(1, GAIN_END), (CONV, XBC), (1, XBC), (1, HEADS), (1, HEADS), (1, HEADS), (1, INNER)]

    def in_block(i):
        return (i, 0)

    def same(i):
        return (0, 0)

    def same3(i):
        return (0, 0, 0)

    return pl.pallas_call(
        finish_kernel,
        grid=(steps,),
        out_shape=[jax.ShapeDtypeStruct(home_rows.shape, BF16)] * 2
        + [jax.ShapeDtypeStruct(s, F32) for s in [final.shape, final_out.shape] + smalls],
        in_specs=[
            pl.BlockSpec(home_rows.shape, same3),
            pl.BlockSpec(home_rows.shape, same3),
            pl.BlockSpec((block, shard), in_block),
            pl.BlockSpec((out_block, width), in_block),
            pl.BlockSpec(small.shape, same),
        ],
        out_specs=[
            pl.BlockSpec(home_rows.shape, same3),
            pl.BlockSpec(home_rows.shape, same3),
            pl.BlockSpec((block, shard), in_block),
            pl.BlockSpec((out_block, width), in_block),
        ]
        + [pl.BlockSpec(s, same) for s in smalls],
        compiler_params=pltpu.CompilerParams(**PARAMS),
        name="finish",
    )(home_rows, home_grads, final, final_out, small)


def shards(
    tokens, cotangent, norm_gain, w_in, conv_weight, conv_bias, dt_bias, a_log, skip_gain, gate_gain, w_out
):
    section = lax.axis_index("section")
    place = lax.axis_index("seq")
    depth = lax.axis_index("fsdp")
    plan = Plan(lax.axis_size("seq"), lax.axis_size("fsdp"))
    half = depth // plan.mates
    micro, _, span, width = tokens.shape
    layers = lax.axis_size("section")
    wide, channels, heads = plan.wide, plan.channels, plan.heads

    shard = w_in[0]
    gate_part = widened(plan.take(shard[:, :INNER], 1, place), 2, wide)
    x_part = widened(plan.take(shard[:, INNER : 2 * INNER], 1, place), 2, wide)
    shared_part = jnp.broadcast_to(
        shard[:, 2 * INNER : INNER + XBC], (plan.halves, shard.shape[0], SHARED)
    )
    dt_part = widened(plan.take(shard[:, INNER + XBC :], 1, place), 2, LANES)
    tile = jnp.concatenate([gate_part, x_part, shared_part, dt_part], axis=2)
    tile = jnp.repeat(tile, plan.mates, axis=0)
    tile = lax.all_to_all(tile, "fsdp", 0, 0, tiled=True).reshape(width, -1).T
    w_tiles = lax.all_gather(tile, "section", axis=0)
    if plan.pieces == plan.mates:
        piece = w_out[0].reshape(plan.seq, -1, width)
        piece = lax.dynamic_index_in_dim(piece, place, 0, False)
        rows_out = lax.all_gather(
            piece, "fsdp", axis=0, tiled=True, axis_index_groups=plan.mate_groups
        )
    else:
        rows_out = lax.all_gather(w_out[0], "fsdp", axis=0, tiled=True)
        rows_out = lax.dynamic_index_in_dim(plan.take(rows_out, 0, place), half, 0, False)
    wo_tiles = lax.all_gather(widened(rows_out, 0, wide), "section", axis=0)

    def own(array, axis, size):
        part = lax.dynamic_index_in_dim(plan.take(array, axis, place), half, 0, False)
        return widened(part, axis, size)

    skip_wide = jnp.repeat(skip_gain[0], HEADDIM)[None]
    by_channel = jnp.concatenate(
        [conv_weight[0, :, :INNER], conv_bias[:, :INNER], skip_wide, gate_gain, jnp.zeros((1, INNER))], 0
    )
    by_channel = own(by_channel, 1, wide)
    by_shared = jnp.concatenate(
        [conv_weight[0, :, INNER:], conv_bias[:, INNER:], jnp.zeros((3, SHARED))], 0
    )
    by_head = jnp.concatenate([dt_bias, a_log, jnp.zeros((6, HEADS))], 0)
    by_head = own(by_head, 1, LANES)
    smalls = jnp.concatenate(
        [by_channel.ravel(), by_shared.ravel(), by_head.ravel(), norm_gain[0]]
    )
    smalls = lax.all_gather(smalls, "section", axis=0)
    cuts = [8 * wide, 8 * (wide + SHARED), 8 * (wide + SHARED + LANES)]
    params = []
    for l in range(layers):
        ch, bc, dtp, gain = jnp.split(smalls[l], cuts)
        params.append((gain[None], ch.reshape(8, -1), bc.reshape(8, -1), dtp.reshape(8, -1)))

    def gather_rows(own_rows):
        rows = lax.all_gather(own_rows, "seq", axis=0, tiled=True)
        if plan.halves == 1:
            return rows[None]
        return lax.all_gather(rows, "fsdp", axis=0, axis_index_groups=plan.peer_groups)

    def sum_rows(parts):
        if plan.halves == 1:
            rows = parts[0]
        else:
            rows = lax.psum_scatter(
                parts, "fsdp", scatter_dimension=0, axis_index_groups=plan.peer_groups
            )
        return lax.psum_scatter(rows, "seq", scatter_dimension=0, tiled=True)

    own_tokens = lax.dynamic_index_in_dim(tokens, section, 0, False)[0]
    own_cot = lax.dynamic_index_in_dim(cotangent, section, 0, False)[0]
    inputs, outputs, branch, saved, scales = [own_tokens], [], [], [], []
    for l in range(layers):
        rows = gather_rows(inputs[l])
        parts, square, normed, *kept = run_forward(
            heads, wide, rows, w_tiles[l], wo_tiles[l], params[l]
        )
        saved.append((normed, kept))
        total = sum_rows(parts).astype(F32)
        square = sum_rows(square)[:, :1]
        scale = lax.rsqrt(square / INNER + NORM_EPS)
        branch.append(total * scale)
        scales.append(scale)
        outputs.append((inputs[l].astype(F32) + branch[l]).astype(BF16))
        inputs.append(outputs[l])
    grads_in, small_grads = [None] * layers, [None] * layers
    w_grads, wo_grads = [None] * layers, [None] * layers
    grad_rows = own_cot
    for l in reversed(range(layers)):
        rdot = jnp.sum(grad_rows.astype(F32) * branch[l], axis=-1, keepdims=True)
        aux = widened(jnp.concatenate([scales[l], rdot], axis=1), 1, LANES)
        all_grads = gather_rows(grad_rows)
        aux = gather_rows(aux)
        normed, kept = saved[l]
        parts, proj_grad, normed_out, g_ch, g_bc, g_dt = run_backward(
            heads, wide, all_grads, aux, kept, w_tiles[l], wo_tiles[l], params[l]
        )
        w_grads[l] = dot_tn(normed.reshape(-1, width), proj_grad.reshape(-1, proj_grad.shape[-1])).astype(BF16)
        wo_grads[l] = dot_tn(normed_out.reshape(-1, wide), all_grads.reshape(-1, width)).astype(BF16)
        grad_normed = sum_rows(parts).astype(F32)
        rows = inputs[l].astype(F32)
        scale = lax.rsqrt(jnp.mean(rows * rows, axis=-1, keepdims=True) + NORM_EPS)
        scaled = rows * scale
        g_gain = jnp.sum(grad_normed * scaled, axis=0)
        pulled = grad_normed * params[l][0]
        inner = jnp.mean(pulled * scaled, axis=-1, keepdims=True)
        grad = scale * (pulled - scaled * inner) + grad_rows.astype(F32)
        grad_rows = grad.astype(BF16)
        grads_in[l] = grad_rows

        def placed(value, size):
            value = value[..., :size]
            full = jnp.zeros((plan.seq, plan.halves) + value.shape, F32)
            full = lax.dynamic_update_slice(full, value[None, None], (place, half, 0, 0))
            return plan.put(full, 1)

        by_channel = placed(g_ch, channels)
        by_head = placed(g_dt, heads)
        skip = by_channel[5].reshape(HEADS, HEADDIM).sum(-1)
        small_grads[l] = jnp.concatenate(
            [
                g_gain, by_channel[:5].ravel(), g_bc[:5].ravel(), by_head[0], by_head[1], skip, by_channel[6]
            ]
        )

    smalls = lax.psum(jnp.stack(small_grads), ("section", "seq", "fsdp"))
    smalls = lax.dynamic_index_in_dim(smalls, section, 0, False)
    cuts, at = [], 0
    for size in (width, (CONV + 1) * INNER, (CONV + 1) * SHARED, HEADS, HEADS, HEADS):
        at += size
        cuts.append(at)
    g_gain, g_x, g_bc, g_shift, g_rate, g_skip, g_gate = jnp.split(smalls, cuts)
    conv_rows = jnp.concatenate([g_x.reshape(CONV + 1, -1), g_bc.reshape(CONV + 1, -1)], axis=1)

    w_grad = lax.psum_scatter(jnp.stack(w_grads), "section", scatter_dimension=0)
    w_grad = lax.all_to_all(w_grad, "fsdp", 0, 0, tiled=True)
    w_grad = w_grad.reshape(plan.halves, plan.mates, -1, w_grad.shape[-1]).astype(F32).sum(1)
    shared_grad = lax.psum(w_grad[..., 2 * wide : 2 * wide + SHARED].sum(0), "seq")
    head_grads = jnp.concatenate(
        [
            w_grad[..., :channels],
            w_grad[..., wide : wide + channels],
            w_grad[..., 2 * wide + SHARED : 2 * wide + SHARED + heads],
        ],
        axis=-1,
    ).astype(BF16)
    head_grads = lax.all_gather(head_grads, "seq", axis=0)
    grad_w_in = jnp.concatenate(
        [
            plan.put(head_grads[..., :channels], 1),
            plan.put(head_grads[..., channels : 2 * channels], 1),
            shared_grad.astype(BF16),
            plan.put(head_grads[..., 2 * channels :], 1),
        ],
        axis=-1,
    ).astype(F32)
    wo_grad = lax.psum_scatter(jnp.stack(wo_grads)[:, :channels], "section", scatter_dimension=0)
    if plan.pieces == plan.mates:
        wo_grad = lax.psum_scatter(
            wo_grad, "fsdp", scatter_dimension=0, tiled=True, axis_index_groups=plan.mate_groups
        )
        wo_grad = lax.all_gather(wo_grad, "seq", axis=0, tiled=True)
    else:
        full = jnp.zeros((plan.seq, plan.halves) + wo_grad.shape, BF16)
        full = lax.dynamic_update_slice(full, wo_grad[None, None], (place, half, 0, 0))
        full = plan.put(full, 0)
        wo_grad = lax.psum_scatter(full, "fsdp", scatter_dimension=0, tiled=True)
        wo_grad = lax.psum(wo_grad, "seq")

    def home(per_layer):
        return lax.all_to_all(jnp.stack(per_layer), "section", 0, 0, tiled=True)[None, :, None]

    return (
        home(outputs),
        home(grads_in),
        g_gain[None],
        grad_w_in[None],
        conv_rows[None, :CONV],
        conv_rows[CONV:],
        g_shift[None],
        g_rate[None],
        g_skip[None],
        g_gate[None],
        wo_grad.astype(F32)[None],
    )


def solution(mesh):
    shape = tuple(mesh.shape[a] for a in ("section", "seq", "fsdp"))
    return jax.shard_map(
        fast_shards if shape == (2, 4, 4) else shards,
        mesh=mesh,
        in_specs=(
            P(None, "fsdp", "seq", None),
            P(None, "fsdp", "seq", None),
            P("section", None),
            P("section", "fsdp", None),
            P("section", None, None),
            P("section", None),
            P("section", None),
            P("section", None),
            P("section", None),
            P("section", None),
            P("section", "fsdp", None),
        ),
        out_specs=(
            P("section", None, "fsdp", "seq", None),
            P("section", None, "fsdp", "seq", None),
            P("section", None),
            P("section", "fsdp", None),
            P("section", None, None),
            P("section", None),
            P("section", None),
            P("section", None),
            P("section", None),
            P("section", None),
            P("section", "fsdp", None),
        ),
        check_vma=False,
    )
```
